32 devices in a mesh: fsdp: 32 (over z, y, x, core).
Axes of the slice: x: 2, y: 2, z: 4, core: 2. Of those that a mesh axis runs over, the one named last changes fastest.
Arguments:
- latents: float32 [64, 256, 16], P('fsdp'), may hold values from -6 to 6
- noise: float32 [64, 256, 16], P('fsdp'), may hold values from -6 to 6
- times: float32 [64], P('fsdp'), may hold values from 0 to 1, as said below
- labels: int32 [64], P('fsdp'), may hold values from 0 to 999
- dropped: int32 [64], P('fsdp'), may hold values 0 or 1
- features: bfloat16 [64, 256, 768], P('fsdp'), may hold values from -6 to 6
- layer_flat: float32 [2, 10627584], P(None, 'fsdp'), may hold values from -0.21875 to 0.21875
- layer_mean: float32 [2, 10627584], P(None, 'fsdp'), may hold values from -1.4284782e-06 to 1.4284782e-06
- layer_square: float32 [2, 10627584], P(None, 'fsdp'), may hold values from 1.2753436e-13 to 5.1013745e-13
- root_flat: float32 [10108928], P('fsdp'), may hold values from -0.21875 to 0.21875
- root_mean: float32 [10108928], P('fsdp'), may hold values from -1.4284782e-06 to 1.4284782e-06
- root_square: float32 [10108928], P('fsdp'), may hold values from 4.0810996e-12 to 1.6324398e-11
Outputs:
- loss_sum: float32 [], replicated
- grad_norm: float32 [], replicated
- activation_rms: float32 [2, 3], replicated
- new_layer: float32 [2, 10627584], P(None, 'fsdp')
- new_layer_mean: float32 [2, 10627584], P(None, 'fsdp')
- new_layer_square: float32 [2, 10627584], P(None, 'fsdp')
- new_root: float32 [10108928], P('fsdp')
- new_root_mean: float32 [10108928], P('fsdp')
- new_root_square: float32 [10108928], P('fsdp')
The draws below stay inside these ranges and needn't reach their ends.
Inputs may be any that keep to these rules, and one draw needn't show every extreme that they name: `times`: sample s has its time in [s / 64, (s + 1) / 64).
All inputs are finite; a program needn't handle non-finite values. No bound on the sum of `dropped` on one device may be relied on, other than what follows from the above.
Results may differ from the reference program's by a relative error of at most 0.0052.
Values may be sent and summed in bfloat16 or wider, within the bound.
A program may use at most 704 MiB of HBM per device.

```python
import math
import jax
import jax.numpy as jnp
from jax import lax

D = 768
HD = 64
FF = 3072
PD = 16
CLS = 1001
PH = 2048
ZD = 768
FREQ = 256
GRID = 16
LAYERS = 2
DEPTH_Z = 2
STEP = 10
SEQ = 256
SAMPLES = 64
PL = 10627584
ROOT = 10108928


def draw_times(key, part):
    key = jax.random.fold_in(key, 7)
    offsets = jax.random.uniform(key, (SAMPLES,), jnp.float32)
    return (jnp.arange(SAMPLES, dtype=jnp.float32) + offsets) / SAMPLES


def draw_features(key, part):
    key = jax.random.fold_in(key, 11)
    sign_key, size_key, token_key = jax.random.split(key, 3)
    signs = jnp.where(jax.random.bernoulli(sign_key, 0.5, (ZD,)), 1.0, -1.0).astype(jnp.float32)
    common = signs * jax.random.uniform(size_key, (ZD,), jnp.float32, 1.5, 2.5)
    own = jax.random.normal(token_key, (SAMPLES, SEQ, ZD), jnp.float32)
    return jnp.clip(common[None, None, :] + own, -6.0, 6.0).astype(jnp.bfloat16)


def with_ends(values, key, least, largest):
    spot = [jax.random.randint(jax.random.fold_in(key, axis), (), 0, length) for axis, length in enumerate(values.shape)]
    widest = values.shape.index(max(values.shape))
    neighbour = spot[:widest] + [(spot[widest] + 1) % values.shape[widest]] + spot[widest + 1:]
    return values.at[tuple(spot)].set(least).at[tuple(neighbour)].set(largest)


def steps_of(rng, shape, cuts, least, top_value):
    def one(axis_at, blocks):
        heights = jax.random.uniform(jax.random.fold_in(jax.random.fold_in(rng, 6), axis_at), (blocks,), jnp.float32, least / len(cuts), top_value / len(cuts))
        return jnp.repeat(jnp.exp(heights), shape[axis_at] // blocks).reshape((-1,) + (1,) * (len(shape) - axis_at - 1))

    factor_of = one(*cuts[0])
    for cut in cuts[1:]:
        factor_of = factor_of * one(*cut)
    return factor_of


def scatter_about(own_key, extent, width, reach, shards=(), kind=jnp.bfloat16):
    array = jax.random.normal(own_key, extent, jnp.float32) * width
    if len(shards) > 0:
        array = steps_of(own_key, extent, shards, -0.22, 0.18) * array
    return jnp.clip(array, min=-reach, max=reach).astype(kind)


def setup_inputs(seed: int = 0) -> dict:
    keys = jax.random.split(jax.random.key(seed), 13)
    latents = scatter_about(keys[0], (SAMPLES, SEQ, PD), 1.0, 6.0, ((0, 32),), jnp.float32)
    noise = scatter_about(keys[1], (SAMPLES, SEQ, PD), 1.0, 6.0, ((0, 32),), jnp.float32)
    times = draw_times(jax.random.fold_in(keys[12], 71), 0)
    labels = with_ends(jax.random.randint(keys[3], (SAMPLES,), 0, CLS - 1), jax.random.fold_in(keys[3], 1), 0, (CLS - 1) - 1).astype(jnp.int32)
    dropped = with_ends((jax.random.randint(keys[4], (SAMPLES,), 0, 10) < 1).astype(jnp.int32), jax.random.fold_in(keys[4], 1), 0, 1)
    features = draw_features(jax.random.fold_in(keys[12], 71), 0)
    layer_flat = scatter_about(keys[6], (LAYERS, PL), D ** -0.5, 0.21875, ((1, 32),), jnp.float32)
    layer_mean = scatter_about(keys[7], (LAYERS, PL), (0.002 * (LAYERS * PL + ROOT) ** -0.5), 1.428478185516724e-06, ((1, 32),), jnp.float32)
    layer_square = jnp.clip(jnp.exp(math.log(5.101374509451639e-13) - 1.3862944 * jax.random.uniform(keys[8], (LAYERS, PL), jnp.float32) ** steps_of(keys[8], (LAYERS, PL), ((1, 32),), -0.2, 0.2)), 1.2753436273629098e-13, 5.101374509451639e-13)
    root_flat = scatter_about(keys[9], (ROOT,), D ** -0.5, 0.21875, ((0, 32),), jnp.float32)
    root_mean = scatter_about(keys[10], (ROOT,), (0.002 * (LAYERS * PL + ROOT) ** -0.5), 1.428478185516724e-06, ((0, 32),), jnp.float32)
    root_square = jnp.clip(jnp.exp(math.log(1.6324398430245246e-11) - 1.3862944 * jax.random.uniform(keys[11], (ROOT,), jnp.float32) ** steps_of(keys[11], (ROOT,), ((0, 32),), -0.2, 0.2)), 4.0810996075613115e-12, 1.6324398430245246e-11)
    return dict(latents=latents, noise=noise, times=times, labels=labels, dropped=dropped, features=features, layer_flat=layer_flat, layer_mean=layer_mean, layer_square=layer_square, root_flat=root_flat, root_mean=root_mean, root_square=root_square)


@jax.custom_vjp
def low(v):
    return lax.optimization_barrier(v.astype(jnp.bfloat16)).astype(jnp.float32)

@jax.custom_vjp
def low_back(v):
    return v

def low_keep(v):
    return (low(v), None)

def low_pass(kept, grad):
    return (grad,)

def back_keep(v):
    return (v, None)

def back_low(kept, grad):
    return (low(grad),)
low.defvjp(low_keep, low_pass)
low_back.defvjp(back_keep, back_low)
norm_eps = 1e-06
clip_limit = 0.002
learn_rate = 0.08
beta_one = 0.5
beta_two = 0.5
adam_eps = 1e-08
decay_rate = 0.01
proj_coeff = 0.5
highest = lax.Precision.HIGHEST

def layer_layout():
    return [(D, 3 * D), (D, D), (D, FF), (FF, D), (D, 6 * D), (D,), (D,), (D,), (FF,), (D,), (6 * D,)]

def root_layout():
    return [(PD, D), (D,), (FREQ, D), (D,), (D, D), (D,), (CLS, D), (D, PH), (PH,), (PH, PH), (PH,), (PH, ZD), (ZD,), (D, 2 * D), (2 * D,), (D, PD), (PD,)]

def unflatten(vector, layout):
    pieces = []
    offset = 0
    for dimensions in layout:
        amount = math.prod(dimensions)
        pieces.append(vector[offset:offset + amount].reshape(dimensions))
        offset += amount
    return pieces

def position_table():
    quarter = D // 4
    frequency = 1.0 / 10000.0 ** (jnp.arange(quarter, dtype=jnp.float32) / quarter)
    coords = jnp.arange(GRID, dtype=jnp.float32)
    angles = coords[:, None] * frequency[None, :]
    one_axis = jnp.concatenate([jnp.sin(angles), jnp.cos(angles)], axis=1)
    row_part = jnp.repeat(one_axis, GRID, axis=0)
    col_part = jnp.tile(one_axis, (GRID, 1))
    return jnp.concatenate([row_part, col_part], axis=1)

def time_features(times_in):
    half_freq = FREQ // 2
    frequency = jnp.exp(-math.log(10000.0) * jnp.arange(half_freq, dtype=jnp.float32) / half_freq)
    angles = times_in[:, None] * frequency[None, :]
    return jnp.concatenate([jnp.cos(angles), jnp.sin(angles)], axis=1)

def modulated_norm(values, offsets, scales):
    centred = values - lax.optimization_barrier(jnp.mean(values, axis=-1, keepdims=True))
    spread = lax.optimization_barrier(jnp.mean(centred * centred, axis=-1, keepdims=True))
    return centred * lax.rsqrt(spread + norm_eps) * (1.0 + scales) + offsets

def softmax_rows(scores):
    row_max = lax.optimization_barrier(jnp.max(scores, axis=-1, keepdims=True))
    exponent = jnp.exp(scores - row_max)
    return exponent / lax.optimization_barrier(jnp.sum(exponent, axis=-1, keepdims=True))

def cosine_rows(predicted, target):
    target_full = target.astype(jnp.float32)
    inner_sum = lax.optimization_barrier(jnp.sum(predicted * target_full, axis=-1))
    return inner_sum * lax.rsqrt(lax.optimization_barrier(jnp.sum(predicted * predicted, axis=-1)) + norm_eps) * lax.rsqrt(lax.optimization_barrier(jnp.sum(target_full * target_full, axis=-1)) + norm_eps)

def linear(inputs, weight):
    return jnp.einsum('...k,kn->...n', inputs, weight, precision=highest)

def layer_block(weights, residual, modulator):
    w_attn_in, w_attn_out, w_mlp_in, w_mlp_out, w_modulate, b_query, b_value, b_attn_out, b_mlp_in, b_mlp_out, b_modulate = weights
    group_size, seq_len = (residual.shape[0], residual.shape[1])
    head_count = D // HD
    modulation = jnp.split(low_back(linear(modulator, w_modulate) + b_modulate)[:, None, :], 6, axis=-1)
    normed = low(modulated_norm(residual, modulation[0], modulation[1]))
    bias_qkv = jnp.concatenate([b_query, jnp.zeros_like(b_query), b_value])
    qkv = low(low_back(linear(normed, w_attn_in) + bias_qkv)).reshape(group_size, seq_len, 3, head_count, HD)
    scores = low_back(jnp.einsum('gqhd,gkhd->ghqk', qkv[:, :, 0], qkv[:, :, 1], precision=highest) * HD ** (-0.5))
    probs_low = low(softmax_rows(scores))
    heads_out = low(low_back(jnp.einsum('ghqk,gkhd->gqhd', probs_low, qkv[:, :, 2], precision=highest)))
    attn_out = low_back(linear(heads_out.reshape(group_size, seq_len, D), w_attn_out) + b_attn_out)
    middle = residual + modulation[2] * attn_out
    normed_m = low(modulated_norm(middle, modulation[3], modulation[4]))
    mlp_pre = low_back(linear(normed_m, w_mlp_in) + b_mlp_in)
    mlp_act = low(jax.nn.gelu(mlp_pre, approximate=True))
    mlp_out = low_back(linear(mlp_act, w_mlp_out) + b_mlp_out)
    return (middle + modulation[5] * mlp_out, attn_out, mlp_out)

def projector_loss(pieces, residual, target):
    act_a = low(jax.nn.silu(low_back(linear(low(residual), pieces[7]) + pieces[8])))
    act_b = low(jax.nn.silu(low_back(linear(act_a, pieces[9]) + pieces[10])))
    predicted = low_back(linear(act_b, pieces[11]) + pieces[12])
    return -proj_coeff * jnp.sum(cosine_rows(predicted, target)) / SEQ

def head_loss(pieces, residual, modulator, target, weight_t):
    modulation = low_back(linear(modulator, pieces[13]) + pieces[14])[:, None, :]
    shift_f, scale_f = jnp.split(modulation, 2, axis=-1)
    normed = low(modulated_norm(residual, shift_f, scale_f))
    deviation = low_back(linear(normed, pieces[15]) + pieces[16]) - target
    return jnp.sum(weight_t * lax.optimization_barrier(jnp.mean(deviation * deviation, axis=(1, 2))))

def group_forward(layer_list, root_list, positions, group_data):
    latent_g, noise_g, times_g, labels_g, dropped_g, features_g = group_data
    mixing = times_g[:, None, None]
    noisy = low((1.0 - mixing) * latent_g + mixing * noise_g)
    residual = low_back(linear(noisy, root_list[0]) + root_list[1]) + positions
    basis = low(time_features(times_g))
    time_act = low(jax.nn.silu(low_back(linear(basis, root_list[2]) + root_list[3])))
    time_emb = low_back(linear(time_act, root_list[4]) + root_list[5])
    classes = jnp.where(dropped_g == 1, CLS - 1, labels_g)
    condition = time_emb + root_list[6][classes]
    modulator = low(jax.nn.silu(condition))
    loss_part = jnp.zeros((), jnp.float32)
    layer_sums = []
    for ordinal in range(LAYERS):
        residual, attn_out, mlp_out = layer_block(layer_list[ordinal], residual, modulator)
        layer_sums.append(jnp.stack([jnp.sum(residual * residual), jnp.sum(attn_out * attn_out), jnp.sum(mlp_out * mlp_out)]))
        if ordinal + 1 == DEPTH_Z:
            loss_part = loss_part + projector_loss(root_list, residual, features_g)
    loss_part = loss_part + head_loss(root_list, residual, modulator, noise_g - latent_g, 1.0 + 2.0 * times_g)
    return (loss_part, jnp.stack(layer_sums))

def total_loss(layer_f, root_f, inputs):
    layer_low = low(layer_f)
    root_low = low(root_f)
    layer_list = [unflatten(layer_low[ordinal], layer_layout()) for ordinal in range(LAYERS)]
    root_list = unflatten(root_low, root_layout())
    positions = position_table()
    group = math.gcd(SAMPLES, max(1, 4096 // SEQ))
    grouped = tuple((source.reshape((SAMPLES // group, group) + source.shape[1:]) for source in inputs))

    def accumulate(running, group_data):
        loss_part, layer_sums = jax.checkpoint(group_forward)(layer_list, root_list, positions, group_data)
        return ((running[0] + loss_part, running[1] + layer_sums), None)
    start = (jnp.zeros((), jnp.float32), jnp.zeros((LAYERS, 3), jnp.float32))
    (loss_all, sums_all), _ = lax.scan(accumulate, start, grouped)
    return (loss_all, sums_all)

def adam_update(weight, grad, first, second, clip_factor):
    clipped = grad * clip_factor
    first_new = beta_one * first + (1.0 - beta_one) * clipped
    second_new = beta_two * second + (1.0 - beta_two) * clipped * clipped
    first_hat = first_new / (1.0 - beta_one ** STEP)
    second_hat = second_new / (1.0 - beta_two ** STEP)
    weight_new = weight - learn_rate * (first_hat / (jnp.sqrt(second_hat) + adam_eps) + decay_rate * weight)
    return (weight_new, first_new, second_new)

def reference(latents, noise, times, labels, dropped, features, layer_flat, layer_mean, layer_square, root_flat, root_mean, root_square):
    inputs = (latents, noise, times, labels, dropped, features.astype(jnp.float32))

    def objective(layer_f, root_f):
        loss_all, sums_all = total_loss(layer_f, root_f, inputs)
        return (loss_all / SAMPLES, (loss_all, sums_all))
    _, pullback, (loss_sum, sums_all) = jax.vjp(objective, layer_flat, root_flat, has_aux=True)
    grad_layer, grad_root = pullback(jnp.ones((), jnp.float32))
    grad_norm = jnp.sqrt(jnp.sum(grad_layer * grad_layer) + jnp.sum(grad_root * grad_root))
    clip_factor = clip_limit / jnp.maximum(grad_norm, clip_limit)
    new_layer, new_layer_mean, new_layer_square = adam_update(layer_flat, grad_layer, layer_mean, layer_square, clip_factor)
    new_root, new_root_mean, new_root_square = adam_update(root_flat, grad_root, root_mean, root_square, clip_factor)
    activation_rms = jnp.sqrt(sums_all / (SAMPLES * SEQ * D))
    return (loss_sum, grad_norm, activation_rms, new_layer, new_layer_mean, new_layer_square, new_root, new_root_mean, new_root_square)
```

```python
import functools
import math

import jax
import jax.numpy as jnp
from jax import lax
from jax.experimental import pallas as pl
from jax.experimental.pallas import tpu as pltpu
from jax.sharding import PartitionSpec as P

D = 768
HD = 64
FF = 3072
PD = 16
CLS = 1001
PH = 2048
ZD = 768
FREQ = 256
GRID = 16
LAYERS = 2
DEPTH_Z = 2
STEP = 10
SEQ = 256


norm_eps = 1e-06
clip_limit = 0.002
learn_rate = 0.08
beta_one = 0.5
beta_two = 0.5
adam_eps = 1e-08
decay_rate = 0.01
proj_coeff = 0.5
low_type = jnp.bfloat16
full_type = jnp.float32


LANES = 128
ROWS = 16
UNIT = LANES * ROWS
MESH = pl.DeviceIdType.MESH

def up(value, step):
    return -(-value // step) * step

class Plan:
    def __init__(self, layout, length, devices):
        self.length = length
        self.devices = devices
        self.share = length // devices
        self.segments = []
        offset = units = 0
        for shape in layout:
            amount = math.prod(shape)
            matrix = len(shape) == 2 and shape[0] % ROWS == 0 and shape[1] % LANES == 0
            chunks = shape[1] // LANES if matrix else 1
            count = up(amount, UNIT) // UNIT
            self.segments.append((offset // LANES, chunks, count, units, shape, matrix))
            offset += amount
            units += count
        self.units = units
        self.per = up(up(units, devices) // devices, 4)
        rows_of = []
        for base, chunks, count, _, _, _ in self.segments:
            for u in range(count):
                b, c = divmod(u, chunks)
                first = base + b * ROWS * chunks + c
                rows_of.append((first, first + (ROWS - 1) * chunks))
        before = after = 0
        for d in range(devices):
            start, stop = d * self.share // LANES, (d + 1) * self.share // LANES
            for lo, hi in rows_of[self.per * d : self.per * d + self.per]:
                before, after = max(before, start - lo), max(after, hi + 1 - stop)
        self.before, self.after = up(before, 8), up(after, 8)
        units_before = units_after = 0
        for u, (lo, hi) in enumerate(rows_of):
            first = lo * LANES // self.share
            last = min(((hi + 1) * LANES - 1) // self.share, devices - 1)
            for d in range(first, last + 1):
                units_before = max(units_before, self.per * d - u)
                units_after = max(units_after, u + 1 - self.per * d - self.per)
        self.units_before, self.units_after = units_before, units_after
        self.half = self.per // 2
        self.raw = up(up(self.share, LANES) // LANES + 9, 64)
        self.ext = self.before + self.raw + self.after
        margin = tail = 0
        for d in range(devices):
            start = d * self.share // LANES
            lo = max(self.per * d - units_before, 0)
            for first, last in rows_of[lo : self.per * d + self.per + units_after]:
                margin, tail = max(margin, start - first), max(tail, last + 1 - start)
        self.margin = up(margin, 8)
        self.spread = up(max(tail, self.raw + 8), 8) + self.margin
        least = self.share // LANES
        self.fits = max(self.before, self.after) < least and max(units_before, units_after) < self.per

def place(index, zs):
    return index // 8, index // 4 % 2, index // 2 % 2, index % 2

def gather_kernel(plans, zs, *refs):
    nb = len(plans)
    raw_hbm = refs[:nb]
    outs = refs[nb : 2 * nb]
    raw, ext, tail, from_prev, from_next, slots = (refs[2 * nb + i * nb : 3 * nb + i * nb] for i in range(6))
    rest = refs[8 * nb :]
    load_sem, halo_send, halo_recv, own_sem, send_sem, zr, xa, xb, yb, ya, cr = rest
    n = zs * 8
    me = lax.axis_index("fsdp")
    z, y, x, c = place(me, zs)
    index = lambda zz, yy, xx, cc: ((zz * 2 + yy) * 2 + xx) * 2 + cc
    prev, following = lax.rem(me + n - 1, n), lax.rem(me + 1, n)
    xpeer, ypeer, cpeer = index(z, y, 1 - x, c), index(z, 1 - y, x, c), index(z, y, x, 1 - c)
    zpeer = [index(lax.rem(z + k, zs), y, x, c) for k in range(zs)]
    loads = []
    for b in range(nb):
        p = plans[b]
        loads.append(pltpu.make_async_copy(raw_hbm[b], raw[b].at[pl.ds(8, p.raw)], load_sem.at[b]))
        loads[b].start()
    barrier = pltpu.get_barrier_semaphore()
    peers = [prev, following, xpeer, ypeer, cpeer] + zpeer[1:]
    for peer in peers:
        pl.semaphore_signal(barrier, inc=1, device_id=(peer,), device_id_type=MESH)
    halos = []
    lane = lax.broadcasted_iota(jnp.int32, (64, LANES), 1)
    for b in range(nb):
        p = plans[b]
        shift = lax.rem(me * p.share, LANES)
        delta = (me + 1) * p.share // LANES - me * p.share // LANES
        raw[b][pl.ds(0, 8), :] = jnp.zeros((8, LANES), full_type)
        ext[b][pl.ds(0, p.before), :] = jnp.zeros((p.before, LANES), full_type)
        ext[b][pl.ds(p.before + p.raw, p.after), :] = jnp.zeros((p.after, LANES), full_type)
        loads[b].wait()

        def align(i, carry):
            row = pl.multiple_of(i * 64, 64)
            here = pltpu.roll(raw[b][pl.ds(row + 8, 64), :], shift, 1)
            above = pltpu.roll(raw[b][pl.ds(row + 7, 64), :], shift, 1)
            ext[b][pl.ds(row + p.before, 64), :] = jnp.where(lane >= shift, here, above)
            return carry

        lax.fori_loop(0, p.raw // 64, align, 0)
        tail[b][...] = ext[b][pl.ds(delta, p.before + 8), :]
        if b == 0:
            pl.semaphore_wait(barrier, len(peers))
        for s, (src, dst, to) in enumerate(((ext[b].at[pl.ds(p.before, p.after)], from_next[b], prev), (tail[b], from_prev[b], following))):
            copy = pltpu.make_async_remote_copy(src, dst, halo_send.at[2 * b + s], halo_recv.at[2 * b + s], device_id=(to,), device_id_type=MESH)
            copy.start()
            halos.append(copy)
    sends = []

    def send(src, dst, sem, to):
        copy = pltpu.make_async_remote_copy(src, dst, send_sem.at[len(sends)], sem, device_id=(to,), device_id_type=MESH)
        copy.start()
        sends.append(copy)

    def span(b, h):
        p = plans[b]
        return (0, p.half) if h == 0 else (p.half, p.per - p.half)

    def slot(k, dy, dx, dc):
        return index(lax.rem(z + zs - k, zs), 1 - y if dy else y, 1 - x if dx else x, 1 - c if dc else c)

    def part(b, h, k, dy, dx, dc=0):
        first, count = span(b, h)
        return outs[b].at[pl.ds(slot(k, dy, dx, dc) * plans[b].per + first, count)]

    def whole(b, k, dy, dx, dc=0):
        return outs[b].at[pl.ds(slot(k, dy, dx, dc) * plans[b].per, plans[b].per)]

    def arrived(ref, sem):
        pltpu.make_async_copy(ref, ref, sem).wait()

    owns = []
    for b in range(nb):
        p = plans[b]
        delta = (me + 1) * p.share // LANES - me * p.share // LANES
        for copy in halos[2 * b : 2 * b + 2]:
            copy.wait()
        ext[b][pl.ds(0, p.before + 8), :] += from_prev[b][...]
        ext[b][pl.ds(p.before + delta, p.after), :] += from_next[b][...]
        top = me * p.share // LANES - p.before
        for base, chunks, count, first_unit, _, _ in p.segments:
            lo = jnp.clip(p.per * me - first_unit, 0, count)
            hi = jnp.clip(p.per * me + p.per - first_unit, 0, count)

            def unit(u, carry):
                block = u // chunks
                row = base + block * (ROWS * chunks) + (u - block * chunks) - top
                if chunks == 1:
                    value = ext[b][pl.ds(row, ROWS), :]
                else:
                    value = ext[b][pl.ds(row, ROWS, stride=chunks), :]
                slots[b][first_unit + u - p.per * me] = value.astype(low_type)
                return carry

            lax.fori_loop(lo, hi, unit, 0)
        own = pltpu.make_async_copy(slots[b], whole(b, 0, 0, 0), own_sem.at[b])
        own.start()
        owns.append(own)
        mine = lambda h: slots[b].at[pl.ds(*span(b, h))]
        for k in range(1, zs):
            for h in range(2):
                send(mine(h), part(b, h, 0, 0, 0), zr.at[b, h, k], zpeer[k])
        send(mine(0), part(b, 0, 0, 0, 0), xa.at[b, 0], xpeer)
        send(mine(1), part(b, 1, 0, 0, 0), yb.at[b, 0], ypeer)
        send(mine(0), part(b, 0, 0, 0, 0), ya.at[b, 0, 0], ypeer)
        send(mine(1), part(b, 1, 0, 0, 0), xb.at[b, 0, 0], xpeer)
        send(slots[b], whole(b, 0, 0, 0), cr.at[b, 0, 0, 0], cpeer)
    for b in range(nb):
        for k in range(1, zs):
            arrived(part(b, 0, k, 0, 0), zr.at[b, 0, k])
            send(part(b, 0, k, 0, 0), part(b, 0, k, 0, 0), xa.at[b, k], xpeer)
            arrived(part(b, 1, k, 0, 0), zr.at[b, 1, k])
            send(part(b, 1, k, 0, 0), part(b, 1, k, 0, 0), yb.at[b, k], ypeer)
            send(part(b, 0, k, 0, 0), part(b, 0, k, 0, 0), ya.at[b, k, 0], ypeer)
            send(part(b, 1, k, 0, 0), part(b, 1, k, 0, 0), xb.at[b, k, 0], xpeer)
            send(whole(b, k, 0, 0), whole(b, k, 0, 0), cr.at[b, k, 0, 0], cpeer)
        for k in range(zs):
            arrived(part(b, 0, k, 0, 1), xa.at[b, k])
            send(part(b, 0, k, 0, 1), part(b, 0, k, 0, 1), ya.at[b, k, 1], ypeer)
            arrived(part(b, 1, k, 1, 0), yb.at[b, k])
            send(part(b, 1, k, 1, 0), part(b, 1, k, 1, 0), xb.at[b, k, 1], xpeer)
        for k in range(zs):
            arrived(part(b, 1, k, 0, 1), xb.at[b, k, 0])
            send(whole(b, k, 0, 1), whole(b, k, 0, 1), cr.at[b, k, 0, 1], cpeer)
            arrived(part(b, 0, k, 1, 0), ya.at[b, k, 0])
            send(whole(b, k, 1, 0), whole(b, k, 1, 0), cr.at[b, k, 1, 0], cpeer)
        for k in range(zs):
            arrived(part(b, 1, k, 1, 1), xb.at[b, k, 1])
            arrived(part(b, 0, k, 1, 1), ya.at[b, k, 1])
            send(whole(b, k, 1, 1), whole(b, k, 1, 1), cr.at[b, k, 1, 1], cpeer)
    for b in range(nb):
        owns[b].wait()
        for k in range(zs):
            for dy in range(2):
                for dx in range(2):
                    arrived(whole(b, k, dy, dx, 1), cr.at[b, k, dy, dx])
    for copy in sends:
        copy.wait_send()

def gather_units(plans, raws):
    n = plans[0].devices
    zs = n // 8
    nb = len(plans)
    per_bucket = 2 * (zs - 1) + 10 * zs
    dma = pltpu.SemaphoreType.DMA
    scratch = [pltpu.VMEM((p.raw + 8, LANES), full_type) for p in plans]
    scratch += [pltpu.VMEM((p.ext, LANES), full_type) for p in plans]
    scratch += [pltpu.VMEM((p.before + 8, LANES), full_type) for p in plans]
    scratch += [pltpu.VMEM((p.before + 8, LANES), full_type) for p in plans]
    scratch += [pltpu.VMEM((p.after, LANES), full_type) for p in plans]
    scratch += [pltpu.VMEM((p.per, ROWS, LANES), low_type) for p in plans]
    scratch += [dma((nb,)), dma((2 * nb,)), dma((2 * nb,)), dma((nb,)), dma((nb * per_bucket,))]
    scratch += [dma((nb, 2, zs)), dma((nb, zs)), dma((nb, zs, 2)), dma((nb, zs)), dma((nb, zs, 2)), dma((nb, zs, 2, 2))]
    return pl.pallas_call(
        functools.partial(gather_kernel, plans, zs),
        out_shape=[jax.ShapeDtypeStruct((n * p.per, ROWS, LANES), low_type) for p in plans],
        in_specs=[pl.BlockSpec(memory_space=pl.ANY)] * nb,
        out_specs=[pl.BlockSpec(memory_space=pl.ANY)] * nb,
        scratch_shapes=scratch,
        compiler_params=pltpu.CompilerParams(collective_id=0, has_side_effects=True, vmem_limit_bytes=48 * 1024 * 1024),
        name="gather_units",
    )(*raws)

def reduce_kernel(plans, zs, *refs):
    nb = len(plans)
    take = lambda count: tuple(next(feed) for _ in range(count))
    feed = iter(refs)
    grads, (stats_in,) = take(nb), take(1)
    outs, (stats_out,), first = take(nb), take(1), take(nb)
    kept_a, kept_b, two_a, two_b, three_a, three_b, four = (take(nb) for _ in range(7))
    local, other = take(1)[0], take(1)[0]
    units_f, rows_f, flat_f = take(1)[0], take(1)[0], take(1)[0]
    from_prev, from_next = take(nb), take(nb)
    total, total_in = take(1)[0], take(1)[0]
    s1, r1, s2a, r2a, s2b, r2b, s3a, r3a, s3b, r3b, s4, r4, load_sem, halo_s, halo_r, out_sem, ss, sr = take(18)
    n = zs * 8
    me = lax.axis_index("fsdp")
    z, y, x, c = place(me, zs)
    index = lambda zz, yy, xx, cc: ((zz * 2 + yy) * 2 + xx) * 2 + cc
    prev, following = lax.rem(me + n - 1, n), lax.rem(me + 1, n)
    xpeer, ypeer, cpeer = index(z, y, 1 - x, c), index(z, 1 - y, x, c), index(z, y, x, 1 - c)
    below = lambda k: index(lax.rem(z + zs - k, zs), y, x, c)
    above = lambda k: index(lax.rem(z + k, zs), y, x, c)
    barrier = pltpu.get_barrier_semaphore()
    peers = [prev, following, xpeer, ypeer, cpeer] + [above(k) for k in range(1, zs)]
    for peer in peers:
        pl.semaphore_signal(barrier, inc=1, device_id=(peer,), device_id_type=MESH)
    pl.semaphore_wait(barrier, len(peers))

    def remote(src, dst, send_sem, recv_sem, to):
        return pltpu.make_async_remote_copy(src, dst, send_sem, recv_sem, device_id=(to,), device_id_type=MESH)

    def arrived(ref, sem):
        pltpu.make_async_copy(ref, ref, sem).wait()

    def slot(b, k, dy, dx, dc):
        where = index(lax.rem(z + zs - k, zs), 1 - y if dy else y, 1 - x if dx else x, 1 - c if dc else c)
        return grads[b].at[pl.ds(where * plans[b].per, plans[b].per)]

    order = ((1, 1), (1, 0), (0, 1), (0, 0))

    def sibling(b, k, dy, dx):
        return remote(slot(b, k, dy, dx, 1), first[b].at[k, dy, dx], s1.at[b, k, dy, dx], r1.at[b, k, dy, dx], cpeer)

    for b in range(nb):
        for dy, dx in order:
            for k in range(zs):
                sibling(b, k, dy, dx).start()

    def add(p, dst, at, one, one_at, two, two_at):
        step = p.half // 2

        def body(i, carry):
            span = lambda ref, off: ref[pl.ds(off + i * step, step)].astype(full_type)
            dst[pl.ds(at + i * step, step)] = (span(one, one_at) + span(two, two_at)).astype(low_type)
            return carry

        lax.fori_loop(0, 2, body, 0)

    ring = local.shape[0]
    used = []

    def send_of(b, h, k, dy, dx, src):
        if h == 0:
            return remote(src, two_a[b].at[k, dx], s2a.at[b, k, dx], r2a.at[b, k, dx], ypeer)
        return remote(src, two_b[b].at[k, dy], s2b.at[b, k, dy], r2b.at[b, k, dy], xpeer)

    steps = [(b, dy, dx, k) for b in range(nb) for dy, dx in order for k in range(zs)]

    def loads(number):
        b, dy, dx, k = steps[number]
        at = number % ring
        p = plans[b]
        one = pltpu.make_async_copy(slot(b, k, dy, dx, 0), local.at[at, pl.ds(0, p.per)], load_sem.at[at, 0])
        two = pltpu.make_async_copy(first[b].at[k, dy, dx], other.at[number % 2, pl.ds(0, p.per)], load_sem.at[at, 1])
        return one, two

    pending = {}

    def prepare(number):
        b, dy, dx, k = steps[number]
        for copy in pending.pop(number % ring, ()):
            copy.wait_send()
        one, two = loads(number)
        one.start()
        arrived(first[b].at[k, dy, dx], r1.at[b, k, dy, dx])
        two.start()

    def phase_one(number):
        b, dy, dx, k = steps[number]
        p = plans[b]
        at = number % ring
        if number == 0:
            prepare(0)
        if number + 1 < len(steps):
            prepare(number + 1)
        for copy in loads(number):
            copy.wait()
        mine, theirs = local.at[at], other.at[number % 2]
        going = []
        if dy:
            add(p, mine, 0, mine, 0, theirs, 0)
            going.append(send_of(b, 0, k, dy, dx, local.at[at, pl.ds(0, p.half)]))
        else:
            add(p, kept_a[b].at[k, dx], 0, mine, 0, theirs, 0)
        if dx:
            add(p, mine, p.half, mine, p.half, theirs, p.half)
            going.append(send_of(b, 1, k, dy, dx, local.at[at, pl.ds(p.half, p.half)]))
        else:
            add(p, kept_b[b].at[k, dy], 0, mine, p.half, theirs, p.half)
        for copy in going:
            copy.start()
        pending[at] = going

    def three(b, h, k):
        if h == 0:
            return remote(two_a[b].at[k, 1], three_a[b].at[k], s3a.at[b, k], r3a.at[b, k], xpeer)
        return remote(two_b[b].at[k, 1], three_b[b].at[k], s3b.at[b, k], r3b.at[b, k], ypeer)

    def last(b, h, k):
        src = (three_a if h == 0 else three_b)[b].at[k]
        return remote(src, four[b].at[h, k - 1], s4.at[b, h, k - 1], r4.at[b, h, k - 1], below(k))

    def phase_two(b):
        p = plans[b]
        for far in (1, 0):
            for k in range(zs):
                for h, kept, two, sem in ((0, kept_a, two_a, r2a), (1, kept_b, two_b, r2b)):
                    arrived(two[b].at[k, far], sem.at[b, k, far])
                    if far:
                        add(p, two[b].at[k, 1], 0, two[b].at[k, 1], 0, kept[b].at[k, 1], 0)
                        three(b, h, k).start()
                    else:
                        add(p, kept[b].at[k, 0], 0, two[b].at[k, 0], 0, kept[b].at[k, 0], 0)

    def phase_three(b):
        p = plans[b]
        for k in list(range(1, zs)) + [0]:
            for h, kept, got, sem in ((0, kept_a, three_a, r3a), (1, kept_b, three_b, r3b)):
                arrived(got[b].at[k], sem.at[b, k])
                if k:
                    add(p, got[b].at[k], 0, got[b].at[k], 0, kept[b].at[k, 0], 0)
                    last(b, h, k).start()

    def finish(b):
        p = plans[b]
        base = p.units_before
        for h, kept, got in ((0, kept_a, three_a), (1, kept_b, three_b)):
            for k in range(1, zs):
                arrived(four[b].at[h, k - 1], r4.at[b, h, k - 1])
            step = p.half // 2

            def body(i, carry):
                part = pl.ds(i * step, step)
                value = kept[b][0, 0, part].astype(full_type) + got[b][0, part].astype(full_type)
                for k in range(1, zs):
                    value = value + four[b][h, k - 1, part].astype(full_type)
                units_f[pl.ds(base + h * p.half + i * step, step)] = value
                return carry

            lax.fori_loop(0, 2, body, 0)
        forward = remote(units_f.at[pl.ds(p.per, base)], from_prev[b], halo_s.at[b, 0], halo_r.at[b, 0], following)
        backward = remote(units_f.at[pl.ds(base, p.units_after)], from_next[b], halo_s.at[b, 1], halo_r.at[b, 1], prev)
        forward.start()
        backward.start()
        forward.wait()
        backward.wait()
        units_f[pl.ds(0, base)] = from_prev[b][...]
        units_f[pl.ds(base + p.per, p.units_after)] = from_next[b][...]
        top = me * p.share // LANES - p.margin
        for origin, chunks, count, first_unit, _, _ in p.segments:
            lo = jnp.clip(p.per * me - base - first_unit, 0, count)
            hi = jnp.clip(p.per * me + p.per + p.units_after - first_unit, 0, count)

            def unit(u, carry):
                block = u // chunks
                row = origin + block * (ROWS * chunks) + (u - block * chunks) - top
                value = units_f[first_unit + u - p.per * me + base]
                if chunks == 1:
                    rows_f[pl.ds(row, ROWS), :] = value
                else:
                    rows_f[pl.ds(row, ROWS, stride=chunks), :] = value
                return carry

            lax.fori_loop(lo, hi, unit, 0)
        shift = lax.rem(me * p.share, LANES)
        turn = lax.rem(LANES - shift, LANES)
        lane = lax.broadcasted_iota(jnp.int32, (64, LANES), 1)
        spot = lax.broadcasted_iota(jnp.int32, (64, LANES), 0) * LANES + lane
        if b:
            pltpu.make_async_copy(flat_f.at[pl.ds(0, plans[b - 1].raw)], outs[b - 1], out_sem.at[b - 1]).wait()

        def unalign(i, squares):
            row = pl.multiple_of(i * 64, 64)
            here = pltpu.roll(rows_f[pl.ds(row + p.margin, 64), :], turn, 1)
            below_row = pltpu.roll(rows_f[pl.ds(row + p.margin + 1, 64), :], turn, 1)
            value = jnp.where(lane < LANES - shift, here, below_row)
            value = jnp.where(spot + row * LANES < p.share, value, 0.0)
            flat_f[pl.ds(row, 64), :] = value
            return squares + jnp.sum((value * value).reshape(8, 8, LANES), axis=0)

        squares = lax.fori_loop(0, p.raw // 64, unalign, jnp.zeros((8, LANES), full_type))
        pltpu.make_async_copy(flat_f.at[pl.ds(0, p.raw)], outs[b], out_sem.at[b]).start()
        return squares

    per_bucket = 4 * zs
    for b in range(nb):
        for number in range(b * per_bucket, (b + 1) * per_bucket):
            phase_one(number)
        if b:
            phase_two(b - 1)
            phase_three(b - 1)
    phase_two(nb - 1)
    phase_three(nb - 1)
    squares = jnp.zeros((8, LANES), full_type)
    for b in range(nb):
        squares = squares + finish(b)
    pltpu.make_async_copy(flat_f.at[pl.ds(0, plans[nb - 1].raw)], outs[nb - 1], out_sem.at[nb - 1]).wait()
    total[0] = stats_in[...]
    total[1] = squares
    step = 0
    for to in ((cpeer,), (xpeer,), (ypeer,), tuple(above(k) for k in range(1, zs))):
        copies = []
        for peer in to:
            copies.append(remote(total, total_in.at[step], ss.at[step], sr.at[step], peer))
            copies[-1].start()
            step += 1
        for copy in copies:
            copy.wait()
        value = total[...]
        for i in range(len(to)):
            value = value + total_in[step - 1 - i]
        total[...] = value
    stats_out[...] = total[...]
    for group in pending.values():
        for copy in group:
            copy.wait_send()
    for b in range(nb):
        for dy, dx in order:
            for k in range(zs):
                sibling(b, k, dy, dx).wait_send()
        for h in range(2):
            for k in range(zs):
                three(b, h, k).wait_send()
                if k:
                    last(b, h, k).wait_send()

def reduce_units(plans, grads, stats):
    n = plans[0].devices
    zs = n // 8
    nb = len(plans)
    dma = pltpu.SemaphoreType.DMA
    most = max(p.per for p in plans)
    tile = (ROWS, LANES)
    half = lambda p, *lead: pltpu.VMEM(lead + (p.half,) + tile, low_type)
    scratch = [half(p, zs, 2) for p in plans] + [half(p, zs, 2) for p in plans]
    scratch += [half(p, zs, 2) for p in plans] + [half(p, zs, 2) for p in plans]
    scratch += [half(p, zs) for p in plans] + [half(p, zs) for p in plans]
    scratch += [half(p, 2, zs - 1) for p in plans]
    ring = 4
    scratch += [pltpu.VMEM((ring, most) + tile, low_type), pltpu.VMEM((2, most) + tile, low_type)]
    scratch += [pltpu.VMEM((max(p.units_before + p.per + p.units_after for p in plans),) + tile, full_type)]
    scratch += [pltpu.VMEM((max(p.spread for p in plans), LANES), full_type)]
    scratch += [pltpu.VMEM((max(p.raw for p in plans), LANES), full_type)]
    scratch += [pltpu.VMEM((p.units_before,) + tile, full_type) for p in plans]
    scratch += [pltpu.VMEM((p.units_after,) + tile, full_type) for p in plans]
    hops = 2 + zs
    scratch += [pltpu.VMEM((2, 8, LANES), full_type), pltpu.VMEM((hops, 2, 8, LANES), full_type)]
    scratch += [dma((nb, zs, 2, 2))] * 2 + [dma((nb, zs, 2))] * 4 + [dma((nb, zs))] * 4
    scratch += [dma((nb, 2, zs - 1))] * 2 + [dma((ring, 2)), dma((nb, 2)), dma((nb, 2)), dma((nb,)), dma((hops,)), dma((hops,))]
    anywhere = pl.BlockSpec(memory_space=pl.ANY)
    inside = pl.BlockSpec(memory_space=pltpu.VMEM)
    out_shape = [jax.ShapeDtypeStruct((p.raw, LANES), full_type) for p in plans]
    out_shape += [jax.ShapeDtypeStruct((2, 8, LANES), full_type)]
    out_shape += [jax.ShapeDtypeStruct((zs, 2, 2, p.per) + tile, low_type) for p in plans]
    results = pl.pallas_call(
        functools.partial(reduce_kernel, plans, zs),
        out_shape=out_shape,
        in_specs=[anywhere] * nb + [inside],
        out_specs=[anywhere] * nb + [inside] + [anywhere] * nb,
        scratch_shapes=scratch,
        compiler_params=pltpu.CompilerParams(collective_id=1, has_side_effects=True, vmem_limit_bytes=62 * 1024 * 1024),
        name="reduce_units",
    )(*grads, stats)
    return results[:nb], results[nb]

def to_rows(flat, plan):
    padded = jnp.pad(flat, ((0, plan.raw * LANES - flat.shape[0]),))
    return padded.reshape(plan.raw, LANES)


def layer_layout():
    return [
        (D, 3 * D),
        (D, D),
        (D, FF),
        (FF, D),
        (D, 6 * D),
        (D,),
        (D,),
        (D,),
        (FF,),
        (D,),
        (6 * D,),
    ]


def root_layout():
    return [
        (PD, D),
        (D,),
        (FREQ, D),
        (D,),
        (D, D),
        (D,),
        (CLS, D),
        (D, PH),
        (PH,),
        (PH, PH),
        (PH,),
        (PH, ZD),
        (ZD,),
        (D, 2 * D),
        (2 * D,),
        (D, PD),
        (PD,),
    ]


def unflatten(vector, layout):
    pieces = []
    offset = 0
    for dimensions in layout:
        amount = math.prod(dimensions)
        pieces.append(vector[offset : offset + amount].reshape(dimensions))
        offset += amount
    return pieces


def flatten_grads(grad_list, length):
    joined = jnp.concatenate([piece.reshape(-1) for piece in grad_list])
    return jnp.concatenate([joined, jnp.zeros((length - joined.shape[0],), full_type)])


def position_table():
    quarter = D // 4
    frequency = 1.0 / 10000.0 ** (jnp.arange(quarter, dtype=jnp.float32) / quarter)
    coords = jnp.arange(GRID, dtype=jnp.float32)
    angles = coords[:, None] * frequency[None, :]
    one_axis = jnp.concatenate([jnp.sin(angles), jnp.cos(angles)], axis=1)
    row_part = jnp.repeat(one_axis, GRID, axis=0)
    col_part = jnp.tile(one_axis, (GRID, 1))
    return jnp.concatenate([row_part, col_part], axis=1)


def time_features(times_in):
    half_freq = FREQ // 2
    frequency = jnp.exp(-math.log(10000.0) * jnp.arange(half_freq, dtype=jnp.float32) / half_freq)
    angles = times_in[:, None] * frequency[None, :]
    return jnp.concatenate([jnp.cos(angles), jnp.sin(angles)], axis=1)


def modulated_norm(values, offsets, scales):
    centred = values - jnp.mean(values, axis=-1, keepdims=True)
    spread = jnp.mean(centred * centred, axis=-1, keepdims=True)
    return centred * lax.rsqrt(spread + norm_eps) * (1.0 + scales) + offsets


def softmax_rows(scores):
    row_max = jnp.max(scores, axis=-1, keepdims=True)
    exponent = jnp.exp(scores - row_max)
    return exponent / jnp.sum(exponent, axis=-1, keepdims=True)


def gelu_tanh(values):
    return jax.nn.gelu(values, approximate=True)


def cosine_rows(predicted, target):
    target_full = target.astype(full_type)
    inner_sum = jnp.sum(predicted * target_full, axis=-1)
    return (
        inner_sum
        * lax.rsqrt(jnp.sum(predicted * predicted, axis=-1) + norm_eps)
        * lax.rsqrt(jnp.sum(target_full * target_full, axis=-1) + norm_eps)
    )


def silu_back(values, grad_in):
    _, pullback = jax.vjp(jax.nn.silu, values)
    return pullback(grad_in)[0]


def linear_fwd(inputs, weight):
    leading = inputs.shape[:-1]
    product = jnp.dot(
        inputs.reshape(-1, inputs.shape[-1]), weight, preferred_element_type=full_type
    )
    return product.reshape(leading + (weight.shape[1],))


def linear_back(inputs, weight, grad_out, with_input=True):
    rows_in = inputs.reshape(-1, inputs.shape[-1])
    rows_out = grad_out.reshape(-1, grad_out.shape[-1])
    grad_weight = lax.dot_general(
        rows_in, rows_out, (((0,), (0,)), ((), ())), preferred_element_type=full_type
    )
    grad_bias = jnp.sum(rows_out.astype(full_type), axis=0)
    grad_in = None
    if with_input:
        grad_in = lax.dot_general(
            rows_out, weight, (((1,), (1,)), ((), ())), preferred_element_type=full_type
        ).reshape(inputs.shape)
    return (grad_in, grad_weight, grad_bias)


def layer_forward(weights, residual, modulator):
    (
        w_attn_in,
        w_attn_out,
        w_mlp_in,
        w_mlp_out,
        w_modulate,
        b_query,
        b_value,
        b_attn_out,
        b_mlp_in,
        b_mlp_out,
        b_modulate,
    ) = weights
    samples_mb, seq_len = (residual.shape[0], residual.shape[1])
    head_count = D // HD
    modulation = jnp.split((linear_fwd(modulator, w_modulate) + b_modulate)[:, None, :], 6, axis=-1)
    normed_a = modulated_norm(residual, modulation[0], modulation[1]).astype(low_type)
    bias_qkv = jnp.concatenate([b_query, jnp.zeros_like(b_query), b_value])
    qkv_low = (linear_fwd(normed_a, w_attn_in) + bias_qkv).astype(low_type)
    qkv_low = qkv_low.reshape(samples_mb, seq_len, 3, head_count, HD)
    query_bf, key_bf, value_bf = (qkv_low[:, :, 0], qkv_low[:, :, 1], qkv_low[:, :, 2])
    scores = jnp.einsum(
        "bqhd,bkhd->bhqk", query_bf, key_bf, preferred_element_type=full_type
    ) * HD ** (-0.5)
    attn_probs = softmax_rows(scores)
    probs_bf = attn_probs.astype(low_type)
    heads_bf = jnp.einsum("bhqk,bkhd->bqhd", probs_bf, value_bf, preferred_element_type=full_type)
    heads_bf = heads_bf.astype(low_type).reshape(samples_mb, seq_len, D)
    attn_out = linear_fwd(heads_bf, w_attn_out) + b_attn_out
    middle = residual + modulation[2] * attn_out
    normed_m = modulated_norm(middle, modulation[3], modulation[4]).astype(low_type)
    mlp_pre = linear_fwd(normed_m, w_mlp_in) + b_mlp_in
    act_bf = gelu_tanh(mlp_pre).astype(low_type)
    mlp_out = linear_fwd(act_bf, w_mlp_out) + b_mlp_out
    residual_out = middle + modulation[5] * mlp_out
    square_sums = jnp.stack(
        [
            jnp.sum(residual_out * residual_out),
            jnp.sum(attn_out * attn_out),
            jnp.sum(mlp_out * mlp_out),
        ]
    )
    saved = (
        modulation,
        normed_a,
        query_bf,
        key_bf,
        value_bf,
        attn_probs,
        probs_bf,
        heads_bf,
        attn_out,
        middle,
        normed_m,
        mlp_pre,
        act_bf,
        mlp_out,
    )
    return (residual_out, saved, square_sums)


def layer_backward(weights, saved, residual, modulator, grad_out):
    w_attn_in, w_attn_out, w_mlp_in, w_mlp_out, w_modulate = weights[:5]
    (
        modulation,
        normed_a,
        query_bf,
        key_bf,
        value_bf,
        attn_probs,
        probs_bf,
        heads_bf,
        attn_out,
        middle,
        normed_m,
        mlp_pre,
        act_bf,
        mlp_out,
    ) = saved
    samples_mb, seq_len = (residual.shape[0], residual.shape[1])
    grad_mlp = (modulation[5] * grad_out).astype(low_type)
    grad_act, grad_w_mlp_out, grad_b_mlp_out = linear_back(act_bf, w_mlp_out, grad_mlp)
    _, gelu_pull = jax.vjp(gelu_tanh, mlp_pre)
    grad_pre = gelu_pull(grad_act)[0].astype(low_type)
    grad_normed_m, grad_w_mlp_in, grad_b_mlp_in = linear_back(normed_m, w_mlp_in, grad_pre)
    _, norm_pull_m = jax.vjp(modulated_norm, middle, modulation[3], modulation[4])
    grad_from_m, grad_shift_m, grad_scale_m = norm_pull_m(grad_normed_m)
    grad_middle = grad_out + grad_from_m
    grad_attn = (modulation[2] * grad_middle).astype(low_type)
    grad_heads, grad_w_attn_out, grad_b_attn_out = linear_back(heads_bf, w_attn_out, grad_attn)
    grad_heads_bf = grad_heads.astype(low_type).reshape(samples_mb, seq_len, D // HD, HD)
    grad_probs = jnp.einsum(
        "bqhd,bkhd->bhqk", grad_heads_bf, value_bf, preferred_element_type=full_type
    )
    grad_value = jnp.einsum(
        "bhqk,bqhd->bkhd", probs_bf, grad_heads_bf, preferred_element_type=full_type
    )
    grad_scores = attn_probs * (
        grad_probs - jnp.sum(attn_probs * grad_probs, axis=-1, keepdims=True)
    )
    grad_scores = grad_scores.astype(low_type)
    grad_query = jnp.einsum(
        "bhqk,bkhd->bqhd", grad_scores, key_bf, preferred_element_type=full_type
    ) * HD ** (-0.5)
    grad_key = jnp.einsum(
        "bhqk,bqhd->bkhd", grad_scores, query_bf, preferred_element_type=full_type
    ) * HD ** (-0.5)
    grad_qkv = jnp.stack([grad_query, grad_key, grad_value], axis=2).reshape(
        samples_mb, seq_len, 3 * D
    )
    grad_normed_a, grad_w_attn_in, grad_b_qkv = linear_back(
        normed_a, w_attn_in, grad_qkv.astype(low_type)
    )
    _, norm_pull_a = jax.vjp(modulated_norm, residual, modulation[0], modulation[1])
    grad_from_a, grad_shift_a, grad_scale_a = norm_pull_a(grad_normed_a)
    grad_gate_a = jnp.sum(attn_out * grad_middle, axis=1, keepdims=True)
    grad_gate_m = jnp.sum(mlp_out * grad_out, axis=1, keepdims=True)
    grad_mod = jnp.concatenate(
        [grad_shift_a, grad_scale_a, grad_gate_a, grad_shift_m, grad_scale_m, grad_gate_m], axis=-1
    )[:, 0, :].astype(low_type)
    grad_cond, grad_w_mod, grad_b_mod = linear_back(modulator, w_modulate, grad_mod)
    grad_list = [
        grad_w_attn_in,
        grad_w_attn_out,
        grad_w_mlp_in,
        grad_w_mlp_out,
        grad_w_mod,
        grad_b_qkv[:D],
        grad_b_qkv[2 * D :],
        grad_b_attn_out,
        grad_b_mlp_in,
        grad_b_mlp_out,
        grad_b_mod,
    ]
    return (grad_middle + grad_from_a, grad_cond, grad_list)


def embed_forward(pieces, latent_part, noise_part, times_part, labels_part, dropped_part):
    mixing = times_part[:, None, None]
    noisy_bf = ((1.0 - mixing) * latent_part + mixing * noise_part).astype(low_type)
    tokens = linear_fwd(noisy_bf, pieces[0]) + pieces[1] + position_table()
    basis_bf = time_features(times_part).astype(low_type)
    time_pre = linear_fwd(basis_bf, pieces[2]) + pieces[3]
    time_act = jax.nn.silu(time_pre).astype(low_type)
    time_emb = linear_fwd(time_act, pieces[4]) + pieces[5]
    classes = jnp.where(dropped_part == 1, CLS - 1, labels_part)
    onehot = (classes[:, None] == jnp.arange(CLS, dtype=jnp.int32)[None, :]).astype(low_type)
    condition = time_emb + jnp.dot(onehot, pieces[6], preferred_element_type=full_type)
    saved = (noisy_bf, basis_bf, time_pre, time_act, onehot, condition)
    return (tokens, jax.nn.silu(condition).astype(low_type), saved)


def embed_backward(pieces, saved, grad_tokens, grad_modulator):
    noisy_bf, basis_bf, time_pre, time_act, onehot, condition = saved
    grad_cond = silu_back(condition, grad_modulator)
    grad_table = lax.dot_general(
        onehot.astype(full_type),
        grad_cond,
        (((0,), (0,)), ((), ())),
        precision=lax.Precision.HIGHEST,
    )
    grad_time_act, grad_w_time_out, grad_b_time_out = linear_back(
        time_act, pieces[4], grad_cond.astype(low_type)
    )
    grad_time_pre = silu_back(time_pre, grad_time_act).astype(low_type)
    _, grad_w_time_in, grad_b_time_in = linear_back(basis_bf, pieces[2], grad_time_pre, False)
    _, grad_w_patch, grad_b_patch = linear_back(
        noisy_bf, pieces[0], grad_tokens.astype(low_type), False
    )
    return [
        grad_w_patch,
        grad_b_patch,
        grad_w_time_in,
        grad_b_time_in,
        grad_w_time_out,
        grad_b_time_out,
        grad_table,
    ]


def projector_forward(pieces, residual, features_part):
    residual_bf = residual.astype(low_type)
    pre_a = linear_fwd(residual_bf, pieces[7]) + pieces[8]
    act_a = jax.nn.silu(pre_a).astype(low_type)
    pre_b = linear_fwd(act_a, pieces[9]) + pieces[10]
    act_b = jax.nn.silu(pre_b).astype(low_type)
    predicted = linear_fwd(act_b, pieces[11]) + pieces[12]
    loss_part = -proj_coeff * jnp.sum(cosine_rows(predicted, features_part)) / residual.shape[1]
    return (loss_part, (residual_bf, pre_a, act_a, pre_b, act_b, predicted))


def projector_backward(pieces, saved, features_part, seq_len, sample_total):
    residual_bf, pre_a, act_a, pre_b, act_b, predicted = saved
    _, cosine_pull = jax.vjp(
        lambda predicted_in: cosine_rows(predicted_in, features_part), predicted
    )
    seed = jnp.full(predicted.shape[:2], -proj_coeff / (seq_len * sample_total), full_type)
    grad_pred = cosine_pull(seed)[0].astype(low_type)
    grad_act_b, grad_w_c, grad_b_c = linear_back(act_b, pieces[11], grad_pred)
    grad_pre_b = silu_back(pre_b, grad_act_b).astype(low_type)
    grad_act_a, grad_w_b, grad_b_b = linear_back(act_a, pieces[9], grad_pre_b)
    grad_pre_a = silu_back(pre_a, grad_act_a).astype(low_type)
    grad_residual, grad_w_a, grad_b_a = linear_back(residual_bf, pieces[7], grad_pre_a)
    return (grad_residual, [grad_w_a, grad_b_a, grad_w_b, grad_b_b, grad_w_c, grad_b_c])


def head_forward(pieces, residual, modulator, target, weight_t):
    modulation = (linear_fwd(modulator, pieces[13]) + pieces[14])[:, None, :]
    shift_f, scale_f = jnp.split(modulation, 2, axis=-1)
    normed = modulated_norm(residual, shift_f, scale_f).astype(low_type)
    deviation = linear_fwd(normed, pieces[15]) + pieces[16] - target
    loss_part = jnp.sum(weight_t * jnp.mean(deviation * deviation, axis=(1, 2)))
    return (loss_part, (shift_f, scale_f, normed, deviation))


def head_backward(pieces, saved, residual, modulator, weight_t, sample_total):
    shift_f, scale_f, normed, deviation = saved
    scaled = (
        2.0 * weight_t[:, None, None] / (deviation.shape[1] * deviation.shape[2] * sample_total)
    )
    grad_output = (scaled * deviation).astype(low_type)
    grad_normed, grad_w_head, grad_b_head = linear_back(normed, pieces[15], grad_output)
    _, pullback = jax.vjp(modulated_norm, residual, shift_f, scale_f)
    grad_residual, grad_shift, grad_scale = pullback(grad_normed)
    grad_mod = jnp.concatenate([grad_shift, grad_scale], axis=-1)[:, 0, :].astype(low_type)
    grad_cond, grad_w_mod, grad_b_mod = linear_back(modulator, pieces[13], grad_mod)
    return (grad_residual, grad_cond, [grad_w_mod, grad_b_mod, grad_w_head, grad_b_head])


def from_units(units, plan):
    pieces = []
    for _, chunks, count, first, shape, matrix in plan.segments:
        part = units[first : first + count]
        if matrix:
            part = part.reshape(shape[0] // ROWS, chunks, ROWS, LANES).transpose(0, 2, 1, 3)
            pieces.append(part.reshape(shape))
        else:
            pieces.append(part.reshape(-1)[: math.prod(shape)].reshape(shape))
    return pieces


def into_units(grad_list, plan):
    parts = []
    for grad, (_, chunks, count, _, shape, matrix) in zip(grad_list, plan.segments):
        low = grad.astype(low_type)
        if matrix:
            low = low.reshape(shape[0] // ROWS, ROWS, chunks, LANES).transpose(0, 2, 1, 3)
            parts.append(low.reshape(count, ROWS, LANES))
        else:
            flat = jnp.pad(low.reshape(-1), ((0, count * UNIT - low.size),))
            parts.append(flat.reshape(count, ROWS, LANES))
    missing = plan.devices * plan.per - plan.units
    parts.append(jnp.zeros((missing, ROWS, LANES), low_type))
    return jnp.concatenate(parts)


def model_step(layer_lists, pieces, latents, noise, times, labels, dropped, features, devices):
    sample_total = latents.shape[0] * devices
    residual, modulator, embed_saved = embed_forward(
        pieces, latents, noise, times, labels, dropped
    )
    loss_total = jnp.zeros((), full_type)
    inputs, kept, square_sums = [], [], []
    for ordinal in range(LAYERS):
        inputs.append(residual)
        residual, saved, sums = layer_forward(layer_lists[ordinal], residual, modulator)
        kept.append(saved)
        square_sums.append(sums)
        if ordinal + 1 == DEPTH_Z:
            part, proj_saved = projector_forward(pieces, residual, features)
            loss_total = loss_total + part
    target = noise - latents
    weight_t = 1.0 + 2.0 * times
    part, head_saved = head_forward(pieces, residual, modulator, target, weight_t)
    loss_total = loss_total + part
    grad_residual, grad_cond, head_grads = head_backward(
        pieces, head_saved, residual, modulator, weight_t, sample_total
    )
    layer_grads = [None] * LAYERS
    for ordinal in reversed(range(LAYERS)):
        if ordinal + 1 == DEPTH_Z:
            grad_proj, proj_grads = projector_backward(
                pieces, proj_saved, features, residual.shape[1], sample_total
            )
            grad_residual = grad_residual + grad_proj
        grad_residual, cond_part, layer_grads[ordinal] = layer_backward(
            layer_lists[ordinal], kept[ordinal], inputs[ordinal], modulator, grad_residual
        )
        grad_cond = grad_cond + cond_part
    embed_grads = embed_backward(pieces, embed_saved, grad_residual, grad_cond)
    return (loss_total, jnp.stack(square_sums), layer_grads, embed_grads + proj_grads + head_grads)


def adam_update(weight, grad, first, second, clip_factor):
    clipped = grad * clip_factor
    first_new = beta_one * first + (1.0 - beta_one) * clipped
    second_new = beta_two * second + (1.0 - beta_two) * clipped * clipped
    first_hat = first_new / (1.0 - beta_one**STEP)
    second_hat = second_new / (1.0 - beta_two**STEP)
    weight_new = weight - learn_rate * (
        first_hat / (jnp.sqrt(second_hat) + adam_eps) + decay_rate * weight
    )
    return (weight_new, first_new, second_new)


def by_kernels(plan, root_plan, layer_flat, root_flat, data, devices):
    plans = (root_plan,) + (plan,) * LAYERS
    raws = [to_rows(root_flat, root_plan)]
    raws += [to_rows(layer_flat[ordinal], plan) for ordinal in range(LAYERS)]
    gathered = gather_units(plans, raws)
    pieces = from_units(gathered[0], root_plan)
    layer_lists = [from_units(units, plan) for units in gathered[1:]]
    loss_part, square_sums, layer_grads, root_grads = model_step(
        layer_lists, pieces, *data, devices
    )
    grads = [into_units(root_grads, root_plan)]
    grads += [into_units(grad_list, plan) for grad_list in layer_grads]
    numbers = jnp.concatenate([loss_part[None], square_sums.reshape(-1)])
    stats = jnp.pad(numbers, (0, 8 * LANES - numbers.shape[0])).reshape(8, LANES)
    rows, stats = reduce_units(plans, grads, stats)
    numbers = stats[0].reshape(-1)
    shard_root = rows[0].reshape(-1)[: root_plan.share]
    shard_layers = jnp.stack([r.reshape(-1)[: plan.share] for r in rows[1:]])
    sums = numbers[1 : 1 + 3 * LAYERS].reshape(LAYERS, 3)
    return (shard_layers, shard_root, numbers[0], sums, jnp.sum(stats[1]))


def by_collectives(layer_flat, root_flat, data, devices):
    whole = lambda part: lax.all_gather(part.astype(low_type), "fsdp", axis=0, tiled=True)
    layer_lists = [unflatten(whole(layer_flat[i]), layer_layout()) for i in range(LAYERS)]
    pieces = unflatten(whole(root_flat), root_layout())
    loss_part, square_sums, layer_grads, root_grads = model_step(
        layer_lists, pieces, *data, devices
    )

    def owned(grad_list, share):
        joined = jnp.concatenate([piece.reshape(-1) for piece in grad_list])
        joined = jnp.pad(joined, (0, share * devices - joined.shape[0]))
        return lax.psum_scatter(joined, "fsdp", scatter_dimension=0, tiled=True)

    shard_layers = jnp.stack([owned(grads, layer_flat.shape[1]) for grads in layer_grads])
    shard_root = owned(root_grads, root_flat.shape[0])
    local = jnp.sum(shard_layers * shard_layers) + jnp.sum(shard_root * shard_root)
    loss_sum, sums, square_total = lax.psum((loss_part, square_sums, local), "fsdp")
    return (shard_layers, shard_root, loss_sum, sums, square_total)


def shards(
    latents,
    noise,
    times,
    labels,
    dropped,
    features,
    layer_flat,
    layer_mean,
    layer_square,
    root_flat,
    root_mean,
    root_square,
):
    devices = lax.axis_size("fsdp")
    data = (latents, noise, times, labels, dropped, features)
    plan = Plan(layer_layout(), layer_flat.shape[1] * devices, devices)
    root_plan = Plan(root_layout(), root_flat.shape[0] * devices, devices)
    if devices % 8 == 0 and plan.fits and root_plan.fits:
        reduced = by_kernels(plan, root_plan, layer_flat, root_flat, data, devices)
    else:
        reduced = by_collectives(layer_flat, root_flat, data, devices)
    shard_layers, shard_root, loss_sum, stream_sums, square_total = reduced
    sample_total = latents.shape[0] * devices
    grad_norm = jnp.sqrt(square_total)
    clip_factor = clip_limit / jnp.maximum(grad_norm, clip_limit)
    activation_rms = jnp.sqrt(stream_sums / (sample_total * SEQ * D))
    new_layer, new_layer_mean, new_layer_square = adam_update(
        layer_flat, shard_layers, layer_mean, layer_square, clip_factor
    )
    new_root, new_root_mean, new_root_square = adam_update(
        root_flat, shard_root, root_mean, root_square, clip_factor
    )
    return (
        loss_sum,
        grad_norm,
        activation_rms,
        new_layer,
        new_layer_mean,
        new_layer_square,
        new_root,
        new_root_mean,
        new_root_square,
    )


def solution(mesh):
    in_specs = (
        P("fsdp", None, None),
        P("fsdp", None, None),
        P("fsdp"),
        P("fsdp"),
        P("fsdp"),
        P("fsdp", None, None),
        P(None, "fsdp"),
        P(None, "fsdp"),
        P(None, "fsdp"),
        P("fsdp"),
        P("fsdp"),
        P("fsdp"),
    )
    out_specs = (
        P(),
        P(),
        P(),
        P(None, "fsdp"),
        P(None, "fsdp"),
        P(None, "fsdp"),
        P("fsdp"),
        P("fsdp"),
        P("fsdp"),
    )
    return jax.shard_map(shards, mesh=mesh, in_specs=in_specs, out_specs=out_specs, check_vma=False)
```

```python
import functools
import math

import jax
import jax.numpy as jnp
from jax import lax
from jax.experimental import pallas as pl
from jax.experimental.pallas import tpu as pltpu
from jax.sharding import PartitionSpec as P

D = 768
HD = 64
FF = 3072
PD = 16
CLS = 1001
PH = 2048
ZD = 768
FREQ = 256
GRID = 16
LAYERS = 2
DEPTH_Z = 2
STEP = 10
SEQ = 256


norm_eps = 1e-06
clip_limit = 0.002
learn_rate = 0.08
beta_one = 0.5
beta_two = 0.5
adam_eps = 1e-08
decay_rate = 0.01
proj_coeff = 0.5
low_type = jnp.bfloat16
full_type = jnp.float32


LANES = 128
ROWS = 16
UNIT = LANES * ROWS
MESH = pl.DeviceIdType.MESH

def up(value, step):
    return -(-value // step) * step

class Plan:
    def __init__(self, layout, length, devices):
        self.length = length
        self.devices = devices
        self.share = length // devices
        self.segments = []
        offset = units = 0
        for shape in layout:
            amount = math.prod(shape)
            matrix = len(shape) == 2 and shape[0] % ROWS == 0 and shape[1] % LANES == 0
            chunks = shape[1] // LANES if matrix else 1
            count = up(amount, UNIT) // UNIT
            self.segments.append((offset // LANES, chunks, count, units, shape, matrix))
            offset += amount
            units += count
        self.units = units
        self.per = up(up(units, devices) // devices, 4)
        rows_of = []
        for base, chunks, count, _, _, _ in self.segments:
            for u in range(count):
                b, c = divmod(u, chunks)
                first = base + b * ROWS * chunks + c
                rows_of.append((first, first + (ROWS - 1) * chunks))
        before = after = 0
        for d in range(devices):
            start, stop = d * self.share // LANES, (d + 1) * self.share // LANES
            for lo, hi in rows_of[self.per * d : self.per * d + self.per]:
                before, after = max(before, start - lo), max(after, hi + 1 - stop)
        self.before, self.after = up(before, 8), up(after, 8)
        units_before = units_after = 0
        for u, (lo, hi) in enumerate(rows_of):
            first = lo * LANES // self.share
            last = min(((hi + 1) * LANES - 1) // self.share, devices - 1)
            for d in range(first, last + 1):
                units_before = max(units_before, self.per * d - u)
                units_after = max(units_after, u + 1 - self.per * d - self.per)
        self.units_before, self.units_after = units_before, units_after
        self.half = self.per // 2
        self.raw = up(up(self.share, LANES) // LANES + 9, 64)
        self.ext = self.before + self.raw + self.after
        margin = tail = 0
        for d in range(devices):
            start = d * self.share // LANES
            lo = max(self.per * d - units_before, 0)
            for first, last in rows_of[lo : self.per * d + self.per + units_after]:
                margin, tail = max(margin, start - first), max(tail, last + 1 - start)
        self.margin = up(margin, 8)
        self.spread = up(max(tail, self.raw + 8), 8) + self.margin
        least = self.share // LANES
        self.fits = max(self.before, self.after) < least and max(units_before, units_after) < self.per

def place(index, zs):
    return index // 8, index // 4 % 2, index // 2 % 2, index % 2

def gather_kernel(plans, zs, *refs):
    nb = len(plans)
    raw_hbm = refs[:nb]
    outs = refs[nb : 2 * nb]
    raw, ext, tail, from_prev, from_next, slots = (refs[2 * nb + i * nb : 3 * nb + i * nb] for i in range(6))
    rest = refs[8 * nb :]
    load_sem, halo_send, halo_recv, own_sem, send_sem, zr, xa, xb, yb, ya, cr = rest
    n = zs * 8
    me = lax.axis_index("fsdp")
    z, y, x, c = place(me, zs)
    index = lambda zz, yy, xx, cc: ((zz * 2 + yy) * 2 + xx) * 2 + cc
    prev, following = lax.rem(me + n - 1, n), lax.rem(me + 1, n)
    xpeer, ypeer, cpeer = index(z, y, 1 - x, c), index(z, 1 - y, x, c), index(z, y, x, 1 - c)
    zpeer = [index(lax.rem(z + k, zs), y, x, c) for k in range(zs)]
    loads = []
    for b in range(nb):
        p = plans[b]
        loads.append(pltpu.make_async_copy(raw_hbm[b], raw[b].at[pl.ds(8, p.raw)], load_sem.at[b]))
        loads[b].start()
    barrier = pltpu.get_barrier_semaphore()
    peers = [prev, following, xpeer, ypeer, cpeer] + zpeer[1:]
    for peer in peers:
        pl.semaphore_signal(barrier, inc=1, device_id=(peer,), device_id_type=MESH)
    halos = []
    lane = lax.broadcasted_iota(jnp.int32, (64, LANES), 1)
    for b in range(nb):
        p = plans[b]
        shift = lax.rem(me * p.share, LANES)
        delta = (me + 1) * p.share // LANES - me * p.share // LANES
        raw[b][pl.ds(0, 8), :] = jnp.zeros((8, LANES), full_type)
        ext[b][pl.ds(0, p.before), :] = jnp.zeros((p.before, LANES), full_type)
        ext[b][pl.ds(p.before + p.raw, p.after), :] = jnp.zeros((p.after, LANES), full_type)
        loads[b].wait()

        def align(i, carry):
            row = pl.multiple_of(i * 64, 64)
            here = pltpu.roll(raw[b][pl.ds(row + 8, 64), :], shift, 1)
            above = pltpu.roll(raw[b][pl.ds(row + 7, 64), :], shift, 1)
            ext[b][pl.ds(row + p.before, 64), :] = jnp.where(lane >= shift, here, above)
            return carry

        lax.fori_loop(0, p.raw // 64, align, 0)
        tail[b][...] = ext[b][pl.ds(delta, p.before + 8), :]
        if b == 0:
            pl.semaphore_wait(barrier, len(peers))
        for s, (src, dst, to) in enumerate(((ext[b].at[pl.ds(p.before, p.after)], from_next[b], prev), (tail[b], from_prev[b], following))):
            copy = pltpu.make_async_remote_copy(src, dst, halo_send.at[2 * b + s], halo_recv.at[2 * b + s], device_id=(to,), device_id_type=MESH)
            copy.start()
            halos.append(copy)
    sends = []

    def send(src, dst, sem, to):
        copy = pltpu.make_async_remote_copy(src, dst, send_sem.at[len(sends)], sem, device_id=(to,), device_id_type=MESH)
        copy.start()
        sends.append(copy)

    def span(b, h):
        p = plans[b]
        return (0, p.half) if h == 0 else (p.half, p.per - p.half)

    def slot(k, dy, dx, dc):
        return index(lax.rem(z + zs - k, zs), 1 - y if dy else y, 1 - x if dx else x, 1 - c if dc else c)

    def part(b, h, k, dy, dx, dc=0):
        first, count = span(b, h)
        return outs[b].at[pl.ds(slot(k, dy, dx, dc) * plans[b].per + first, count)]

    def whole(b, k, dy, dx, dc=0):
        return outs[b].at[pl.ds(slot(k, dy, dx, dc) * plans[b].per, plans[b].per)]

    def arrived(ref, sem):
        pltpu.make_async_copy(ref, ref, sem).wait()

    owns = []
    for b in range(nb):
        p = plans[b]
        delta = (me + 1) * p.share // LANES - me * p.share // LANES
        for copy in halos[2 * b : 2 * b + 2]:
            copy.wait()
        ext[b][pl.ds(0, p.before + 8), :] += from_prev[b][...]
        ext[b][pl.ds(p.before + delta, p.after), :] += from_next[b][...]
        top = me * p.share // LANES - p.before
        for base, chunks, count, first_unit, _, _ in p.segments:
            lo = jnp.clip(p.per * me - first_unit, 0, count)
            hi = jnp.clip(p.per * me + p.per - first_unit, 0, count)

            def unit(u, carry):
                block = u // chunks
                row = base + block * (ROWS * chunks) + (u - block * chunks) - top
                if chunks == 1:
                    value = ext[b][pl.ds(row, ROWS), :]
                else:
                    value = ext[b][pl.ds(row, ROWS, stride=chunks), :]
                slots[b][first_unit + u - p.per * me] = value.astype(low_type)
                return carry

            lax.fori_loop(lo, hi, unit, 0)
        own = pltpu.make_async_copy(slots[b], whole(b, 0, 0, 0), own_sem.at[b])
        own.start()
        owns.append(own)
        mine = lambda h: slots[b].at[pl.ds(*span(b, h))]
        for k in range(1, zs):
            for h in range(2):
                send(mine(h), part(b, h, 0, 0, 0), zr.at[b, h, k], zpeer[k])
        send(mine(0), part(b, 0, 0, 0, 0), xa.at[b, 0], xpeer)
        send(mine(1), part(b, 1, 0, 0, 0), yb.at[b, 0], ypeer)
        send(mine(0), part(b, 0, 0, 0, 0), ya.at[b, 0, 0], ypeer)
        send(mine(1), part(b, 1, 0, 0, 0), xb.at[b, 0, 0], xpeer)
        send(slots[b], whole(b, 0, 0, 0), cr.at[b, 0, 0, 0], cpeer)
    for b in range(nb):
        for k in range(1, zs):
            arrived(part(b, 0, k, 0, 0), zr.at[b, 0, k])
            send(part(b, 0, k, 0, 0), part(b, 0, k, 0, 0), xa.at[b, k], xpeer)
            arrived(part(b, 1, k, 0, 0), zr.at[b, 1, k])
            send(part(b, 1, k, 0, 0), part(b, 1, k, 0, 0), yb.at[b, k], ypeer)
            send(part(b, 0, k, 0, 0), part(b, 0, k, 0, 0), ya.at[b, k, 0], ypeer)
            send(part(b, 1, k, 0, 0), part(b, 1, k, 0, 0), xb.at[b, k, 0], xpeer)
            send(whole(b, k, 0, 0), whole(b, k, 0, 0), cr.at[b, k, 0, 0], cpeer)
        for k in range(zs):
            arrived(part(b, 0, k, 0, 1), xa.at[b, k])
            send(part(b, 0, k, 0, 1), part(b, 0, k, 0, 1), ya.at[b, k, 1], ypeer)
            arrived(part(b, 1, k, 1, 0), yb.at[b, k])
            send(part(b, 1, k, 1, 0), part(b, 1, k, 1, 0), xb.at[b, k, 1], xpeer)
        for k in range(zs):
            arrived(part(b, 1, k, 0, 1), xb.at[b, k, 0])
            send(whole(b, k, 0, 1), whole(b, k, 0, 1), cr.at[b, k, 0, 1], cpeer)
            arrived(part(b, 0, k, 1, 0), ya.at[b, k, 0])
            send(whole(b, k, 1, 0), whole(b, k, 1, 0), cr.at[b, k, 1, 0], cpeer)
        for k in range(zs):
            arrived(part(b, 1, k, 1, 1), xb.at[b, k, 1])
            arrived(part(b, 0, k, 1, 1), ya.at[b, k, 1])
            send(whole(b, k, 1, 1), whole(b, k, 1, 1), cr.at[b, k, 1, 1], cpeer)
    for b in range(nb):
        owns[b].wait()
        for k in range(zs):
            for dy in range(2):
                for dx in range(2):
                    arrived(whole(b, k, dy, dx, 1), cr.at[b, k, dy, dx])
    for copy in sends:
        copy.wait_send()

def gather_units(plans, raws):
    n = plans[0].devices
    zs = n // 8
    nb = len(plans)
    per_bucket = 2 * (zs - 1) + 10 * zs
    dma = pltpu.SemaphoreType.DMA
    scratch = [pltpu.VMEM((p.raw + 8, LANES), full_type) for p in plans]
    scratch += [pltpu.VMEM((p.ext, LANES), full_type) for p in plans]
    scratch += [pltpu.VMEM((p.before + 8, LANES), full_type) for p in plans]
    scratch += [pltpu.VMEM((p.before + 8, LANES), full_type) for p in plans]
    scratch += [pltpu.VMEM((p.after, LANES), full_type) for p in plans]
    scratch += [pltpu.VMEM((p.per, ROWS, LANES), low_type) for p in plans]
    scratch += [dma((nb,)), dma((2 * nb,)), dma((2 * nb,)), dma((nb,)), dma((nb * per_bucket,))]
    scratch += [dma((nb, 2, zs)), dma((nb, zs)), dma((nb, zs, 2)), dma((nb, zs)), dma((nb, zs, 2)), dma((nb, zs, 2, 2))]
    return pl.pallas_call(
        functools.partial(gather_kernel, plans, zs),
        out_shape=[jax.ShapeDtypeStruct((n * p.per, ROWS, LANES), low_type) for p in plans],
        in_specs=[pl.BlockSpec(memory_space=pl.ANY)] * nb,
        out_specs=[pl.BlockSpec(memory_space=pl.ANY)] * nb,
        scratch_shapes=scratch,
        compiler_params=pltpu.CompilerParams(collective_id=0, has_side_effects=True, vmem_limit_bytes=48 * 1024 * 1024),
        name="gather_units",
    )(*raws)

def reduce_kernel(plans, zs, *refs):
    nb = len(plans)
    take = lambda count: tuple(next(feed) for _ in range(count))
    feed = iter(refs)
    grads, (stats_in,) = take(nb), take(1)
    outs, (stats_out,), first = take(nb), take(1), take(nb)
    kept_a, kept_b, two_a, two_b, three_a, three_b, four = (take(nb) for _ in range(7))
    local, other = take(1)[0], take(1)[0]
    units_f, rows_f, flat_f = take(1)[0], take(1)[0], take(1)[0]
    from_prev, from_next = take(nb), take(nb)
    total, total_in = take(1)[0], take(1)[0]
    s1, r1, s2a, r2a, s2b, r2b, s3a, r3a, s3b, r3b, s4, r4, load_sem, halo_s, halo_r, out_sem, ss, sr = take(18)
    n = zs * 8
    me = lax.axis_index("fsdp")
    z, y, x, c = place(me, zs)
    index = lambda zz, yy, xx, cc: ((zz * 2 + yy) * 2 + xx) * 2 + cc
    prev, following = lax.rem(me + n - 1, n), lax.rem(me + 1, n)
    xpeer, ypeer, cpeer = index(z, y, 1 - x, c), index(z, 1 - y, x, c), index(z, y, x, 1 - c)
    below = lambda k: index(lax.rem(z + zs - k, zs), y, x, c)
    above = lambda k: index(lax.rem(z + k, zs), y, x, c)
    barrier = pltpu.get_barrier_semaphore()
    peers = [prev, following, xpeer, ypeer, cpeer] + [above(k) for k in range(1, zs)]
    for peer in peers:
        pl.semaphore_signal(barrier, inc=1, device_id=(peer,), device_id_type=MESH)
    pl.semaphore_wait(barrier, len(peers))

    def remote(src, dst, send_sem, recv_sem, to):
        return pltpu.make_async_remote_copy(src, dst, send_sem, recv_sem, device_id=(to,), device_id_type=MESH)

    def arrived(ref, sem):
        pltpu.make_async_copy(ref, ref, sem).wait()

    def slot(b, k, dy, dx, dc):
        where = index(lax.rem(z + zs - k, zs), 1 - y if dy else y, 1 - x if dx else x, 1 - c if dc else c)
        return grads[b].at[pl.ds(where * plans[b].per, plans[b].per)]

    order = ((1, 1), (1, 0), (0, 1), (0, 0))

    def sibling(b, k, dy, dx):
        return remote(slot(b, k, dy, dx, 1), first[b].at[k, dy, dx], s1.at[b, k, dy, dx], r1.at[b, k, dy, dx], cpeer)

    for b in range(nb):
        for dy, dx in order:
            for k in range(zs):
                sibling(b, k, dy, dx).start()

    def add(p, dst, at, one, one_at, two, two_at):
        step = p.half // 2

        def body(i, carry):
            span = lambda ref, off: ref[pl.ds(off + i * step, step)].astype(full_type)
            dst[pl.ds(at + i * step, step)] = (span(one, one_at) + span(two, two_at)).astype(low_type)
            return carry

        lax.fori_loop(0, 2, body, 0)

    ring = local.shape[0]
    used = []

    def send_of(b, h, k, dy, dx, src):
        if h == 0:
            return remote(src, two_a[b].at[k, dx], s2a.at[b, k, dx], r2a.at[b, k, dx], ypeer)
        return remote(src, two_b[b].at[k, dy], s2b.at[b, k, dy], r2b.at[b, k, dy], xpeer)

    steps = [(b, dy, dx, k) for b in range(nb) for dy, dx in order for k in range(zs)]

    def loads(number):
        b, dy, dx, k = steps[number]
        at = number % ring
        p = plans[b]
        one = pltpu.make_async_copy(slot(b, k, dy, dx, 0), local.at[at, pl.ds(0, p.per)], load_sem.at[at, 0])
        two = pltpu.make_async_copy(first[b].at[k, dy, dx], other.at[number % 2, pl.ds(0, p.per)], load_sem.at[at, 1])
        return one, two

    pending = {}

    def prepare(number):
        b, dy, dx, k = steps[number]
        for copy in pending.pop(number % ring, ()):
            copy.wait_send()
        one, two = loads(number)
        one.start()
        arrived(first[b].at[k, dy, dx], r1.at[b, k, dy, dx])
        two.start()

    def phase_one(number):
        b, dy, dx, k = steps[number]
        p = plans[b]
        at = number % ring
        if number == 0:
            prepare(0)
        if number + 1 < len(steps):
            prepare(number + 1)
        for copy in loads(number):
            copy.wait()
        mine, theirs = local.at[at], other.at[number % 2]
        going = []
        if dy:
            add(p, mine, 0, mine, 0, theirs, 0)
            going.append(send_of(b, 0, k, dy, dx, local.at[at, pl.ds(0, p.half)]))
        else:
            add(p, kept_a[b].at[k, dx], 0, mine, 0, theirs, 0)
        if dx:
            add(p, mine, p.half, mine, p.half, theirs, p.half)
            going.append(send_of(b, 1, k, dy, dx, local.at[at, pl.ds(p.half, p.half)]))
        else:
            add(p, kept_b[b].at[k, dy], 0, mine, p.half, theirs, p.half)
        for copy in going:
            copy.start()
        pending[at] = going

    def three(b, h, k):
        if h == 0:
            return remote(two_a[b].at[k, 1], three_a[b].at[k], s3a.at[b, k], r3a.at[b, k], xpeer)
        return remote(two_b[b].at[k, 1], three_b[b].at[k], s3b.at[b, k], r3b.at[b, k], ypeer)

    def last(b, h, k):
        src = (three_a if h == 0 else three_b)[b].at[k]
        return remote(src, four[b].at[h, k - 1], s4.at[b, h, k - 1], r4.at[b, h, k - 1], below(k))

    def phase_two(b):
        p = plans[b]
        for far in (1, 0):
            for k in range(zs):
                for h, kept, two, sem in ((0, kept_a, two_a, r2a), (1, kept_b, two_b, r2b)):
                    arrived(two[b].at[k, far], sem.at[b, k, far])
                    if far:
                        add(p, two[b].at[k, 1], 0, two[b].at[k, 1], 0, kept[b].at[k, 1], 0)
                        three(b, h, k).start()
                    else:
                        add(p, kept[b].at[k, 0], 0, two[b].at[k, 0], 0, kept[b].at[k, 0], 0)

    def phase_three(b):
        p = plans[b]
        for k in list(range(1, zs)) + [0]:
            for h, kept, got, sem in ((0, kept_a, three_a, r3a), (1, kept_b, three_b, r3b)):
                arrived(got[b].at[k], sem.at[b, k])
                if k:
                    add(p, got[b].at[k], 0, got[b].at[k], 0, kept[b].at[k, 0], 0)
                    last(b, h, k).start()

    def finish(b):
        p = plans[b]
        base = p.units_before
        for h, kept, got in ((0, kept_a, three_a), (1, kept_b, three_b)):
            for k in range(1, zs):
                arrived(four[b].at[h, k - 1], r4.at[b, h, k - 1])
            step = p.half // 2

            def body(i, carry):
                part = pl.ds(i * step, step)
                value = kept[b][0, 0, part].astype(full_type) + got[b][0, part].astype(full_type)
                for k in range(1, zs):
                    value = value + four[b][h, k - 1, part].astype(full_type)
                units_f[pl.ds(base + h * p.half + i * step, step)] = value
                return carry

            lax.fori_loop(0, 2, body, 0)
        forward = remote(units_f.at[pl.ds(p.per, base)], from_prev[b], halo_s.at[b, 0], halo_r.at[b, 0], following)
        backward = remote(units_f.at[pl.ds(base, p.units_after)], from_next[b], halo_s.at[b, 1], halo_r.at[b, 1], prev)
        forward.start()
        backward.start()
        forward.wait()
        backward.wait()
        units_f[pl.ds(0, base)] = from_prev[b][...]
        units_f[pl.ds(base + p.per, p.units_after)] = from_next[b][...]
        top = me * p.share // LANES - p.margin
        for origin, chunks, count, first_unit, _, _ in p.segments:
            lo = jnp.clip(p.per * me - base - first_unit, 0, count)
            hi = jnp.clip(p.per * me + p.per + p.units_after - first_unit, 0, count)

            def unit(u, carry):
                block = u // chunks
                row = origin + block * (ROWS * chunks) + (u - block * chunks) - top
                value = units_f[first_unit + u - p.per * me + base]
                if chunks == 1:
                    rows_f[pl.ds(row, ROWS), :] = value
                else:
                    rows_f[pl.ds(row, ROWS, stride=chunks), :] = value
                return carry

            lax.fori_loop(lo, hi, unit, 0)
        shift = lax.rem(me * p.share, LANES)
        turn = lax.rem(LANES - shift, LANES)
        lane = lax.broadcasted_iota(jnp.int32, (64, LANES), 1)
        spot = lax.broadcasted_iota(jnp.int32, (64, LANES), 0) * LANES + lane
        if b:
            pltpu.make_async_copy(flat_f.at[pl.ds(0, plans[b - 1].raw)], outs[b - 1], out_sem.at[b - 1]).wait()

        def unalign(i, squares):
            row = pl.multiple_of(i * 64, 64)
            here = pltpu.roll(rows_f[pl.ds(row + p.margin, 64), :], turn, 1)
            below_row = pltpu.roll(rows_f[pl.ds(row + p.margin + 1, 64), :], turn, 1)
            value = jnp.where(lane < LANES - shift, here, below_row)
            value = jnp.where(spot + row * LANES < p.share, value, 0.0)
            flat_f[pl.ds(row, 64), :] = value
            return squares + jnp.sum((value * value).reshape(8, 8, LANES), axis=0)

        squares = lax.fori_loop(0, p.raw // 64, unalign, jnp.zeros((8, LANES), full_type))
        pltpu.make_async_copy(flat_f.at[pl.ds(0, p.raw)], outs[b], out_sem.at[b]).start()
        return squares

    per_bucket = 4 * zs
    for b in range(nb):
        for number in range(b * per_bucket, (b + 1) * per_bucket):
            phase_one(number)
        if b:
            phase_two(b - 1)
            phase_three(b - 1)
    phase_two(nb - 1)
    phase_three(nb - 1)
    squares = jnp.zeros((8, LANES), full_type)
    for b in range(nb):
        squares = squares + finish(b)
    pltpu.make_async_copy(flat_f.at[pl.ds(0, plans[nb - 1].raw)], outs[nb - 1], out_sem.at[nb - 1]).wait()
    total[0] = stats_in[...]
    total[1] = squares
    step = 0
    for to in ((cpeer,), (xpeer,), (ypeer,), tuple(above(k) for k in range(1, zs))):
        copies = []
        for peer in to:
            copies.append(remote(total, total_in.at[step], ss.at[step], sr.at[step], peer))
            copies[-1].start()
            step += 1
        for copy in copies:
            copy.wait()
        value = total[...]
        for i in range(len(to)):
            value = value + total_in[step - 1 - i]
        total[...] = value
    stats_out[...] = total[...]
    for group in pending.values():
        for copy in group:
            copy.wait_send()
    for b in range(nb):
        for dy, dx in order:
            for k in range(zs):
                sibling(b, k, dy, dx).wait_send()
        for h in range(2):
            for k in range(zs):
                three(b, h, k).wait_send()
                if k:
                    last(b, h, k).wait_send()

def reduce_units(plans, grads, stats):
    n = plans[0].devices
    zs = n // 8
    nb = len(plans)
    dma = pltpu.SemaphoreType.DMA
    most = max(p.per for p in plans)
    tile = (ROWS, LANES)
    half = lambda p, *lead: pltpu.VMEM(lead + (p.half,) + tile, low_type)
    scratch = [half(p, zs, 2) for p in plans] + [half(p, zs, 2) for p in plans]
    scratch += [half(p, zs, 2) for p in plans] + [half(p, zs, 2) for p in plans]
    scratch += [half(p, zs) for p in plans] + [half(p, zs) for p in plans]
    scratch += [half(p, 2, zs - 1) for p in plans]
    ring = 4
    scratch += [pltpu.VMEM((ring, most) + tile, low_type), pltpu.VMEM((2, most) + tile, low_type)]
    scratch += [pltpu.VMEM((max(p.units_before + p.per + p.units_after for p in plans),) + tile, full_type)]
    scratch += [pltpu.VMEM((max(p.spread for p in plans), LANES), full_type)]
    scratch += [pltpu.VMEM((max(p.raw for p in plans), LANES), full_type)]
    scratch += [pltpu.VMEM((p.units_before,) + tile, full_type) for p in plans]
    scratch += [pltpu.VMEM((p.units_after,) + tile, full_type) for p in plans]
    hops = 2 + zs
    scratch += [pltpu.VMEM((2, 8, LANES), full_type), pltpu.VMEM((hops, 2, 8, LANES), full_type)]
    scratch += [dma((nb, zs, 2, 2))] * 2 + [dma((nb, zs, 2))] * 4 + [dma((nb, zs))] * 4
    scratch += [dma((nb, 2, zs - 1))] * 2 + [dma((ring, 2)), dma((nb, 2)), dma((nb, 2)), dma((nb,)), dma((hops,)), dma((hops,))]
    anywhere = pl.BlockSpec(memory_space=pl.ANY)
    inside = pl.BlockSpec(memory_space=pltpu.VMEM)
    out_shape = [jax.ShapeDtypeStruct((p.raw, LANES), full_type) for p in plans]
    out_shape += [jax.ShapeDtypeStruct((2, 8, LANES), full_type)]
    out_shape += [jax.ShapeDtypeStruct((zs, 2, 2, p.per) + tile, low_type) for p in plans]
    results = pl.pallas_call(
        functools.partial(reduce_kernel, plans, zs),
        out_shape=out_shape,
        in_specs=[anywhere] * nb + [inside],
        out_specs=[anywhere] * nb + [inside] + [anywhere] * nb,
        scratch_shapes=scratch,
        compiler_params=pltpu.CompilerParams(collective_id=1, has_side_effects=True, vmem_limit_bytes=62 * 1024 * 1024),
        name="reduce_units",
    )(*grads, stats)
    return results[:nb], results[nb]

def to_rows(flat, plan):
    padded = jnp.pad(flat, ((0, plan.raw * LANES - flat.shape[0]),))
    return padded.reshape(plan.raw, LANES)


def layer_layout():
    return [
        (D, 3 * D),
        (D, D),
        (D, FF),
        (FF, D),
        (D, 6 * D),
        (D,),
        (D,),
        (D,),
        (FF,),
        (D,),
        (6 * D,),
    ]


def root_layout():
    return [
        (PD, D),
        (D,),
        (FREQ, D),
        (D,),
        (D, D),
        (D,),
        (CLS, D),
        (D, PH),
        (PH,),
        (PH, PH),
        (PH,),
        (PH, ZD),
        (ZD,),
        (D, 2 * D),
        (2 * D,),
        (D, PD),
        (PD,),
    ]


def unflatten(vector, layout):
    pieces = []
    offset = 0
    for dimensions in layout:
        amount = math.prod(dimensions)
        pieces.append(vector[offset : offset + amount].reshape(dimensions))
        offset += amount
    return pieces


def flatten_grads(grad_list, length):
    joined = jnp.concatenate([piece.reshape(-1) for piece in grad_list])
    return jnp.concatenate([joined, jnp.zeros((length - joined.shape[0],), full_type)])


def position_table():
    quarter = D // 4
    frequency = 1.0 / 10000.0 ** (jnp.arange(quarter, dtype=jnp.float32) / quarter)
    coords = jnp.arange(GRID, dtype=jnp.float32)
    angles = coords[:, None] * frequency[None, :]
    one_axis = jnp.concatenate([jnp.sin(angles), jnp.cos(angles)], axis=1)
    row_part = jnp.repeat(one_axis, GRID, axis=0)
    col_part = jnp.tile(one_axis, (GRID, 1))
    return jnp.concatenate([row_part, col_part], axis=1)


def time_features(times_in):
    half_freq = FREQ // 2
    frequency = jnp.exp(-math.log(10000.0) * jnp.arange(half_freq, dtype=jnp.float32) / half_freq)
    angles = times_in[:, None] * frequency[None, :]
    return jnp.concatenate([jnp.cos(angles), jnp.sin(angles)], axis=1)


def modulated_norm(values, offsets, scales):
    centred = values - jnp.mean(values, axis=-1, keepdims=True)
    spread = jnp.mean(centred * centred, axis=-1, keepdims=True)
    return centred * lax.rsqrt(spread + norm_eps) * (1.0 + scales) + offsets


def softmax_rows(scores):
    row_max = jnp.max(scores, axis=-1, keepdims=True)
    exponent = jnp.exp(scores - row_max)
    return exponent / jnp.sum(exponent, axis=-1, keepdims=True)


def gelu_tanh(values):
    return jax.nn.gelu(values, approximate=True)


def cosine_rows(predicted, target):
    target_full = target.astype(full_type)
    inner_sum = jnp.sum(predicted * target_full, axis=-1)
    return (
        inner_sum
        * lax.rsqrt(jnp.sum(predicted * predicted, axis=-1) + norm_eps)
        * lax.rsqrt(jnp.sum(target_full * target_full, axis=-1) + norm_eps)
    )


def silu_back(values, grad_in):
    _, pullback = jax.vjp(jax.nn.silu, values)
    return pullback(grad_in)[0]


def linear_fwd(inputs, weight):
    leading = inputs.shape[:-1]
    product = jnp.dot(
        inputs.reshape(-1, inputs.shape[-1]), weight, preferred_element_type=full_type
    )
    return product.reshape(leading + (weight.shape[1],))


def linear_back(inputs, weight, grad_out, with_input=True):
    rows_in = inputs.reshape(-1, inputs.shape[-1])
    rows_out = grad_out.reshape(-1, grad_out.shape[-1])
    grad_weight = lax.dot_general(
        rows_in, rows_out, (((0,), (0,)), ((), ())), preferred_element_type=full_type
    )
    grad_bias = jnp.sum(rows_out.astype(full_type), axis=0)
    grad_in = None
    if with_input:
        grad_in = lax.dot_general(
            rows_out, weight, (((1,), (1,)), ((), ())), preferred_element_type=full_type
        ).reshape(inputs.shape)
    return (grad_in, grad_weight, grad_bias)


def layer_forward(weights, residual, modulator):
    (
        w_attn_in,
        w_attn_out,
        w_mlp_in,
        w_mlp_out,
        w_modulate,
        b_query,
        b_value,
        b_attn_out,
        b_mlp_in,
        b_mlp_out,
        b_modulate,
    ) = weights
    samples_mb, seq_len = (residual.shape[0], residual.shape[1])
    head_count = D // HD
    modulation = jnp.split((linear_fwd(modulator, w_modulate) + b_modulate)[:, None, :], 6, axis=-1)
    normed_a = modulated_norm(residual, modulation[0], modulation[1]).astype(low_type)
    bias_qkv = jnp.concatenate([b_query, jnp.zeros_like(b_query), b_value])
    qkv_low = (linear_fwd(normed_a, w_attn_in) + bias_qkv).astype(low_type)
    qkv_low = qkv_low.reshape(samples_mb, seq_len, 3, head_count, HD)
    query_bf, key_bf, value_bf = (qkv_low[:, :, 0], qkv_low[:, :, 1], qkv_low[:, :, 2])
    scores = jnp.einsum(
        "bqhd,bkhd->bhqk", query_bf, key_bf, preferred_element_type=full_type
    ) * HD ** (-0.5)
    attn_probs = softmax_rows(scores)
    probs_bf = attn_probs.astype(low_type)
    heads_bf = jnp.einsum("bhqk,bkhd->bqhd", probs_bf, value_bf, preferred_element_type=full_type)
    heads_bf = heads_bf.astype(low_type).reshape(samples_mb, seq_len, D)
    attn_out = linear_fwd(heads_bf, w_attn_out) + b_attn_out
    middle = residual + modulation[2] * attn_out
    normed_m = modulated_norm(middle, modulation[3], modulation[4]).astype(low_type)
    mlp_pre = linear_fwd(normed_m, w_mlp_in) + b_mlp_in
    act_bf = gelu_tanh(mlp_pre).astype(low_type)
    mlp_out = linear_fwd(act_bf, w_mlp_out) + b_mlp_out
    residual_out = middle + modulation[5] * mlp_out
    square_sums = jnp.stack(
        [
            jnp.sum(residual_out * residual_out),
            jnp.sum(attn_out * attn_out),
            jnp.sum(mlp_out * mlp_out),
        ]
    )
    saved = (
        modulation,
        normed_a,
        query_bf,
        key_bf,
        value_bf,
        attn_probs,
        probs_bf,
        heads_bf,
        attn_out,
        middle,
        normed_m,
        mlp_pre,
        act_bf,
        mlp_out,
    )
    return (residual_out, saved, square_sums)


def layer_backward(weights, saved, residual, modulator, grad_out):
    w_attn_in, w_attn_out, w_mlp_in, w_mlp_out, w_modulate = weights[:5]
    (
        modulation,
        normed_a,
        query_bf,
        key_bf,
        value_bf,
        attn_probs,
        probs_bf,
        heads_bf,
        attn_out,
        middle,
        normed_m,
        mlp_pre,
        act_bf,
        mlp_out,
    ) = saved
    samples_mb, seq_len = (residual.shape[0], residual.shape[1])
    grad_mlp = (modulation[5] * grad_out).astype(low_type)
    grad_act, grad_w_mlp_out, grad_b_mlp_out = linear_back(act_bf, w_mlp_out, grad_mlp)
    _, gelu_pull = jax.vjp(gelu_tanh, mlp_pre)
    grad_pre = gelu_pull(grad_act)[0].astype(low_type)
    grad_normed_m, grad_w_mlp_in, grad_b_mlp_in = linear_back(normed_m, w_mlp_in, grad_pre)
    _, norm_pull_m = jax.vjp(modulated_norm, middle, modulation[3], modulation[4])
    grad_from_m, grad_shift_m, grad_scale_m = norm_pull_m(grad_normed_m)
    grad_middle = grad_out + grad_from_m
    grad_attn = (modulation[2] * grad_middle).astype(low_type)
    grad_heads, grad_w_attn_out, grad_b_attn_out = linear_back(heads_bf, w_attn_out, grad_attn)
    grad_heads_bf = grad_heads.astype(low_type).reshape(samples_mb, seq_len, D // HD, HD)
    grad_probs = jnp.einsum(
        "bqhd,bkhd->bhqk", grad_heads_bf, value_bf, preferred_element_type=full_type
    )
    grad_value = jnp.einsum(
        "bhqk,bqhd->bkhd", probs_bf, grad_heads_bf, preferred_element_type=full_type
    )
    grad_scores = attn_probs * (
        grad_probs - jnp.sum(attn_probs * grad_probs, axis=-1, keepdims=True)
    )
    grad_scores = grad_scores.astype(low_type)
    grad_query = jnp.einsum(
        "bhqk,bkhd->bqhd", grad_scores, key_bf, preferred_element_type=full_type
    ) * HD ** (-0.5)
    grad_key = jnp.einsum(
        "bhqk,bqhd->bkhd", grad_scores, query_bf, preferred_element_type=full_type
    ) * HD ** (-0.5)
    grad_qkv = jnp.stack([grad_query, grad_key, grad_value], axis=2).reshape(
        samples_mb, seq_len, 3 * D
    )
    grad_normed_a, grad_w_attn_in, grad_b_qkv = linear_back(
        normed_a, w_attn_in, grad_qkv.astype(low_type)
    )
    _, norm_pull_a = jax.vjp(modulated_norm, residual, modulation[0], modulation[1])
    grad_from_a, grad_shift_a, grad_scale_a = norm_pull_a(grad_normed_a)
    grad_gate_a = jnp.sum(attn_out * grad_middle, axis=1, keepdims=True)
    grad_gate_m = jnp.sum(mlp_out * grad_out, axis=1, keepdims=True)
    grad_mod = jnp.concatenate(
        [grad_shift_a, grad_scale_a, grad_gate_a, grad_shift_m, grad_scale_m, grad_gate_m], axis=-1
    )[:, 0, :].astype(low_type)
    grad_cond, grad_w_mod, grad_b_mod = linear_back(modulator, w_modulate, grad_mod)
    grad_list = [
        grad_w_attn_in,
        grad_w_attn_out,
        grad_w_mlp_in,
        grad_w_mlp_out,
        grad_w_mod,
        grad_b_qkv[:D],
        grad_b_qkv[2 * D :],
        grad_b_attn_out,
        grad_b_mlp_in,
        grad_b_mlp_out,
        grad_b_mod,
    ]
    return (grad_middle + grad_from_a, grad_cond, grad_list)


def embed_forward(pieces, latent_part, noise_part, times_part, labels_part, dropped_part):
    mixing = times_part[:, None, None]
    noisy_bf = ((1.0 - mixing) * latent_part + mixing * noise_part).astype(low_type)
    tokens = linear_fwd(noisy_bf, pieces[0]) + pieces[1] + position_table()
    basis_bf = time_features(times_part).astype(low_type)
    time_pre = linear_fwd(basis_bf, pieces[2]) + pieces[3]
    time_act = jax.nn.silu(time_pre).astype(low_type)
    time_emb = linear_fwd(time_act, pieces[4]) + pieces[5]
    classes = jnp.where(dropped_part == 1, CLS - 1, labels_part)
    onehot = (classes[:, None] == jnp.arange(CLS, dtype=jnp.int32)[None, :]).astype(low_type)
    condition = time_emb + jnp.dot(onehot, pieces[6], preferred_element_type=full_type)
    saved = (noisy_bf, basis_bf, time_pre, time_act, onehot, condition)
    return (tokens, jax.nn.silu(condition).astype(low_type), saved)


def embed_backward(pieces, saved, grad_tokens, grad_modulator):
    noisy_bf, basis_bf, time_pre, time_act, onehot, condition = saved
    grad_cond = silu_back(condition, grad_modulator)
    grad_table = lax.dot_general(
        onehot.astype(full_type),
        grad_cond,
        (((0,), (0,)), ((), ())),
        precision=lax.Precision.HIGHEST,
    )
    grad_time_act, grad_w_time_out, grad_b_time_out = linear_back(
        time_act, pieces[4], grad_cond.astype(low_type)
    )
    grad_time_pre = silu_back(time_pre, grad_time_act).astype(low_type)
    _, grad_w_time_in, grad_b_time_in = linear_back(basis_bf, pieces[2], grad_time_pre, False)
    _, grad_w_patch, grad_b_patch = linear_back(
        noisy_bf, pieces[0], grad_tokens.astype(low_type), False
    )
    return [
        grad_w_patch,
        grad_b_patch,
        grad_w_time_in,
        grad_b_time_in,
        grad_w_time_out,
        grad_b_time_out,
        grad_table,
    ]


def projector_forward(pieces, residual, features_part):
    residual_bf = residual.astype(low_type)
    pre_a = linear_fwd(residual_bf, pieces[7]) + pieces[8]
    act_a = jax.nn.silu(pre_a).astype(low_type)
    pre_b = linear_fwd(act_a, pieces[9]) + pieces[10]
    act_b = jax.nn.silu(pre_b).astype(low_type)
    predicted = linear_fwd(act_b, pieces[11]) + pieces[12]
    loss_part = -proj_coeff * jnp.sum(cosine_rows(predicted, features_part)) / residual.shape[1]
    return (loss_part, (residual_bf, pre_a, act_a, pre_b, act_b, predicted))


def projector_backward(pieces, saved, features_part, seq_len, sample_total):
    residual_bf, pre_a, act_a, pre_b, act_b, predicted = saved
    _, cosine_pull = jax.vjp(
        lambda predicted_in: cosine_rows(predicted_in, features_part), predicted
    )
    seed = jnp.full(predicted.shape[:2], -proj_coeff / (seq_len * sample_total), full_type)
    grad_pred = cosine_pull(seed)[0].astype(low_type)
    grad_act_b, grad_w_c, grad_b_c = linear_back(act_b, pieces[11], grad_pred)
    grad_pre_b = silu_back(pre_b, grad_act_b).astype(low_type)
    grad_act_a, grad_w_b, grad_b_b = linear_back(act_a, pieces[9], grad_pre_b)
    grad_pre_a = silu_back(pre_a, grad_act_a).astype(low_type)
    grad_residual, grad_w_a, grad_b_a = linear_back(residual_bf, pieces[7], grad_pre_a)
    return (grad_residual, [grad_w_a, grad_b_a, grad_w_b, grad_b_b, grad_w_c, grad_b_c])


def head_forward(pieces, residual, modulator, target, weight_t):
    modulation = (linear_fwd(modulator, pieces[13]) + pieces[14])[:, None, :]
    shift_f, scale_f = jnp.split(modulation, 2, axis=-1)
    normed = modulated_norm(residual, shift_f, scale_f).astype(low_type)
    deviation = linear_fwd(normed, pieces[15]) + pieces[16] - target
    loss_part = jnp.sum(weight_t * jnp.mean(deviation * deviation, axis=(1, 2)))
    return (loss_part, (shift_f, scale_f, normed, deviation))


def head_backward(pieces, saved, residual, modulator, weight_t, sample_total):
    shift_f, scale_f, normed, deviation = saved
    scaled = (
        2.0 * weight_t[:, None, None] / (deviation.shape[1] * deviation.shape[2] * sample_total)
    )
    grad_output = (scaled * deviation).astype(low_type)
    grad_normed, grad_w_head, grad_b_head = linear_back(normed, pieces[15], grad_output)
    _, pullback = jax.vjp(modulated_norm, residual, shift_f, scale_f)
    grad_residual, grad_shift, grad_scale = pullback(grad_normed)
    grad_mod = jnp.concatenate([grad_shift, grad_scale], axis=-1)[:, 0, :].astype(low_type)
    grad_cond, grad_w_mod, grad_b_mod = linear_back(modulator, pieces[13], grad_mod)
    return (grad_residual, grad_cond, [grad_w_mod, grad_b_mod, grad_w_head, grad_b_head])


WIDE = 2 * LANES
HEADS = D // HD
CHUNK = 64
MB = 1024 * 1024


def dot(one, two):
    return jnp.dot(one, two, preferred_element_type=full_type)


def dot_nt(one, two):
    return lax.dot_general(one, two, (((1,), (1,)), ((), ())), preferred_element_type=full_type)


def dot_tn(one, two):
    return lax.dot_general(one, two, (((0,), (0,)), ((), ())), preferred_element_type=full_type)


def block_of(w, block, blocks, chunk, chunks):
    pieces = [w[pl.ds(block, blocks), chunk + i].reshape(blocks * ROWS, LANES) for i in range(chunks)]
    return jnp.concatenate(pieces, axis=1) if chunks > 1 else pieces[0]


def put_block(out, block, chunk, value):
    blocks = value.shape[0] // ROWS
    for i in range(value.shape[1] // LANES):
        piece = value[:, i * LANES : (i + 1) * LANES].astype(low_type)
        out[pl.ds(block, blocks), chunk + i] = piece.reshape(blocks, ROWS, LANES)


def loop(count, body):
    lax.fori_loop(0, count, lambda i, carry: (body(i), carry)[1], 0)


def norm_parts(values):
    centred = values - jnp.mean(values, axis=-1, keepdims=True)
    spread = jnp.mean(centred * centred, axis=-1, keepdims=True)
    scale = lax.rsqrt(spread + norm_eps)
    return centred * scale, scale


def norm_back(values, grad, gain):
    hat, scale = norm_parts(values)
    inner = grad * gain
    mean_a = jnp.mean(inner, axis=-1, keepdims=True)
    mean_b = jnp.mean(inner * hat, axis=-1, keepdims=True)
    return scale * (inner - mean_a - hat * mean_b), grad * hat


def gelu_parts(values):
    root = math.sqrt(2.0 / math.pi)
    square = values * values
    bend = jnp.tanh(root * values * (1.0 + 0.044715 * square))
    half = 0.5 * (1.0 + bend)
    slope = half + 0.5 * values * (1.0 - bend * bend) * root * (1.0 + 3.0 * 0.044715 * square)
    return values * half, slope


def rows_sum(values):
    return jnp.sum(values, axis=0, keepdims=True)


def segment_ref(units, plan, number):
    _, chunks, count, first, shape, matrix = plan.segments[number]
    part = units.at[pl.ds(first, count)]
    if not matrix:
        return part
    return part.reshape(shape[0] // ROWS, chunks, ROWS, LANES)


def segment_scratch(plan, number):
    _, chunks, _, _, shape, _ = plan.segments[number]
    return pltpu.VMEM((shape[0] // ROWS, chunks, ROWS, LANES), low_type)


def attention_pairs(rows):
    return (rows // SEQ) * (HEADS // 2)


def head_masks():
    lane = lax.broadcasted_iota(jnp.int32, (SEQ, LANES), 1)
    return lane < HD


def softmax_f32(scores):
    exponent = jnp.exp(scores - jnp.max(scores, axis=-1, keepdims=True))
    return exponent * (1.0 / jnp.sum(exponent, axis=-1, keepdims=True))


def mods_kernel(plan, modulator, bias, units, out, w, sem):
    load = pltpu.make_async_copy(segment_ref(units, plan, 4), w, sem)
    load.start()
    load.wait()
    value = modulator[...]

    def body(j):
        cols = pl.ds(pl.multiple_of(j * WIDE, WIDE), WIDE)
        out[:, cols] = dot(value, block_of(w, 0, D // ROWS, 2 * j, 2)) + bias[:, cols]

    loop(6 * D // WIDE, body)


def mods_call(plan, modulator, bias, units):
    vm = pl.BlockSpec(memory_space=pltpu.VMEM)
    return pl.pallas_call(
        functools.partial(mods_kernel, plan),
        out_shape=jax.ShapeDtypeStruct((modulator.shape[0], 6 * D), full_type),
        in_specs=[vm, vm, pl.BlockSpec(memory_space=pl.ANY)],
        out_specs=vm,
        scratch_shapes=[segment_scratch(plan, 4), pltpu.SemaphoreType.DMA],
        compiler_params=pltpu.CompilerParams(vmem_limit_bytes=32 * MB),
        name="modulation",
    )(modulator, bias, units)


def mods_back_kernel(plan, modulator, grad, units, before, grads, cond, w, dw, sem):
    load = pltpu.make_async_copy(segment_ref(units, plan, 4), w, sem.at[0])
    load.start()
    turned = modulator[...].astype(full_type).T.astype(low_type)

    def weight(j):
        cols = pl.ds(pl.multiple_of(j * WIDE, WIDE), WIDE)
        put_block(dw, 0, 2 * j, dot(turned, grad[:, cols]))

    loop(6 * D // WIDE, weight)
    store = pltpu.make_async_copy(dw, segment_ref(grads, plan, 4), sem.at[1])
    store.start()
    load.wait()
    cond[...] = jnp.zeros(cond.shape, full_type)

    def back(j):
        cols = pl.ds(pl.multiple_of(j * WIDE, WIDE), WIDE)
        cond[...] += dot_nt(grad[:, cols], block_of(w, 0, D // ROWS, 2 * j, 2))

    loop(6 * D // WIDE, back)
    store.wait()


def mods_back_call(plan, modulator, grad, units, grads):
    vm = pl.BlockSpec(memory_space=pltpu.VMEM)
    anywhere = pl.BlockSpec(memory_space=pl.ANY)
    return pl.pallas_call(
        functools.partial(mods_back_kernel, plan),
        out_shape=[jax.ShapeDtypeStruct(grads.shape, low_type), jax.ShapeDtypeStruct((modulator.shape[0], D), full_type)],
        in_specs=[vm, vm, anywhere, anywhere],
        out_specs=[anywhere, vm],
        input_output_aliases={3: 0},
        scratch_shapes=[segment_scratch(plan, 4), segment_scratch(plan, 4), pltpu.SemaphoreType.DMA((2,))],
        compiler_params=pltpu.CompilerParams(vmem_limit_bytes=40 * MB),
        name="modulation_back",
    )(modulator, grad, units, grads)


SAVED = (("h1", D, low_type), ("qkv", 3 * D, low_type), ("heads", D, low_type), ("attn", D, full_type), ("middle", D, full_type), ("h2", D, low_type), ("pre", FF, full_type), ("mlp", D, full_type))


def layer_forward_kernel(plan, rows, x, mod, bias_qkv, bias_o, bias_1, bias_2, units, out, sums, *refs):
    ns = len(SAVED)
    saved_out = refs[:ns]
    h1, qkv, heads, attn, middle, h2, pre, mlp = refs[ns : 2 * ns]
    w_qkv, w_o, w_1, w_2, load_sem, save_sem = refs[2 * ns :]
    weights = (w_qkv, w_o, w_1, w_2)
    loads = [pltpu.make_async_copy(segment_ref(units, plan, i), weights[i], load_sem.at[i]) for i in range(4)]
    for copy in loads:
        copy.start()
    saves = [pltpu.make_async_copy(refs[ns + i], saved_out[i], save_sem.at[i]) for i in range(ns)]
    part = lambda s, i: mod[pl.ds(s, 1), i * D : (i + 1) * D]
    per = SEQ // CHUNK

    def norm_a(i):
        at = pl.ds(pl.multiple_of(i * CHUNK, CHUNK), CHUNK)
        s = i // per
        hat, _ = norm_parts(x[at, :])
        h1[at, :] = (hat * (1.0 + part(s, 1)) + part(s, 0)).astype(low_type)

    loop(rows // CHUNK, norm_a)
    saves[0].start()
    loads[0].wait()

    def project(j):
        cols = pl.ds(pl.multiple_of(j * WIDE, WIDE), WIDE)
        value = dot(h1[...], block_of(w_qkv, 0, D // ROWS, 2 * j, 2)) + bias_qkv[:, cols]
        qkv[:, cols] = value.astype(low_type)

    loop(3 * D // WIDE, project)
    saves[1].start()
    first = head_masks()

    def attend(i):
        s, j = i // (HEADS // 2), i % (HEADS // 2)
        at = pl.ds(pl.multiple_of(s * SEQ, SEQ), SEQ)
        cut = lambda o: qkv[at, pl.ds(pl.multiple_of(o * D + j * LANES, LANES), LANES)]
        q, k, v = cut(0), cut(1), cut(2)
        q = q * jnp.asarray(HD ** (-0.5), low_type)
        zero = jnp.zeros_like(q)
        halves = []
        for mask in (first, ~first):
            probs = softmax_f32(dot_nt(jnp.where(mask, q, zero), k)).astype(low_type)
            halves.append(dot(probs, v))
        heads[at, pl.ds(pl.multiple_of(j * LANES, LANES), LANES)] = jnp.where(first, halves[0], halves[1]).astype(low_type)

    loop(attention_pairs(rows), attend)
    saves[2].start()
    loads[1].wait()

    def project_out(j):
        cols = pl.ds(pl.multiple_of(j * WIDE, WIDE), WIDE)
        attn[:, cols] = dot(heads[...], block_of(w_o, 0, D // ROWS, 2 * j, 2)) + bias_o[:, cols]

    loop(D // WIDE, project_out)
    saves[3].start()
    zero_sum = jnp.zeros((1, D), full_type)

    def norm_m(i, total):
        at = pl.ds(pl.multiple_of(i * CHUNK, CHUNK), CHUNK)
        s = i // per
        value = attn[at, :]
        mid = x[at, :] + part(s, 2) * value
        middle[at, :] = mid
        hat, _ = norm_parts(mid)
        h2[at, :] = (hat * (1.0 + part(s, 4)) + part(s, 3)).astype(low_type)
        return total + rows_sum(value * value)

    attn_sum = lax.fori_loop(0, rows // CHUNK, norm_m, zero_sum)
    saves[4].start()
    saves[5].start()
    loads[2].wait()
    loads[3].wait()
    mlp[...] = jnp.broadcast_to(bias_2[...], (rows, D))

    def feed(j):
        cols = pl.ds(pl.multiple_of(j * WIDE, WIDE), WIDE)
        value = dot(h2[...], block_of(w_1, 0, D // ROWS, 2 * j, 2)) + bias_1[:, cols]
        pre[:, cols] = value
        act = gelu_parts(value)[0].astype(low_type)
        mlp[...] += dot(act, block_of(w_2, j * (WIDE // ROWS), WIDE // ROWS, 0, D // LANES))

    loop(FF // WIDE, feed)
    saves[6].start()
    saves[7].start()

    def finish(i, carry):
        at = pl.ds(pl.multiple_of(i * CHUNK, CHUNK), CHUNK)
        value = mlp[at, :]
        result = middle[at, :] + part(i // per, 5) * value
        out[at, :] = result
        return (carry[0] + rows_sum(result * result), carry[1] + rows_sum(value * value))

    out_sum, mlp_sum = lax.fori_loop(0, rows // CHUNK, finish, (zero_sum, zero_sum))
    sums[...] = jnp.zeros(sums.shape, full_type)
    sums[0:1, :] = out_sum
    sums[1:2, :] = attn_sum
    sums[2:3, :] = mlp_sum
    for copy in saves:
        copy.wait()


def layer_forward_call(plan, x, mod, biases, units):
    rows = x.shape[0]
    vm = pl.BlockSpec(memory_space=pltpu.VMEM)
    anywhere = pl.BlockSpec(memory_space=pl.ANY)
    dma = pltpu.SemaphoreType.DMA
    shapes = [((rows, width), kind) for _, width, kind in SAVED]
    results = pl.pallas_call(
        functools.partial(layer_forward_kernel, plan, rows),
        out_shape=[jax.ShapeDtypeStruct((rows, D), full_type), jax.ShapeDtypeStruct((8, D), full_type)]
        + [jax.ShapeDtypeStruct(*s) for s in shapes],
        in_specs=[vm] * 6 + [anywhere],
        out_specs=[vm, vm] + [anywhere] * len(SAVED),
        scratch_shapes=[pltpu.VMEM(*s) for s in shapes] + [segment_scratch(plan, i) for i in range(4)] + [dma((4,)), dma((len(SAVED),))],
        compiler_params=pltpu.CompilerParams(vmem_limit_bytes=56 * MB),
        name="layer_forward",
    )(x, mod, *biases, units)
    return results[0], results[1], results[2:]


def layer_backward_kernel(plan, rows, x, grad_in, mod, *refs):
    ns = len(SAVED)
    saved_hbm = refs[:ns]
    units, grad_out, grad_mod, bias_out, grads = refs[ns : ns + 5]
    h1, qkv, heads, attn, middle, h2, pre, mlp = refs[ns + 5 : 2 * ns + 5]
    w_qkv, w_o, w_1, w_2, d_qkv, g_low, wide, turned, dx, d_one, d_two, load_sem, save_sem, out_sem = refs[2 * ns + 5 :]
    weights = (w_qkv, w_o, w_1, w_2)
    inside = dict(zip(range(ns), refs[ns + 5 : 2 * ns + 5]))
    saves = [pltpu.make_async_copy(saved_hbm[i], inside[i], save_sem.at[i]) for i in range(ns)]
    loads = [pltpu.make_async_copy(segment_ref(units, plan, i), weights[i], load_sem.at[i]) for i in range(4)]
    for copy in (saves[7], saves[6], loads[3], saves[5], loads[2], saves[4], saves[3], loads[1], saves[2], saves[1], loads[0], saves[0]):
        copy.start()
    part = lambda s, i: mod[pl.ds(s, 1), i * D : (i + 1) * D]
    per = SEQ // CHUNK
    grad_mod[...] = jnp.zeros(grad_mod.shape, full_type)
    bias_out[...] = jnp.zeros(bias_out.shape, full_type)

    def add_mod(s, i, value):
        grad_mod[pl.ds(s, 1), i * D : (i + 1) * D] += value

    def each_chunk(body):
        loop(rows // CHUNK, lambda i: body(pl.ds(pl.multiple_of(i * CHUNK, CHUNK), CHUNK), i // per))

    B_Q, B_V, B_O, B_1, B_2 = 0, D, 2 * D, 3 * D, 3 * D + FF
    saves[7].wait()

    def start_mlp(at, s):
        grad = grad_in[at, :]
        low = (part(s, 5) * grad).astype(low_type)
        g_low[at, :] = low
        bias_out[:, B_2 : B_2 + D] += rows_sum(low.astype(full_type))
        add_mod(s, 5, rows_sum(mlp[at, :] * grad))

    each_chunk(start_mlp)
    saves[5].wait()
    turned[...] = h2[...].astype(full_type).T.astype(low_type)
    saves[6].wait()
    loads[3].wait()
    loads[2].wait()
    dx[...] = jnp.zeros(dx.shape, full_type)
    half = WIDE // ROWS

    def outer(slot, segment, block, blocks, chunk, chunks, buffer):
        target = segment_ref(grads, plan, segment).at[pl.ds(block, blocks), pl.ds(chunk, chunks)]
        return pltpu.make_async_copy(buffer, target, out_sem.at[slot])

    def mlp_store(j, kind):
        at = j % 2
        if kind == 0:
            return outer(2 * at, 3, j * half, half, 0, D // LANES, d_one.at[at])
        return outer(2 * at + 1, 2, 0, D // ROWS, 2 * j, 2, d_two.at[at])

    def feed_back(j):
        cols = pl.ds(pl.multiple_of(j * WIDE, WIDE), WIDE)
        at = j % 2

        @pl.when(j >= 2)
        def _():
            mlp_store(j - 2, 0).wait()
            mlp_store(j - 2, 1).wait()

        act, slope = gelu_parts(pre[:, cols])
        grad_act = dot_nt(g_low[...], block_of(w_2, j * half, half, 0, D // LANES))
        low = (grad_act * slope).astype(low_type)
        wide[...] = low
        bias_out[:, pl.ds(pl.multiple_of(B_1 + j * WIDE, WIDE), WIDE)] += rows_sum(low.astype(full_type))
        put_block(d_one.at[at], 0, 0, dot_tn(act.astype(low_type), g_low[...]))
        mlp_store(j, 0).start()
        put_block(d_two.at[at], 0, 0, dot(turned[...], wide[...]))
        mlp_store(j, 1).start()
        dx[...] += dot_nt(wide[...], block_of(w_1, 0, D // ROWS, 2 * j, 2))

    steps = FF // WIDE
    loop(steps, feed_back)
    saves[4].wait()
    saves[3].wait()

    def middle_back(at, s):
        grad = dx[at, :]
        back, scaled = norm_back(middle[at, :], grad, 1.0 + part(s, 4))
        add_mod(s, 3, rows_sum(grad))
        add_mod(s, 4, rows_sum(scaled))
        total = grad_in[at, :] + back
        grad_out[at, :] = total
        low = (part(s, 2) * total).astype(low_type)
        g_low[at, :] = low
        bias_out[:, B_O : B_O + D] += rows_sum(low.astype(full_type))
        add_mod(s, 2, rows_sum(attn[at, :] * total))

    each_chunk(middle_back)
    loads[1].wait()
    saves[2].wait()
    for j in (steps - 2, steps - 1):
        mlp_store(j, 0).wait()
        mlp_store(j, 1).wait()
    turned[...] = heads[...].astype(full_type).T.astype(low_type)

    def wo_store(j):
        return outer(j % 2, 1, 0, D // ROWS, 2 * j, 2, d_two.at[j % 2])

    def out_back(j):
        cols = pl.ds(pl.multiple_of(j * WIDE, WIDE), WIDE)

        @pl.when(j >= 2)
        def _():
            wo_store(j - 2).wait()

        put_block(d_two.at[j % 2], 0, 0, dot(turned[...], g_low[:, cols]))
        wo_store(j).start()
        heads[:, cols] = dot_nt(g_low[...], block_of(w_o, j * half, half, 0, D // LANES)).astype(low_type)

    loop(D // WIDE, out_back)
    saves[1].wait()
    first = head_masks()

    def attend_back(i):
        s, j = i // (HEADS // 2), i % (HEADS // 2)
        at = pl.ds(pl.multiple_of(s * SEQ, SEQ), SEQ)
        cut = lambda o: qkv[at, pl.ds(pl.multiple_of(o * D + j * LANES, LANES), LANES)]
        q, k, v = cut(0), cut(1), cut(2)
        go = heads[at, pl.ds(pl.multiple_of(j * LANES, LANES), LANES)]
        q = q * jnp.asarray(HD ** (-0.5), low_type)
        zero = jnp.zeros_like(q)
        dq, dk, dv = [], 0.0, 0.0
        for mask in (first, ~first):
            q_h, go_h = jnp.where(mask, q, zero), jnp.where(mask, go, zero)
            probs = softmax_f32(dot_nt(q_h, k))
            grad_probs = dot_nt(go_h, v)
            dv = dv + dot_tn(probs.astype(low_type), go_h)
            inner = jnp.sum(probs * grad_probs, axis=-1, keepdims=True)
            ds = (probs * (grad_probs - inner)).astype(low_type)
            dq.append(dot(ds, k) * HD ** (-0.5))
            dk = dk + dot_tn(ds, q_h)
        put = lambda o, value: d_qkv.at[at, pl.ds(pl.multiple_of(o * D + j * LANES, LANES), LANES)].set(value)
        for o, value in enumerate((jnp.where(first, dq[0], dq[1]), dk, dv)):
            low = value.astype(low_type)
            d_qkv[at, pl.ds(pl.multiple_of(o * D + j * LANES, LANES), LANES)] = low
            if o != 1:
                start = (B_Q if o == 0 else B_V) + j * LANES
                bias_out[:, pl.ds(pl.multiple_of(start, LANES), LANES)] += rows_sum(low.astype(full_type))

    loop(attention_pairs(rows), attend_back)
    saves[0].wait()
    loads[0].wait()
    wo_store(1).wait()
    wo_store(2).wait()
    turned[...] = h1[...].astype(full_type).T.astype(low_type)
    dx[...] = jnp.zeros(dx.shape, full_type)

    def qkv_store(j):
        return outer(j % 2, 0, 0, D // ROWS, 2 * j, 2, d_two.at[j % 2])

    def project_back(j):
        cols = pl.ds(pl.multiple_of(j * WIDE, WIDE), WIDE)

        @pl.when(j >= 2)
        def _():
            qkv_store(j - 2).wait()

        put_block(d_two.at[j % 2], 0, 0, dot(turned[...], d_qkv[:, cols]))
        qkv_store(j).start()
        dx[...] += dot_nt(d_qkv[:, cols], block_of(w_qkv, 0, D // ROWS, 2 * j, 2))

    count = 3 * D // WIDE
    loop(count, project_back)

    def input_back(at, s):
        grad = dx[at, :]
        back, scaled = norm_back(x[at, :], grad, 1.0 + part(s, 1))
        add_mod(s, 0, rows_sum(grad))
        add_mod(s, 1, rows_sum(scaled))
        grad_out[at, :] += back

    each_chunk(input_back)
    for j in (count - 2, count - 1):
        qkv_store(j).wait()


def layer_backward_call(plan, x, grad, mod, saved, units):
    rows = x.shape[0]
    vm = pl.BlockSpec(memory_space=pltpu.VMEM)
    anywhere = pl.BlockSpec(memory_space=pl.ANY)
    dma = pltpu.SemaphoreType.DMA
    shapes = [((rows, width), kind) for _, width, kind in SAVED]
    tile = (ROWS, LANES)
    return pl.pallas_call(
        functools.partial(layer_backward_kernel, plan, rows),
        out_shape=[
            jax.ShapeDtypeStruct((rows, D), full_type),
            jax.ShapeDtypeStruct((8, 6 * D), full_type),
            jax.ShapeDtypeStruct((1, 4 * D + FF), full_type),
            jax.ShapeDtypeStruct(units.shape, low_type),
        ],
        in_specs=[vm] * 3 + [anywhere] * (len(SAVED) + 1),
        out_specs=[vm, vm, vm, anywhere],
        scratch_shapes=[pltpu.VMEM(*s) for s in shapes]
        + [segment_scratch(plan, i) for i in range(4)]
        + [
            pltpu.VMEM((rows, 3 * D), low_type),
            pltpu.VMEM((rows, D), low_type),
            pltpu.VMEM((rows, WIDE), low_type),
            pltpu.VMEM((D, rows), low_type),
            pltpu.VMEM((rows, D), full_type),
            pltpu.VMEM((2, WIDE // ROWS, D // LANES) + tile, low_type),
            pltpu.VMEM((2, D // ROWS, 2) + tile, low_type),
            dma((4,)),
            dma((len(SAVED),)),
            dma((4,)),
        ],
        compiler_params=pltpu.CompilerParams(vmem_limit_bytes=60 * MB),
        name="layer_backward",
    )(x, grad, mod, *saved, units)


def sigmoid(values):
    return 1.0 / (1.0 + jnp.exp(-values))


def silu_parts(values):
    gate = sigmoid(values)
    return values * gate, gate * (1.0 + values * (1.0 - gate))


TOP = (7, 9, 11, 13)


def top_kernel(plan, rows, sample_total, x, features, target, weight_t, modulator, b_1, b_2, b_3, b_f, w_h, b_h, units, *refs):
    grad_x, stats, cond, bias_out, dw_h, grads = refs[:6]
    p_1, p_2, p_3, w_f, pre_a, act_a, pre_b, act_b, pred, low, g_b, g_a, hidden, modf, d_modf, stage, dw_f, load_sem, out_sem = refs[6:]
    weights = (p_1, p_2, p_3, w_f)
    loads = [pltpu.make_async_copy(segment_ref(units, plan, s), weights[i], load_sem.at[i]) for i, s in enumerate(TOP)]
    for copy in loads:
        copy.start()
    per = SEQ // CHUNK
    half = WIDE // ROWS
    stats[...] = jnp.zeros(stats.shape, full_type)
    bias_out[...] = jnp.zeros(bias_out.shape, full_type)
    d_modf[...] = jnp.zeros(d_modf.shape, full_type)
    A_1, A_2, A_3, A_F, A_H = 0, PH, 2 * PH, 2 * PH + ZD, 2 * PH + ZD + 2 * D
    wide_at = lambda j, base=0: pl.ds(pl.multiple_of(base + j * WIDE, LANES), WIDE)

    def each_chunk(body):
        loop(rows // CHUNK, lambda i: body(pl.ds(pl.multiple_of(i * CHUNK, CHUNK), CHUNK), i // per))

    def to_low(at, s):
        low[at, :] = x[at, :].astype(low_type)

    each_chunk(to_low)
    loads[0].wait()

    def first_layer(j):
        value = dot(low[...], block_of(p_1, 0, D // ROWS, 2 * j, 2)) + b_1[:, wide_at(j)]
        pre_a[:, wide_at(j)] = value
        act_a[:, wide_at(j)] = silu_parts(value)[0].astype(low_type)

    loop(PH // WIDE, first_layer)
    loads[1].wait()

    def second_layer(j):
        value = dot(act_a[...], block_of(p_2, 0, PH // ROWS, 2 * j, 2)) + b_2[:, wide_at(j)]
        pre_b[:, wide_at(j)] = value
        act_b[:, wide_at(j)] = silu_parts(value)[0].astype(low_type)

    loop(PH // WIDE, second_layer)
    loads[2].wait()

    def third_layer(j):
        pred[:, wide_at(j)] = dot(act_b[...], block_of(p_3, 0, PH // ROWS, 2 * j, 2)) + b_3[:, wide_at(j)]

    loop(ZD // WIDE, third_layer)
    seed = -proj_coeff / (SEQ * sample_total)

    def cosine(at, s):
        value = pred[at, :]
        want = features[at, :].astype(full_type)
        inner = jnp.sum(value * want, axis=-1, keepdims=True)
        scale_a = lax.rsqrt(jnp.sum(value * value, axis=-1, keepdims=True) + norm_eps)
        scale_b = lax.rsqrt(jnp.sum(want * want, axis=-1, keepdims=True) + norm_eps)
        both = scale_a * scale_b
        stats[0:1, 0:1] += jnp.sum(inner * both, axis=0, keepdims=True)
        grad = seed * (want * both - value * (inner * both * scale_a * scale_a))
        grad = grad.astype(low_type)
        hidden[at, :] = grad
        bias_out[:, A_3 : A_3 + ZD] += rows_sum(grad.astype(full_type))

    each_chunk(cosine)

    def store(segment, j, chunks):
        where = segment_ref(grads, plan, segment).at[pl.ds(j * half, half)]
        return pltpu.make_async_copy(stage.at[j % 2, :, pl.ds(0, chunks)], where, out_sem.at[j % 2])

    def stored(segment, j, chunks):
        @pl.when(j >= 2)
        def _():
            store(segment, j - 2, chunks).wait()

    def third_back(j):
        stored(11, j, ZD // LANES)
        put_block(stage.at[j % 2], 0, 0, dot_tn(act_b[:, wide_at(j)], hidden[...]))
        store(11, j, ZD // LANES).start()
        grad = dot_nt(hidden[...], block_of(p_3, j * half, half, 0, ZD // LANES))
        grad = (grad * silu_parts(pre_b[:, wide_at(j)])[1]).astype(low_type)
        g_b[:, wide_at(j)] = grad
        bias_out[:, wide_at(j, A_2)] += rows_sum(grad.astype(full_type))

    def drain(segment, count, chunks):
        for j in range(max(0, count - 2), count):
            store(segment, j, chunks).wait()

    loop(PH // WIDE, third_back)
    drain(11, PH // WIDE, ZD // LANES)
    span = 4 * LANES

    def second_back(j):
        stored(9, j, PH // LANES)
        for i in range(PH // span):
            put_block(stage.at[j % 2], 0, i * (span // LANES), dot_tn(act_a[:, wide_at(j)], g_b[:, i * span : (i + 1) * span]))
        store(9, j, PH // LANES).start()
        grad = dot_nt(g_b[...], block_of(p_2, j * half, half, 0, PH // LANES))
        grad = (grad * silu_parts(pre_a[:, wide_at(j)])[1]).astype(low_type)
        g_a[:, wide_at(j)] = grad
        bias_out[:, wide_at(j, A_1)] += rows_sum(grad.astype(full_type))

    loop(PH // WIDE, second_back)
    drain(9, PH // WIDE, PH // LANES)

    def first_back(j):
        stored(7, j, PH // LANES)
        for i in range(PH // span):
            put_block(stage.at[j % 2], 0, i * (span // LANES), dot_tn(low[:, wide_at(j)], g_a[:, i * span : (i + 1) * span]))
        store(7, j, PH // LANES).start()
        grad_x[:, wide_at(j)] = dot_nt(g_a[...], block_of(p_1, j * half, half, 0, PH // LANES))

    loop(D // WIDE, first_back)
    loads[3].wait()

    def final_mod(j):
        modf[:, wide_at(j)] = dot(modulator[...], block_of(w_f, 0, D // ROWS, 2 * j, 2)) + b_f[:, wide_at(j)]

    loop(2 * D // WIDE, final_mod)
    part = lambda s, i: modf[pl.ds(s, 1), i * D : (i + 1) * D]
    dw_h[...] = jnp.zeros(dw_h.shape, full_type)

    def head(at, s):
        hat, scale = norm_parts(x[at, :])
        gain = 1.0 + part(s, 1)
        normed = (hat * gain + part(s, 0)).astype(low_type)
        off = dot(normed, w_h[...]) + b_h[...] - target[at, :]
        weight = weight_t[pl.ds(s, 1), :]
        stats[1:2, :] += rows_sum(weight * off * off)
        grad = (2.0 * weight / (SEQ * PD * sample_total) * off).astype(low_type)
        bias_out[:, A_H : A_H + LANES] += rows_sum(grad.astype(full_type))
        dw_h[...] += dot_tn(normed, grad)
        back = dot_nt(grad, w_h[...])
        d_modf[pl.ds(s, 1), 0:D] += rows_sum(back)
        d_modf[pl.ds(s, 1), D : 2 * D] += rows_sum(back * hat)
        inner = back * gain
        mean_a = jnp.mean(inner, axis=-1, keepdims=True)
        mean_b = jnp.mean(inner * hat, axis=-1, keepdims=True)
        grad_x[at, :] += scale * (inner - mean_a - hat * mean_b)

    each_chunk(head)
    turned = modulator[...].astype(full_type).T.astype(low_type)
    cond[...] = jnp.zeros(cond.shape, full_type)

    def final_back(j):
        grad = d_modf[:, wide_at(j)].astype(low_type)
        bias_out[:, wide_at(j, A_F)] += rows_sum(grad.astype(full_type))
        put_block(dw_f, 0, 2 * j, dot(turned, grad))
        cond[...] += dot_nt(grad, block_of(w_f, 0, D // ROWS, 2 * j, 2))

    loop(2 * D // WIDE, final_back)
    last = pltpu.make_async_copy(dw_f, segment_ref(grads, plan, 13), out_sem.at[2])
    last.start()
    last.wait()
    drain(7, D // WIDE, PH // LANES)


def top_call(plan, sample_total, x, features, target, weight_t, modulator, biases, w_h, b_h, units):
    rows = x.shape[0]
    vm = pl.BlockSpec(memory_space=pltpu.VMEM)
    anywhere = pl.BlockSpec(memory_space=pl.ANY)
    dma = pltpu.SemaphoreType.DMA
    few = modulator.shape[0]
    f32 = lambda *shape: pltpu.VMEM(shape, full_type)
    bf16 = lambda *shape: pltpu.VMEM(shape, low_type)
    shape = lambda *dims: jax.ShapeDtypeStruct(dims, full_type)
    return pl.pallas_call(
        functools.partial(top_kernel, plan, rows, sample_total),
        out_shape=[
            shape(rows, D),
            shape(8, LANES),
            shape(few, D),
            shape(1, 2 * PH + ZD + 2 * D + LANES),
            shape(D, LANES),
            jax.ShapeDtypeStruct(units.shape, low_type),
        ],
        in_specs=[vm] * 11 + [anywhere],
        out_specs=[vm] * 5 + [anywhere],
        scratch_shapes=[segment_scratch(plan, s) for s in TOP]
        + [f32(rows, PH), bf16(rows, PH), f32(rows, PH), bf16(rows, PH), f32(rows, ZD), bf16(rows, D)]
        + [bf16(rows, PH), bf16(rows, PH), bf16(rows, ZD), f32(few, 2 * D), f32(few, 2 * D)]
        + [bf16(2, WIDE // ROWS, PH // LANES, ROWS, LANES), segment_scratch(plan, 13)]
        + [dma((4,)), dma((3,))],
        compiler_params=pltpu.CompilerParams(vmem_limit_bytes=60 * MB),
        name="projector_and_head",
    )(x, features, target, weight_t, modulator, *biases, w_h, b_h, units)


def model_step(layer_lists, pieces, latents, noise, times, labels, dropped, features, devices):
    sample_total = latents.shape[0] * devices
    residual, modulator, embed_saved = embed_forward(
        pieces, latents, noise, times, labels, dropped
    )
    loss_total = jnp.zeros((), full_type)
    inputs, kept, square_sums = [], [], []
    for ordinal in range(LAYERS):
        inputs.append(residual)
        residual, saved, sums = layer_forward(layer_lists[ordinal], residual, modulator)
        kept.append(saved)
        square_sums.append(sums)
        if ordinal + 1 == DEPTH_Z:
            part, proj_saved = projector_forward(pieces, residual, features)
            loss_total = loss_total + part
    target = noise - latents
    weight_t = 1.0 + 2.0 * times
    part, head_saved = head_forward(pieces, residual, modulator, target, weight_t)
    loss_total = loss_total + part
    grad_residual, grad_cond, head_grads = head_backward(
        pieces, head_saved, residual, modulator, weight_t, sample_total
    )
    layer_grads = [None] * LAYERS
    for ordinal in reversed(range(LAYERS)):
        if ordinal + 1 == DEPTH_Z:
            grad_proj, proj_grads = projector_backward(
                pieces, proj_saved, features, residual.shape[1], sample_total
            )
            grad_residual = grad_residual + grad_proj
        grad_residual, cond_part, layer_grads[ordinal] = layer_backward(
            layer_lists[ordinal], kept[ordinal], inputs[ordinal], modulator, grad_residual
        )
        grad_cond = grad_cond + cond_part
    embed_grads = embed_backward(pieces, embed_saved, grad_residual, grad_cond)
    return (loss_total, jnp.stack(square_sums), layer_grads, embed_grads + proj_grads + head_grads)


def adam_update(weight, grad, first, second, clip_factor):
    clipped = grad * clip_factor
    first_new = beta_one * first + (1.0 - beta_one) * clipped
    second_new = beta_two * second + (1.0 - beta_two) * clipped * clipped
    first_hat = first_new / (1.0 - beta_one**STEP)
    second_hat = second_new / (1.0 - beta_two**STEP)
    weight_new = weight - learn_rate * (
        first_hat / (jnp.sqrt(second_hat) + adam_eps) + decay_rate * weight
    )
    return (weight_new, first_new, second_new)


def vector_of(units, plan, number):
    _, _, count, first, shape, _ = plan.segments[number]
    flat = units[first : first + count].reshape(-1)[: math.prod(shape)]
    return flat.reshape(shape)


def matrix_of(units, plan, number):
    _, chunks, count, first, shape, _ = plan.segments[number]
    part = units[first : first + count].reshape(shape[0] // ROWS, chunks, ROWS, LANES)
    return part.transpose(0, 2, 1, 3).reshape(shape)


def units_of(grad, plan, number):
    _, chunks, count, _, shape, matrix = plan.segments[number]
    low = grad.astype(low_type)
    if matrix:
        low = low.reshape(shape[0] // ROWS, ROWS, chunks, LANES).transpose(0, 2, 1, 3)
        return low.reshape(count, ROWS, LANES)
    flat = jnp.pad(low.reshape(-1), ((0, count * UNIT - low.size),))
    return flat.reshape(count, ROWS, LANES)


def put_units(grads, plan, first_number, values):
    parts = [units_of(value, plan, first_number + i) for i, value in enumerate(values)]
    joined = jnp.concatenate(parts) if len(parts) > 1 else parts[0]
    return lax.dynamic_update_slice(grads, joined, (plan.segments[first_number][3], 0, 0))


def as_row(vector):
    return vector.astype(full_type).reshape(1, -1)


def embed_step(pieces, table_rows, latents, noise, times):
    mixing = times[:, None, None]
    noisy_bf = ((1.0 - mixing) * latents + mixing * noise).astype(low_type)
    tokens = linear_fwd(noisy_bf, pieces[0]) + pieces[1] + position_table()
    basis_bf = time_features(times).astype(low_type)
    time_pre = linear_fwd(basis_bf, pieces[2]) + pieces[3]
    time_act = jax.nn.silu(time_pre).astype(low_type)
    condition = linear_fwd(time_act, pieces[4]) + pieces[5] + table_rows.astype(full_type)
    saved = (noisy_bf, basis_bf, time_pre, time_act, condition)
    return (tokens, jax.nn.silu(condition).astype(low_type), saved)


def embed_step_back(pieces, saved, classes, grad_tokens, grad_modulator):
    noisy_bf, basis_bf, time_pre, time_act, condition = saved
    onehot = (classes[:, None] == jnp.arange(CLS, dtype=jnp.int32)[None, :]).astype(low_type)
    return embed_backward(
        pieces, (noisy_bf, basis_bf, time_pre, time_act, onehot, condition), grad_tokens, grad_modulator
    )


def by_kernels(plan, root_plan, layer_flat, root_flat, data, devices):
    latents, noise, times, labels, dropped, features = data
    samples = latents.shape[0]
    sample_total = samples * devices
    rows = samples * SEQ
    plans = (root_plan,) + (plan,) * LAYERS
    raws = [to_rows(root_flat, root_plan)]
    raws += [to_rows(layer_flat[ordinal], plan) for ordinal in range(LAYERS)]
    root_units, *layer_units = gather_units(plans, raws)
    early = [matrix_of(root_units, root_plan, i) if i % 2 == 0 else vector_of(root_units, root_plan, i) for i in range(6)]
    classes = jnp.where(dropped == 1, CLS - 1, labels)
    table_first = root_plan.segments[6][3]
    table = root_units[table_first : table_first + root_plan.segments[6][2]].reshape(-1, LANES)
    wide = D // LANES
    table_rows = jnp.stack(
        [lax.dynamic_slice(table, (classes[s] * wide, 0), (wide, LANES)).reshape(D) for s in range(samples)]
    )
    tokens, modulator, embed_saved = embed_step(early, table_rows, latents, noise, times)
    few = up(samples, ROWS)
    modulator_rows = jnp.pad(modulator, ((0, few - samples), (0, 0)))
    residual = tokens.reshape(rows, D)
    inputs, mods, kept, sums = [], [], [], []
    for ordinal in range(LAYERS):
        units = layer_units[ordinal]
        b_q, b_v, b_o, b_1, b_2, b_mod = (as_row(vector_of(units, plan, i)) for i in range(5, 11))
        bias_qkv = jnp.concatenate([b_q, jnp.zeros_like(b_q), b_v], axis=1)
        mods.append(mods_call(plan, modulator_rows, b_mod, units))
        inputs.append(residual)
        residual, total, saved = layer_forward_call(
            plan, residual, mods[ordinal], (bias_qkv, b_o, b_1, b_2), units
        )
        kept.append(saved)
        sums.append(total)
    target = jnp.pad((noise - latents).reshape(rows, PD), ((0, 0), (0, LANES - PD)))
    weight_t = jnp.broadcast_to(jnp.pad(1.0 + 2.0 * times, (0, 8 - samples))[:, None], (8, LANES))
    w_h = jnp.pad(vector_of(root_units, root_plan, 15), ((0, 0), (0, LANES - PD)))
    b_h = jnp.pad(as_row(vector_of(root_units, root_plan, 16)), ((0, 0), (0, LANES - PD)))
    biases = [as_row(vector_of(root_units, root_plan, i)) for i in (8, 10, 12, 14)]
    grad, losses, grad_cond, bias_grads, grad_w_h, root_grads = top_call(
        root_plan, sample_total, residual, features.reshape(rows, ZD), target, weight_t, modulator_rows, biases, w_h, b_h, root_units
    )
    loss_part = -proj_coeff / SEQ * losses[0, 0] + jnp.sum(losses[1]) / (SEQ * PD)
    grad_cond = grad_cond[:samples]
    layer_grads = [None] * LAYERS
    for ordinal in reversed(range(LAYERS)):
        units = layer_units[ordinal]
        grad, grad_mod, bias_grad, grads = layer_backward_call(
            plan, inputs[ordinal], grad, mods[ordinal], kept[ordinal], units
        )
        low_mod = jnp.pad(grad_mod.astype(low_type), ((0, few - grad_mod.shape[0]), (0, 0)))
        grads, cond_part = mods_back_call(plan, modulator_rows, low_mod, units, grads)
        grad_cond = grad_cond + cond_part[:samples]
        cuts = jnp.split(bias_grad[0], (D, 2 * D, 3 * D, 3 * D + FF))
        grad_b_mod = jnp.sum(low_mod.astype(full_type), axis=0)
        layer_grads[ordinal] = put_units(grads, plan, 5, cuts + [grad_b_mod])
    embed_grads = embed_step_back(early, embed_saved, classes, grad.reshape(samples, SEQ, D), grad_cond)
    cuts = jnp.split(bias_grads[0], (PH, 2 * PH, 2 * PH + ZD, 2 * PH + ZD + 2 * D))
    for number, value in zip((8, 10, 12), cuts):
        root_grads = put_units(root_grads, root_plan, number, [value])
    root_grads = put_units(root_grads, root_plan, 14, [cuts[3], grad_w_h[:, :PD], cuts[4][:PD]])
    root_grads = put_units(root_grads, root_plan, 0, embed_grads)
    square_sums = jnp.stack([jnp.sum(total[:3], axis=1) for total in sums])
    numbers = jnp.concatenate([loss_part[None], square_sums.reshape(-1)])
    stats = jnp.pad(numbers, (0, 8 * LANES - numbers.shape[0])).reshape(8, LANES)
    rows_out, stats = reduce_units(plans, [root_grads] + layer_grads, stats)
    numbers = stats[0].reshape(-1)
    shard_root = rows_out[0].reshape(-1)[: root_plan.share]
    shard_layers = jnp.stack([r.reshape(-1)[: plan.share] for r in rows_out[1:]])
    stream = numbers[1 : 1 + 3 * LAYERS].reshape(LAYERS, 3)
    return (shard_layers, shard_root, numbers[0], stream, jnp.sum(stats[1]))


def by_collectives(layer_flat, root_flat, data, devices):
    whole = lambda part: lax.all_gather(part.astype(low_type), "fsdp", axis=0, tiled=True)
    layer_lists = [unflatten(whole(layer_flat[i]), layer_layout()) for i in range(LAYERS)]
    pieces = unflatten(whole(root_flat), root_layout())
    loss_part, square_sums, layer_grads, root_grads = model_step(
        layer_lists, pieces, *data, devices
    )

    def owned(grad_list, share):
        joined = jnp.concatenate([piece.reshape(-1) for piece in grad_list])
        joined = jnp.pad(joined, (0, share * devices - joined.shape[0]))
        return lax.psum_scatter(joined, "fsdp", scatter_dimension=0, tiled=True)

    shard_layers = jnp.stack([owned(grads, layer_flat.shape[1]) for grads in layer_grads])
    shard_root = owned(root_grads, root_flat.shape[0])
    local = jnp.sum(shard_layers * shard_layers) + jnp.sum(shard_root * shard_root)
    loss_sum, sums, square_total = lax.psum((loss_part, square_sums, local), "fsdp")
    return (shard_layers, shard_root, loss_sum, sums, square_total)


def shards(
    latents,
    noise,
    times,
    labels,
    dropped,
    features,
    layer_flat,
    layer_mean,
    layer_square,
    root_flat,
    root_mean,
    root_square,
):
    devices = lax.axis_size("fsdp")
    data = (latents, noise, times, labels, dropped, features)
    plan = Plan(layer_layout(), layer_flat.shape[1] * devices, devices)
    root_plan = Plan(root_layout(), root_flat.shape[0] * devices, devices)
    if devices % 8 == 0 and plan.fits and root_plan.fits:
        reduced = by_kernels(plan, root_plan, layer_flat, root_flat, data, devices)
    else:
        reduced = by_collectives(layer_flat, root_flat, data, devices)
    shard_layers, shard_root, loss_sum, stream_sums, square_total = reduced
    sample_total = latents.shape[0] * devices
    grad_norm = jnp.sqrt(square_total)
    clip_factor = clip_limit / jnp.maximum(grad_norm, clip_limit)
    activation_rms = jnp.sqrt(stream_sums / (sample_total * SEQ * D))
    new_layer, new_layer_mean, new_layer_square = adam_update(
        layer_flat, shard_layers, layer_mean, layer_square, clip_factor
    )
    new_root, new_root_mean, new_root_square = adam_update(
        root_flat, shard_root, root_mean, root_square, clip_factor
    )
    return (
        loss_sum,
        grad_norm,
        activation_rms,
        new_layer,
        new_layer_mean,
        new_layer_square,
        new_root,
        new_root_mean,
        new_root_square,
    )


def solution(mesh):
    in_specs = (
        P("fsdp", None, None),
        P("fsdp", None, None),
        P("fsdp"),
        P("fsdp"),
        P("fsdp"),
        P("fsdp", None, None),
        P(None, "fsdp"),
        P(None, "fsdp"),
        P(None, "fsdp"),
        P("fsdp"),
        P("fsdp"),
        P("fsdp"),
    )
    out_specs = (
        P(),
        P(),
        P(),
        P(None, "fsdp"),
        P(None, "fsdp"),
        P(None, "fsdp"),
        P("fsdp"),
        P("fsdp"),
        P("fsdp"),
    )
    return jax.shard_map(shards, mesh=mesh, in_specs=in_specs, out_specs=out_specs, check_vma=False)
```

```python
import functools
import math

import jax
import jax.numpy as jnp
from jax import lax
from jax.experimental import pallas as pl
from jax.experimental.pallas import tpu as pltpu
from jax.sharding import PartitionSpec as P

D = 768
HD = 64
FF = 3072
PD = 16
CLS = 1001
PH = 2048
ZD = 768
FREQ = 256
GRID = 16
LAYERS = 2
DEPTH_Z = 2
STEP = 10
SEQ = 256


norm_eps = 1e-06
clip_limit = 0.002
learn_rate = 0.08
beta_one = 0.5
beta_two = 0.5
adam_eps = 1e-08
decay_rate = 0.01
proj_coeff = 0.5
low_type = jnp.bfloat16
full_type = jnp.float32


LANES = 128
ROWS = 16
UNIT = LANES * ROWS
MESH = pl.DeviceIdType.MESH

def up(value, step):
    return -(-value // step) * step

class Plan:
    def __init__(self, layout, length, devices):
        self.length = length
        self.devices = devices
        self.share = length // devices
        self.segments = []
        offset = units = 0
        for shape in layout:
            amount = math.prod(shape)
            matrix = len(shape) == 2 and shape[0] % ROWS == 0 and shape[1] % LANES == 0
            chunks = shape[1] // LANES if matrix else 1
            count = up(amount, UNIT) // UNIT
            self.segments.append((offset // LANES, chunks, count, units, shape, matrix))
            offset += amount
            units += count
        self.units = units
        self.per = up(up(units, devices) // devices, 4)
        rows_of = []
        for base, chunks, count, _, _, _ in self.segments:
            for u in range(count):
                b, c = divmod(u, chunks)
                first = base + b * ROWS * chunks + c
                rows_of.append((first, first + (ROWS - 1) * chunks))
        before = after = 0
        for d in range(devices):
            start, stop = d * self.share // LANES, (d + 1) * self.share // LANES
            for lo, hi in rows_of[self.per * d : self.per * d + self.per]:
                before, after = max(before, start - lo), max(after, hi + 1 - stop)
        self.before, self.after = up(before, 8), up(after, 8)
        units_before = units_after = 0
        for u, (lo, hi) in enumerate(rows_of):
            first = lo * LANES // self.share
            last = min(((hi + 1) * LANES - 1) // self.share, devices - 1)
            for d in range(first, last + 1):
                units_before = max(units_before, self.per * d - u)
                units_after = max(units_after, u + 1 - self.per * d - self.per)
        self.units_before, self.units_after = units_before, units_after
        self.half = self.per // 2
        self.raw = up(up(self.share, LANES) // LANES + 9, 64)
        self.ext = self.before + self.raw + self.after
        margin = tail = 0
        for d in range(devices):
            start = d * self.share // LANES
            lo = max(self.per * d - units_before, 0)
            for first, last in rows_of[lo : self.per * d + self.per + units_after]:
                margin, tail = max(margin, start - first), max(tail, last + 1 - start)
        self.margin = up(margin, 8)
        self.spread = up(max(tail, self.raw + 8), 8) + self.margin
        least = self.share // LANES
        self.fits = max(self.before, self.after) < least and max(units_before, units_after) < self.per

def place(index, zs):
    return index // 8, index // 4 % 2, index // 2 % 2, index % 2

def gather_kernel(plans, zs, *refs):
    nb = len(plans)
    raw_hbm = refs[:nb]
    outs = refs[nb : 2 * nb]
    raw, ext, tail, from_prev, from_next, slots = (refs[2 * nb + i * nb : 3 * nb + i * nb] for i in range(6))
    rest = refs[8 * nb :]
    load_sem, halo_send, halo_recv, own_sem, send_sem, zr, xa, xb, yb, ya, cr = rest
    n = zs * 8
    me = lax.axis_index("fsdp")
    z, y, x, c = place(me, zs)
    index = lambda zz, yy, xx, cc: ((zz * 2 + yy) * 2 + xx) * 2 + cc
    prev, following = lax.rem(me + n - 1, n), lax.rem(me + 1, n)
    xpeer, ypeer, cpeer = index(z, y, 1 - x, c), index(z, 1 - y, x, c), index(z, y, x, 1 - c)
    zpeer = [index(lax.rem(z + k, zs), y, x, c) for k in range(zs)]
    loads = []
    for b in range(nb):
        p = plans[b]
        loads.append(pltpu.make_async_copy(raw_hbm[b], raw[b].at[pl.ds(8, p.raw)], load_sem.at[b]))
        loads[b].start()
    barrier = pltpu.get_barrier_semaphore()
    peers = [prev, following, xpeer, ypeer, cpeer] + zpeer[1:]
    for peer in peers:
        pl.semaphore_signal(barrier, inc=1, device_id=(peer,), device_id_type=MESH)
    halos = []
    lane = lax.broadcasted_iota(jnp.int32, (64, LANES), 1)
    for b in range(nb):
        p = plans[b]
        shift = lax.rem(me * p.share, LANES)
        delta = (me + 1) * p.share // LANES - me * p.share // LANES
        raw[b][pl.ds(0, 8), :] = jnp.zeros((8, LANES), full_type)
        ext[b][pl.ds(0, p.before), :] = jnp.zeros((p.before, LANES), full_type)
        ext[b][pl.ds(p.before + p.raw, p.after), :] = jnp.zeros((p.after, LANES), full_type)
        loads[b].wait()

        def align(i, carry):
            row = pl.multiple_of(i * 64, 64)
            here = pltpu.roll(raw[b][pl.ds(row + 8, 64), :], shift, 1)
            above = pltpu.roll(raw[b][pl.ds(row + 7, 64), :], shift, 1)
            ext[b][pl.ds(row + p.before, 64), :] = jnp.where(lane >= shift, here, above)
            return carry

        lax.fori_loop(0, p.raw // 64, align, 0)
        tail[b][...] = ext[b][pl.ds(delta, p.before + 8), :]
        if b == 0:
            pl.semaphore_wait(barrier, len(peers))
        for s, (src, dst, to) in enumerate(((ext[b].at[pl.ds(p.before, p.after)], from_next[b], prev), (tail[b], from_prev[b], following))):
            copy = pltpu.make_async_remote_copy(src, dst, halo_send.at[2 * b + s], halo_recv.at[2 * b + s], device_id=(to,), device_id_type=MESH)
            copy.start()
            halos.append(copy)
    sends = []

    def send(src, dst, sem, to):
        copy = pltpu.make_async_remote_copy(src, dst, send_sem.at[len(sends)], sem, device_id=(to,), device_id_type=MESH)
        copy.start()
        sends.append(copy)

    def span(b, h):
        p = plans[b]
        return (0, p.half) if h == 0 else (p.half, p.per - p.half)

    def slot(k, dy, dx, dc):
        return index(lax.rem(z + zs - k, zs), 1 - y if dy else y, 1 - x if dx else x, 1 - c if dc else c)

    def part(b, h, k, dy, dx, dc=0):
        first, count = span(b, h)
        return outs[b].at[pl.ds(slot(k, dy, dx, dc) * plans[b].per + first, count)]

    def whole(b, k, dy, dx, dc=0):
        return outs[b].at[pl.ds(slot(k, dy, dx, dc) * plans[b].per, plans[b].per)]

    def arrived(ref, sem):
        pltpu.make_async_copy(ref, ref, sem).wait()

    owns = []
    for b in range(nb):
        p = plans[b]
        delta = (me + 1) * p.share // LANES - me * p.share // LANES
        for copy in halos[2 * b : 2 * b + 2]:
            copy.wait()
        ext[b][pl.ds(0, p.before + 8), :] += from_prev[b][...]
        ext[b][pl.ds(p.before + delta, p.after), :] += from_next[b][...]
        top = me * p.share // LANES - p.before
        for base, chunks, count, first_unit, _, _ in p.segments:
            lo = jnp.clip(p.per * me - first_unit, 0, count)
            hi = jnp.clip(p.per * me + p.per - first_unit, 0, count)

            def unit(u, carry):
                block = u // chunks
                row = base + block * (ROWS * chunks) + (u - block * chunks) - top
                if chunks == 1:
                    value = ext[b][pl.ds(row, ROWS), :]
                else:
                    value = ext[b][pl.ds(row, ROWS, stride=chunks), :]
                slots[b][first_unit + u - p.per * me] = value.astype(low_type)
                return carry

            lax.fori_loop(lo, hi, unit, 0)
        own = pltpu.make_async_copy(slots[b], whole(b, 0, 0, 0), own_sem.at[b])
        own.start()
        owns.append(own)
        mine = lambda h: slots[b].at[pl.ds(*span(b, h))]
        for k in range(1, zs):
            for h in range(2):
                send(mine(h), part(b, h, 0, 0, 0), zr.at[b, h, k], zpeer[k])
        send(mine(0), part(b, 0, 0, 0, 0), xa.at[b, 0], xpeer)
        send(mine(1), part(b, 1, 0, 0, 0), yb.at[b, 0], ypeer)
        send(mine(0), part(b, 0, 0, 0, 0), ya.at[b, 0, 0], ypeer)
        send(mine(1), part(b, 1, 0, 0, 0), xb.at[b, 0, 0], xpeer)
        send(slots[b], whole(b, 0, 0, 0), cr.at[b, 0, 0, 0], cpeer)
    for b in range(nb):
        for k in range(1, zs):
            arrived(part(b, 0, k, 0, 0), zr.at[b, 0, k])
            send(part(b, 0, k, 0, 0), part(b, 0, k, 0, 0), xa.at[b, k], xpeer)
            arrived(part(b, 1, k, 0, 0), zr.at[b, 1, k])
            send(part(b, 1, k, 0, 0), part(b, 1, k, 0, 0), yb.at[b, k], ypeer)
            send(part(b, 0, k, 0, 0), part(b, 0, k, 0, 0), ya.at[b, k, 0], ypeer)
            send(part(b, 1, k, 0, 0), part(b, 1, k, 0, 0), xb.at[b, k, 0], xpeer)
            send(whole(b, k, 0, 0), whole(b, k, 0, 0), cr.at[b, k, 0, 0], cpeer)
        for k in range(zs):
            arrived(part(b, 0, k, 0, 1), xa.at[b, k])
            send(part(b, 0, k, 0, 1), part(b, 0, k, 0, 1), ya.at[b, k, 1], ypeer)
            arrived(part(b, 1, k, 1, 0), yb.at[b, k])
            send(part(b, 1, k, 1, 0), part(b, 1, k, 1, 0), xb.at[b, k, 1], xpeer)
        for k in range(zs):
            arrived(part(b, 1, k, 0, 1), xb.at[b, k, 0])
            send(whole(b, k, 0, 1), whole(b, k, 0, 1), cr.at[b, k, 0, 1], cpeer)
            arrived(part(b, 0, k, 1, 0), ya.at[b, k, 0])
            send(whole(b, k, 1, 0), whole(b, k, 1, 0), cr.at[b, k, 1, 0], cpeer)
        for k in range(zs):
            arrived(part(b, 1, k, 1, 1), xb.at[b, k, 1])
            arrived(part(b, 0, k, 1, 1), ya.at[b, k, 1])
            send(whole(b, k, 1, 1), whole(b, k, 1, 1), cr.at[b, k, 1, 1], cpeer)
    for b in range(nb):
        owns[b].wait()
        for k in range(zs):
            for dy in range(2):
                for dx in range(2):
                    arrived(whole(b, k, dy, dx, 1), cr.at[b, k, dy, dx])
    for copy in sends:
        copy.wait_send()

def gather_units(plans, raws):
    n = plans[0].devices
    zs = n // 8
    nb = len(plans)
    per_bucket = 2 * (zs - 1) + 10 * zs
    dma = pltpu.SemaphoreType.DMA
    scratch = [pltpu.VMEM((p.raw + 8, LANES), full_type) for p in plans]
    scratch += [pltpu.VMEM((p.ext, LANES), full_type) for p in plans]
    scratch += [pltpu.VMEM((p.before + 8, LANES), full_type) for p in plans]
    scratch += [pltpu.VMEM((p.before + 8, LANES), full_type) for p in plans]
    scratch += [pltpu.VMEM((p.after, LANES), full_type) for p in plans]
    scratch += [pltpu.VMEM((p.per, ROWS, LANES), low_type) for p in plans]
    scratch += [dma((nb,)), dma((2 * nb,)), dma((2 * nb,)), dma((nb,)), dma((nb * per_bucket,))]
    scratch += [dma((nb, 2, zs)), dma((nb, zs)), dma((nb, zs, 2)), dma((nb, zs)), dma((nb, zs, 2)), dma((nb, zs, 2, 2))]
    return pl.pallas_call(
        functools.partial(gather_kernel, plans, zs),
        out_shape=[jax.ShapeDtypeStruct((n * p.per, ROWS, LANES), low_type) for p in plans],
        in_specs=[pl.BlockSpec(memory_space=pltpu.HBM)] * nb,
        out_specs=[pl.BlockSpec(memory_space=pltpu.HBM)] * nb,
        scratch_shapes=scratch,
        compiler_params=pltpu.CompilerParams(collective_id=0, has_side_effects=True, vmem_limit_bytes=48 * 1024 * 1024),
        name="gather_units",
    )(*raws)

AHEAD = 4


def reduce_kernel(plans, zs, *refs):
    nb = len(plans)
    take = lambda count: tuple(next(feed) for _ in range(count))
    feed = iter(refs)
    grads, (stats_in,) = take(nb), take(1)
    outs, (stats_out,), first = take(nb), take(1), take(nb)
    kept_a, kept_b, two_a, two_b, three_a, three_b, four = (take(nb) for _ in range(7))
    local, other = take(1)[0], take(1)[0]
    units_f, rows_f, flat_f = take(1)[0], take(1)[0], take(1)[0]
    from_prev, from_next = take(nb), take(nb)
    total, total_in = take(1)[0], take(1)[0]
    s1, r1, s2a, r2a, s2b, r2b, s3a, r3a, s3b, r3b, s4, r4, load_sem, halo_s, halo_r, out_sem, ss, sr = take(18)
    n = zs * 8
    me = lax.axis_index("fsdp")
    z, y, x, c = place(me, zs)
    index = lambda zz, yy, xx, cc: ((zz * 2 + yy) * 2 + xx) * 2 + cc
    prev, following = lax.rem(me + n - 1, n), lax.rem(me + 1, n)
    xpeer, ypeer, cpeer = index(z, y, 1 - x, c), index(z, 1 - y, x, c), index(z, y, x, 1 - c)
    below = lambda k: index(lax.rem(z + zs - k, zs), y, x, c)
    above = lambda k: index(lax.rem(z + k, zs), y, x, c)
    barrier = pltpu.get_barrier_semaphore()
    peers = [prev, following, xpeer, ypeer, cpeer] + [above(k) for k in range(1, zs)]
    for peer in peers:
        pl.semaphore_signal(barrier, inc=1, device_id=(peer,), device_id_type=MESH)
    pl.semaphore_wait(barrier, len(peers))

    def remote(src, dst, send_sem, recv_sem, to):
        return pltpu.make_async_remote_copy(src, dst, send_sem, recv_sem, device_id=(to,), device_id_type=MESH)

    def arrived(ref, sem):
        pltpu.make_async_copy(ref, ref, sem).wait()

    def slot(b, k, dy, dx, dc):
        where = index(lax.rem(z + zs - k, zs), 1 - y if dy else y, 1 - x if dx else x, 1 - c if dc else c)
        return grads[b].at[pl.ds(where * plans[b].per, plans[b].per)]

    order = ((1, 1), (1, 0), (0, 1), (0, 0))

    def sibling(b, k, dy, dx):
        return remote(slot(b, k, dy, dx, 1), first[b].at[k, dy, dx], s1.at[b, k, dy, dx], r1.at[b, k, dy, dx], cpeer)

    def add(p, dst, at, one, one_at, two, two_at):
        step = p.half // 2

        def body(i, carry):
            span = lambda ref, off: ref[pl.ds(off + i * step, step)].astype(full_type)
            dst[pl.ds(at + i * step, step)] = (span(one, one_at) + span(two, two_at)).astype(low_type)
            return carry

        lax.fori_loop(0, 2, body, 0)

    ring = local.shape[0]
    planes = list(range(1, zs)) + [0]
    used = []

    def send_of(b, h, k, dy, dx, src):
        if h == 0:
            return remote(src, two_a[b].at[k, dx], s2a.at[b, k, dx], r2a.at[b, k, dx], ypeer)
        return remote(src, two_b[b].at[k, dy], s2b.at[b, k, dy], r2b.at[b, k, dy], xpeer)

    steps = [(b, dy, dx, k) for b in range(nb) for k in planes for dy, dx in order]

    def loads(number):
        b, dy, dx, k = steps[number]
        at = number % ring
        p = plans[b]
        one = pltpu.make_async_copy(slot(b, k, dy, dx, 0), local.at[at, pl.ds(0, p.per)], load_sem.at[at, 0])
        two = pltpu.make_async_copy(first[b].at[k, dy, dx], other.at[number % 2, pl.ds(0, p.per)], load_sem.at[at, 1])
        return one, two

    pending = {}
    steps_args = lambda number: (steps[number][0], steps[number][3], steps[number][1], steps[number][2])

    def prepare(number):
        b, dy, dx, k = steps[number]
        for copy in pending.pop(number % ring, ()):
            copy.wait_send()
        one, two = loads(number)
        one.start()
        arrived(first[b].at[k, dy, dx], r1.at[b, k, dy, dx])
        two.start()

    def phase_one(number):
        b, dy, dx, k = steps[number]
        p = plans[b]
        at = number % ring
        if number == 0:
            for ahead in range(AHEAD):
                sibling(*steps_args(ahead)).start()
            prepare(0)
        if number + AHEAD < len(steps):
            sibling(*steps_args(number + AHEAD)).start()
        if number + 1 < len(steps):
            prepare(number + 1)
        for copy in loads(number):
            copy.wait()
        mine, theirs = local.at[at], other.at[number % 2]
        going = []
        if dy:
            add(p, mine, 0, mine, 0, theirs, 0)
            going.append(send_of(b, 0, k, dy, dx, local.at[at, pl.ds(0, p.half)]))
        else:
            add(p, kept_a[b].at[k, dx], 0, mine, 0, theirs, 0)
        if dx:
            add(p, mine, p.half, mine, p.half, theirs, p.half)
            going.append(send_of(b, 1, k, dy, dx, local.at[at, pl.ds(p.half, p.half)]))
        else:
            add(p, kept_b[b].at[k, dy], 0, mine, p.half, theirs, p.half)
        for copy in going:
            copy.start()
        pending[at] = going

    def three(b, h, k):
        if h == 0:
            return remote(two_a[b].at[k, 1], three_a[b].at[k], s3a.at[b, k], r3a.at[b, k], xpeer)
        return remote(two_b[b].at[k, 1], three_b[b].at[k], s3b.at[b, k], r3b.at[b, k], ypeer)

    def last(b, h, k):
        src = (three_a if h == 0 else three_b)[b].at[k]
        return remote(src, four[b].at[h, k - 1], s4.at[b, h, k - 1], r4.at[b, h, k - 1], below(k))

    def phase_two(b, k):
        p = plans[b]
        for far in (1, 0):
            for h, kept, two, sem in ((0, kept_a, two_a, r2a), (1, kept_b, two_b, r2b)):
                arrived(two[b].at[k, far], sem.at[b, k, far])
                if far:
                    add(p, two[b].at[k, 1], 0, two[b].at[k, 1], 0, kept[b].at[k, 1], 0)
                    three(b, h, k).start()
                else:
                    add(p, kept[b].at[k, 0], 0, two[b].at[k, 0], 0, kept[b].at[k, 0], 0)

    def phase_three(b, k):
        p = plans[b]
        for h, kept, got, sem in ((0, kept_a, three_a, r3a), (1, kept_b, three_b, r3b)):
            arrived(got[b].at[k], sem.at[b, k])
            if k:
                add(p, got[b].at[k], 0, got[b].at[k], 0, kept[b].at[k, 0], 0)
                last(b, h, k).start()

    def halo(b):
        p = plans[b]
        base = p.units_before
        held = units_f.at[b % 2]
        forward = remote(held.at[pl.ds(p.per, base)], from_prev[b], halo_s.at[b, 0], halo_r.at[b, 0], following)
        backward = remote(held.at[pl.ds(base, p.units_after)], from_next[b], halo_s.at[b, 1], halo_r.at[b, 1], prev)
        return forward, backward

    def collect(b):
        p = plans[b]
        base = p.units_before
        for h, kept, got in ((0, kept_a, three_a), (1, kept_b, three_b)):
            for k in range(1, zs):
                arrived(four[b].at[h, k - 1], r4.at[b, h, k - 1])
            step = p.half // 2

            def body(i, carry):
                part = pl.ds(i * step, step)
                value = kept[b][0, 0, part].astype(full_type) + got[b][0, part].astype(full_type)
                for k in range(1, zs):
                    value = value + four[b][h, k - 1, part].astype(full_type)
                units_f[b % 2, pl.ds(base + h * p.half + i * step, step)] = value
                return carry

            lax.fori_loop(0, 2, body, 0)
        for copy in halo(b):
            copy.start()

    def finish(b):
        p = plans[b]
        base = p.units_before
        for copy in halo(b):
            copy.wait()
        held = b % 2
        units_f[held, pl.ds(0, base)] = from_prev[b][...]
        units_f[held, pl.ds(base + p.per, p.units_after)] = from_next[b][...]
        top = me * p.share // LANES - p.margin
        for origin, chunks, count, first_unit, _, _ in p.segments:
            lo = jnp.clip(p.per * me - base - first_unit, 0, count)
            hi = jnp.clip(p.per * me + p.per + p.units_after - first_unit, 0, count)

            def unit(u, carry):
                block = u // chunks
                row = origin + block * (ROWS * chunks) + (u - block * chunks) - top
                value = units_f[held, first_unit + u - p.per * me + base]
                if chunks == 1:
                    rows_f[pl.ds(row, ROWS), :] = value
                else:
                    rows_f[pl.ds(row, ROWS, stride=chunks), :] = value
                return carry

            lax.fori_loop(lo, hi, unit, 0)
        shift = lax.rem(me * p.share, LANES)
        turn = lax.rem(LANES - shift, LANES)
        lane = lax.broadcasted_iota(jnp.int32, (64, LANES), 1)
        spot = lax.broadcasted_iota(jnp.int32, (64, LANES), 0) * LANES + lane
        if b:
            pltpu.make_async_copy(flat_f.at[pl.ds(0, plans[b - 1].raw)], outs[b - 1], out_sem.at[b - 1]).wait()

        def unalign(i, squares):
            row = pl.multiple_of(i * 64, 64)
            here = pltpu.roll(rows_f[pl.ds(row + p.margin, 64), :], turn, 1)
            below_row = pltpu.roll(rows_f[pl.ds(row + p.margin + 1, 64), :], turn, 1)
            value = jnp.where(lane < LANES - shift, here, below_row)
            value = jnp.where(spot + row * LANES < p.share, value, 0.0)
            flat_f[pl.ds(row, 64), :] = value
            return squares + jnp.sum((value * value).reshape(8, 8, LANES), axis=0)

        squares = lax.fori_loop(0, p.raw // 64, unalign, jnp.zeros((8, LANES), full_type))
        pltpu.make_async_copy(flat_f.at[pl.ds(0, p.raw)], outs[b], out_sem.at[b]).start()
        return squares

    squares = jnp.zeros((8, LANES), full_type)
    groups = [(b, k) for b in range(nb) for k in planes]
    for g in range(len(groups) + 2):
        if g < len(groups):
            for number in range(4 * g, 4 * g + 4):
                phase_one(number)
        if 0 <= g - 1 < len(groups):
            phase_two(*groups[g - 1])
        if 0 <= g - 2 < len(groups):
            phase_three(*groups[g - 2])
        b = (g - 3) // zs - 1
        if (g - 3) % zs == 0 and 0 <= b < nb - 1:
            collect(b)
        b = (g - 4) // zs - 1
        if (g - 4) % zs == 0 and 0 <= b < nb - 1:
            squares = squares + finish(b)
    collect(nb - 1)
    squares = squares + finish(nb - 1)
    pltpu.make_async_copy(flat_f.at[pl.ds(0, plans[nb - 1].raw)], outs[nb - 1], out_sem.at[nb - 1]).wait()
    total[0] = stats_in[...]
    total[1] = squares
    step = 0
    for to in ((cpeer,), (xpeer,), (ypeer,), tuple(above(k) for k in range(1, zs))):
        copies = []
        for peer in to:
            copies.append(remote(total, total_in.at[step], ss.at[step], sr.at[step], peer))
            copies[-1].start()
            step += 1
        for copy in copies:
            copy.wait()
        value = total[...]
        for i in range(len(to)):
            value = value + total_in[step - 1 - i]
        total[...] = value
    stats_out[...] = total[...]
    for group in pending.values():
        for copy in group:
            copy.wait_send()
    for b in range(nb):
        for dy, dx in order:
            for k in range(zs):
                sibling(b, k, dy, dx).wait_send()
        for h in range(2):
            for k in range(zs):
                three(b, h, k).wait_send()
                if k:
                    last(b, h, k).wait_send()

def reduce_units(plans, grads, stats):
    n = plans[0].devices
    zs = n // 8
    nb = len(plans)
    dma = pltpu.SemaphoreType.DMA
    most = max(p.per for p in plans)
    tile = (ROWS, LANES)
    half = lambda p, *lead: pltpu.VMEM(lead + (p.half,) + tile, low_type)
    scratch = [half(p, zs, 2) for p in plans] + [half(p, zs, 2) for p in plans]
    scratch += [half(p, zs, 2) for p in plans] + [half(p, zs, 2) for p in plans]
    scratch += [half(p, zs) for p in plans] + [half(p, zs) for p in plans]
    scratch += [half(p, 2, zs - 1) for p in plans]
    ring = 8
    scratch += [pltpu.VMEM((ring, most) + tile, low_type), pltpu.VMEM((2, most) + tile, low_type)]
    scratch += [pltpu.VMEM((2, max(p.units_before + p.per + p.units_after for p in plans)) + tile, full_type)]
    scratch += [pltpu.VMEM((max(p.spread for p in plans), LANES), full_type)]
    scratch += [pltpu.VMEM((max(p.raw for p in plans), LANES), full_type)]
    scratch += [pltpu.VMEM((p.units_before,) + tile, full_type) for p in plans]
    scratch += [pltpu.VMEM((p.units_after,) + tile, full_type) for p in plans]
    hops = 2 + zs
    scratch += [pltpu.VMEM((2, 8, LANES), full_type), pltpu.VMEM((hops, 2, 8, LANES), full_type)]
    scratch += [dma((nb, zs, 2, 2))] * 2 + [dma((nb, zs, 2))] * 4 + [dma((nb, zs))] * 4
    scratch += [dma((nb, 2, zs - 1))] * 2 + [dma((ring, 2)), dma((nb, 2)), dma((nb, 2)), dma((nb,)), dma((hops,)), dma((hops,))]
    anywhere = pl.BlockSpec(memory_space=pltpu.HBM)
    inside = pl.BlockSpec(memory_space=pltpu.VMEM)
    out_shape = [jax.ShapeDtypeStruct((p.raw, LANES), full_type) for p in plans]
    out_shape += [jax.ShapeDtypeStruct((2, 8, LANES), full_type)]
    out_shape += [jax.ShapeDtypeStruct((zs, 2, 2, p.per) + tile, low_type) for p in plans]
    results = pl.pallas_call(
        functools.partial(reduce_kernel, plans, zs),
        out_shape=out_shape,
        in_specs=[anywhere] * nb + [inside],
        out_specs=[anywhere] * nb + [inside] + [anywhere] * nb,
        scratch_shapes=scratch,
        compiler_params=pltpu.CompilerParams(collective_id=1, has_side_effects=True, vmem_limit_bytes=62 * 1024 * 1024),
        name="reduce_units",
    )(*grads, stats)
    return results[:nb], results[nb]

def to_rows(flat, plan):
    padded = jnp.pad(flat, ((0, plan.raw * LANES - flat.shape[0]),))
    return padded.reshape(plan.raw, LANES)


def layer_layout():
    return [
        (D, 3 * D),
        (D, D),
        (D, FF),
        (FF, D),
        (D, 6 * D),
        (D,),
        (D,),
        (D,),
        (FF,),
        (D,),
        (6 * D,),
    ]


def root_layout():
    return [
        (PD, D),
        (D,),
        (FREQ, D),
        (D,),
        (D, D),
        (D,),
        (CLS, D),
        (D, PH),
        (PH,),
        (PH, PH),
        (PH,),
        (PH, ZD),
        (ZD,),
        (D, 2 * D),
        (2 * D,),
        (D, PD),
        (PD,),
    ]


def unflatten(vector, layout):
    pieces = []
    offset = 0
    for dimensions in layout:
        amount = math.prod(dimensions)
        pieces.append(vector[offset : offset + amount].reshape(dimensions))
        offset += amount
    return pieces


def flatten_grads(grad_list, length):
    joined = jnp.concatenate([piece.reshape(-1) for piece in grad_list])
    return jnp.concatenate([joined, jnp.zeros((length - joined.shape[0],), full_type)])


def position_table():
    quarter = D // 4
    frequency = 1.0 / 10000.0 ** (jnp.arange(quarter, dtype=jnp.float32) / quarter)
    coords = jnp.arange(GRID, dtype=jnp.float32)
    angles = coords[:, None] * frequency[None, :]
    one_axis = jnp.concatenate([jnp.sin(angles), jnp.cos(angles)], axis=1)
    row_part = jnp.repeat(one_axis, GRID, axis=0)
    col_part = jnp.tile(one_axis, (GRID, 1))
    return jnp.concatenate([row_part, col_part], axis=1)


def time_features(times_in):
    half_freq = FREQ // 2
    frequency = jnp.exp(-math.log(10000.0) * jnp.arange(half_freq, dtype=jnp.float32) / half_freq)
    angles = times_in[:, None] * frequency[None, :]
    return jnp.concatenate([jnp.cos(angles), jnp.sin(angles)], axis=1)


def modulated_norm(values, offsets, scales):
    centred = values - jnp.mean(values, axis=-1, keepdims=True)
    spread = jnp.mean(centred * centred, axis=-1, keepdims=True)
    return centred * lax.rsqrt(spread + norm_eps) * (1.0 + scales) + offsets


def softmax_rows(scores):
    row_max = jnp.max(scores, axis=-1, keepdims=True)
    exponent = jnp.exp(scores - row_max)
    return exponent / jnp.sum(exponent, axis=-1, keepdims=True)


def gelu_tanh(values):
    return jax.nn.gelu(values, approximate=True)


def cosine_rows(predicted, target):
    target_full = target.astype(full_type)
    inner_sum = jnp.sum(predicted * target_full, axis=-1)
    return (
        inner_sum
        * lax.rsqrt(jnp.sum(predicted * predicted, axis=-1) + norm_eps)
        * lax.rsqrt(jnp.sum(target_full * target_full, axis=-1) + norm_eps)
    )


def silu_back(values, grad_in):
    _, pullback = jax.vjp(jax.nn.silu, values)
    return pullback(grad_in)[0]


def linear_fwd(inputs, weight):
    leading = inputs.shape[:-1]
    product = jnp.dot(
        inputs.reshape(-1, inputs.shape[-1]), weight, preferred_element_type=full_type
    )
    return product.reshape(leading + (weight.shape[1],))


def linear_back(inputs, weight, grad_out, with_input=True):
    rows_in = inputs.reshape(-1, inputs.shape[-1])
    rows_out = grad_out.reshape(-1, grad_out.shape[-1])
    grad_weight = lax.dot_general(
        rows_in, rows_out, (((0,), (0,)), ((), ())), preferred_element_type=full_type
    )
    grad_bias = jnp.sum(rows_out.astype(full_type), axis=0)
    grad_in = None
    if with_input:
        grad_in = lax.dot_general(
            rows_out, weight, (((1,), (1,)), ((), ())), preferred_element_type=full_type
        ).reshape(inputs.shape)
    return (grad_in, grad_weight, grad_bias)


def layer_forward(weights, residual, modulator):
    (
        w_attn_in,
        w_attn_out,
        w_mlp_in,
        w_mlp_out,
        w_modulate,
        b_query,
        b_value,
        b_attn_out,
        b_mlp_in,
        b_mlp_out,
        b_modulate,
    ) = weights
    samples_mb, seq_len = (residual.shape[0], residual.shape[1])
    head_count = D // HD
    modulation = jnp.split((linear_fwd(modulator, w_modulate) + b_modulate)[:, None, :], 6, axis=-1)
    normed_a = modulated_norm(residual, modulation[0], modulation[1]).astype(low_type)
    bias_qkv = jnp.concatenate([b_query, jnp.zeros_like(b_query), b_value])
    qkv_low = (linear_fwd(normed_a, w_attn_in) + bias_qkv).astype(low_type)
    qkv_low = qkv_low.reshape(samples_mb, seq_len, 3, head_count, HD)
    query_bf, key_bf, value_bf = (qkv_low[:, :, 0], qkv_low[:, :, 1], qkv_low[:, :, 2])
    scores = jnp.einsum(
        "bqhd,bkhd->bhqk", query_bf, key_bf, preferred_element_type=full_type
    ) * HD ** (-0.5)
    attn_probs = softmax_rows(scores)
    probs_bf = attn_probs.astype(low_type)
    heads_bf = jnp.einsum("bhqk,bkhd->bqhd", probs_bf, value_bf, preferred_element_type=full_type)
    heads_bf = heads_bf.astype(low_type).reshape(samples_mb, seq_len, D)
    attn_out = linear_fwd(heads_bf, w_attn_out) + b_attn_out
    middle = residual + modulation[2] * attn_out
    normed_m = modulated_norm(middle, modulation[3], modulation[4]).astype(low_type)
    mlp_pre = linear_fwd(normed_m, w_mlp_in) + b_mlp_in
    act_bf = gelu_tanh(mlp_pre).astype(low_type)
    mlp_out = linear_fwd(act_bf, w_mlp_out) + b_mlp_out
    residual_out = middle + modulation[5] * mlp_out
    square_sums = jnp.stack(
        [
            jnp.sum(residual_out * residual_out),
            jnp.sum(attn_out * attn_out),
            jnp.sum(mlp_out * mlp_out),
        ]
    )
    saved = (
        modulation,
        normed_a,
        query_bf,
        key_bf,
        value_bf,
        attn_probs,
        probs_bf,
        heads_bf,
        attn_out,
        middle,
        normed_m,
        mlp_pre,
        act_bf,
        mlp_out,
    )
    return (residual_out, saved, square_sums)


def layer_backward(weights, saved, residual, modulator, grad_out):
    w_attn_in, w_attn_out, w_mlp_in, w_mlp_out, w_modulate = weights[:5]
    (
        modulation,
        normed_a,
        query_bf,
        key_bf,
        value_bf,
        attn_probs,
        probs_bf,
        heads_bf,
        attn_out,
        middle,
        normed_m,
        mlp_pre,
        act_bf,
        mlp_out,
    ) = saved
    samples_mb, seq_len = (residual.shape[0], residual.shape[1])
    grad_mlp = (modulation[5] * grad_out).astype(low_type)
    grad_act, grad_w_mlp_out, grad_b_mlp_out = linear_back(act_bf, w_mlp_out, grad_mlp)
    _, gelu_pull = jax.vjp(gelu_tanh, mlp_pre)
    grad_pre = gelu_pull(grad_act)[0].astype(low_type)
    grad_normed_m, grad_w_mlp_in, grad_b_mlp_in = linear_back(normed_m, w_mlp_in, grad_pre)
    _, norm_pull_m = jax.vjp(modulated_norm, middle, modulation[3], modulation[4])
    grad_from_m, grad_shift_m, grad_scale_m = norm_pull_m(grad_normed_m)
    grad_middle = grad_out + grad_from_m
    grad_attn = (modulation[2] * grad_middle).astype(low_type)
    grad_heads, grad_w_attn_out, grad_b_attn_out = linear_back(heads_bf, w_attn_out, grad_attn)
    grad_heads_bf = grad_heads.astype(low_type).reshape(samples_mb, seq_len, D // HD, HD)
    grad_probs = jnp.einsum(
        "bqhd,bkhd->bhqk", grad_heads_bf, value_bf, preferred_element_type=full_type
    )
    grad_value = jnp.einsum(
        "bhqk,bqhd->bkhd", probs_bf, grad_heads_bf, preferred_element_type=full_type
    )
    grad_scores = attn_probs * (
        grad_probs - jnp.sum(attn_probs * grad_probs, axis=-1, keepdims=True)
    )
    grad_scores = grad_scores.astype(low_type)
    grad_query = jnp.einsum(
        "bhqk,bkhd->bqhd", grad_scores, key_bf, preferred_element_type=full_type
    ) * HD ** (-0.5)
    grad_key = jnp.einsum(
        "bhqk,bqhd->bkhd", grad_scores, query_bf, preferred_element_type=full_type
    ) * HD ** (-0.5)
    grad_qkv = jnp.stack([grad_query, grad_key, grad_value], axis=2).reshape(
        samples_mb, seq_len, 3 * D
    )
    grad_normed_a, grad_w_attn_in, grad_b_qkv = linear_back(
        normed_a, w_attn_in, grad_qkv.astype(low_type)
    )
    _, norm_pull_a = jax.vjp(modulated_norm, residual, modulation[0], modulation[1])
    grad_from_a, grad_shift_a, grad_scale_a = norm_pull_a(grad_normed_a)
    grad_gate_a = jnp.sum(attn_out * grad_middle, axis=1, keepdims=True)
    grad_gate_m = jnp.sum(mlp_out * grad_out, axis=1, keepdims=True)
    grad_mod = jnp.concatenate(
        [grad_shift_a, grad_scale_a, grad_gate_a, grad_shift_m, grad_scale_m, grad_gate_m], axis=-1
    )[:, 0, :].astype(low_type)
    grad_cond, grad_w_mod, grad_b_mod = linear_back(modulator, w_modulate, grad_mod)
    grad_list = [
        grad_w_attn_in,
        grad_w_attn_out,
        grad_w_mlp_in,
        grad_w_mlp_out,
        grad_w_mod,
        grad_b_qkv[:D],
        grad_b_qkv[2 * D :],
        grad_b_attn_out,
        grad_b_mlp_in,
        grad_b_mlp_out,
        grad_b_mod,
    ]
    return (grad_middle + grad_from_a, grad_cond, grad_list)


def embed_forward(pieces, latent_part, noise_part, times_part, labels_part, dropped_part):
    mixing = times_part[:, None, None]
    noisy_bf = ((1.0 - mixing) * latent_part + mixing * noise_part).astype(low_type)
    tokens = linear_fwd(noisy_bf, pieces[0]) + pieces[1] + position_table()
    basis_bf = time_features(times_part).astype(low_type)
    time_pre = linear_fwd(basis_bf, pieces[2]) + pieces[3]
    time_act = jax.nn.silu(time_pre).astype(low_type)
    time_emb = linear_fwd(time_act, pieces[4]) + pieces[5]
    classes = jnp.where(dropped_part == 1, CLS - 1, labels_part)
    onehot = (classes[:, None] == jnp.arange(CLS, dtype=jnp.int32)[None, :]).astype(low_type)
    condition = time_emb + jnp.dot(onehot, pieces[6], preferred_element_type=full_type)
    saved = (noisy_bf, basis_bf, time_pre, time_act, onehot, condition)
    return (tokens, jax.nn.silu(condition).astype(low_type), saved)


def embed_backward(pieces, saved, grad_tokens, grad_modulator):
    noisy_bf, basis_bf, time_pre, time_act, onehot, condition = saved
    grad_cond = silu_back(condition, grad_modulator)
    grad_table = lax.dot_general(
        onehot.astype(full_type),
        grad_cond,
        (((0,), (0,)), ((), ())),
        precision=lax.Precision.HIGHEST,
    )
    grad_time_act, grad_w_time_out, grad_b_time_out = linear_back(
        time_act, pieces[4], grad_cond.astype(low_type)
    )
    grad_time_pre = silu_back(time_pre, grad_time_act).astype(low_type)
    _, grad_w_time_in, grad_b_time_in = linear_back(basis_bf, pieces[2], grad_time_pre, False)
    _, grad_w_patch, grad_b_patch = linear_back(
        noisy_bf, pieces[0], grad_tokens.astype(low_type), False
    )
    return [
        grad_w_patch,
        grad_b_patch,
        grad_w_time_in,
        grad_b_time_in,
        grad_w_time_out,
        grad_b_time_out,
        grad_table,
    ]


def projector_forward(pieces, residual, features_part):
    residual_bf = residual.astype(low_type)
    pre_a = linear_fwd(residual_bf, pieces[7]) + pieces[8]
    act_a = jax.nn.silu(pre_a).astype(low_type)
    pre_b = linear_fwd(act_a, pieces[9]) + pieces[10]
    act_b = jax.nn.silu(pre_b).astype(low_type)
    predicted = linear_fwd(act_b, pieces[11]) + pieces[12]
    loss_part = -proj_coeff * jnp.sum(cosine_rows(predicted, features_part)) / residual.shape[1]
    return (loss_part, (residual_bf, pre_a, act_a, pre_b, act_b, predicted))


def projector_backward(pieces, saved, features_part, seq_len, sample_total):
    residual_bf, pre_a, act_a, pre_b, act_b, predicted = saved
    _, cosine_pull = jax.vjp(
        lambda predicted_in: cosine_rows(predicted_in, features_part), predicted
    )
    seed = jnp.full(predicted.shape[:2], -proj_coeff / (seq_len * sample_total), full_type)
    grad_pred = cosine_pull(seed)[0].astype(low_type)
    grad_act_b, grad_w_c, grad_b_c = linear_back(act_b, pieces[11], grad_pred)
    grad_pre_b = silu_back(pre_b, grad_act_b).astype(low_type)
    grad_act_a, grad_w_b, grad_b_b = linear_back(act_a, pieces[9], grad_pre_b)
    grad_pre_a = silu_back(pre_a, grad_act_a).astype(low_type)
    grad_residual, grad_w_a, grad_b_a = linear_back(residual_bf, pieces[7], grad_pre_a)
    return (grad_residual, [grad_w_a, grad_b_a, grad_w_b, grad_b_b, grad_w_c, grad_b_c])


def head_forward(pieces, residual, modulator, target, weight_t):
    modulation = (linear_fwd(modulator, pieces[13]) + pieces[14])[:, None, :]
    shift_f, scale_f = jnp.split(modulation, 2, axis=-1)
    normed = modulated_norm(residual, shift_f, scale_f).astype(low_type)
    deviation = linear_fwd(normed, pieces[15]) + pieces[16] - target
    loss_part = jnp.sum(weight_t * jnp.mean(deviation * deviation, axis=(1, 2)))
    return (loss_part, (shift_f, scale_f, normed, deviation))


def head_backward(pieces, saved, residual, modulator, weight_t, sample_total):
    shift_f, scale_f, normed, deviation = saved
    scaled = (
        2.0 * weight_t[:, None, None] / (deviation.shape[1] * deviation.shape[2] * sample_total)
    )
    grad_output = (scaled * deviation).astype(low_type)
    grad_normed, grad_w_head, grad_b_head = linear_back(normed, pieces[15], grad_output)
    _, pullback = jax.vjp(modulated_norm, residual, shift_f, scale_f)
    grad_residual, grad_shift, grad_scale = pullback(grad_normed)
    grad_mod = jnp.concatenate([grad_shift, grad_scale], axis=-1)[:, 0, :].astype(low_type)
    grad_cond, grad_w_mod, grad_b_mod = linear_back(modulator, pieces[13], grad_mod)
    return (grad_residual, grad_cond, [grad_w_mod, grad_b_mod, grad_w_head, grad_b_head])


WIDE = 2 * LANES
HEADS = D // HD
CHUNK = 64
MB = 1024 * 1024


def dot(one, two):
    return jnp.dot(one, two, preferred_element_type=full_type)


def dot_nt(one, two):
    return lax.dot_general(one, two, (((1,), (1,)), ((), ())), preferred_element_type=full_type)


def dot_tn(one, two):
    return lax.dot_general(one, two, (((0,), (0,)), ((), ())), preferred_element_type=full_type)


def block_of(w, block, blocks, chunk, chunks):
    pieces = [w[pl.ds(block, blocks), chunk + i].reshape(blocks * ROWS, LANES) for i in range(chunks)]
    return jnp.concatenate(pieces, axis=1) if chunks > 1 else pieces[0]


def put_block(out, block, chunk, value):
    blocks = value.shape[0] // ROWS
    for i in range(value.shape[1] // LANES):
        piece = value[:, i * LANES : (i + 1) * LANES].astype(low_type)
        out[pl.ds(block, blocks), chunk + i] = piece.reshape(blocks, ROWS, LANES)


def loop(count, body):
    lax.fori_loop(0, count, lambda i, carry: (body(i), carry)[1], 0)


def norm_parts(values):
    centred = values - jnp.mean(values, axis=-1, keepdims=True)
    spread = jnp.mean(centred * centred, axis=-1, keepdims=True)
    scale = lax.rsqrt(spread + norm_eps)
    return centred * scale, scale


def norm_back(values, grad, gain):
    hat, scale = norm_parts(values)
    inner = grad * gain
    mean_a = jnp.mean(inner, axis=-1, keepdims=True)
    mean_b = jnp.mean(inner * hat, axis=-1, keepdims=True)
    return scale * (inner - mean_a - hat * mean_b), grad * hat


def gelu_parts(values):
    root = math.sqrt(2.0 / math.pi)
    square = values * values
    bend = jnp.tanh(root * values * (1.0 + 0.044715 * square))
    half = 0.5 * (1.0 + bend)
    slope = half + 0.5 * values * (1.0 - bend * bend) * root * (1.0 + 3.0 * 0.044715 * square)
    return values * half, slope


def rows_sum(values):
    return jnp.sum(values, axis=0, keepdims=True)


def segment_ref(units, plan, number):
    _, chunks, count, first, shape, matrix = plan.segments[number]
    part = units.at[pl.ds(first, count)]
    if not matrix:
        return part
    return part.reshape(shape[0] // ROWS, chunks, ROWS, LANES)


def segment_scratch(plan, number):
    _, chunks, _, _, shape, _ = plan.segments[number]
    return pltpu.VMEM((shape[0] // ROWS, chunks, ROWS, LANES), low_type)


def attention_pairs(rows):
    return (rows // SEQ) * (HEADS // 2)


def head_masks():
    lane = lax.broadcasted_iota(jnp.int32, (SEQ, LANES), 1)
    return lane < HD


def softmax_f32(scores):
    exponent = jnp.exp(scores - jnp.max(scores, axis=-1, keepdims=True))
    return exponent * (1.0 / jnp.sum(exponent, axis=-1, keepdims=True))


def mods_kernel(plan, modulator, bias, units, out, w, sem):
    load = pltpu.make_async_copy(segment_ref(units, plan, 4), w, sem)
    load.start()
    load.wait()
    value = modulator[...]

    def body(j):
        cols = pl.ds(pl.multiple_of(j * WIDE, WIDE), WIDE)
        out[:, cols] = dot(value, block_of(w, 0, D // ROWS, 2 * j, 2)) + bias[:, cols]

    loop(6 * D // WIDE, body)


def mods_call(plan, modulator, bias, units):
    vm = pl.BlockSpec(memory_space=pltpu.VMEM)
    return pl.pallas_call(
        functools.partial(mods_kernel, plan),
        out_shape=jax.ShapeDtypeStruct((modulator.shape[0], 6 * D), full_type),
        in_specs=[vm, vm, pl.BlockSpec(memory_space=pltpu.HBM)],
        out_specs=vm,
        scratch_shapes=[segment_scratch(plan, 4), pltpu.SemaphoreType.DMA],
        compiler_params=pltpu.CompilerParams(vmem_limit_bytes=32 * MB),
        name="modulation",
    )(modulator, bias, units)


def mods_back_kernel(plan, modulator, grad, units, before, grads, cond, w, dw, sem):
    load = pltpu.make_async_copy(segment_ref(units, plan, 4), w, sem.at[0])
    load.start()
    turned = modulator[...].astype(full_type).T.astype(low_type)

    def weight(j):
        cols = pl.ds(pl.multiple_of(j * WIDE, WIDE), WIDE)
        put_block(dw, 0, 2 * j, dot(turned, grad[:, cols]))

    loop(6 * D // WIDE, weight)
    store = pltpu.make_async_copy(dw, segment_ref(grads, plan, 4), sem.at[1])
    store.start()
    load.wait()
    cond[...] = jnp.zeros(cond.shape, full_type)

    def back(j):
        cols = pl.ds(pl.multiple_of(j * WIDE, WIDE), WIDE)
        cond[...] += dot_nt(grad[:, cols], block_of(w, 0, D // ROWS, 2 * j, 2))

    loop(6 * D // WIDE, back)
    store.wait()


def mods_back_call(plan, modulator, grad, units, grads):
    vm = pl.BlockSpec(memory_space=pltpu.VMEM)
    anywhere = pl.BlockSpec(memory_space=pltpu.HBM)
    return pl.pallas_call(
        functools.partial(mods_back_kernel, plan),
        out_shape=[jax.ShapeDtypeStruct(grads.shape, low_type), jax.ShapeDtypeStruct((modulator.shape[0], D), full_type)],
        in_specs=[vm, vm, anywhere, anywhere],
        out_specs=[anywhere, vm],
        input_output_aliases={3: 0},
        scratch_shapes=[segment_scratch(plan, 4), segment_scratch(plan, 4), pltpu.SemaphoreType.DMA((2,))],
        compiler_params=pltpu.CompilerParams(vmem_limit_bytes=40 * MB),
        name="modulation_back",
    )(modulator, grad, units, grads)


SAVED = (("h1", D, low_type), ("qkv", 3 * D, low_type), ("heads", D, low_type), ("attn", D, full_type), ("middle", D, full_type), ("h2", D, low_type), ("pre", FF, full_type), ("mlp", D, full_type))


def layer_forward_kernel(plan, rows, x, mod, bias_qkv, bias_o, bias_1, bias_2, units, out, sums, *refs):
    ns = len(SAVED)
    saved_out = refs[:ns]
    h1, qkv, heads, attn, middle, h2, pre, mlp = refs[ns : 2 * ns]
    w_qkv, w_o, w_1, w_2, load_sem, save_sem = refs[2 * ns :]
    weights = (w_qkv, w_o, w_1, w_2)
    loads = [pltpu.make_async_copy(segment_ref(units, plan, i), weights[i], load_sem.at[i]) for i in range(4)]
    for copy in loads:
        copy.start()
    saves = [pltpu.make_async_copy(refs[ns + i], saved_out[i], save_sem.at[i]) for i in range(ns)]
    part = lambda s, i: mod[pl.ds(s, 1), i * D : (i + 1) * D]
    per = SEQ // CHUNK

    def norm_a(i):
        at = pl.ds(pl.multiple_of(i * CHUNK, CHUNK), CHUNK)
        s = i // per
        hat, _ = norm_parts(x[at, :])
        h1[at, :] = (hat * (1.0 + part(s, 1)) + part(s, 0)).astype(low_type)

    loop(rows // CHUNK, norm_a)
    saves[0].start()
    loads[0].wait()

    def project(j):
        cols = pl.ds(pl.multiple_of(j * WIDE, WIDE), WIDE)
        value = dot(h1[...], block_of(w_qkv, 0, D // ROWS, 2 * j, 2)) + bias_qkv[:, cols]
        qkv[:, cols] = value.astype(low_type)

    loop(3 * D // WIDE, project)
    saves[1].start()
    first = head_masks()

    def attend(i):
        s, j = i // (HEADS // 2), i % (HEADS // 2)
        at = pl.ds(pl.multiple_of(s * SEQ, SEQ), SEQ)
        cut = lambda o: qkv[at, pl.ds(pl.multiple_of(o * D + j * LANES, LANES), LANES)]
        q, k, v = cut(0), cut(1), cut(2)
        q = q * jnp.asarray(HD ** (-0.5), low_type)
        zero = jnp.zeros_like(q)
        halves = []
        for mask in (first, ~first):
            probs = softmax_f32(dot_nt(jnp.where(mask, q, zero), k)).astype(low_type)
            halves.append(dot(probs, v))
        heads[at, pl.ds(pl.multiple_of(j * LANES, LANES), LANES)] = jnp.where(first, halves[0], halves[1]).astype(low_type)

    loop(attention_pairs(rows), attend)
    saves[2].start()
    loads[1].wait()

    def project_out(j):
        cols = pl.ds(pl.multiple_of(j * WIDE, WIDE), WIDE)
        attn[:, cols] = dot(heads[...], block_of(w_o, 0, D // ROWS, 2 * j, 2)) + bias_o[:, cols]

    loop(D // WIDE, project_out)
    saves[3].start()
    zero_sum = jnp.zeros((1, D), full_type)

    def norm_m(i, total):
        at = pl.ds(pl.multiple_of(i * CHUNK, CHUNK), CHUNK)
        s = i // per
        value = attn[at, :]
        mid = x[at, :] + part(s, 2) * value
        middle[at, :] = mid
        hat, _ = norm_parts(mid)
        h2[at, :] = (hat * (1.0 + part(s, 4)) + part(s, 3)).astype(low_type)
        return total + rows_sum(value * value)

    attn_sum = lax.fori_loop(0, rows // CHUNK, norm_m, zero_sum)
    saves[4].start()
    saves[5].start()
    loads[2].wait()
    loads[3].wait()
    mlp[...] = jnp.broadcast_to(bias_2[...], (rows, D))

    def feed(j):
        cols = pl.ds(pl.multiple_of(j * WIDE, WIDE), WIDE)
        value = dot(h2[...], block_of(w_1, 0, D // ROWS, 2 * j, 2)) + bias_1[:, cols]
        pre[:, cols] = value
        act = gelu_parts(value)[0].astype(low_type)
        mlp[...] += dot(act, block_of(w_2, j * (WIDE // ROWS), WIDE // ROWS, 0, D // LANES))

    loop(FF // WIDE, feed)
    saves[6].start()
    saves[7].start()

    def finish(i, carry):
        at = pl.ds(pl.multiple_of(i * CHUNK, CHUNK), CHUNK)
        value = mlp[at, :]
        result = middle[at, :] + part(i // per, 5) * value
        out[at, :] = result
        return (carry[0] + rows_sum(result * result), carry[1] + rows_sum(value * value))

    out_sum, mlp_sum = lax.fori_loop(0, rows // CHUNK, finish, (zero_sum, zero_sum))
    sums[...] = jnp.zeros(sums.shape, full_type)
    sums[0:1, :] = out_sum
    sums[1:2, :] = attn_sum
    sums[2:3, :] = mlp_sum
    for copy in saves:
        copy.wait()


def layer_forward_call(plan, x, mod, biases, units):
    rows = x.shape[0]
    vm = pl.BlockSpec(memory_space=pltpu.VMEM)
    anywhere = pl.BlockSpec(memory_space=pltpu.HBM)
    dma = pltpu.SemaphoreType.DMA
    shapes = [((rows, width), kind) for _, width, kind in SAVED]
    results = pl.pallas_call(
        functools.partial(layer_forward_kernel, plan, rows),
        out_shape=[jax.ShapeDtypeStruct((rows, D), full_type), jax.ShapeDtypeStruct((8, D), full_type)]
        + [jax.ShapeDtypeStruct(*s) for s in shapes],
        in_specs=[vm] * 6 + [anywhere],
        out_specs=[vm, vm] + [anywhere] * len(SAVED),
        scratch_shapes=[pltpu.VMEM(*s) for s in shapes] + [segment_scratch(plan, i) for i in range(4)] + [dma((4,)), dma((len(SAVED),))],
        compiler_params=pltpu.CompilerParams(vmem_limit_bytes=56 * MB),
        name="layer_forward",
    )(x, mod, *biases, units)
    return results[0], results[1], results[2:]


def layer_backward_kernel(plan, rows, x, grad_in, mod, *refs):
    ns = len(SAVED)
    saved_hbm = refs[:ns]
    units, grad_out, grad_mod, bias_out, grads = refs[ns : ns + 5]
    h1, qkv, heads, attn, middle, h2, pre, mlp = refs[ns + 5 : 2 * ns + 5]
    w_qkv, w_o, w_1, w_2, d_qkv, g_low, wide, turned, dx, d_one, d_two, load_sem, save_sem, out_sem = refs[2 * ns + 5 :]
    weights = (w_qkv, w_o, w_1, w_2)
    inside = dict(zip(range(ns), refs[ns + 5 : 2 * ns + 5]))
    saves = [pltpu.make_async_copy(saved_hbm[i], inside[i], save_sem.at[i]) for i in range(ns)]
    loads = [pltpu.make_async_copy(segment_ref(units, plan, i), weights[i], load_sem.at[i]) for i in range(4)]
    for copy in (saves[7], saves[6], loads[3], saves[5], loads[2], saves[4], saves[3], loads[1], saves[2], saves[1], loads[0], saves[0]):
        copy.start()
    part = lambda s, i: mod[pl.ds(s, 1), i * D : (i + 1) * D]
    per = SEQ // CHUNK
    grad_mod[...] = jnp.zeros(grad_mod.shape, full_type)
    bias_out[...] = jnp.zeros(bias_out.shape, full_type)

    def add_mod(s, i, value):
        grad_mod[pl.ds(s, 1), i * D : (i + 1) * D] += value

    def each_chunk(body):
        loop(rows // CHUNK, lambda i: body(pl.ds(pl.multiple_of(i * CHUNK, CHUNK), CHUNK), i // per))

    B_Q, B_V, B_O, B_1, B_2 = 0, D, 2 * D, 3 * D, 3 * D + FF
    saves[7].wait()

    def start_mlp(at, s):
        grad = grad_in[at, :]
        low = (part(s, 5) * grad).astype(low_type)
        g_low[at, :] = low
        bias_out[:, B_2 : B_2 + D] += rows_sum(low.astype(full_type))
        add_mod(s, 5, rows_sum(mlp[at, :] * grad))

    each_chunk(start_mlp)
    saves[5].wait()
    turned[...] = h2[...].astype(full_type).T.astype(low_type)
    saves[6].wait()
    loads[3].wait()
    loads[2].wait()
    dx[...] = jnp.zeros(dx.shape, full_type)
    half = WIDE // ROWS

    def outer(slot, segment, block, blocks, chunk, chunks, buffer):
        target = segment_ref(grads, plan, segment).at[pl.ds(block, blocks), pl.ds(chunk, chunks)]
        return pltpu.make_async_copy(buffer, target, out_sem.at[slot])

    def mlp_store(j, kind):
        at = j % 2
        if kind == 0:
            return outer(2 * at, 3, j * half, half, 0, D // LANES, d_one.at[at])
        return outer(2 * at + 1, 2, 0, D // ROWS, 2 * j, 2, d_two.at[at])

    def feed_back(j):
        cols = pl.ds(pl.multiple_of(j * WIDE, WIDE), WIDE)
        at = j % 2

        @pl.when(j >= 2)
        def _():
            mlp_store(j - 2, 0).wait()
            mlp_store(j - 2, 1).wait()

        act, slope = gelu_parts(pre[:, cols])
        grad_act = dot_nt(g_low[...], block_of(w_2, j * half, half, 0, D // LANES))
        low = (grad_act * slope).astype(low_type)
        wide[...] = low
        bias_out[:, pl.ds(pl.multiple_of(B_1 + j * WIDE, WIDE), WIDE)] += rows_sum(low.astype(full_type))
        put_block(d_one.at[at], 0, 0, dot_tn(act.astype(low_type), g_low[...]))
        mlp_store(j, 0).start()
        put_block(d_two.at[at], 0, 0, dot(turned[...], wide[...]))
        mlp_store(j, 1).start()
        dx[...] += dot_nt(wide[...], block_of(w_1, 0, D // ROWS, 2 * j, 2))

    steps = FF // WIDE
    loop(steps, feed_back)
    saves[4].wait()
    saves[3].wait()

    def middle_back(at, s):
        grad = dx[at, :]
        back, scaled = norm_back(middle[at, :], grad, 1.0 + part(s, 4))
        add_mod(s, 3, rows_sum(grad))
        add_mod(s, 4, rows_sum(scaled))
        total = grad_in[at, :] + back
        grad_out[at, :] = total
        low = (part(s, 2) * total).astype(low_type)
        g_low[at, :] = low
        bias_out[:, B_O : B_O + D] += rows_sum(low.astype(full_type))
        add_mod(s, 2, rows_sum(attn[at, :] * total))

    each_chunk(middle_back)
    loads[1].wait()
    saves[2].wait()
    for j in (steps - 2, steps - 1):
        mlp_store(j, 0).wait()
        mlp_store(j, 1).wait()
    turned[...] = heads[...].astype(full_type).T.astype(low_type)

    def wo_store(j):
        return outer(j % 2, 1, 0, D // ROWS, 2 * j, 2, d_two.at[j % 2])

    def out_back(j):
        cols = pl.ds(pl.multiple_of(j * WIDE, WIDE), WIDE)

        @pl.when(j >= 2)
        def _():
            wo_store(j - 2).wait()

        put_block(d_two.at[j % 2], 0, 0, dot(turned[...], g_low[:, cols]))
        wo_store(j).start()
        heads[:, cols] = dot_nt(g_low[...], block_of(w_o, j * half, half, 0, D // LANES)).astype(low_type)

    loop(D // WIDE, out_back)
    saves[1].wait()
    first = head_masks()

    def attend_back(i):
        s, j = i // (HEADS // 2), i % (HEADS // 2)
        at = pl.ds(pl.multiple_of(s * SEQ, SEQ), SEQ)
        cut = lambda o: qkv[at, pl.ds(pl.multiple_of(o * D + j * LANES, LANES), LANES)]
        q, k, v = cut(0), cut(1), cut(2)
        go = heads[at, pl.ds(pl.multiple_of(j * LANES, LANES), LANES)]
        q = q * jnp.asarray(HD ** (-0.5), low_type)
        zero = jnp.zeros_like(q)
        dq, dk, dv = [], 0.0, 0.0
        for mask in (first, ~first):
            q_h, go_h = jnp.where(mask, q, zero), jnp.where(mask, go, zero)
            probs = softmax_f32(dot_nt(q_h, k))
            grad_probs = dot_nt(go_h, v)
            dv = dv + dot_tn(probs.astype(low_type), go_h)
            inner = jnp.sum(probs * grad_probs, axis=-1, keepdims=True)
            ds = (probs * (grad_probs - inner)).astype(low_type)
            dq.append(dot(ds, k) * HD ** (-0.5))
            dk = dk + dot_tn(ds, q_h)
        put = lambda o, value: d_qkv.at[at, pl.ds(pl.multiple_of(o * D + j * LANES, LANES), LANES)].set(value)
        for o, value in enumerate((jnp.where(first, dq[0], dq[1]), dk, dv)):
            low = value.astype(low_type)
            d_qkv[at, pl.ds(pl.multiple_of(o * D + j * LANES, LANES), LANES)] = low
            if o != 1:
                start = (B_Q if o == 0 else B_V) + j * LANES
                bias_out[:, pl.ds(pl.multiple_of(start, LANES), LANES)] += rows_sum(low.astype(full_type))

    loop(attention_pairs(rows), attend_back)
    saves[0].wait()
    loads[0].wait()
    wo_store(1).wait()
    wo_store(2).wait()
    turned[...] = h1[...].astype(full_type).T.astype(low_type)
    dx[...] = jnp.zeros(dx.shape, full_type)

    def qkv_store(j):
        return outer(j % 2, 0, 0, D // ROWS, 2 * j, 2, d_two.at[j % 2])

    def project_back(j):
        cols = pl.ds(pl.multiple_of(j * WIDE, WIDE), WIDE)

        @pl.when(j >= 2)
        def _():
            qkv_store(j - 2).wait()

        put_block(d_two.at[j % 2], 0, 0, dot(turned[...], d_qkv[:, cols]))
        qkv_store(j).start()
        dx[...] += dot_nt(d_qkv[:, cols], block_of(w_qkv, 0, D // ROWS, 2 * j, 2))

    count = 3 * D // WIDE
    loop(count, project_back)

    def input_back(at, s):
        grad = dx[at, :]
        back, scaled = norm_back(x[at, :], grad, 1.0 + part(s, 1))
        add_mod(s, 0, rows_sum(grad))
        add_mod(s, 1, rows_sum(scaled))
        grad_out[at, :] += back

    each_chunk(input_back)
    for j in (count - 2, count - 1):
        qkv_store(j).wait()


def layer_backward_call(plan, x, grad, mod, saved, units):
    rows = x.shape[0]
    vm = pl.BlockSpec(memory_space=pltpu.VMEM)
    anywhere = pl.BlockSpec(memory_space=pltpu.HBM)
    dma = pltpu.SemaphoreType.DMA
    shapes = [((rows, width), kind) for _, width, kind in SAVED]
    tile = (ROWS, LANES)
    return pl.pallas_call(
        functools.partial(layer_backward_kernel, plan, rows),
        out_shape=[
            jax.ShapeDtypeStruct((rows, D), full_type),
            jax.ShapeDtypeStruct((8, 6 * D), full_type),
            jax.ShapeDtypeStruct((1, 4 * D + FF), full_type),
            jax.ShapeDtypeStruct(units.shape, low_type),
        ],
        in_specs=[vm] * 3 + [anywhere] * (len(SAVED) + 1),
        out_specs=[vm, vm, vm, anywhere],
        scratch_shapes=[pltpu.VMEM(*s) for s in shapes]
        + [segment_scratch(plan, i) for i in range(4)]
        + [
            pltpu.VMEM((rows, 3 * D), low_type),
            pltpu.VMEM((rows, D), low_type),
            pltpu.VMEM((rows, WIDE), low_type),
            pltpu.VMEM((D, rows), low_type),
            pltpu.VMEM((rows, D), full_type),
            pltpu.VMEM((2, WIDE // ROWS, D // LANES) + tile, low_type),
            pltpu.VMEM((2, D // ROWS, 2) + tile, low_type),
            dma((4,)),
            dma((len(SAVED),)),
            dma((4,)),
        ],
        compiler_params=pltpu.CompilerParams(vmem_limit_bytes=60 * MB),
        name="layer_backward",
    )(x, grad, mod, *saved, units)


def sigmoid(values):
    return 1.0 / (1.0 + jnp.exp(-values))


def silu_parts(values):
    gate = sigmoid(values)
    return values * gate, gate * (1.0 + values * (1.0 - gate))


TOP = (7, 9, 11, 13)


def top_kernel(plan, rows, sample_total, x, features, target, weight_t, modulator, b_1, b_2, b_3, b_f, w_h, b_h, units, *refs):
    grad_x, stats, cond, bias_out, dw_h, grads = refs[:6]
    p_1, p_2, p_3, w_f, pre_a, act_a, pre_b, act_b, pred, low, g_b, g_a, hidden, modf, d_modf, stage, dw_f, load_sem, out_sem = refs[6:]
    weights = (p_1, p_2, p_3, w_f)
    loads = [pltpu.make_async_copy(segment_ref(units, plan, s), weights[i], load_sem.at[i]) for i, s in enumerate(TOP)]
    for copy in loads:
        copy.start()
    per = SEQ // CHUNK
    half = WIDE // ROWS
    stats[...] = jnp.zeros(stats.shape, full_type)
    bias_out[...] = jnp.zeros(bias_out.shape, full_type)
    d_modf[...] = jnp.zeros(d_modf.shape, full_type)
    A_1, A_2, A_3, A_F, A_H = 0, PH, 2 * PH, 2 * PH + ZD, 2 * PH + ZD + 2 * D
    wide_at = lambda j, base=0: pl.ds(pl.multiple_of(base + j * WIDE, LANES), WIDE)

    def each_chunk(body):
        loop(rows // CHUNK, lambda i: body(pl.ds(pl.multiple_of(i * CHUNK, CHUNK), CHUNK), i // per))

    def to_low(at, s):
        low[at, :] = x[at, :].astype(low_type)

    each_chunk(to_low)
    loads[0].wait()

    def first_layer(j):
        value = dot(low[...], block_of(p_1, 0, D // ROWS, 2 * j, 2)) + b_1[:, wide_at(j)]
        pre_a[:, wide_at(j)] = value
        act_a[:, wide_at(j)] = silu_parts(value)[0].astype(low_type)

    loop(PH // WIDE, first_layer)
    loads[1].wait()

    def second_layer(j):
        value = dot(act_a[...], block_of(p_2, 0, PH // ROWS, 2 * j, 2)) + b_2[:, wide_at(j)]
        pre_b[:, wide_at(j)] = value
        act_b[:, wide_at(j)] = silu_parts(value)[0].astype(low_type)

    loop(PH // WIDE, second_layer)
    loads[2].wait()

    def third_layer(j):
        pred[:, wide_at(j)] = dot(act_b[...], block_of(p_3, 0, PH // ROWS, 2 * j, 2)) + b_3[:, wide_at(j)]

    loop(ZD // WIDE, third_layer)
    seed = -proj_coeff / (SEQ * sample_total)

    def cosine(at, s):
        value = pred[at, :]
        want = features[at, :].astype(full_type)
        inner = jnp.sum(value * want, axis=-1, keepdims=True)
        scale_a = lax.rsqrt(jnp.sum(value * value, axis=-1, keepdims=True) + norm_eps)
        scale_b = lax.rsqrt(jnp.sum(want * want, axis=-1, keepdims=True) + norm_eps)
        both = scale_a * scale_b
        stats[0:1, 0:1] += jnp.sum(inner * both, axis=0, keepdims=True)
        grad = seed * (want * both - value * (inner * both * scale_a * scale_a))
        grad = grad.astype(low_type)
        hidden[at, :] = grad
        bias_out[:, A_3 : A_3 + ZD] += rows_sum(grad.astype(full_type))

    each_chunk(cosine)

    def store(segment, j, chunks):
        where = segment_ref(grads, plan, segment).at[pl.ds(j * half, half)]
        return pltpu.make_async_copy(stage.at[j % 2, :, pl.ds(0, chunks)], where, out_sem.at[j % 2])

    def stored(segment, j, chunks):
        @pl.when(j >= 2)
        def _():
            store(segment, j - 2, chunks).wait()

    def third_back(j):
        stored(11, j, ZD // LANES)
        put_block(stage.at[j % 2], 0, 0, dot_tn(act_b[:, wide_at(j)], hidden[...]))
        store(11, j, ZD // LANES).start()
        grad = dot_nt(hidden[...], block_of(p_3, j * half, half, 0, ZD // LANES))
        grad = (grad * silu_parts(pre_b[:, wide_at(j)])[1]).astype(low_type)
        g_b[:, wide_at(j)] = grad
        bias_out[:, wide_at(j, A_2)] += rows_sum(grad.astype(full_type))

    def drain(segment, count, chunks):
        for j in range(max(0, count - 2), count):
            store(segment, j, chunks).wait()

    loop(PH // WIDE, third_back)
    drain(11, PH // WIDE, ZD // LANES)
    span = 4 * LANES

    def second_back(j):
        stored(9, j, PH // LANES)
        for i in range(PH // span):
            put_block(stage.at[j % 2], 0, i * (span // LANES), dot_tn(act_a[:, wide_at(j)], g_b[:, i * span : (i + 1) * span]))
        store(9, j, PH // LANES).start()
        grad = dot_nt(g_b[...], block_of(p_2, j * half, half, 0, PH // LANES))
        grad = (grad * silu_parts(pre_a[:, wide_at(j)])[1]).astype(low_type)
        g_a[:, wide_at(j)] = grad
        bias_out[:, wide_at(j, A_1)] += rows_sum(grad.astype(full_type))

    loop(PH // WIDE, second_back)
    drain(9, PH // WIDE, PH // LANES)

    def first_back(j):
        stored(7, j, PH // LANES)
        for i in range(PH // span):
            put_block(stage.at[j % 2], 0, i * (span // LANES), dot_tn(low[:, wide_at(j)], g_a[:, i * span : (i + 1) * span]))
        store(7, j, PH // LANES).start()
        grad_x[:, wide_at(j)] = dot_nt(g_a[...], block_of(p_1, j * half, half, 0, PH // LANES))

    loop(D // WIDE, first_back)
    loads[3].wait()

    def final_mod(j):
        modf[:, wide_at(j)] = dot(modulator[...], block_of(w_f, 0, D // ROWS, 2 * j, 2)) + b_f[:, wide_at(j)]

    loop(2 * D // WIDE, final_mod)
    part = lambda s, i: modf[pl.ds(s, 1), i * D : (i + 1) * D]
    dw_h[...] = jnp.zeros(dw_h.shape, full_type)

    def head(at, s):
        hat, scale = norm_parts(x[at, :])
        gain = 1.0 + part(s, 1)
        normed = (hat * gain + part(s, 0)).astype(low_type)
        off = dot(normed, w_h[...]) + b_h[...] - target[at, :]
        weight = weight_t[pl.ds(s, 1), :]
        stats[1:2, :] += rows_sum(weight * off * off)
        grad = (2.0 * weight / (SEQ * PD * sample_total) * off).astype(low_type)
        bias_out[:, A_H : A_H + LANES] += rows_sum(grad.astype(full_type))
        dw_h[...] += dot_tn(normed, grad)
        back = dot_nt(grad, w_h[...])
        d_modf[pl.ds(s, 1), 0:D] += rows_sum(back)
        d_modf[pl.ds(s, 1), D : 2 * D] += rows_sum(back * hat)
        inner = back * gain
        mean_a = jnp.mean(inner, axis=-1, keepdims=True)
        mean_b = jnp.mean(inner * hat, axis=-1, keepdims=True)
        grad_x[at, :] += scale * (inner - mean_a - hat * mean_b)

    each_chunk(head)
    turned = modulator[...].astype(full_type).T.astype(low_type)
    cond[...] = jnp.zeros(cond.shape, full_type)

    def final_back(j):
        grad = d_modf[:, wide_at(j)].astype(low_type)
        bias_out[:, wide_at(j, A_F)] += rows_sum(grad.astype(full_type))
        put_block(dw_f, 0, 2 * j, dot(turned, grad))
        cond[...] += dot_nt(grad, block_of(w_f, 0, D // ROWS, 2 * j, 2))

    loop(2 * D // WIDE, final_back)
    last = pltpu.make_async_copy(dw_f, segment_ref(grads, plan, 13), out_sem.at[2])
    last.start()
    last.wait()
    drain(7, D // WIDE, PH // LANES)


def top_call(plan, sample_total, x, features, target, weight_t, modulator, biases, w_h, b_h, units):
    rows = x.shape[0]
    vm = pl.BlockSpec(memory_space=pltpu.VMEM)
    anywhere = pl.BlockSpec(memory_space=pltpu.HBM)
    dma = pltpu.SemaphoreType.DMA
    few = modulator.shape[0]
    f32 = lambda *shape: pltpu.VMEM(shape, full_type)
    bf16 = lambda *shape: pltpu.VMEM(shape, low_type)
    shape = lambda *dims: jax.ShapeDtypeStruct(dims, full_type)
    return pl.pallas_call(
        functools.partial(top_kernel, plan, rows, sample_total),
        out_shape=[
            shape(rows, D),
            shape(8, LANES),
            shape(few, D),
            shape(1, 2 * PH + ZD + 2 * D + LANES),
            shape(D, LANES),
            jax.ShapeDtypeStruct(units.shape, low_type),
        ],
        in_specs=[vm] * 11 + [anywhere],
        out_specs=[vm] * 5 + [anywhere],
        scratch_shapes=[segment_scratch(plan, s) for s in TOP]
        + [f32(rows, PH), bf16(rows, PH), f32(rows, PH), bf16(rows, PH), f32(rows, ZD), bf16(rows, D)]
        + [bf16(rows, PH), bf16(rows, PH), bf16(rows, ZD), f32(few, 2 * D), f32(few, 2 * D)]
        + [bf16(2, WIDE // ROWS, PH // LANES, ROWS, LANES), segment_scratch(plan, 13)]
        + [dma((4,)), dma((3,))],
        compiler_params=pltpu.CompilerParams(vmem_limit_bytes=60 * MB),
        name="projector_and_head",
    )(x, features, target, weight_t, modulator, *biases, w_h, b_h, units)


def busy_loop(count, body, events=()):
    size = max(1, -(-len(events) // count))

    def step(i):
        body(i)
        for first in range(0, len(events), size):

            @pl.when(i == first // size)
            def _():
                for event in events[first : first + size]:
                    event()

    loop(count, step)


def spread(events, weights):
    shares, done, total = [], 0, 0
    for weight in weights:
        total += weight
        upto = len(events) * total // sum(weights)
        shares.append(events[done:upto])
        done = upto
    return shares


def row_vector(units, rows):
    values = units.astype(full_type).reshape(-1, LANES)
    return jnp.concatenate([values[r : r + 1, :] for r in range(rows)], axis=1)


def pick(ref, here, *spots):
    return ref.at[tuple(here.zero + spot for spot in spots)]


class Place:
    def __init__(self, zs):
        self.zs = zs
        self.n = zs * 8
        self.me = lax.axis_index("fsdp")
        self.zero = self.me * 0
        self.z, self.y, self.x, self.c = place(self.me, zs)
        self.prev = lax.rem(self.me + self.n - 1, self.n)
        self.following = lax.rem(self.me + 1, self.n)
        self.xpeer = self.index(self.z, self.y, 1 - self.x, self.c)
        self.ypeer = self.index(self.z, 1 - self.y, self.x, self.c)
        self.cpeer = self.index(self.z, self.y, self.x, 1 - self.c)

    def index(self, z, y, x, c):
        return ((z * 2 + y) * 2 + x) * 2 + c

    def above(self, k):
        return self.index(lax.rem(self.z + k, self.zs), self.y, self.x, self.c)

    def below(self, k):
        return self.index(lax.rem(self.z + self.zs - k, self.zs), self.y, self.x, self.c)

    def slot(self, k, dy, dx, dc):
        z = lax.rem(self.z + self.zs - k, self.zs)
        flip = lambda value, change: 1 - value if change else value
        return self.index(z, flip(self.y, dy), flip(self.x, dx), flip(self.c, dc))

    def peers(self):
        return [self.prev, self.following, self.xpeer, self.ypeer, self.cpeer] + [self.above(k) for k in range(1, self.zs)]

    def greet(self):
        barrier = pltpu.get_barrier_semaphore()
        for peer in self.peers():
            pl.semaphore_signal(barrier, inc=1, device_id=(peer,), device_id_type=MESH)

    def met(self):
        pl.semaphore_wait(pltpu.get_barrier_semaphore(), len(self.peers()))


def remote(src, dst, send_sem, recv_sem, to):
    return pltpu.make_async_remote_copy(src, dst, send_sem, recv_sem, device_id=(to,), device_id_type=MESH)


def arrived(ref, sem):
    pltpu.make_async_copy(ref, ref, sem).wait()


class Gather:
    def __init__(self, here, buckets, sems):
        self.here = here
        self.buckets = buckets
        self.own_sem, self.send_sem, self.zr, self.xa, self.xb, self.yb, self.ya, self.cr = sems
        self.sent = []
        self.made = 0

    def guarded(self, b, k, run):
        plan, _, _, lo, hi = self.buckets[b]
        if lo == 0 and hi == self.here.zs:
            run()
            return
        source = lax.rem(self.here.z + self.here.zs - k, self.here.zs)
        pl.when((source >= lo) & (source < hi))(run)

    def sem(self, name, *spots):
        return lambda: pick(getattr(self, name), self.here, *spots)

    def send(self, b, k, src, dst, sem, to):
        number = self.made
        self.made += 1
        make = lambda: remote(src(), dst(), pick(self.send_sem, self.here, number), sem(), to())
        make().start()
        self.sent.append((b, k, make))

    def part(self, b, h, k, dy, dx, dc=0):
        plan, units = self.buckets[b][:2]
        return units.at[pl.ds(self.here.slot(k, dy, dx, dc) * plan.per + h * plan.half, plan.half)]

    def whole(self, b, k, dy, dx, dc=0):
        plan, units = self.buckets[b][:2]
        return units.at[pl.ds(self.here.slot(k, dy, dx, dc) * plan.per, plan.per)]

    def own_copy(self, b):
        return pltpu.make_async_copy(self.buckets[b][2], self.whole(b, 0, 0, 0), pick(self.own_sem, self.here, b))

    def start(self, b):
        here, slot = self.here, self.buckets[b][2]
        plan = self.buckets[b][0]

        def run():
            self.own_copy(b).start()
            mine = lambda h: lambda: slot.at[pl.ds(h * plan.half, plan.half)]
            to = lambda h: lambda: self.part(b, h, 0, 0, 0)
            for k in range(1, here.zs):
                for h in range(2):
                    self.send(b, 0, mine(h), to(h), self.sem("zr", b, h, k), lambda k=k: here.above(k))
            self.send(b, 0, mine(0), to(0), self.sem("xa", b, 0), lambda: here.xpeer)
            self.send(b, 0, mine(1), to(1), self.sem("yb", b, 0), lambda: here.ypeer)
            self.send(b, 0, mine(0), to(0), self.sem("ya", b, 0, 0), lambda: here.ypeer)
            self.send(b, 0, mine(1), to(1), self.sem("xb", b, 0, 0), lambda: here.xpeer)
            self.send(b, 0, lambda: slot, lambda: self.whole(b, 0, 0, 0), self.sem("cr", b, 0, 0, 0), lambda: here.cpeer)

        self.guarded(b, 0, run)

    def pass_on(self, b, k, h, dy, dx, sem, to):
        ref = lambda: self.part(b, h, k, dy, dx)
        self.send(b, k, ref, ref, sem, to)

    def share(self, b, k, dy, dx):
        ref = lambda: self.whole(b, k, dy, dx)
        self.send(b, k, ref, ref, self.sem("cr", b, k, dy, dx), lambda: self.here.cpeer)

    def events(self, b):
        here = self.here
        found = []

        def add(k, run):
            found.append(lambda: self.guarded(b, k, run))

        for k in range(1, here.zs):

            def from_z(k=k):
                arrived(self.part(b, 0, k, 0, 0), pick(self.zr, self.here, b, 0, k))
                self.pass_on(b, k, 0, 0, 0, self.sem("xa", b, k), lambda: here.xpeer)
                arrived(self.part(b, 1, k, 0, 0), pick(self.zr, self.here, b, 1, k))
                self.pass_on(b, k, 1, 0, 0, self.sem("yb", b, k), lambda: here.ypeer)
                self.pass_on(b, k, 0, 0, 0, self.sem("ya", b, k, 0), lambda: here.ypeer)
                self.pass_on(b, k, 1, 0, 0, self.sem("xb", b, k, 0), lambda: here.xpeer)
                self.share(b, k, 0, 0)

            add(k, from_z)
        for k in range(here.zs):

            def across(k=k):
                arrived(self.part(b, 0, k, 0, 1), pick(self.xa, self.here, b, k))
                self.pass_on(b, k, 0, 0, 1, self.sem("ya", b, k, 1), lambda: here.ypeer)
                arrived(self.part(b, 1, k, 1, 0), pick(self.yb, self.here, b, k))
                self.pass_on(b, k, 1, 1, 0, self.sem("xb", b, k, 1), lambda: here.xpeer)

            add(k, across)
        for k in range(here.zs):

            def beside(k=k):
                arrived(self.part(b, 1, k, 0, 1), pick(self.xb, self.here, b, k, 0))
                self.share(b, k, 0, 1)
                arrived(self.part(b, 0, k, 1, 0), pick(self.ya, self.here, b, k, 0))
                self.share(b, k, 1, 0)

            add(k, beside)
        for k in range(here.zs):

            def corner(k=k):
                arrived(self.part(b, 1, k, 1, 1), pick(self.xb, self.here, b, k, 1))
                arrived(self.part(b, 0, k, 1, 1), pick(self.ya, self.here, b, k, 1))
                self.share(b, k, 1, 1)

            add(k, corner)
        return found

    def complete(self, b):
        self.guarded(b, 0, lambda: self.own_copy(b).wait())
        for k in range(self.here.zs):

            def run(k=k):
                for dy in range(2):
                    for dx in range(2):
                        arrived(self.whole(b, k, dy, dx, 1), pick(self.cr, self.here, b, k, dy, dx))

            self.guarded(b, k, run)

    def drain(self):
        for b, k, make in self.sent:
            self.guarded(b, k, lambda: make().wait_send())


FRONT = 7


def cut_units(here, plan, ext, slot):
    top = here.me * plan.share // LANES - plan.before
    for base, chunks, count, first_unit, _, _ in plan.segments:
        lo = jnp.clip(plan.per * here.me - first_unit, 0, count)
        hi = jnp.clip(plan.per * here.me + plan.per - first_unit, 0, count)

        def unit(u, carry):
            block = u // chunks
            row = base + block * (ROWS * chunks) + (u - block * chunks) - top
            if chunks == 1:
                value = ext[pl.ds(row, ROWS), :]
            else:
                value = ext[pl.ds(row, ROWS, stride=chunks), :]
            slot[first_unit + u - plan.per * here.me] = value.astype(low_type)
            return carry

        lax.fori_loop(lo, hi, unit, 0)


def forward_kernel(plans, zs, rows, *refs):
    np_ = len(plans)
    feed = iter(refs)
    take = lambda count: tuple(next(feed) for _ in range(count))
    one = lambda: next(feed)
    raw_hbm = take(np_)
    noisy, positions, basis, chosen = take(4)
    units = take(np_)
    stream = take(LAYERS + 1)
    mods = take(LAYERS)
    sums = take(LAYERS)
    modulator, condition, time_pre = take(3)
    saved_out = [take(len(SAVED)) for _ in range(LAYERS)]
    from_prev, from_next, slots = take(np_), take(np_), take(np_)
    raw_sem, halo_send, halo_recv, front_sem, load_sem, save_sem = take(6)
    gather_sems = take(8)
    here = Place(zs)
    here.greet()
    root = plans[0]
    front_units = root.segments[FRONT][3]
    front_planes = min(zs, -(-front_units // (8 * root.per)))
    buckets = [(root, units[0], slots[0], 0, front_planes)]
    buckets += [(plans[1 + i], units[1 + i], slots[1 + i], 0, zs) for i in range(LAYERS)]
    buckets += [(root, units[0], slots[0], front_planes, zs)]
    gather = Gather(here, buckets, gather_sems)
    last = len(buckets) - 1
    starts = [[0]] + [[1 + i] for i in range(LAYERS)]
    starts[-1].append(last)

    def prepare(*scratch):
        raw, ext, tail = (scratch[i * np_ : (i + 1) * np_] for i in range(3))
        loads = [pltpu.make_async_copy(raw_hbm[i], raw[i].at[pl.ds(8, p.raw)], raw_sem.at[i]) for i, p in enumerate(plans)]
        for copy in loads:
            copy.start()
        lane = lax.broadcasted_iota(jnp.int32, (64, LANES), 1)
        halos = []
        for i, p in enumerate(plans):
            shift = lax.rem(here.me * p.share, LANES)
            delta = (here.me + 1) * p.share // LANES - here.me * p.share // LANES
            raw[i][pl.ds(0, 8), :] = jnp.zeros((8, LANES), full_type)
            ext[i][pl.ds(0, p.before), :] = jnp.zeros((p.before, LANES), full_type)
            ext[i][pl.ds(p.before + p.raw, p.after), :] = jnp.zeros((p.after, LANES), full_type)
            loads[i].wait()

            def align(j):
                row = pl.multiple_of(j * 64, 64)
                level = pltpu.roll(raw[i][pl.ds(row + 8, 64), :], shift, 1)
                above = pltpu.roll(raw[i][pl.ds(row + 7, 64), :], shift, 1)
                ext[i][pl.ds(row + p.before, 64), :] = jnp.where(lane >= shift, level, above)

            loop(p.raw // 64, align)
            tail[i][...] = ext[i][pl.ds(delta, p.before + 8), :]
            if i == 0:
                here.met()
            halos.append(remote(ext[i].at[pl.ds(p.before, p.after)], from_next[i], halo_send.at[2 * i], halo_recv.at[2 * i], here.prev))
            halos.append(remote(tail[i], from_prev[i], halo_send.at[2 * i + 1], halo_recv.at[2 * i + 1], here.following))
            halos[-2].start()
            halos[-1].start()
        for i, p in enumerate(plans):
            delta = (here.me + 1) * p.share // LANES - here.me * p.share // LANES
            halos[2 * i].wait()
            halos[2 * i + 1].wait()
            ext[i][pl.ds(0, p.before + 8), :] += from_prev[i][...]
            ext[i][pl.ds(p.before + delta, p.after), :] += from_next[i][...]
            cut_units(here, p, ext[i], slots[i])
            for b in starts[i]:
                gather.start(b)

    f32 = lambda *dims: pltpu.VMEM(dims, full_type)
    pl.run_scoped(
        prepare,
        *[f32(p.raw + 8, LANES) for p in plans],
        *[f32(p.ext, LANES) for p in plans],
        *[f32(p.before + 8, LANES) for p in plans],
    )
    for event in gather.events(0):
        event()
    gather.complete(0)

    def compute(front, w_qkv, w_o, w_1, w_2, w_mod, raw_bias, *held):
        copy = pltpu.make_async_copy(units[0].at[pl.ds(0, front_units)], front, front_sem)
        copy.start()
        copy.wait()
        matrix = lambda number, blocks: front_matrix(front, root, number, blocks)
        vector = lambda number: row_vector(front[pl.ds(root.segments[number][3], 1)], D // LANES)
        events = spread(gather.events(1), (1, 1, 1, 1))
        stream[0][...] = dot(noisy[...], matrix(0, 1)) + vector(1) + positions[...]
        for event in events[0]:
            event()
        pre = dot(basis[...], matrix(2, FREQ // ROWS)) + vector(3)
        time_pre[...] = pre
        act = silu_parts(pre)[0].astype(low_type)
        total = dot(act, matrix(4, D // ROWS)) + vector(5)
        few = basis.shape[0]
        first = root.segments[6][3]
        picked = dot(chosen[...], front[pl.ds(first, root.segments[6][2])].reshape(-1, LANES))
        total = total + jnp.concatenate([picked[i * few : (i + 1) * few, :] for i in range(D // LANES)], axis=1)
        condition[...] = total
        modulator[...] = silu_parts(total)[0].astype(low_type)
        for group in events[1:]:
            for event in group:
                event()
        for ordinal in range(LAYERS):
            gather.complete(1 + ordinal)
            queue = gather.events(2 + ordinal)
            layer_forward_body(
                plans[1 + ordinal], rows, stream[ordinal], modulator, mods[ordinal], units[1 + ordinal],
                stream[ordinal + 1], sums[ordinal], saved_out[ordinal], held, (w_qkv, w_o, w_1, w_2, w_mod), raw_bias,
                load_sem, save_sem, spread(queue, (18, 9, 12, 3, 12)),
            )
        gather.complete(last)

    plan = plans[1]
    bias_units = plan.units - plan.segments[5][3]
    pl.run_scoped(
        compute,
        pltpu.VMEM((front_units, ROWS, LANES), low_type),
        *[segment_scratch(plan, i) for i in range(5)],
        pltpu.VMEM((bias_units, ROWS, LANES), low_type),
        *[pltpu.VMEM((rows, width), kind) for _, width, kind in SAVED],
    )
    gather.drain()


def front_matrix(front, plan, number, blocks):
    _, chunks, _, first, _, _ = plan.segments[number]
    columns = [jnp.concatenate([front[first + b * chunks + c] for b in range(blocks)], axis=0) for c in range(chunks)]
    return jnp.concatenate(columns, axis=1)


def layer_forward_body(plan, rows, x, modulator, mod, units, out, sums, saved_out, held, weights, raw_bias, load_sem, save_sem, events):
    ns = len(SAVED)
    h1, qkv, heads, attn, middle, h2, pre, mlp = held
    w_qkv, w_o, w_1, w_2, w_mod = weights
    bias_first = plan.segments[5][3]
    loads = [pltpu.make_async_copy(segment_ref(units, plan, i), weights[i], load_sem.at[i]) for i in range(5)]
    bias_load = pltpu.make_async_copy(units.at[pl.ds(bias_first, raw_bias.shape[0])], raw_bias, load_sem.at[5])
    bias_load.start()
    for i in (4, 0, 1, 2, 3):
        loads[i].start()
    saves = [pltpu.make_async_copy(held[i], saved_out[i], save_sem.at[i]) for i in range(ns)]
    part = lambda s, i: mod[pl.ds(s, 1), i * D : (i + 1) * D]
    per = SEQ // CHUNK
    wide_at = lambda j: pl.ds(pl.multiple_of(j * WIDE, WIDE), WIDE)
    chunk_at = lambda i: pl.ds(pl.multiple_of(i * CHUNK, CHUNK), CHUNK)
    bias_load.wait()

    def bias(number):
        _, _, count, first, shape, _ = plan.segments[number]
        return row_vector(raw_bias[pl.ds(first - bias_first, count)], shape[0] // LANES)

    loads[4].wait()
    mod[...] = jnp.broadcast_to(bias(10), mod.shape)
    value_of = modulator[...]

    def modulate(j):
        mod[:, wide_at(j)] += dot(value_of, block_of(w_mod, 0, D // ROWS, 2 * j, 2))

    busy_loop(6 * D // WIDE, modulate, events[0])

    def norm_a(i):
        s = i // per
        hat, _ = norm_parts(x[chunk_at(i), :])
        h1[chunk_at(i), :] = (hat * (1.0 + part(s, 1)) + part(s, 0)).astype(low_type)

    loop(rows // CHUNK, norm_a)
    saves[0].start()
    loads[0].wait()
    first_bias, value_bias = bias(5), bias(6)

    def project_with(base, given, events):
        pieces = D // WIDE

        def project(j):
            value = dot(h1[...], block_of(w_qkv, 0, D // ROWS, 2 * (base + j), 2))
            cols = wide_at(base + j)
            if given is not None:
                value = value + mlp[0:1, wide_at(j)]
            qkv[:, cols] = value.astype(low_type)

        if given is not None:
            mlp[0:1, :] = given
        busy_loop(pieces, project, events)

    third = spread(events[1], (1, 1, 1))
    project_with(0, first_bias, third[0])
    project_with(D // WIDE, None, third[1])
    project_with(2 * D // WIDE, value_bias, third[2])
    saves[1].start()
    first = head_masks()

    def attend(i):
        s, j = i // (HEADS // 2), i % (HEADS // 2)
        at = pl.ds(pl.multiple_of(s * SEQ, SEQ), SEQ)
        cut = lambda o: qkv[at, pl.ds(pl.multiple_of(o * D + j * LANES, LANES), LANES)]
        q, k, v = cut(0), cut(1), cut(2)
        q = q * jnp.asarray(HD ** (-0.5), low_type)
        zero = jnp.zeros_like(q)
        halves = []
        for mask in (first, ~first):
            probs = softmax_f32(dot_nt(jnp.where(mask, q, zero), k)).astype(low_type)
            halves.append(dot(probs, v))
        heads[at, pl.ds(pl.multiple_of(j * LANES, LANES), LANES)] = jnp.where(first, halves[0], halves[1]).astype(low_type)

    busy_loop(attention_pairs(rows), attend, events[2])
    saves[2].start()
    loads[1].wait()
    attn[...] = jnp.broadcast_to(bias(7), (rows, D))

    def project_out(j):
        attn[:, wide_at(j)] += dot(heads[...], block_of(w_o, 0, D // ROWS, 2 * j, 2))

    busy_loop(D // WIDE, project_out, events[3])
    saves[3].start()
    zero_sum = jnp.zeros((1, D), full_type)

    def norm_m(i, total):
        s = i // per
        value = attn[chunk_at(i), :]
        mid = x[chunk_at(i), :] + part(s, 2) * value
        middle[chunk_at(i), :] = mid
        hat, _ = norm_parts(mid)
        h2[chunk_at(i), :] = (hat * (1.0 + part(s, 4)) + part(s, 3)).astype(low_type)
        return total + rows_sum(value * value)

    attn_sum = lax.fori_loop(0, rows // CHUNK, norm_m, zero_sum)
    saves[4].start()
    saves[5].start()
    loads[2].wait()
    loads[3].wait()
    pre[0:1, :] = bias(8)
    mlp[...] = jnp.broadcast_to(bias(9), (rows, D))

    def feed(j):
        value = dot(h2[...], block_of(w_1, 0, D // ROWS, 2 * j, 2)) + pre[0:1, wide_at(j)]
        pre[:, wide_at(j)] = value
        act = gelu_parts(value)[0].astype(low_type)
        mlp[...] += dot(act, block_of(w_2, j * (WIDE // ROWS), WIDE // ROWS, 0, D // LANES))

    busy_loop(FF // WIDE, feed, events[4])
    saves[6].start()
    saves[7].start()

    def finish(i, carry):
        value = mlp[chunk_at(i), :]
        result = middle[chunk_at(i), :] + part(i // per, 5) * value
        out[chunk_at(i), :] = result
        return (carry[0] + rows_sum(result * result), carry[1] + rows_sum(value * value))

    out_sum, mlp_sum = lax.fori_loop(0, rows // CHUNK, finish, (zero_sum, zero_sum))
    sums[...] = jnp.zeros(sums.shape, full_type)
    sums[0:1, :] = out_sum
    sums[1:2, :] = attn_sum
    sums[2:3, :] = mlp_sum
    for copy in saves:
        copy.wait()


def forward_call(plans, raws, noisy, positions, basis, chosen):
    n = plans[0].devices
    zs = n // 8
    rows, few = noisy.shape[0], basis.shape[0]
    dma = pltpu.SemaphoreType.DMA
    np_, nb = len(plans), len(plans) + 1
    vm = pl.BlockSpec(memory_space=pltpu.VMEM)
    hbm = pl.BlockSpec(memory_space=pltpu.HBM)
    shape = jax.ShapeDtypeStruct
    saved_shapes = [shape((rows, width), kind) for _, width, kind in SAVED]
    out_shape = [shape((n * p.per, ROWS, LANES), low_type) for p in plans]
    out_shape += [shape((rows, D), full_type)] * (LAYERS + 1)
    out_shape += [shape((few, 6 * D), full_type)] * LAYERS + [shape((8, D), full_type)] * LAYERS
    out_shape += [shape((few, D), low_type), shape((few, D), full_type), shape((few, D), full_type)]
    out_shape += saved_shapes * LAYERS
    scratch = [pltpu.VMEM((p.before + 8, LANES), full_type) for p in plans]
    scratch += [pltpu.VMEM((p.after, LANES), full_type) for p in plans]
    scratch += [pltpu.VMEM((p.per, ROWS, LANES), low_type) for p in plans]
    scratch += [dma((np_,)), dma((2 * np_,)), dma((2 * np_,)), dma, dma((6,)), dma((len(SAVED),))]
    scratch += [dma((nb,)), dma((nb * (2 * (zs - 1) + 10 * zs),)), dma((nb, 2, zs)), dma((nb, zs)), dma((nb, zs, 2))]
    scratch += [dma((nb, zs)), dma((nb, zs, 2)), dma((nb, zs, 2, 2))]
    results = pl.pallas_call(
        functools.partial(forward_kernel, plans, zs, rows),
        out_shape=out_shape,
        in_specs=[hbm] * np_ + [vm] * 4,
        out_specs=[hbm] * np_ + [vm] * (LAYERS + 1 + 2 * LAYERS + 3) + [hbm] * (len(SAVED) * LAYERS),
        scratch_shapes=scratch,
        compiler_params=pltpu.CompilerParams(collective_id=0, has_side_effects=True, vmem_limit_bytes=62 * MB),
        name="gather_and_forward",
    )(*raws, noisy, positions, basis, chosen)
    feed = iter(results)
    take = lambda count: [next(feed) for _ in range(count)]
    units, stream, mods, sums = take(np_), take(LAYERS + 1), take(LAYERS), take(LAYERS)
    modulator, condition, time_pre = take(3)
    return units, stream, mods, sums, modulator, condition, time_pre, [take(len(SAVED)) for _ in range(LAYERS)]


def model_step(layer_lists, pieces, latents, noise, times, labels, dropped, features, devices):
    sample_total = latents.shape[0] * devices
    residual, modulator, embed_saved = embed_forward(
        pieces, latents, noise, times, labels, dropped
    )
    loss_total = jnp.zeros((), full_type)
    inputs, kept, square_sums = [], [], []
    for ordinal in range(LAYERS):
        inputs.append(residual)
        residual, saved, sums = layer_forward(layer_lists[ordinal], residual, modulator)
        kept.append(saved)
        square_sums.append(sums)
        if ordinal + 1 == DEPTH_Z:
            part, proj_saved = projector_forward(pieces, residual, features)
            loss_total = loss_total + part
    target = noise - latents
    weight_t = 1.0 + 2.0 * times
    part, head_saved = head_forward(pieces, residual, modulator, target, weight_t)
    loss_total = loss_total + part
    grad_residual, grad_cond, head_grads = head_backward(
        pieces, head_saved, residual, modulator, weight_t, sample_total
    )
    layer_grads = [None] * LAYERS
    for ordinal in reversed(range(LAYERS)):
        if ordinal + 1 == DEPTH_Z:
            grad_proj, proj_grads = projector_backward(
                pieces, proj_saved, features, residual.shape[1], sample_total
            )
            grad_residual = grad_residual + grad_proj
        grad_residual, cond_part, layer_grads[ordinal] = layer_backward(
            layer_lists[ordinal], kept[ordinal], inputs[ordinal], modulator, grad_residual
        )
        grad_cond = grad_cond + cond_part
    embed_grads = embed_backward(pieces, embed_saved, grad_residual, grad_cond)
    return (loss_total, jnp.stack(square_sums), layer_grads, embed_grads + proj_grads + head_grads)


def adam_update(weight, grad, first, second, clip_factor):
    clipped = grad * clip_factor
    first_new = beta_one * first + (1.0 - beta_one) * clipped
    second_new = beta_two * second + (1.0 - beta_two) * clipped * clipped
    first_hat = first_new / (1.0 - beta_one**STEP)
    second_hat = second_new / (1.0 - beta_two**STEP)
    weight_new = weight - learn_rate * (
        first_hat / (jnp.sqrt(second_hat) + adam_eps) + decay_rate * weight
    )
    return (weight_new, first_new, second_new)


def vector_of(units, plan, number):
    _, _, count, first, shape, _ = plan.segments[number]
    flat = units[first : first + count].reshape(-1)[: math.prod(shape)]
    return flat.reshape(shape)


def matrix_of(units, plan, number):
    _, chunks, count, first, shape, _ = plan.segments[number]
    part = units[first : first + count].reshape(shape[0] // ROWS, chunks, ROWS, LANES)
    return part.transpose(0, 2, 1, 3).reshape(shape)


def units_of(grad, plan, number):
    _, chunks, count, _, shape, matrix = plan.segments[number]
    low = grad.astype(low_type)
    if matrix:
        low = low.reshape(shape[0] // ROWS, ROWS, chunks, LANES).transpose(0, 2, 1, 3)
        return low.reshape(count, ROWS, LANES)
    flat = jnp.pad(low.reshape(-1), ((0, count * UNIT - low.size),))
    return flat.reshape(count, ROWS, LANES)


def put_units(grads, plan, first_number, values):
    parts = [units_of(value, plan, first_number + i) for i, value in enumerate(values)]
    joined = jnp.concatenate(parts) if len(parts) > 1 else parts[0]
    return lax.dynamic_update_slice(grads, joined, (plan.segments[first_number][3], 0, 0))


def as_row(vector):
    return vector.astype(full_type).reshape(1, -1)


def by_kernels(plan, root_plan, layer_flat, root_flat, data, devices):
    latents, noise, times, labels, dropped, features = data
    samples = latents.shape[0]
    sample_total = samples * devices
    rows = samples * SEQ
    few = up(samples, ROWS)
    wide = D // LANES
    plans = (root_plan,) + (plan,) * LAYERS
    raws = [to_rows(root_flat, root_plan)]
    raws += [to_rows(layer_flat[ordinal], plan) for ordinal in range(LAYERS)]
    mixing = times[:, None, None]
    noisy_bf = ((1.0 - mixing) * latents + mixing * noise).astype(low_type)
    positions = jnp.tile(position_table(), (samples, 1))
    basis_bf = time_features(times).astype(low_type)
    classes = jnp.where(dropped == 1, CLS - 1, labels)
    extra = lambda value: jnp.pad(value, ((0, few - samples),) + ((0, 0),) * (value.ndim - 1))
    wanted = jnp.pad(classes, (0, few - samples), constant_values=-1)
    wanted = jnp.where(wanted < 0, -wide, wanted * wide)[None, :] + jnp.arange(wide)[:, None]
    wanted = jnp.where(wanted < 0, -1, wanted).reshape(-1, 1)
    table_rows = root_plan.segments[6][2] * ROWS
    chosen = (wanted == jnp.arange(table_rows, dtype=jnp.int32)[None, :]).astype(low_type)
    units, stream, mods, sums, modulator_rows, condition, time_pre, kept = forward_call(
        plans, raws, noisy_bf.reshape(rows, PD), positions, extra(basis_bf), chosen
    )
    root_units, *layer_units = units
    residual = stream[-1]
    target = jnp.pad((noise - latents).reshape(rows, PD), ((0, 0), (0, LANES - PD)))
    weight_t = jnp.broadcast_to(jnp.pad(1.0 + 2.0 * times, (0, 8 - samples))[:, None], (8, LANES))
    w_h = jnp.pad(vector_of(root_units, root_plan, 15), ((0, 0), (0, LANES - PD)))
    b_h = jnp.pad(as_row(vector_of(root_units, root_plan, 16)), ((0, 0), (0, LANES - PD)))
    biases = [as_row(vector_of(root_units, root_plan, i)) for i in (8, 10, 12, 14)]
    grad, losses, grad_cond, bias_grads, grad_w_h, root_grads = top_call(
        root_plan, sample_total, residual, features.reshape(rows, ZD), target, weight_t, modulator_rows, biases, w_h, b_h, root_units
    )
    loss_part = -proj_coeff / SEQ * losses[0, 0] + jnp.sum(losses[1]) / (SEQ * PD)
    grad_cond = grad_cond[:samples]
    layer_grads = [None] * LAYERS
    for ordinal in reversed(range(LAYERS)):
        units = layer_units[ordinal]
        grad, grad_mod, bias_grad, grads = layer_backward_call(
            plan, stream[ordinal], grad, mods[ordinal], kept[ordinal], units
        )
        low_mod = jnp.pad(grad_mod.astype(low_type), ((0, few - grad_mod.shape[0]), (0, 0)))
        grads, cond_part = mods_back_call(plan, modulator_rows, low_mod, units, grads)
        grad_cond = grad_cond + cond_part[:samples]
        cuts = jnp.split(bias_grad[0], (D, 2 * D, 3 * D, 3 * D + FF))
        grad_b_mod = jnp.sum(low_mod.astype(full_type), axis=0)
        layer_grads[ordinal] = put_units(grads, plan, 5, cuts + [grad_b_mod])
    pieces = {4: matrix_of(root_units, root_plan, 4), 2: None, 0: None}
    onehot = (classes[:, None] == jnp.arange(CLS, dtype=jnp.int32)[None, :]).astype(low_type)
    time_pre = time_pre[:samples]
    embed_saved = (noisy_bf, basis_bf, time_pre, jax.nn.silu(time_pre).astype(low_type), onehot, condition[:samples])
    embed_grads = embed_backward(pieces, embed_saved, grad.reshape(samples, SEQ, D), grad_cond)
    cuts = jnp.split(bias_grads[0], (PH, 2 * PH, 2 * PH + ZD, 2 * PH + ZD + 2 * D))
    for number, value in zip((8, 10, 12), cuts):
        root_grads = put_units(root_grads, root_plan, number, [value])
    root_grads = put_units(root_grads, root_plan, 14, [cuts[3], grad_w_h[:, :PD], cuts[4][:PD]])
    root_grads = put_units(root_grads, root_plan, 0, embed_grads)
    square_sums = jnp.stack([jnp.sum(total[:3], axis=1) for total in sums])
    numbers = jnp.concatenate([loss_part[None], square_sums.reshape(-1)])
    stats = jnp.pad(numbers, (0, 8 * LANES - numbers.shape[0])).reshape(8, LANES)
    rows_out, stats = reduce_units(plans, [root_grads] + layer_grads, stats)
    numbers = stats[0].reshape(-1)
    shard_root = rows_out[0].reshape(-1)[: root_plan.share]
    shard_layers = jnp.stack([r.reshape(-1)[: plan.share] for r in rows_out[1:]])
    stream_sums = numbers[1 : 1 + 3 * LAYERS].reshape(LAYERS, 3)
    return (shard_layers, shard_root, numbers[0], stream_sums, jnp.sum(stats[1]))


def by_collectives(layer_flat, root_flat, data, devices):
    whole = lambda part: lax.all_gather(part.astype(low_type), "fsdp", axis=0, tiled=True)
    layer_lists = [unflatten(whole(layer_flat[i]), layer_layout()) for i in range(LAYERS)]
    pieces = unflatten(whole(root_flat), root_layout())
    loss_part, square_sums, layer_grads, root_grads = model_step(
        layer_lists, pieces, *data, devices
    )

    def owned(grad_list, share):
        joined = jnp.concatenate([piece.reshape(-1) for piece in grad_list])
        joined = jnp.pad(joined, (0, share * devices - joined.shape[0]))
        return lax.psum_scatter(joined, "fsdp", scatter_dimension=0, tiled=True)

    shard_layers = jnp.stack([owned(grads, layer_flat.shape[1]) for grads in layer_grads])
    shard_root = owned(root_grads, root_flat.shape[0])
    local = jnp.sum(shard_layers * shard_layers) + jnp.sum(shard_root * shard_root)
    loss_sum, sums, square_total = lax.psum((loss_part, square_sums, local), "fsdp")
    return (shard_layers, shard_root, loss_sum, sums, square_total)


def shards(
    latents,
    noise,
    times,
    labels,
    dropped,
    features,
    layer_flat,
    layer_mean,
    layer_square,
    root_flat,
    root_mean,
    root_square,
):
    devices = lax.axis_size("fsdp")
    data = (latents, noise, times, labels, dropped, features)
    plan = Plan(layer_layout(), layer_flat.shape[1] * devices, devices)
    root_plan = Plan(root_layout(), root_flat.shape[0] * devices, devices)
    if devices % 8 == 0 and plan.fits and root_plan.fits:
        reduced = by_kernels(plan, root_plan, layer_flat, root_flat, data, devices)
    else:
        reduced = by_collectives(layer_flat, root_flat, data, devices)
    shard_layers, shard_root, loss_sum, stream_sums, square_total = reduced
    sample_total = latents.shape[0] * devices
    grad_norm = jnp.sqrt(square_total)
    clip_factor = clip_limit / jnp.maximum(grad_norm, clip_limit)
    activation_rms = jnp.sqrt(stream_sums / (sample_total * SEQ * D))
    new_layer, new_layer_mean, new_layer_square = adam_update(
        layer_flat, shard_layers, layer_mean, layer_square, clip_factor
    )
    new_root, new_root_mean, new_root_square = adam_update(
        root_flat, shard_root, root_mean, root_square, clip_factor
    )
    return (
        loss_sum,
        grad_norm,
        activation_rms,
        new_layer,
        new_layer_mean,
        new_layer_square,
        new_root,
        new_root_mean,
        new_root_square,
    )


def solution(mesh):
    in_specs = (
        P("fsdp", None, None),
        P("fsdp", None, None),
        P("fsdp"),
        P("fsdp"),
        P("fsdp"),
        P("fsdp", None, None),
        P(None, "fsdp"),
        P(None, "fsdp"),
        P(None, "fsdp"),
        P("fsdp"),
        P("fsdp"),
        P("fsdp"),
    )
    out_specs = (
        P(),
        P(),
        P(),
        P(None, "fsdp"),
        P(None, "fsdp"),
        P(None, "fsdp"),
        P("fsdp"),
        P("fsdp"),
        P("fsdp"),
    )
    return jax.shard_map(shards, mesh=mesh, in_specs=in_specs, out_specs=out_specs, check_vma=False)
```

```python
import functools
import math

import jax
import jax.numpy as jnp
from jax import lax
from jax.experimental import pallas as pl
from jax.experimental.pallas import tpu as pltpu
from jax.sharding import PartitionSpec as P

D = 768
HD = 64
FF = 3072
PD = 16
CLS = 1001
PH = 2048
ZD = 768
FREQ = 256
GRID = 16
LAYERS = 2
DEPTH_Z = 2
STEP = 10
SEQ = 256


norm_eps = 1e-06
clip_limit = 0.002
learn_rate = 0.08
beta_one = 0.5
beta_two = 0.5
adam_eps = 1e-08
decay_rate = 0.01
proj_coeff = 0.5
low_type = jnp.bfloat16
full_type = jnp.float32


LANES = 128
ROWS = 16
UNIT = LANES * ROWS
MESH = pl.DeviceIdType.MESH

def up(value, step):
    return -(-value // step) * step

class Plan:
    def __init__(self, layout, length, devices):
        self.length = length
        self.devices = devices
        self.share = length // devices
        self.segments = []
        offset = units = 0
        for shape in layout:
            amount = math.prod(shape)
            matrix = len(shape) == 2 and shape[0] % ROWS == 0 and shape[1] % LANES == 0
            chunks = shape[1] // LANES if matrix else 1
            count = up(amount, UNIT) // UNIT
            self.segments.append((offset // LANES, chunks, count, units, shape, matrix))
            offset += amount
            units += count
        self.units = units
        self.per = up(up(units, devices) // devices, 4)
        rows_of = []
        for base, chunks, count, _, _, _ in self.segments:
            for u in range(count):
                b, c = divmod(u, chunks)
                first = base + b * ROWS * chunks + c
                rows_of.append((first, first + (ROWS - 1) * chunks))
        before = after = 0
        for d in range(devices):
            start, stop = d * self.share // LANES, (d + 1) * self.share // LANES
            for lo, hi in rows_of[self.per * d : self.per * d + self.per]:
                before, after = max(before, start - lo), max(after, hi + 1 - stop)
        self.before, self.after = up(before, 8), up(after, 8)
        units_before = units_after = 0
        for u, (lo, hi) in enumerate(rows_of):
            first = lo * LANES // self.share
            last = min(((hi + 1) * LANES - 1) // self.share, devices - 1)
            for d in range(first, last + 1):
                units_before = max(units_before, self.per * d - u)
                units_after = max(units_after, u + 1 - self.per * d - self.per)
        self.units_before, self.units_after = units_before, units_after
        self.half = self.per // 2
        self.raw = up(up(self.share, LANES) // LANES + 9, 64)
        self.ext = self.before + self.raw + self.after
        margin = tail = 0
        for d in range(devices):
            start = d * self.share // LANES
            lo = max(self.per * d - units_before, 0)
            for first, last in rows_of[lo : self.per * d + self.per + units_after]:
                margin, tail = max(margin, start - first), max(tail, last + 1 - start)
        self.margin = up(margin, 8)
        self.spread = up(max(tail, self.raw + 8), 8) + self.margin
        least = self.share // LANES
        self.fits = max(self.before, self.after) < least and max(units_before, units_after) < self.per

def place(index, zs):
    return index // 8, index // 4 % 2, index // 2 % 2, index % 2

def gather_kernel(plans, zs, *refs):
    nb = len(plans)
    raw_hbm = refs[:nb]
    outs = refs[nb : 2 * nb]
    raw, ext, tail, from_prev, from_next, slots = (refs[2 * nb + i * nb : 3 * nb + i * nb] for i in range(6))
    rest = refs[8 * nb :]
    load_sem, halo_send, halo_recv, own_sem, send_sem, zr, xa, xb, yb, ya, cr = rest
    n = zs * 8
    me = lax.axis_index("fsdp")
    z, y, x, c = place(me, zs)
    index = lambda zz, yy, xx, cc: ((zz * 2 + yy) * 2 + xx) * 2 + cc
    prev, following = lax.rem(me + n - 1, n), lax.rem(me + 1, n)
    xpeer, ypeer, cpeer = index(z, y, 1 - x, c), index(z, 1 - y, x, c), index(z, y, x, 1 - c)
    zpeer = [index(lax.rem(z + k, zs), y, x, c) for k in range(zs)]
    loads = []
    for b in range(nb):
        p = plans[b]
        loads.append(pltpu.make_async_copy(raw_hbm[b], raw[b].at[pl.ds(8, p.raw)], load_sem.at[b]))
        loads[b].start()
    barrier = pltpu.get_barrier_semaphore()
    peers = [prev, following, xpeer, ypeer, cpeer] + zpeer[1:]
    for peer in peers:
        pl.semaphore_signal(barrier, inc=1, device_id=(peer,), device_id_type=MESH)
    halos = []
    lane = lax.broadcasted_iota(jnp.int32, (64, LANES), 1)
    for b in range(nb):
        p = plans[b]
        shift = lax.rem(me * p.share, LANES)
        delta = (me + 1) * p.share // LANES - me * p.share // LANES
        raw[b][pl.ds(0, 8), :] = jnp.zeros((8, LANES), full_type)
        ext[b][pl.ds(0, p.before), :] = jnp.zeros((p.before, LANES), full_type)
        ext[b][pl.ds(p.before + p.raw, p.after), :] = jnp.zeros((p.after, LANES), full_type)
        loads[b].wait()

        def align(i, carry):
            row = pl.multiple_of(i * 64, 64)
            here = pltpu.roll(raw[b][pl.ds(row + 8, 64), :], shift, 1)
            above = pltpu.roll(raw[b][pl.ds(row + 7, 64), :], shift, 1)
            ext[b][pl.ds(row + p.before, 64), :] = jnp.where(lane >= shift, here, above)
            return carry

        lax.fori_loop(0, p.raw // 64, align, 0)
        tail[b][...] = ext[b][pl.ds(delta, p.before + 8), :]
        if b == 0:
            pl.semaphore_wait(barrier, len(peers))
        for s, (src, dst, to) in enumerate(((ext[b].at[pl.ds(p.before, p.after)], from_next[b], prev), (tail[b], from_prev[b], following))):
            copy = pltpu.make_async_remote_copy(src, dst, halo_send.at[2 * b + s], halo_recv.at[2 * b + s], device_id=(to,), device_id_type=MESH)
            copy.start()
            halos.append(copy)
    sends = []

    def send(src, dst, sem, to):
        copy = pltpu.make_async_remote_copy(src, dst, send_sem.at[len(sends)], sem, device_id=(to,), device_id_type=MESH)
        copy.start()
        sends.append(copy)

    def span(b, h):
        p = plans[b]
        return (0, p.half) if h == 0 else (p.half, p.per - p.half)

    def slot(k, dy, dx, dc):
        return index(lax.rem(z + zs - k, zs), 1 - y if dy else y, 1 - x if dx else x, 1 - c if dc else c)

    def part(b, h, k, dy, dx, dc=0):
        first, count = span(b, h)
        return outs[b].at[pl.ds(slot(k, dy, dx, dc) * plans[b].per + first, count)]

    def whole(b, k, dy, dx, dc=0):
        return outs[b].at[pl.ds(slot(k, dy, dx, dc) * plans[b].per, plans[b].per)]

    def arrived(ref, sem):
        pltpu.make_async_copy(ref, ref, sem).wait()

    owns = []
    for b in range(nb):
        p = plans[b]
        delta = (me + 1) * p.share // LANES - me * p.share // LANES
        for copy in halos[2 * b : 2 * b + 2]:
            copy.wait()
        ext[b][pl.ds(0, p.before + 8), :] += from_prev[b][...]
        ext[b][pl.ds(p.before + delta, p.after), :] += from_next[b][...]
        top = me * p.share // LANES - p.before
        for base, chunks, count, first_unit, _, _ in p.segments:
            lo = jnp.clip(p.per * me - first_unit, 0, count)
            hi = jnp.clip(p.per * me + p.per - first_unit, 0, count)

            def unit(u, carry):
                block = u // chunks
                row = base + block * (ROWS * chunks) + (u - block * chunks) - top
                if chunks == 1:
                    value = ext[b][pl.ds(row, ROWS), :]
                else:
                    value = ext[b][pl.ds(row, ROWS, stride=chunks), :]
                slots[b][first_unit + u - p.per * me] = value.astype(low_type)
                return carry

            lax.fori_loop(lo, hi, unit, 0)
        own = pltpu.make_async_copy(slots[b], whole(b, 0, 0, 0), own_sem.at[b])
        own.start()
        owns.append(own)
        mine = lambda h: slots[b].at[pl.ds(*span(b, h))]
        for k in range(1, zs):
            for h in range(2):
                send(mine(h), part(b, h, 0, 0, 0), zr.at[b, h, k], zpeer[k])
        send(mine(0), part(b, 0, 0, 0, 0), xa.at[b, 0], xpeer)
        send(mine(1), part(b, 1, 0, 0, 0), yb.at[b, 0], ypeer)
        send(mine(0), part(b, 0, 0, 0, 0), ya.at[b, 0, 0], ypeer)
        send(mine(1), part(b, 1, 0, 0, 0), xb.at[b, 0, 0], xpeer)
        send(slots[b], whole(b, 0, 0, 0), cr.at[b, 0, 0, 0], cpeer)
    for b in range(nb):
        for k in range(1, zs):
            arrived(part(b, 0, k, 0, 0), zr.at[b, 0, k])
            send(part(b, 0, k, 0, 0), part(b, 0, k, 0, 0), xa.at[b, k], xpeer)
            arrived(part(b, 1, k, 0, 0), zr.at[b, 1, k])
            send(part(b, 1, k, 0, 0), part(b, 1, k, 0, 0), yb.at[b, k], ypeer)
            send(part(b, 0, k, 0, 0), part(b, 0, k, 0, 0), ya.at[b, k, 0], ypeer)
            send(part(b, 1, k, 0, 0), part(b, 1, k, 0, 0), xb.at[b, k, 0], xpeer)
            send(whole(b, k, 0, 0), whole(b, k, 0, 0), cr.at[b, k, 0, 0], cpeer)
        for k in range(zs):
            arrived(part(b, 0, k, 0, 1), xa.at[b, k])
            send(part(b, 0, k, 0, 1), part(b, 0, k, 0, 1), ya.at[b, k, 1], ypeer)
            arrived(part(b, 1, k, 1, 0), yb.at[b, k])
            send(part(b, 1, k, 1, 0), part(b, 1, k, 1, 0), xb.at[b, k, 1], xpeer)
        for k in range(zs):
            arrived(part(b, 1, k, 0, 1), xb.at[b, k, 0])
            send(whole(b, k, 0, 1), whole(b, k, 0, 1), cr.at[b, k, 0, 1], cpeer)
            arrived(part(b, 0, k, 1, 0), ya.at[b, k, 0])
            send(whole(b, k, 1, 0), whole(b, k, 1, 0), cr.at[b, k, 1, 0], cpeer)
        for k in range(zs):
            arrived(part(b, 1, k, 1, 1), xb.at[b, k, 1])
            arrived(part(b, 0, k, 1, 1), ya.at[b, k, 1])
            send(whole(b, k, 1, 1), whole(b, k, 1, 1), cr.at[b, k, 1, 1], cpeer)
    for b in range(nb):
        owns[b].wait()
        for k in range(zs):
            for dy in range(2):
                for dx in range(2):
                    arrived(whole(b, k, dy, dx, 1), cr.at[b, k, dy, dx])
    for copy in sends:
        copy.wait_send()

def gather_units(plans, raws):
    n = plans[0].devices
    zs = n // 8
    nb = len(plans)
    per_bucket = 2 * (zs - 1) + 10 * zs
    dma = pltpu.SemaphoreType.DMA
    scratch = [pltpu.VMEM((p.raw + 8, LANES), full_type) for p in plans]
    scratch += [pltpu.VMEM((p.ext, LANES), full_type) for p in plans]
    scratch += [pltpu.VMEM((p.before + 8, LANES), full_type) for p in plans]
    scratch += [pltpu.VMEM((p.before + 8, LANES), full_type) for p in plans]
    scratch += [pltpu.VMEM((p.after, LANES), full_type) for p in plans]
    scratch += [pltpu.VMEM((p.per, ROWS, LANES), low_type) for p in plans]
    scratch += [dma((nb,)), dma((2 * nb,)), dma((2 * nb,)), dma((nb,)), dma((nb * per_bucket,))]
    scratch += [dma((nb, 2, zs)), dma((nb, zs)), dma((nb, zs, 2)), dma((nb, zs)), dma((nb, zs, 2)), dma((nb, zs, 2, 2))]
    return pl.pallas_call(
        functools.partial(gather_kernel, plans, zs),
        out_shape=[jax.ShapeDtypeStruct((n * p.per, ROWS, LANES), low_type) for p in plans],
        in_specs=[pl.BlockSpec(memory_space=pltpu.HBM)] * nb,
        out_specs=[pl.BlockSpec(memory_space=pltpu.HBM)] * nb,
        scratch_shapes=scratch,
        compiler_params=pltpu.CompilerParams(collective_id=0, has_side_effects=True, vmem_limit_bytes=48 * 1024 * 1024),
        name="gather_units",
    )(*raws)

AHEAD = 4


def reduce_kernel(plans, zs, *refs):
    nb = len(plans)
    take = lambda count: tuple(next(feed) for _ in range(count))
    feed = iter(refs)
    grads, (stats_in,) = take(nb), take(1)
    outs, (stats_out,), first = take(nb), take(1), take(nb)
    kept_a, kept_b, two_a, two_b, three_a, three_b, four = (take(nb) for _ in range(7))
    local, other = take(1)[0], take(1)[0]
    units_f, rows_f, flat_f = take(1)[0], take(1)[0], take(1)[0]
    from_prev, from_next = take(nb), take(nb)
    total, total_in = take(1)[0], take(1)[0]
    s1, r1, s2a, r2a, s2b, r2b, s3a, r3a, s3b, r3b, s4, r4, load_sem, halo_s, halo_r, out_sem, ss, sr = take(18)
    n = zs * 8
    me = lax.axis_index("fsdp")
    z, y, x, c = place(me, zs)
    index = lambda zz, yy, xx, cc: ((zz * 2 + yy) * 2 + xx) * 2 + cc
    prev, following = lax.rem(me + n - 1, n), lax.rem(me + 1, n)
    xpeer, ypeer, cpeer = index(z, y, 1 - x, c), index(z, 1 - y, x, c), index(z, y, x, 1 - c)
    below = lambda k: index(lax.rem(z + zs - k, zs), y, x, c)
    above = lambda k: index(lax.rem(z + k, zs), y, x, c)
    barrier = pltpu.get_barrier_semaphore()
    peers = [prev, following, xpeer, ypeer, cpeer] + [above(k) for k in range(1, zs)]
    for peer in peers:
        pl.semaphore_signal(barrier, inc=1, device_id=(peer,), device_id_type=MESH)
    pl.semaphore_wait(barrier, len(peers))

    def remote(src, dst, send_sem, recv_sem, to):
        return pltpu.make_async_remote_copy(src, dst, send_sem, recv_sem, device_id=(to,), device_id_type=MESH)

    def arrived(ref, sem):
        pltpu.make_async_copy(ref, ref, sem).wait()

    def slot(b, k, dy, dx, dc):
        where = index(lax.rem(z + zs - k, zs), 1 - y if dy else y, 1 - x if dx else x, 1 - c if dc else c)
        return grads[b].at[pl.ds(where * plans[b].per, plans[b].per)]

    order = ((1, 1), (1, 0), (0, 1), (0, 0))

    def sibling(b, k, dy, dx):
        return remote(slot(b, k, dy, dx, 1), first[b].at[k, dy, dx], s1.at[b, k, dy, dx], r1.at[b, k, dy, dx], cpeer)

    def add(p, dst, at, one, one_at, two, two_at):
        step = p.half // 2

        def body(i, carry):
            span = lambda ref, off: ref[pl.ds(off + i * step, step)].astype(full_type)
            dst[pl.ds(at + i * step, step)] = (span(one, one_at) + span(two, two_at)).astype(low_type)
            return carry

        lax.fori_loop(0, 2, body, 0)

    ring = local.shape[0]
    planes = list(range(1, zs)) + [0]
    used = []

    def send_of(b, h, k, dy, dx, src):
        if h == 0:
            return remote(src, two_a[b].at[k, dx], s2a.at[b, k, dx], r2a.at[b, k, dx], ypeer)
        return remote(src, two_b[b].at[k, dy], s2b.at[b, k, dy], r2b.at[b, k, dy], xpeer)

    steps = [(b, dy, dx, k) for b in range(nb) for k in planes for dy, dx in order]

    def loads(number):
        b, dy, dx, k = steps[number]
        at = number % ring
        p = plans[b]
        one = pltpu.make_async_copy(slot(b, k, dy, dx, 0), local.at[at, pl.ds(0, p.per)], load_sem.at[at, 0])
        two = pltpu.make_async_copy(first[b].at[k, dy, dx], other.at[number % 2, pl.ds(0, p.per)], load_sem.at[at, 1])
        return one, two

    pending = {}
    steps_args = lambda number: (steps[number][0], steps[number][3], steps[number][1], steps[number][2])

    def prepare(number):
        b, dy, dx, k = steps[number]
        for copy in pending.pop(number % ring, ()):
            copy.wait_send()
        one, two = loads(number)
        one.start()
        arrived(first[b].at[k, dy, dx], r1.at[b, k, dy, dx])
        two.start()

    def phase_one(number):
        b, dy, dx, k = steps[number]
        p = plans[b]
        at = number % ring
        if number == 0:
            for ahead in range(AHEAD):
                sibling(*steps_args(ahead)).start()
            prepare(0)
        if number + AHEAD < len(steps):
            sibling(*steps_args(number + AHEAD)).start()
        if number + 1 < len(steps):
            prepare(number + 1)
        for copy in loads(number):
            copy.wait()
        mine, theirs = local.at[at], other.at[number % 2]
        going = []
        if dy:
            add(p, mine, 0, mine, 0, theirs, 0)
            going.append(send_of(b, 0, k, dy, dx, local.at[at, pl.ds(0, p.half)]))
        else:
            add(p, kept_a[b].at[k, dx], 0, mine, 0, theirs, 0)
        if dx:
            add(p, mine, p.half, mine, p.half, theirs, p.half)
            going.append(send_of(b, 1, k, dy, dx, local.at[at, pl.ds(p.half, p.half)]))
        else:
            add(p, kept_b[b].at[k, dy], 0, mine, p.half, theirs, p.half)
        for copy in going:
            copy.start()
        pending[at] = going

    def three(b, h, k):
        if h == 0:
            return remote(two_a[b].at[k, 1], three_a[b].at[k], s3a.at[b, k], r3a.at[b, k], xpeer)
        return remote(two_b[b].at[k, 1], three_b[b].at[k], s3b.at[b, k], r3b.at[b, k], ypeer)

    def last(b, h, k):
        src = (three_a if h == 0 else three_b)[b].at[k]
        return remote(src, four[b].at[h, k - 1], s4.at[b, h, k - 1], r4.at[b, h, k - 1], below(k))

    def phase_two(b, k):
        p = plans[b]
        for far in (1, 0):
            for h, kept, two, sem in ((0, kept_a, two_a, r2a), (1, kept_b, two_b, r2b)):
                arrived(two[b].at[k, far], sem.at[b, k, far])
                if far:
                    add(p, two[b].at[k, 1], 0, two[b].at[k, 1], 0, kept[b].at[k, 1], 0)
                    three(b, h, k).start()
                else:
                    add(p, kept[b].at[k, 0], 0, two[b].at[k, 0], 0, kept[b].at[k, 0], 0)

    def phase_three(b, k):
        p = plans[b]
        for h, kept, got, sem in ((0, kept_a, three_a, r3a), (1, kept_b, three_b, r3b)):
            arrived(got[b].at[k], sem.at[b, k])
            if k:
                add(p, got[b].at[k], 0, got[b].at[k], 0, kept[b].at[k, 0], 0)
                last(b, h, k).start()

    def halo(b):
        p = plans[b]
        base = p.units_before
        held = units_f.at[b % 2]
        forward = remote(held.at[pl.ds(p.per, base)], from_prev[b], halo_s.at[b, 0], halo_r.at[b, 0], following)
        backward = remote(held.at[pl.ds(base, p.units_after)], from_next[b], halo_s.at[b, 1], halo_r.at[b, 1], prev)
        return forward, backward

    def collect(b):
        p = plans[b]
        base = p.units_before
        for h, kept, got in ((0, kept_a, three_a), (1, kept_b, three_b)):
            for k in range(1, zs):
                arrived(four[b].at[h, k - 1], r4.at[b, h, k - 1])
            step = p.half // 2

            def body(i, carry):
                part = pl.ds(i * step, step)
                value = kept[b][0, 0, part].astype(full_type) + got[b][0, part].astype(full_type)
                for k in range(1, zs):
                    value = value + four[b][h, k - 1, part].astype(full_type)
                units_f[b % 2, pl.ds(base + h * p.half + i * step, step)] = value
                return carry

            lax.fori_loop(0, 2, body, 0)
        for copy in halo(b):
            copy.start()

    def finish(b):
        p = plans[b]
        base = p.units_before
        for copy in halo(b):
            copy.wait()
        held = b % 2
        units_f[held, pl.ds(0, base)] = from_prev[b][...]
        units_f[held, pl.ds(base + p.per, p.units_after)] = from_next[b][...]
        top = me * p.share // LANES - p.margin
        for origin, chunks, count, first_unit, _, _ in p.segments:
            lo = jnp.clip(p.per * me - base - first_unit, 0, count)
            hi = jnp.clip(p.per * me + p.per + p.units_after - first_unit, 0, count)

            def unit(u, carry):
                block = u // chunks
                row = origin + block * (ROWS * chunks) + (u - block * chunks) - top
                value = units_f[held, first_unit + u - p.per * me + base]
                if chunks == 1:
                    rows_f[pl.ds(row, ROWS), :] = value
                else:
                    rows_f[pl.ds(row, ROWS, stride=chunks), :] = value
                return carry

            lax.fori_loop(lo, hi, unit, 0)
        shift = lax.rem(me * p.share, LANES)
        turn = lax.rem(LANES - shift, LANES)
        lane = lax.broadcasted_iota(jnp.int32, (64, LANES), 1)
        spot = lax.broadcasted_iota(jnp.int32, (64, LANES), 0) * LANES + lane
        if b:
            pltpu.make_async_copy(flat_f.at[pl.ds(0, plans[b - 1].raw)], outs[b - 1], out_sem.at[b - 1]).wait()

        def unalign(i, squares):
            row = pl.multiple_of(i * 64, 64)
            here = pltpu.roll(rows_f[pl.ds(row + p.margin, 64), :], turn, 1)
            below_row = pltpu.roll(rows_f[pl.ds(row + p.margin + 1, 64), :], turn, 1)
            value = jnp.where(lane < LANES - shift, here, below_row)
            value = jnp.where(spot + row * LANES < p.share, value, 0.0)
            flat_f[pl.ds(row, 64), :] = value
            return squares + jnp.sum((value * value).reshape(8, 8, LANES), axis=0)

        squares = lax.fori_loop(0, p.raw // 64, unalign, jnp.zeros((8, LANES), full_type))
        pltpu.make_async_copy(flat_f.at[pl.ds(0, p.raw)], outs[b], out_sem.at[b]).start()
        return squares

    squares = jnp.zeros((8, LANES), full_type)
    groups = [(b, k) for b in range(nb) for k in planes]
    for g in range(len(groups) + 2):
        if g < len(groups):
            for number in range(4 * g, 4 * g + 4):
                phase_one(number)
        if 0 <= g - 1 < len(groups):
            phase_two(*groups[g - 1])
        if 0 <= g - 2 < len(groups):
            phase_three(*groups[g - 2])
        b = (g - 3) // zs - 1
        if (g - 3) % zs == 0 and 0 <= b < nb - 1:
            collect(b)
        b = (g - 4) // zs - 1
        if (g - 4) % zs == 0 and 0 <= b < nb - 1:
            squares = squares + finish(b)
    collect(nb - 1)
    squares = squares + finish(nb - 1)
    pltpu.make_async_copy(flat_f.at[pl.ds(0, plans[nb - 1].raw)], outs[nb - 1], out_sem.at[nb - 1]).wait()
    total[0] = stats_in[...]
    total[1] = squares
    step = 0
    for to in ((cpeer,), (xpeer,), (ypeer,), tuple(above(k) for k in range(1, zs))):
        copies = []
        for peer in to:
            copies.append(remote(total, total_in.at[step], ss.at[step], sr.at[step], peer))
            copies[-1].start()
            step += 1
        for copy in copies:
            copy.wait()
        value = total[...]
        for i in range(len(to)):
            value = value + total_in[step - 1 - i]
        total[...] = value
    stats_out[...] = total[...]
    for group in pending.values():
        for copy in group:
            copy.wait_send()
    for b in range(nb):
        for dy, dx in order:
            for k in range(zs):
                sibling(b, k, dy, dx).wait_send()
        for h in range(2):
            for k in range(zs):
                three(b, h, k).wait_send()
                if k:
                    last(b, h, k).wait_send()

def reduce_units(plans, grads, stats):
    n = plans[0].devices
    zs = n // 8
    nb = len(plans)
    dma = pltpu.SemaphoreType.DMA
    most = max(p.per for p in plans)
    tile = (ROWS, LANES)
    half = lambda p, *lead: pltpu.VMEM(lead + (p.half,) + tile, low_type)
    scratch = [half(p, zs, 2) for p in plans] + [half(p, zs, 2) for p in plans]
    scratch += [half(p, zs, 2) for p in plans] + [half(p, zs, 2) for p in plans]
    scratch += [half(p, zs) for p in plans] + [half(p, zs) for p in plans]
    scratch += [half(p, 2, zs - 1) for p in plans]
    ring = 8
    scratch += [pltpu.VMEM((ring, most) + tile, low_type), pltpu.VMEM((2, most) + tile, low_type)]
    scratch += [pltpu.VMEM((2, max(p.units_before + p.per + p.units_after for p in plans)) + tile, full_type)]
    scratch += [pltpu.VMEM((max(p.spread for p in plans), LANES), full_type)]
    scratch += [pltpu.VMEM((max(p.raw for p in plans), LANES), full_type)]
    scratch += [pltpu.VMEM((p.units_before,) + tile, full_type) for p in plans]
    scratch += [pltpu.VMEM((p.units_after,) + tile, full_type) for p in plans]
    hops = 2 + zs
    scratch += [pltpu.VMEM((2, 8, LANES), full_type), pltpu.VMEM((hops, 2, 8, LANES), full_type)]
    scratch += [dma((nb, zs, 2, 2))] * 2 + [dma((nb, zs, 2))] * 4 + [dma((nb, zs))] * 4
    scratch += [dma((nb, 2, zs - 1))] * 2 + [dma((ring, 2)), dma((nb, 2)), dma((nb, 2)), dma((nb,)), dma((hops,)), dma((hops,))]
    anywhere = pl.BlockSpec(memory_space=pltpu.HBM)
    inside = pl.BlockSpec(memory_space=pltpu.VMEM)
    out_shape = [jax.ShapeDtypeStruct((p.raw, LANES), full_type) for p in plans]
    out_shape += [jax.ShapeDtypeStruct((2, 8, LANES), full_type)]
    out_shape += [jax.ShapeDtypeStruct((zs, 2, 2, p.per) + tile, low_type) for p in plans]
    results = pl.pallas_call(
        functools.partial(reduce_kernel, plans, zs),
        out_shape=out_shape,
        in_specs=[anywhere] * nb + [inside],
        out_specs=[anywhere] * nb + [inside] + [anywhere] * nb,
        scratch_shapes=scratch,
        compiler_params=pltpu.CompilerParams(collective_id=1, has_side_effects=True, vmem_limit_bytes=62 * 1024 * 1024),
        name="reduce_units",
    )(*grads, stats)
    return results[:nb], results[nb]

def to_rows(flat, plan):
    padded = jnp.pad(flat, ((0, plan.raw * LANES - flat.shape[0]),))
    return padded.reshape(plan.raw, LANES)


def layer_layout():
    return [
        (D, 3 * D),
        (D, D),
        (D, FF),
        (FF, D),
        (D, 6 * D),
        (D,),
        (D,),
        (D,),
        (FF,),
        (D,),
        (6 * D,),
    ]


def root_layout():
    return [
        (PD, D),
        (D,),
        (FREQ, D),
        (D,),
        (D, D),
        (D,),
        (CLS, D),
        (D, PH),
        (PH,),
        (PH, PH),
        (PH,),
        (PH, ZD),
        (ZD,),
        (D, 2 * D),
        (2 * D,),
        (D, PD),
        (PD,),
    ]


def unflatten(vector, layout):
    pieces = []
    offset = 0
    for dimensions in layout:
        amount = math.prod(dimensions)
        pieces.append(vector[offset : offset + amount].reshape(dimensions))
        offset += amount
    return pieces


def flatten_grads(grad_list, length):
    joined = jnp.concatenate([piece.reshape(-1) for piece in grad_list])
    return jnp.concatenate([joined, jnp.zeros((length - joined.shape[0],), full_type)])


def position_table():
    quarter = D // 4
    frequency = 1.0 / 10000.0 ** (jnp.arange(quarter, dtype=jnp.float32) / quarter)
    coords = jnp.arange(GRID, dtype=jnp.float32)
    angles = coords[:, None] * frequency[None, :]
    one_axis = jnp.concatenate([jnp.sin(angles), jnp.cos(angles)], axis=1)
    row_part = jnp.repeat(one_axis, GRID, axis=0)
    col_part = jnp.tile(one_axis, (GRID, 1))
    return jnp.concatenate([row_part, col_part], axis=1)


def time_features(times_in):
    half_freq = FREQ // 2
    frequency = jnp.exp(-math.log(10000.0) * jnp.arange(half_freq, dtype=jnp.float32) / half_freq)
    angles = times_in[:, None] * frequency[None, :]
    return jnp.concatenate([jnp.cos(angles), jnp.sin(angles)], axis=1)


def modulated_norm(values, offsets, scales):
    centred = values - jnp.mean(values, axis=-1, keepdims=True)
    spread = jnp.mean(centred * centred, axis=-1, keepdims=True)
    return centred * lax.rsqrt(spread + norm_eps) * (1.0 + scales) + offsets


def softmax_rows(scores):
    row_max = jnp.max(scores, axis=-1, keepdims=True)
    exponent = jnp.exp(scores - row_max)
    return exponent / jnp.sum(exponent, axis=-1, keepdims=True)


def gelu_tanh(values):
    return jax.nn.gelu(values, approximate=True)


def cosine_rows(predicted, target):
    target_full = target.astype(full_type)
    inner_sum = jnp.sum(predicted * target_full, axis=-1)
    return (
        inner_sum
        * lax.rsqrt(jnp.sum(predicted * predicted, axis=-1) + norm_eps)
        * lax.rsqrt(jnp.sum(target_full * target_full, axis=-1) + norm_eps)
    )


def silu_back(values, grad_in):
    _, pullback = jax.vjp(jax.nn.silu, values)
    return pullback(grad_in)[0]


def linear_fwd(inputs, weight):
    leading = inputs.shape[:-1]
    product = jnp.dot(
        inputs.reshape(-1, inputs.shape[-1]), weight, preferred_element_type=full_type
    )
    return product.reshape(leading + (weight.shape[1],))


def linear_back(inputs, weight, grad_out, with_input=True):
    rows_in = inputs.reshape(-1, inputs.shape[-1])
    rows_out = grad_out.reshape(-1, grad_out.shape[-1])
    grad_weight = lax.dot_general(
        rows_in, rows_out, (((0,), (0,)), ((), ())), preferred_element_type=full_type
    )
    grad_bias = jnp.sum(rows_out.astype(full_type), axis=0)
    grad_in = None
    if with_input:
        grad_in = lax.dot_general(
            rows_out, weight, (((1,), (1,)), ((), ())), preferred_element_type=full_type
        ).reshape(inputs.shape)
    return (grad_in, grad_weight, grad_bias)


def layer_forward(weights, residual, modulator):
    (
        w_attn_in,
        w_attn_out,
        w_mlp_in,
        w_mlp_out,
        w_modulate,
        b_query,
        b_value,
        b_attn_out,
        b_mlp_in,
        b_mlp_out,
        b_modulate,
    ) = weights
    samples_mb, seq_len = (residual.shape[0], residual.shape[1])
    head_count = D // HD
    modulation = jnp.split((linear_fwd(modulator, w_modulate) + b_modulate)[:, None, :], 6, axis=-1)
    normed_a = modulated_norm(residual, modulation[0], modulation[1]).astype(low_type)
    bias_qkv = jnp.concatenate([b_query, jnp.zeros_like(b_query), b_value])
    qkv_low = (linear_fwd(normed_a, w_attn_in) + bias_qkv).astype(low_type)
    qkv_low = qkv_low.reshape(samples_mb, seq_len, 3, head_count, HD)
    query_bf, key_bf, value_bf = (qkv_low[:, :, 0], qkv_low[:, :, 1], qkv_low[:, :, 2])
    scores = jnp.einsum(
        "bqhd,bkhd->bhqk", query_bf, key_bf, preferred_element_type=full_type
    ) * HD ** (-0.5)
    attn_probs = softmax_rows(scores)
    probs_bf = attn_probs.astype(low_type)
    heads_bf = jnp.einsum("bhqk,bkhd->bqhd", probs_bf, value_bf, preferred_element_type=full_type)
    heads_bf = heads_bf.astype(low_type).reshape(samples_mb, seq_len, D)
    attn_out = linear_fwd(heads_bf, w_attn_out) + b_attn_out
    middle = residual + modulation[2] * attn_out
    normed_m = modulated_norm(middle, modulation[3], modulation[4]).astype(low_type)
    mlp_pre = linear_fwd(normed_m, w_mlp_in) + b_mlp_in
    act_bf = gelu_tanh(mlp_pre).astype(low_type)
    mlp_out = linear_fwd(act_bf, w_mlp_out) + b_mlp_out
    residual_out = middle + modulation[5] * mlp_out
    square_sums = jnp.stack(
        [
            jnp.sum(residual_out * residual_out),
            jnp.sum(attn_out * attn_out),
            jnp.sum(mlp_out * mlp_out),
        ]
    )
    saved = (
        modulation,
        normed_a,
        query_bf,
        key_bf,
        value_bf,
        attn_probs,
        probs_bf,
        heads_bf,
        attn_out,
        middle,
        normed_m,
        mlp_pre,
        act_bf,
        mlp_out,
    )
    return (residual_out, saved, square_sums)


def layer_backward(weights, saved, residual, modulator, grad_out):
    w_attn_in, w_attn_out, w_mlp_in, w_mlp_out, w_modulate = weights[:5]
    (
        modulation,
        normed_a,
        query_bf,
        key_bf,
        value_bf,
        attn_probs,
        probs_bf,
        heads_bf,
        attn_out,
        middle,
        normed_m,
        mlp_pre,
        act_bf,
        mlp_out,
    ) = saved
    samples_mb, seq_len = (residual.shape[0], residual.shape[1])
    grad_mlp = (modulation[5] * grad_out).astype(low_type)
    grad_act, grad_w_mlp_out, grad_b_mlp_out = linear_back(act_bf, w_mlp_out, grad_mlp)
    _, gelu_pull = jax.vjp(gelu_tanh, mlp_pre)
    grad_pre = gelu_pull(grad_act)[0].astype(low_type)
    grad_normed_m, grad_w_mlp_in, grad_b_mlp_in = linear_back(normed_m, w_mlp_in, grad_pre)
    _, norm_pull_m = jax.vjp(modulated_norm, middle, modulation[3], modulation[4])
    grad_from_m, grad_shift_m, grad_scale_m = norm_pull_m(grad_normed_m)
    grad_middle = grad_out + grad_from_m
    grad_attn = (modulation[2] * grad_middle).astype(low_type)
    grad_heads, grad_w_attn_out, grad_b_attn_out = linear_back(heads_bf, w_attn_out, grad_attn)
    grad_heads_bf = grad_heads.astype(low_type).reshape(samples_mb, seq_len, D // HD, HD)
    grad_probs = jnp.einsum(
        "bqhd,bkhd->bhqk", grad_heads_bf, value_bf, preferred_element_type=full_type
    )
    grad_value = jnp.einsum(
        "bhqk,bqhd->bkhd", probs_bf, grad_heads_bf, preferred_element_type=full_type
    )
    grad_scores = attn_probs * (
        grad_probs - jnp.sum(attn_probs * grad_probs, axis=-1, keepdims=True)
    )
    grad_scores = grad_scores.astype(low_type)
    grad_query = jnp.einsum(
        "bhqk,bkhd->bqhd", grad_scores, key_bf, preferred_element_type=full_type
    ) * HD ** (-0.5)
    grad_key = jnp.einsum(
        "bhqk,bqhd->bkhd", grad_scores, query_bf, preferred_element_type=full_type
    ) * HD ** (-0.5)
    grad_qkv = jnp.stack([grad_query, grad_key, grad_value], axis=2).reshape(
        samples_mb, seq_len, 3 * D
    )
    grad_normed_a, grad_w_attn_in, grad_b_qkv = linear_back(
        normed_a, w_attn_in, grad_qkv.astype(low_type)
    )
    _, norm_pull_a = jax.vjp(modulated_norm, residual, modulation[0], modulation[1])
    grad_from_a, grad_shift_a, grad_scale_a = norm_pull_a(grad_normed_a)
    grad_gate_a = jnp.sum(attn_out * grad_middle, axis=1, keepdims=True)
    grad_gate_m = jnp.sum(mlp_out * grad_out, axis=1, keepdims=True)
    grad_mod = jnp.concatenate(
        [grad_shift_a, grad_scale_a, grad_gate_a, grad_shift_m, grad_scale_m, grad_gate_m], axis=-1
    )[:, 0, :].astype(low_type)
    grad_cond, grad_w_mod, grad_b_mod = linear_back(modulator, w_modulate, grad_mod)
    grad_list = [
        grad_w_attn_in,
        grad_w_attn_out,
        grad_w_mlp_in,
        grad_w_mlp_out,
        grad_w_mod,
        grad_b_qkv[:D],
        grad_b_qkv[2 * D :],
        grad_b_attn_out,
        grad_b_mlp_in,
        grad_b_mlp_out,
        grad_b_mod,
    ]
    return (grad_middle + grad_from_a, grad_cond, grad_list)


def embed_forward(pieces, latent_part, noise_part, times_part, labels_part, dropped_part):
    mixing = times_part[:, None, None]
    noisy_bf = ((1.0 - mixing) * latent_part + mixing * noise_part).astype(low_type)
    tokens = linear_fwd(noisy_bf, pieces[0]) + pieces[1] + position_table()
    basis_bf = time_features(times_part).astype(low_type)
    time_pre = linear_fwd(basis_bf, pieces[2]) + pieces[3]
    time_act = jax.nn.silu(time_pre).astype(low_type)
    time_emb = linear_fwd(time_act, pieces[4]) + pieces[5]
    classes = jnp.where(dropped_part == 1, CLS - 1, labels_part)
    onehot = (classes[:, None] == jnp.arange(CLS, dtype=jnp.int32)[None, :]).astype(low_type)
    condition = time_emb + jnp.dot(onehot, pieces[6], preferred_element_type=full_type)
    saved = (noisy_bf, basis_bf, time_pre, time_act, onehot, condition)
    return (tokens, jax.nn.silu(condition).astype(low_type), saved)


def embed_backward(pieces, saved, grad_tokens, grad_modulator):
    noisy_bf, basis_bf, time_pre, time_act, onehot, condition = saved
    grad_cond = silu_back(condition, grad_modulator)
    grad_table = lax.dot_general(
        onehot.astype(full_type),
        grad_cond,
        (((0,), (0,)), ((), ())),
        precision=lax.Precision.HIGHEST,
    )
    grad_time_act, grad_w_time_out, grad_b_time_out = linear_back(
        time_act, pieces[4], grad_cond.astype(low_type)
    )
    grad_time_pre = silu_back(time_pre, grad_time_act).astype(low_type)
    _, grad_w_time_in, grad_b_time_in = linear_back(basis_bf, pieces[2], grad_time_pre, False)
    _, grad_w_patch, grad_b_patch = linear_back(
        noisy_bf, pieces[0], grad_tokens.astype(low_type), False
    )
    return [
        grad_w_patch,
        grad_b_patch,
        grad_w_time_in,
        grad_b_time_in,
        grad_w_time_out,
        grad_b_time_out,
        grad_table,
    ]


def projector_forward(pieces, residual, features_part):
    residual_bf = residual.astype(low_type)
    pre_a = linear_fwd(residual_bf, pieces[7]) + pieces[8]
    act_a = jax.nn.silu(pre_a).astype(low_type)
    pre_b = linear_fwd(act_a, pieces[9]) + pieces[10]
    act_b = jax.nn.silu(pre_b).astype(low_type)
    predicted = linear_fwd(act_b, pieces[11]) + pieces[12]
    loss_part = -proj_coeff * jnp.sum(cosine_rows(predicted, features_part)) / residual.shape[1]
    return (loss_part, (residual_bf, pre_a, act_a, pre_b, act_b, predicted))


def projector_backward(pieces, saved, features_part, seq_len, sample_total):
    residual_bf, pre_a, act_a, pre_b, act_b, predicted = saved
    _, cosine_pull = jax.vjp(
        lambda predicted_in: cosine_rows(predicted_in, features_part), predicted
    )
    seed = jnp.full(predicted.shape[:2], -proj_coeff / (seq_len * sample_total), full_type)
    grad_pred = cosine_pull(seed)[0].astype(low_type)
    grad_act_b, grad_w_c, grad_b_c = linear_back(act_b, pieces[11], grad_pred)
    grad_pre_b = silu_back(pre_b, grad_act_b).astype(low_type)
    grad_act_a, grad_w_b, grad_b_b = linear_back(act_a, pieces[9], grad_pre_b)
    grad_pre_a = silu_back(pre_a, grad_act_a).astype(low_type)
    grad_residual, grad_w_a, grad_b_a = linear_back(residual_bf, pieces[7], grad_pre_a)
    return (grad_residual, [grad_w_a, grad_b_a, grad_w_b, grad_b_b, grad_w_c, grad_b_c])


def head_forward(pieces, residual, modulator, target, weight_t):
    modulation = (linear_fwd(modulator, pieces[13]) + pieces[14])[:, None, :]
    shift_f, scale_f = jnp.split(modulation, 2, axis=-1)
    normed = modulated_norm(residual, shift_f, scale_f).astype(low_type)
    deviation = linear_fwd(normed, pieces[15]) + pieces[16] - target
    loss_part = jnp.sum(weight_t * jnp.mean(deviation * deviation, axis=(1, 2)))
    return (loss_part, (shift_f, scale_f, normed, deviation))


def head_backward(pieces, saved, residual, modulator, weight_t, sample_total):
    shift_f, scale_f, normed, deviation = saved
    scaled = (
        2.0 * weight_t[:, None, None] / (deviation.shape[1] * deviation.shape[2] * sample_total)
    )
    grad_output = (scaled * deviation).astype(low_type)
    grad_normed, grad_w_head, grad_b_head = linear_back(normed, pieces[15], grad_output)
    _, pullback = jax.vjp(modulated_norm, residual, shift_f, scale_f)
    grad_residual, grad_shift, grad_scale = pullback(grad_normed)
    grad_mod = jnp.concatenate([grad_shift, grad_scale], axis=-1)[:, 0, :].astype(low_type)
    grad_cond, grad_w_mod, grad_b_mod = linear_back(modulator, pieces[13], grad_mod)
    return (grad_residual, grad_cond, [grad_w_mod, grad_b_mod, grad_w_head, grad_b_head])


WIDE = 2 * LANES
HEADS = D // HD
CHUNK = 64
MB = 1024 * 1024


def dot(one, two):
    return jnp.dot(one, two, preferred_element_type=full_type)


def dot_nt(one, two):
    return lax.dot_general(one, two, (((1,), (1,)), ((), ())), preferred_element_type=full_type)


def dot_tn(one, two):
    return lax.dot_general(one, two, (((0,), (0,)), ((), ())), preferred_element_type=full_type)


def block_of(w, block, blocks, chunk, chunks):
    pieces = [w[pl.ds(block, blocks), chunk + i].reshape(blocks * ROWS, LANES) for i in range(chunks)]
    return jnp.concatenate(pieces, axis=1) if chunks > 1 else pieces[0]


def put_block(out, block, chunk, value):
    blocks = value.shape[0] // ROWS
    for i in range(value.shape[1] // LANES):
        piece = value[:, i * LANES : (i + 1) * LANES].astype(low_type)
        out[pl.ds(block, blocks), chunk + i] = piece.reshape(blocks, ROWS, LANES)


def loop(count, body):
    lax.fori_loop(0, count, lambda i, carry: (body(i), carry)[1], 0)


def norm_parts(values):
    centred = values - jnp.mean(values, axis=-1, keepdims=True)
    spread = jnp.mean(centred * centred, axis=-1, keepdims=True)
    scale = lax.rsqrt(spread + norm_eps)
    return centred * scale, scale


def norm_back(values, grad, gain):
    hat, scale = norm_parts(values)
    inner = grad * gain
    mean_a = jnp.mean(inner, axis=-1, keepdims=True)
    mean_b = jnp.mean(inner * hat, axis=-1, keepdims=True)
    return scale * (inner - mean_a - hat * mean_b), grad * hat


def gelu_parts(values):
    root = math.sqrt(2.0 / math.pi)
    square = values * values
    bend = jnp.tanh(root * values * (1.0 + 0.044715 * square))
    half = 0.5 * (1.0 + bend)
    slope = half + 0.5 * values * (1.0 - bend * bend) * root * (1.0 + 3.0 * 0.044715 * square)
    return values * half, slope


def rows_sum(values):
    return jnp.sum(values, axis=0, keepdims=True)


def segment_ref(units, plan, number):
    _, chunks, count, first, shape, matrix = plan.segments[number]
    part = units.at[pl.ds(first, count)]
    if not matrix:
        return part
    return part.reshape(shape[0] // ROWS, chunks, ROWS, LANES)


def segment_scratch(plan, number):
    _, chunks, _, _, shape, _ = plan.segments[number]
    return pltpu.VMEM((shape[0] // ROWS, chunks, ROWS, LANES), low_type)


def attention_pairs(rows):
    return (rows // SEQ) * (HEADS // 2)


def head_masks():
    lane = lax.broadcasted_iota(jnp.int32, (SEQ, LANES), 1)
    return lane < HD


def softmax_f32(scores):
    exponent = jnp.exp(scores - jnp.max(scores, axis=-1, keepdims=True))
    return exponent * (1.0 / jnp.sum(exponent, axis=-1, keepdims=True))


def mods_kernel(plan, modulator, bias, units, out, w, sem):
    load = pltpu.make_async_copy(segment_ref(units, plan, 4), w, sem)
    load.start()
    load.wait()
    value = modulator[...]

    def body(j):
        cols = pl.ds(pl.multiple_of(j * WIDE, WIDE), WIDE)
        out[:, cols] = dot(value, block_of(w, 0, D // ROWS, 2 * j, 2)) + bias[:, cols]

    loop(6 * D // WIDE, body)


def mods_call(plan, modulator, bias, units):
    vm = pl.BlockSpec(memory_space=pltpu.VMEM)
    return pl.pallas_call(
        functools.partial(mods_kernel, plan),
        out_shape=jax.ShapeDtypeStruct((modulator.shape[0], 6 * D), full_type),
        in_specs=[vm, vm, pl.BlockSpec(memory_space=pltpu.HBM)],
        out_specs=vm,
        scratch_shapes=[segment_scratch(plan, 4), pltpu.SemaphoreType.DMA],
        compiler_params=pltpu.CompilerParams(vmem_limit_bytes=32 * MB),
        name="modulation",
    )(modulator, bias, units)


def mods_back_kernel(plan, modulator, grad, units, before, grads, cond, w, dw, sem):
    load = pltpu.make_async_copy(segment_ref(units, plan, 4), w, sem.at[0])
    load.start()
    turned = modulator[...].astype(full_type).T.astype(low_type)

    def weight(j):
        cols = pl.ds(pl.multiple_of(j * WIDE, WIDE), WIDE)
        put_block(dw, 0, 2 * j, dot(turned, grad[:, cols]))

    loop(6 * D // WIDE, weight)
    store = pltpu.make_async_copy(dw, segment_ref(grads, plan, 4), sem.at[1])
    store.start()
    load.wait()
    cond[...] = jnp.zeros(cond.shape, full_type)

    def back(j):
        cols = pl.ds(pl.multiple_of(j * WIDE, WIDE), WIDE)
        cond[...] += dot_nt(grad[:, cols], block_of(w, 0, D // ROWS, 2 * j, 2))

    loop(6 * D // WIDE, back)
    store.wait()


def mods_back_call(plan, modulator, grad, units, grads):
    vm = pl.BlockSpec(memory_space=pltpu.VMEM)
    anywhere = pl.BlockSpec(memory_space=pltpu.HBM)
    return pl.pallas_call(
        functools.partial(mods_back_kernel, plan),
        out_shape=[jax.ShapeDtypeStruct(grads.shape, low_type), jax.ShapeDtypeStruct((modulator.shape[0], D), full_type)],
        in_specs=[vm, vm, anywhere, anywhere],
        out_specs=[anywhere, vm],
        input_output_aliases={3: 0},
        scratch_shapes=[segment_scratch(plan, 4), segment_scratch(plan, 4), pltpu.SemaphoreType.DMA((2,))],
        compiler_params=pltpu.CompilerParams(vmem_limit_bytes=40 * MB),
        name="modulation_back",
    )(modulator, grad, units, grads)


SAVED = (("h1", D, low_type), ("qkv", 3 * D, low_type), ("heads", D, low_type), ("attn", D, full_type), ("middle", D, full_type), ("h2", D, low_type), ("pre", FF, full_type), ("mlp", D, full_type))


def layer_forward_kernel(plan, rows, x, mod, bias_qkv, bias_o, bias_1, bias_2, units, out, sums, *refs):
    ns = len(SAVED)
    saved_out = refs[:ns]
    h1, qkv, heads, attn, middle, h2, pre, mlp = refs[ns : 2 * ns]
    w_qkv, w_o, w_1, w_2, load_sem, save_sem = refs[2 * ns :]
    weights = (w_qkv, w_o, w_1, w_2)
    loads = [pltpu.make_async_copy(segment_ref(units, plan, i), weights[i], load_sem.at[i]) for i in range(4)]
    for copy in loads:
        copy.start()
    saves = [pltpu.make_async_copy(refs[ns + i], saved_out[i], save_sem.at[i]) for i in range(ns)]
    part = lambda s, i: mod[pl.ds(s, 1), i * D : (i + 1) * D]
    per = SEQ // CHUNK

    def norm_a(i):
        at = pl.ds(pl.multiple_of(i * CHUNK, CHUNK), CHUNK)
        s = i // per
        hat, _ = norm_parts(x[at, :])
        h1[at, :] = (hat * (1.0 + part(s, 1)) + part(s, 0)).astype(low_type)

    loop(rows // CHUNK, norm_a)
    saves[0].start()
    loads[0].wait()

    def project(j):
        cols = pl.ds(pl.multiple_of(j * WIDE, WIDE), WIDE)
        value = dot(h1[...], block_of(w_qkv, 0, D // ROWS, 2 * j, 2)) + bias_qkv[:, cols]
        qkv[:, cols] = value.astype(low_type)

    loop(3 * D // WIDE, project)
    saves[1].start()
    first = head_masks()

    def attend(i):
        s, j = i // (HEADS // 2), i % (HEADS // 2)
        at = pl.ds(pl.multiple_of(s * SEQ, SEQ), SEQ)
        cut = lambda o: qkv[at, pl.ds(pl.multiple_of(o * D + j * LANES, LANES), LANES)]
        q, k, v = cut(0), cut(1), cut(2)
        q = q * jnp.asarray(HD ** (-0.5), low_type)
        zero = jnp.zeros_like(q)
        halves = []
        for mask in (first, ~first):
            probs = softmax_f32(dot_nt(jnp.where(mask, q, zero), k)).astype(low_type)
            halves.append(dot(probs, v))
        heads[at, pl.ds(pl.multiple_of(j * LANES, LANES), LANES)] = jnp.where(first, halves[0], halves[1]).astype(low_type)

    loop(attention_pairs(rows), attend)
    saves[2].start()
    loads[1].wait()

    def project_out(j):
        cols = pl.ds(pl.multiple_of(j * WIDE, WIDE), WIDE)
        attn[:, cols] = dot(heads[...], block_of(w_o, 0, D // ROWS, 2 * j, 2)) + bias_o[:, cols]

    loop(D // WIDE, project_out)
    saves[3].start()
    zero_sum = jnp.zeros((1, D), full_type)

    def norm_m(i, total):
        at = pl.ds(pl.multiple_of(i * CHUNK, CHUNK), CHUNK)
        s = i // per
        value = attn[at, :]
        mid = x[at, :] + part(s, 2) * value
        middle[at, :] = mid
        hat, _ = norm_parts(mid)
        h2[at, :] = (hat * (1.0 + part(s, 4)) + part(s, 3)).astype(low_type)
        return total + rows_sum(value * value)

    attn_sum = lax.fori_loop(0, rows // CHUNK, norm_m, zero_sum)
    saves[4].start()
    saves[5].start()
    loads[2].wait()
    loads[3].wait()
    mlp[...] = jnp.broadcast_to(bias_2[...], (rows, D))

    def feed(j):
        cols = pl.ds(pl.multiple_of(j * WIDE, WIDE), WIDE)
        value = dot(h2[...], block_of(w_1, 0, D // ROWS, 2 * j, 2)) + bias_1[:, cols]
        pre[:, cols] = value
        act = gelu_parts(value)[0].astype(low_type)
        mlp[...] += dot(act, block_of(w_2, j * (WIDE // ROWS), WIDE // ROWS, 0, D // LANES))

    loop(FF // WIDE, feed)
    saves[6].start()
    saves[7].start()

    def finish(i, carry):
        at = pl.ds(pl.multiple_of(i * CHUNK, CHUNK), CHUNK)
        value = mlp[at, :]
        result = middle[at, :] + part(i // per, 5) * value
        out[at, :] = result
        return (carry[0] + rows_sum(result * result), carry[1] + rows_sum(value * value))

    out_sum, mlp_sum = lax.fori_loop(0, rows // CHUNK, finish, (zero_sum, zero_sum))
    sums[...] = jnp.zeros(sums.shape, full_type)
    sums[0:1, :] = out_sum
    sums[1:2, :] = attn_sum
    sums[2:3, :] = mlp_sum
    for copy in saves:
        copy.wait()


def layer_forward_call(plan, x, mod, biases, units):
    rows = x.shape[0]
    vm = pl.BlockSpec(memory_space=pltpu.VMEM)
    anywhere = pl.BlockSpec(memory_space=pltpu.HBM)
    dma = pltpu.SemaphoreType.DMA
    shapes = [((rows, width), kind) for _, width, kind in SAVED]
    results = pl.pallas_call(
        functools.partial(layer_forward_kernel, plan, rows),
        out_shape=[jax.ShapeDtypeStruct((rows, D), full_type), jax.ShapeDtypeStruct((8, D), full_type)]
        + [jax.ShapeDtypeStruct(*s) for s in shapes],
        in_specs=[vm] * 6 + [anywhere],
        out_specs=[vm, vm] + [anywhere] * len(SAVED),
        scratch_shapes=[pltpu.VMEM(*s) for s in shapes] + [segment_scratch(plan, i) for i in range(4)] + [dma((4,)), dma((len(SAVED),))],
        compiler_params=pltpu.CompilerParams(vmem_limit_bytes=56 * MB),
        name="layer_forward",
    )(x, mod, *biases, units)
    return results[0], results[1], results[2:]


def layer_backward_kernel(plan, rows, x, grad_in, mod, *refs):
    ns = len(SAVED)
    saved_hbm = refs[:ns]
    units, grad_out, grad_mod, bias_out, grads = refs[ns : ns + 5]
    h1, qkv, heads, attn, middle, h2, pre, mlp = refs[ns + 5 : 2 * ns + 5]
    w_qkv, w_o, w_1, w_2, d_qkv, g_low, wide, turned, dx, d_one, d_two, load_sem, save_sem, out_sem = refs[2 * ns + 5 :]
    weights = (w_qkv, w_o, w_1, w_2)
    inside = dict(zip(range(ns), refs[ns + 5 : 2 * ns + 5]))
    saves = [pltpu.make_async_copy(saved_hbm[i], inside[i], save_sem.at[i]) for i in range(ns)]
    loads = [pltpu.make_async_copy(segment_ref(units, plan, i), weights[i], load_sem.at[i]) for i in range(4)]
    for copy in (saves[7], saves[6], loads[3], saves[5], loads[2], saves[4], saves[3], loads[1], saves[2], saves[1], loads[0], saves[0]):
        copy.start()
    part = lambda s, i: mod[pl.ds(s, 1), i * D : (i + 1) * D]
    per = SEQ // CHUNK
    grad_mod[...] = jnp.zeros(grad_mod.shape, full_type)
    bias_out[...] = jnp.zeros(bias_out.shape, full_type)

    def add_mod(s, i, value):
        grad_mod[pl.ds(s, 1), i * D : (i + 1) * D] += value

    def each_chunk(body):
        loop(rows // CHUNK, lambda i: body(pl.ds(pl.multiple_of(i * CHUNK, CHUNK), CHUNK), i // per))

    B_Q, B_V, B_O, B_1, B_2 = 0, D, 2 * D, 3 * D, 3 * D + FF
    saves[7].wait()

    def start_mlp(at, s):
        grad = grad_in[at, :]
        low = (part(s, 5) * grad).astype(low_type)
        g_low[at, :] = low
        bias_out[:, B_2 : B_2 + D] += rows_sum(low.astype(full_type))
        add_mod(s, 5, rows_sum(mlp[at, :] * grad))

    each_chunk(start_mlp)
    saves[5].wait()
    turned[...] = h2[...].astype(full_type).T.astype(low_type)
    saves[6].wait()
    loads[3].wait()
    loads[2].wait()
    dx[...] = jnp.zeros(dx.shape, full_type)
    half = WIDE // ROWS

    def outer(slot, segment, block, blocks, chunk, chunks, buffer):
        target = segment_ref(grads, plan, segment).at[pl.ds(block, blocks), pl.ds(chunk, chunks)]
        return pltpu.make_async_copy(buffer, target, out_sem.at[slot])

    def mlp_store(j, kind):
        at = j % 2
        if kind == 0:
            return outer(2 * at, 3, j * half, half, 0, D // LANES, d_one.at[at])
        return outer(2 * at + 1, 2, 0, D // ROWS, 2 * j, 2, d_two.at[at])

    def feed_back(j):
        cols = pl.ds(pl.multiple_of(j * WIDE, WIDE), WIDE)
        at = j % 2

        @pl.when(j >= 2)
        def _():
            mlp_store(j - 2, 0).wait()
            mlp_store(j - 2, 1).wait()

        act, slope = gelu_parts(pre[:, cols])
        grad_act = dot_nt(g_low[...], block_of(w_2, j * half, half, 0, D // LANES))
        low = (grad_act * slope).astype(low_type)
        wide[...] = low
        bias_out[:, pl.ds(pl.multiple_of(B_1 + j * WIDE, WIDE), WIDE)] += rows_sum(low.astype(full_type))
        put_block(d_one.at[at], 0, 0, dot_tn(act.astype(low_type), g_low[...]))
        mlp_store(j, 0).start()
        put_block(d_two.at[at], 0, 0, dot(turned[...], wide[...]))
        mlp_store(j, 1).start()
        dx[...] += dot_nt(wide[...], block_of(w_1, 0, D // ROWS, 2 * j, 2))

    steps = FF // WIDE
    loop(steps, feed_back)
    saves[4].wait()
    saves[3].wait()

    def middle_back(at, s):
        grad = dx[at, :]
        back, scaled = norm_back(middle[at, :], grad, 1.0 + part(s, 4))
        add_mod(s, 3, rows_sum(grad))
        add_mod(s, 4, rows_sum(scaled))
        total = grad_in[at, :] + back
        grad_out[at, :] = total
        low = (part(s, 2) * total).astype(low_type)
        g_low[at, :] = low
        bias_out[:, B_O : B_O + D] += rows_sum(low.astype(full_type))
        add_mod(s, 2, rows_sum(attn[at, :] * total))

    each_chunk(middle_back)
    loads[1].wait()
    saves[2].wait()
    for j in (steps - 2, steps - 1):
        mlp_store(j, 0).wait()
        mlp_store(j, 1).wait()
    turned[...] = heads[...].astype(full_type).T.astype(low_type)

    def wo_store(j):
        return outer(j % 2, 1, 0, D // ROWS, 2 * j, 2, d_two.at[j % 2])

    def out_back(j):
        cols = pl.ds(pl.multiple_of(j * WIDE, WIDE), WIDE)

        @pl.when(j >= 2)
        def _():
            wo_store(j - 2).wait()

        put_block(d_two.at[j % 2], 0, 0, dot(turned[...], g_low[:, cols]))
        wo_store(j).start()
        heads[:, cols] = dot_nt(g_low[...], block_of(w_o, j * half, half, 0, D // LANES)).astype(low_type)

    loop(D // WIDE, out_back)
    saves[1].wait()
    first = head_masks()

    def attend_back(i):
        s, j = i // (HEADS // 2), i % (HEADS // 2)
        at = pl.ds(pl.multiple_of(s * SEQ, SEQ), SEQ)
        cut = lambda o: qkv[at, pl.ds(pl.multiple_of(o * D + j * LANES, LANES), LANES)]
        q, k, v = cut(0), cut(1), cut(2)
        go = heads[at, pl.ds(pl.multiple_of(j * LANES, LANES), LANES)]
        q = q * jnp.asarray(HD ** (-0.5), low_type)
        zero = jnp.zeros_like(q)
        dq, dk, dv = [], 0.0, 0.0
        for mask in (first, ~first):
            q_h, go_h = jnp.where(mask, q, zero), jnp.where(mask, go, zero)
            probs = softmax_f32(dot_nt(q_h, k))
            grad_probs = dot_nt(go_h, v)
            dv = dv + dot_tn(probs.astype(low_type), go_h)
            inner = jnp.sum(probs * grad_probs, axis=-1, keepdims=True)
            ds = (probs * (grad_probs - inner)).astype(low_type)
            dq.append(dot(ds, k) * HD ** (-0.5))
            dk = dk + dot_tn(ds, q_h)
        put = lambda o, value: d_qkv.at[at, pl.ds(pl.multiple_of(o * D + j * LANES, LANES), LANES)].set(value)
        for o, value in enumerate((jnp.where(first, dq[0], dq[1]), dk, dv)):
            low = value.astype(low_type)
            d_qkv[at, pl.ds(pl.multiple_of(o * D + j * LANES, LANES), LANES)] = low
            if o != 1:
                start = (B_Q if o == 0 else B_V) + j * LANES
                bias_out[:, pl.ds(pl.multiple_of(start, LANES), LANES)] += rows_sum(low.astype(full_type))

    loop(attention_pairs(rows), attend_back)
    saves[0].wait()
    loads[0].wait()
    wo_store(1).wait()
    wo_store(2).wait()
    turned[...] = h1[...].astype(full_type).T.astype(low_type)
    dx[...] = jnp.zeros(dx.shape, full_type)

    def qkv_store(j):
        return outer(j % 2, 0, 0, D // ROWS, 2 * j, 2, d_two.at[j % 2])

    def project_back(j):
        cols = pl.ds(pl.multiple_of(j * WIDE, WIDE), WIDE)

        @pl.when(j >= 2)
        def _():
            qkv_store(j - 2).wait()

        put_block(d_two.at[j % 2], 0, 0, dot(turned[...], d_qkv[:, cols]))
        qkv_store(j).start()
        dx[...] += dot_nt(d_qkv[:, cols], block_of(w_qkv, 0, D // ROWS, 2 * j, 2))

    count = 3 * D // WIDE
    loop(count, project_back)

    def input_back(at, s):
        grad = dx[at, :]
        back, scaled = norm_back(x[at, :], grad, 1.0 + part(s, 1))
        add_mod(s, 0, rows_sum(grad))
        add_mod(s, 1, rows_sum(scaled))
        grad_out[at, :] += back

    each_chunk(input_back)
    for j in (count - 2, count - 1):
        qkv_store(j).wait()


def layer_backward_call(plan, x, grad, mod, saved, units):
    rows = x.shape[0]
    vm = pl.BlockSpec(memory_space=pltpu.VMEM)
    anywhere = pl.BlockSpec(memory_space=pltpu.HBM)
    dma = pltpu.SemaphoreType.DMA
    shapes = [((rows, width), kind) for _, width, kind in SAVED]
    tile = (ROWS, LANES)
    return pl.pallas_call(
        functools.partial(layer_backward_kernel, plan, rows),
        out_shape=[
            jax.ShapeDtypeStruct((rows, D), full_type),
            jax.ShapeDtypeStruct((8, 6 * D), full_type),
            jax.ShapeDtypeStruct((1, 4 * D + FF), full_type),
            jax.ShapeDtypeStruct(units.shape, low_type),
        ],
        in_specs=[vm] * 3 + [anywhere] * (len(SAVED) + 1),
        out_specs=[vm, vm, vm, anywhere],
        scratch_shapes=[pltpu.VMEM(*s) for s in shapes]
        + [segment_scratch(plan, i) for i in range(4)]
        + [
            pltpu.VMEM((rows, 3 * D), low_type),
            pltpu.VMEM((rows, D), low_type),
            pltpu.VMEM((rows, WIDE), low_type),
            pltpu.VMEM((D, rows), low_type),
            pltpu.VMEM((rows, D), full_type),
            pltpu.VMEM((2, WIDE // ROWS, D // LANES) + tile, low_type),
            pltpu.VMEM((2, D // ROWS, 2) + tile, low_type),
            dma((4,)),
            dma((len(SAVED),)),
            dma((4,)),
        ],
        compiler_params=pltpu.CompilerParams(vmem_limit_bytes=60 * MB),
        name="layer_backward",
    )(x, grad, mod, *saved, units)


def sigmoid(values):
    return 1.0 / (1.0 + jnp.exp(-values))


def silu_parts(values):
    gate = sigmoid(values)
    return values * gate, gate * (1.0 + values * (1.0 - gate))


TOP = (7, 9, 11, 13)


def top_kernel(plan, rows, sample_total, x, features, target, weight_t, modulator, b_1, b_2, b_3, b_f, w_h, b_h, units, *refs):
    grad_x, stats, cond, bias_out, dw_h, grads = refs[:6]
    p_1, p_2, p_3, w_f, pre_a, act_a, pre_b, act_b, pred, low, g_b, g_a, hidden, modf, d_modf, stage, dw_f, load_sem, out_sem = refs[6:]
    weights = (p_1, p_2, p_3, w_f)
    loads = [pltpu.make_async_copy(segment_ref(units, plan, s), weights[i], load_sem.at[i]) for i, s in enumerate(TOP)]
    for copy in loads:
        copy.start()
    per = SEQ // CHUNK
    half = WIDE // ROWS
    stats[...] = jnp.zeros(stats.shape, full_type)
    bias_out[...] = jnp.zeros(bias_out.shape, full_type)
    d_modf[...] = jnp.zeros(d_modf.shape, full_type)
    A_1, A_2, A_3, A_F, A_H = 0, PH, 2 * PH, 2 * PH + ZD, 2 * PH + ZD + 2 * D
    wide_at = lambda j, base=0: pl.ds(pl.multiple_of(base + j * WIDE, LANES), WIDE)

    def each_chunk(body):
        loop(rows // CHUNK, lambda i: body(pl.ds(pl.multiple_of(i * CHUNK, CHUNK), CHUNK), i // per))

    def to_low(at, s):
        low[at, :] = x[at, :].astype(low_type)

    each_chunk(to_low)
    loads[0].wait()

    def first_layer(j):
        value = dot(low[...], block_of(p_1, 0, D // ROWS, 2 * j, 2)) + b_1[:, wide_at(j)]
        pre_a[:, wide_at(j)] = value
        act_a[:, wide_at(j)] = silu_parts(value)[0].astype(low_type)

    loop(PH // WIDE, first_layer)
    loads[1].wait()

    def second_layer(j):
        value = dot(act_a[...], block_of(p_2, 0, PH // ROWS, 2 * j, 2)) + b_2[:, wide_at(j)]
        pre_b[:, wide_at(j)] = value
        act_b[:, wide_at(j)] = silu_parts(value)[0].astype(low_type)

    loop(PH // WIDE, second_layer)
    loads[2].wait()

    def third_layer(j):
        pred[:, wide_at(j)] = dot(act_b[...], block_of(p_3, 0, PH // ROWS, 2 * j, 2)) + b_3[:, wide_at(j)]

    loop(ZD // WIDE, third_layer)
    seed = -proj_coeff / (SEQ * sample_total)

    def cosine(at, s):
        value = pred[at, :]
        want = features[at, :].astype(full_type)
        inner = jnp.sum(value * want, axis=-1, keepdims=True)
        scale_a = lax.rsqrt(jnp.sum(value * value, axis=-1, keepdims=True) + norm_eps)
        scale_b = lax.rsqrt(jnp.sum(want * want, axis=-1, keepdims=True) + norm_eps)
        both = scale_a * scale_b
        stats[0:1, 0:1] += jnp.sum(inner * both, axis=0, keepdims=True)
        grad = seed * (want * both - value * (inner * both * scale_a * scale_a))
        grad = grad.astype(low_type)
        hidden[at, :] = grad
        bias_out[:, A_3 : A_3 + ZD] += rows_sum(grad.astype(full_type))

    each_chunk(cosine)

    def store(segment, j, chunks):
        where = segment_ref(grads, plan, segment).at[pl.ds(j * half, half)]
        return pltpu.make_async_copy(stage.at[j % 2, :, pl.ds(0, chunks)], where, out_sem.at[j % 2])

    def stored(segment, j, chunks):
        @pl.when(j >= 2)
        def _():
            store(segment, j - 2, chunks).wait()

    def third_back(j):
        stored(11, j, ZD // LANES)
        put_block(stage.at[j % 2], 0, 0, dot_tn(act_b[:, wide_at(j)], hidden[...]))
        store(11, j, ZD // LANES).start()
        grad = dot_nt(hidden[...], block_of(p_3, j * half, half, 0, ZD // LANES))
        grad = (grad * silu_parts(pre_b[:, wide_at(j)])[1]).astype(low_type)
        g_b[:, wide_at(j)] = grad
        bias_out[:, wide_at(j, A_2)] += rows_sum(grad.astype(full_type))

    def drain(segment, count, chunks):
        for j in range(max(0, count - 2), count):
            store(segment, j, chunks).wait()

    loop(PH // WIDE, third_back)
    drain(11, PH // WIDE, ZD // LANES)
    span = 4 * LANES

    def second_back(j):
        stored(9, j, PH // LANES)
        for i in range(PH // span):
            put_block(stage.at[j % 2], 0, i * (span // LANES), dot_tn(act_a[:, wide_at(j)], g_b[:, i * span : (i + 1) * span]))
        store(9, j, PH // LANES).start()
        grad = dot_nt(g_b[...], block_of(p_2, j * half, half, 0, PH // LANES))
        grad = (grad * silu_parts(pre_a[:, wide_at(j)])[1]).astype(low_type)
        g_a[:, wide_at(j)] = grad
        bias_out[:, wide_at(j, A_1)] += rows_sum(grad.astype(full_type))

    loop(PH // WIDE, second_back)
    drain(9, PH // WIDE, PH // LANES)

    def first_back(j):
        stored(7, j, PH // LANES)
        for i in range(PH // span):
            put_block(stage.at[j % 2], 0, i * (span // LANES), dot_tn(low[:, wide_at(j)], g_a[:, i * span : (i + 1) * span]))
        store(7, j, PH // LANES).start()
        grad_x[:, wide_at(j)] = dot_nt(g_a[...], block_of(p_1, j * half, half, 0, PH // LANES))

    loop(D // WIDE, first_back)
    loads[3].wait()

    def final_mod(j):
        modf[:, wide_at(j)] = dot(modulator[...], block_of(w_f, 0, D // ROWS, 2 * j, 2)) + b_f[:, wide_at(j)]

    loop(2 * D // WIDE, final_mod)
    part = lambda s, i: modf[pl.ds(s, 1), i * D : (i + 1) * D]
    dw_h[...] = jnp.zeros(dw_h.shape, full_type)

    def head(at, s):
        hat, scale = norm_parts(x[at, :])
        gain = 1.0 + part(s, 1)
        normed = (hat * gain + part(s, 0)).astype(low_type)
        off = dot(normed, w_h[...]) + b_h[...] - target[at, :]
        weight = weight_t[pl.ds(s, 1), :]
        stats[1:2, :] += rows_sum(weight * off * off)
        grad = (2.0 * weight / (SEQ * PD * sample_total) * off).astype(low_type)
        bias_out[:, A_H : A_H + LANES] += rows_sum(grad.astype(full_type))
        dw_h[...] += dot_tn(normed, grad)
        back = dot_nt(grad, w_h[...])
        d_modf[pl.ds(s, 1), 0:D] += rows_sum(back)
        d_modf[pl.ds(s, 1), D : 2 * D] += rows_sum(back * hat)
        inner = back * gain
        mean_a = jnp.mean(inner, axis=-1, keepdims=True)
        mean_b = jnp.mean(inner * hat, axis=-1, keepdims=True)
        grad_x[at, :] += scale * (inner - mean_a - hat * mean_b)

    each_chunk(head)
    turned = modulator[...].astype(full_type).T.astype(low_type)
    cond[...] = jnp.zeros(cond.shape, full_type)

    def final_back(j):
        grad = d_modf[:, wide_at(j)].astype(low_type)
        bias_out[:, wide_at(j, A_F)] += rows_sum(grad.astype(full_type))
        put_block(dw_f, 0, 2 * j, dot(turned, grad))
        cond[...] += dot_nt(grad, block_of(w_f, 0, D // ROWS, 2 * j, 2))

    loop(2 * D // WIDE, final_back)
    last = pltpu.make_async_copy(dw_f, segment_ref(grads, plan, 13), out_sem.at[2])
    last.start()
    last.wait()
    drain(7, D // WIDE, PH // LANES)


def top_call(plan, sample_total, x, features, target, weight_t, modulator, biases, w_h, b_h, units):
    rows = x.shape[0]
    vm = pl.BlockSpec(memory_space=pltpu.VMEM)
    anywhere = pl.BlockSpec(memory_space=pltpu.HBM)
    dma = pltpu.SemaphoreType.DMA
    few = modulator.shape[0]
    f32 = lambda *shape: pltpu.VMEM(shape, full_type)
    bf16 = lambda *shape: pltpu.VMEM(shape, low_type)
    shape = lambda *dims: jax.ShapeDtypeStruct(dims, full_type)
    return pl.pallas_call(
        functools.partial(top_kernel, plan, rows, sample_total),
        out_shape=[
            shape(rows, D),
            shape(8, LANES),
            shape(few, D),
            shape(1, 2 * PH + ZD + 2 * D + LANES),
            shape(D, LANES),
            jax.ShapeDtypeStruct(units.shape, low_type),
        ],
        in_specs=[vm] * 11 + [anywhere],
        out_specs=[vm] * 5 + [anywhere],
        scratch_shapes=[segment_scratch(plan, s) for s in TOP]
        + [f32(rows, PH), bf16(rows, PH), f32(rows, PH), bf16(rows, PH), f32(rows, ZD), bf16(rows, D)]
        + [bf16(rows, PH), bf16(rows, PH), bf16(rows, ZD), f32(few, 2 * D), f32(few, 2 * D)]
        + [bf16(2, WIDE // ROWS, PH // LANES, ROWS, LANES), segment_scratch(plan, 13)]
        + [dma((4,)), dma((3,))],
        compiler_params=pltpu.CompilerParams(vmem_limit_bytes=60 * MB),
        name="projector_and_head",
    )(x, features, target, weight_t, modulator, *biases, w_h, b_h, units)


def busy_loop(count, body, events=()):
    size = max(1, -(-len(events) // count))

    def step(i):
        body(i)
        for first in range(0, len(events), size):

            @pl.when(i == first // size)
            def _():
                for event in events[first : first + size]:
                    event()

    loop(count, step)


def spread(events, weights):
    shares, done, total = [], 0, 0
    for weight in weights:
        total += weight
        upto = len(events) * total // sum(weights)
        shares.append(events[done:upto])
        done = upto
    return shares


def row_vector(units, rows):
    values = units.astype(full_type).reshape(-1, LANES)
    return jnp.concatenate([values[r : r + 1, :] for r in range(rows)], axis=1)


def pick(ref, here, *spots):
    return ref.at[tuple(here.zero + spot for spot in spots)]


class Place:
    def __init__(self, zs):
        self.zs = zs
        self.n = zs * 8
        self.me = lax.axis_index("fsdp")
        self.zero = self.me * 0
        self.z, self.y, self.x, self.c = place(self.me, zs)
        self.prev = lax.rem(self.me + self.n - 1, self.n)
        self.following = lax.rem(self.me + 1, self.n)
        self.xpeer = self.index(self.z, self.y, 1 - self.x, self.c)
        self.ypeer = self.index(self.z, 1 - self.y, self.x, self.c)
        self.cpeer = self.index(self.z, self.y, self.x, 1 - self.c)

    def index(self, z, y, x, c):
        return ((z * 2 + y) * 2 + x) * 2 + c

    def above(self, k):
        return self.index(lax.rem(self.z + k, self.zs), self.y, self.x, self.c)

    def below(self, k):
        return self.index(lax.rem(self.z + self.zs - k, self.zs), self.y, self.x, self.c)

    def slot(self, k, dy, dx, dc):
        z = lax.rem(self.z + self.zs - k, self.zs)
        flip = lambda value, change: 1 - value if change else value
        return self.index(z, flip(self.y, dy), flip(self.x, dx), flip(self.c, dc))

    def peers(self):
        return [self.prev, self.following, self.xpeer, self.ypeer, self.cpeer] + [self.above(k) for k in range(1, self.zs)]

    def greet(self):
        barrier = pltpu.get_barrier_semaphore()
        for peer in self.peers():
            pl.semaphore_signal(barrier, inc=1, device_id=(peer,), device_id_type=MESH)

    def met(self):
        pl.semaphore_wait(pltpu.get_barrier_semaphore(), len(self.peers()))


def remote(src, dst, send_sem, recv_sem, to):
    return pltpu.make_async_remote_copy(src, dst, send_sem, recv_sem, device_id=(to,), device_id_type=MESH)


def arrived(ref, sem):
    pltpu.make_async_copy(ref, ref, sem).wait()


class Gather:
    def __init__(self, here, buckets, sems):
        self.here = here
        self.buckets = buckets
        self.own_sem, self.send_sem, self.zr, self.xa, self.xb, self.yb, self.ya, self.cr = sems
        self.sent = []
        self.made = 0

    def guarded(self, b, k, run):
        plan, _, _, lo, hi = self.buckets[b]
        if lo == 0 and hi == self.here.zs:
            run()
            return
        source = lax.rem(self.here.z + self.here.zs - k, self.here.zs)
        pl.when((source >= lo) & (source < hi))(run)

    def sem(self, name, *spots):
        return lambda: pick(getattr(self, name), self.here, *spots)

    def send(self, b, k, src, dst, sem, to):
        number = self.made
        self.made += 1
        make = lambda: remote(src(), dst(), pick(self.send_sem, self.here, number), sem(), to())
        make().start()
        self.sent.append((b, k, make))

    def part(self, b, h, k, dy, dx, dc=0):
        plan, units = self.buckets[b][:2]
        return units.at[pl.ds(self.here.slot(k, dy, dx, dc) * plan.per + h * plan.half, plan.half)]

    def whole(self, b, k, dy, dx, dc=0):
        plan, units = self.buckets[b][:2]
        return units.at[pl.ds(self.here.slot(k, dy, dx, dc) * plan.per, plan.per)]

    def own_copy(self, b):
        return pltpu.make_async_copy(self.buckets[b][2], self.whole(b, 0, 0, 0), pick(self.own_sem, self.here, b))

    def start(self, b):
        here, slot = self.here, self.buckets[b][2]
        plan = self.buckets[b][0]

        def run():
            self.own_copy(b).start()
            mine = lambda h: lambda: slot.at[pl.ds(h * plan.half, plan.half)]
            to = lambda h: lambda: self.part(b, h, 0, 0, 0)
            for k in range(1, here.zs):
                for h in range(2):
                    self.send(b, 0, mine(h), to(h), self.sem("zr", b, h, k), lambda k=k: here.above(k))
            self.send(b, 0, mine(0), to(0), self.sem("xa", b, 0), lambda: here.xpeer)
            self.send(b, 0, mine(1), to(1), self.sem("yb", b, 0), lambda: here.ypeer)
            self.send(b, 0, mine(0), to(0), self.sem("ya", b, 0, 0), lambda: here.ypeer)
            self.send(b, 0, mine(1), to(1), self.sem("xb", b, 0, 0), lambda: here.xpeer)
            self.send(b, 0, lambda: slot, lambda: self.whole(b, 0, 0, 0), self.sem("cr", b, 0, 0, 0), lambda: here.cpeer)

        self.guarded(b, 0, run)

    def pass_on(self, b, k, h, dy, dx, sem, to):
        ref = lambda: self.part(b, h, k, dy, dx)
        self.send(b, k, ref, ref, sem, to)

    def share(self, b, k, dy, dx):
        ref = lambda: self.whole(b, k, dy, dx)
        self.send(b, k, ref, ref, self.sem("cr", b, k, dy, dx), lambda: self.here.cpeer)

    def events(self, b):
        here = self.here
        found = []

        def add(k, run):
            found.append(lambda: self.guarded(b, k, run))

        for k in range(1, here.zs):

            def from_z(k=k):
                arrived(self.part(b, 0, k, 0, 0), pick(self.zr, self.here, b, 0, k))
                self.pass_on(b, k, 0, 0, 0, self.sem("xa", b, k), lambda: here.xpeer)
                arrived(self.part(b, 1, k, 0, 0), pick(self.zr, self.here, b, 1, k))
                self.pass_on(b, k, 1, 0, 0, self.sem("yb", b, k), lambda: here.ypeer)
                self.pass_on(b, k, 0, 0, 0, self.sem("ya", b, k, 0), lambda: here.ypeer)
                self.pass_on(b, k, 1, 0, 0, self.sem("xb", b, k, 0), lambda: here.xpeer)
                self.share(b, k, 0, 0)

            add(k, from_z)
        for k in range(here.zs):

            def across(k=k):
                arrived(self.part(b, 0, k, 0, 1), pick(self.xa, self.here, b, k))
                self.pass_on(b, k, 0, 0, 1, self.sem("ya", b, k, 1), lambda: here.ypeer)
                arrived(self.part(b, 1, k, 1, 0), pick(self.yb, self.here, b, k))
                self.pass_on(b, k, 1, 1, 0, self.sem("xb", b, k, 1), lambda: here.xpeer)

            add(k, across)
        for k in range(here.zs):

            def beside(k=k):
                arrived(self.part(b, 1, k, 0, 1), pick(self.xb, self.here, b, k, 0))
                self.share(b, k, 0, 1)
                arrived(self.part(b, 0, k, 1, 0), pick(self.ya, self.here, b, k, 0))
                self.share(b, k, 1, 0)

            add(k, beside)
        for k in range(here.zs):

            def corner(k=k):
                arrived(self.part(b, 1, k, 1, 1), pick(self.xb, self.here, b, k, 1))
                arrived(self.part(b, 0, k, 1, 1), pick(self.ya, self.here, b, k, 1))
                self.share(b, k, 1, 1)

            add(k, corner)
        return found

    def complete(self, b):
        self.guarded(b, 0, lambda: self.own_copy(b).wait())
        for k in range(self.here.zs):

            def run(k=k):
                for dy in range(2):
                    for dx in range(2):
                        arrived(self.whole(b, k, dy, dx, 1), pick(self.cr, self.here, b, k, dy, dx))

            self.guarded(b, k, run)

    def drain(self):
        for b, k, make in self.sent:
            self.guarded(b, k, lambda: make().wait_send())


FRONT = 7


def cut_units(here, plan, ext, slot):
    top = here.me * plan.share // LANES - plan.before
    for base, chunks, count, first_unit, _, _ in plan.segments:
        lo = jnp.clip(plan.per * here.me - first_unit, 0, count)
        hi = jnp.clip(plan.per * here.me + plan.per - first_unit, 0, count)

        def unit(u, carry):
            block = u // chunks
            row = base + block * (ROWS * chunks) + (u - block * chunks) - top
            if chunks == 1:
                value = ext[pl.ds(row, ROWS), :]
            else:
                value = ext[pl.ds(row, ROWS, stride=chunks), :]
            slot[first_unit + u - plan.per * here.me] = value.astype(low_type)
            return carry

        lax.fori_loop(lo, hi, unit, 0)


def forward_kernel(plans, zs, rows, *refs):
    np_ = len(plans)
    feed = iter(refs)
    take = lambda count: tuple(next(feed) for _ in range(count))
    one = lambda: next(feed)
    raw_hbm = take(np_)
    noisy, positions, basis, chosen = take(4)
    units = take(np_)
    stream = take(LAYERS + 1)
    mods = take(LAYERS)
    sums = take(LAYERS)
    modulator, condition, time_pre = take(3)
    saved_out = [take(len(SAVED)) for _ in range(LAYERS)]
    from_prev, from_next, slots = take(np_), take(np_), take(np_)
    raw_sem, halo_send, halo_recv, front_sem, load_sem, save_sem = take(6)
    gather_sems = take(8)
    here = Place(zs)
    here.greet()
    root = plans[0]
    front_units = root.segments[FRONT][3]
    front_planes = min(zs, -(-front_units // (8 * root.per)))
    buckets = [(root, units[0], slots[0], 0, front_planes)]
    buckets += [(plans[1 + i], units[1 + i], slots[1 + i], 0, zs) for i in range(LAYERS)]
    buckets += [(root, units[0], slots[0], front_planes, zs)]
    gather = Gather(here, buckets, gather_sems)
    last = len(buckets) - 1
    starts = [[0]] + [[1 + i] for i in range(LAYERS)]
    starts[-1].append(last)

    def prepare(*scratch):
        raw, ext, tail = (scratch[i * np_ : (i + 1) * np_] for i in range(3))
        loads = [pltpu.make_async_copy(raw_hbm[i], raw[i].at[pl.ds(8, p.raw)], raw_sem.at[i]) for i, p in enumerate(plans)]
        for copy in loads:
            copy.start()
        lane = lax.broadcasted_iota(jnp.int32, (64, LANES), 1)
        halos = []
        for i, p in enumerate(plans):
            shift = lax.rem(here.me * p.share, LANES)
            delta = (here.me + 1) * p.share // LANES - here.me * p.share // LANES
            raw[i][pl.ds(0, 8), :] = jnp.zeros((8, LANES), full_type)
            ext[i][pl.ds(0, p.before), :] = jnp.zeros((p.before, LANES), full_type)
            ext[i][pl.ds(p.before + p.raw, p.after), :] = jnp.zeros((p.after, LANES), full_type)
            loads[i].wait()

            def align(j):
                row = pl.multiple_of(j * 64, 64)
                level = pltpu.roll(raw[i][pl.ds(row + 8, 64), :], shift, 1)
                above = pltpu.roll(raw[i][pl.ds(row + 7, 64), :], shift, 1)
                ext[i][pl.ds(row + p.before, 64), :] = jnp.where(lane >= shift, level, above)

            loop(p.raw // 64, align)
            tail[i][...] = ext[i][pl.ds(delta, p.before + 8), :]
            if i == 0:
                here.met()
            halos.append(remote(ext[i].at[pl.ds(p.before, p.after)], from_next[i], halo_send.at[2 * i], halo_recv.at[2 * i], here.prev))
            halos.append(remote(tail[i], from_prev[i], halo_send.at[2 * i + 1], halo_recv.at[2 * i + 1], here.following))
            halos[-2].start()
            halos[-1].start()
        for i, p in enumerate(plans):
            delta = (here.me + 1) * p.share // LANES - here.me * p.share // LANES
            halos[2 * i].wait()
            halos[2 * i + 1].wait()
            ext[i][pl.ds(0, p.before + 8), :] += from_prev[i][...]
            ext[i][pl.ds(p.before + delta, p.after), :] += from_next[i][...]
            cut_units(here, p, ext[i], slots[i])
            for b in starts[i]:
                gather.start(b)

    f32 = lambda *dims: pltpu.VMEM(dims, full_type)
    pl.run_scoped(
        prepare,
        *[f32(p.raw + 8, LANES) for p in plans],
        *[f32(p.ext, LANES) for p in plans],
        *[f32(p.before + 8, LANES) for p in plans],
    )
    for event in gather.events(0):
        event()
    gather.complete(0)

    def compute(front, w_qkv, w_o, w_1, w_2, w_mod, raw_bias, *held):
        copy = pltpu.make_async_copy(units[0].at[pl.ds(0, front_units)], front, front_sem)
        copy.start()
        copy.wait()
        matrix = lambda number, blocks: front_matrix(front, root, number, blocks)
        vector = lambda number: row_vector(front[pl.ds(root.segments[number][3], 1)], D // LANES)
        events = spread(gather.events(1), (1, 1, 1, 1))
        stream[0][...] = dot(noisy[...], matrix(0, 1)) + vector(1) + positions[...]
        for event in events[0]:
            event()
        pre = dot(basis[...], matrix(2, FREQ // ROWS)) + vector(3)
        time_pre[...] = pre
        act = silu_parts(pre)[0].astype(low_type)
        total = dot(act, matrix(4, D // ROWS)) + vector(5)
        few = basis.shape[0]
        first = root.segments[6][3]
        picked = dot(chosen[...], front[pl.ds(first, root.segments[6][2])].reshape(-1, LANES))
        total = total + jnp.concatenate([picked[i * few : (i + 1) * few, :] for i in range(D // LANES)], axis=1)
        condition[...] = total
        modulator[...] = silu_parts(total)[0].astype(low_type)
        for group in events[1:]:
            for event in group:
                event()
        for ordinal in range(LAYERS):
            gather.complete(1 + ordinal)
            queue = gather.events(2 + ordinal)
            layer_forward_body(
                plans[1 + ordinal], rows, stream[ordinal], modulator, mods[ordinal], units[1 + ordinal],
                stream[ordinal + 1], sums[ordinal], saved_out[ordinal], held, (w_qkv, w_o, w_1, w_2, w_mod), raw_bias,
                load_sem, save_sem, spread(queue, (18, 9, 12, 3, 12)),
            )
        gather.complete(last)

    plan = plans[1]
    bias_units = plan.units - plan.segments[5][3]
    pl.run_scoped(
        compute,
        pltpu.VMEM((front_units, ROWS, LANES), low_type),
        *[segment_scratch(plan, i) for i in range(5)],
        pltpu.VMEM((bias_units, ROWS, LANES), low_type),
        *[pltpu.VMEM((rows, width), kind) for _, width, kind in SAVED],
    )
    gather.drain()


def front_matrix(front, plan, number, blocks):
    _, chunks, _, first, _, _ = plan.segments[number]
    columns = [jnp.concatenate([front[first + b * chunks + c] for b in range(blocks)], axis=0) for c in range(chunks)]
    return jnp.concatenate(columns, axis=1)


def layer_forward_body(plan, rows, x, modulator, mod, units, out, sums, saved_out, held, weights, raw_bias, load_sem, save_sem, events):
    ns = len(SAVED)
    h1, qkv, heads, attn, middle, h2, pre, mlp = held
    w_qkv, w_o, w_1, w_2, w_mod = weights
    bias_first = plan.segments[5][3]
    loads = [pltpu.make_async_copy(segment_ref(units, plan, i), weights[i], load_sem.at[i]) for i in range(5)]
    bias_load = pltpu.make_async_copy(units.at[pl.ds(bias_first, raw_bias.shape[0])], raw_bias, load_sem.at[5])
    bias_load.start()
    for i in (4, 0, 1, 2, 3):
        loads[i].start()
    saves = [pltpu.make_async_copy(held[i], saved_out[i], save_sem.at[i]) for i in range(ns)]
    part = lambda s, i: mod[pl.ds(s, 1), i * D : (i + 1) * D]
    per = SEQ // CHUNK
    wide_at = lambda j: pl.ds(pl.multiple_of(j * WIDE, WIDE), WIDE)
    chunk_at = lambda i: pl.ds(pl.multiple_of(i * CHUNK, CHUNK), CHUNK)
    bias_load.wait()

    def bias(number):
        _, _, count, first, shape, _ = plan.segments[number]
        return row_vector(raw_bias[pl.ds(first - bias_first, count)], shape[0] // LANES)

    loads[4].wait()
    mod[...] = jnp.broadcast_to(bias(10), mod.shape)
    value_of = modulator[...]

    def modulate(j):
        mod[:, wide_at(j)] += dot(value_of, block_of(w_mod, 0, D // ROWS, 2 * j, 2))

    busy_loop(6 * D // WIDE, modulate, events[0])

    def norm_a(i):
        s = i // per
        hat, _ = norm_parts(x[chunk_at(i), :])
        h1[chunk_at(i), :] = (hat * (1.0 + part(s, 1)) + part(s, 0)).astype(low_type)

    loop(rows // CHUNK, norm_a)
    saves[0].start()
    loads[0].wait()
    first_bias, value_bias = bias(5), bias(6)

    def project_with(base, given, events):
        pieces = D // WIDE

        def project(j):
            value = dot(h1[...], block_of(w_qkv, 0, D // ROWS, 2 * (base + j), 2))
            cols = wide_at(base + j)
            if given is not None:
                value = value + mlp[0:1, wide_at(j)]
            qkv[:, cols] = value.astype(low_type)

        if given is not None:
            mlp[0:1, :] = given
        busy_loop(pieces, project, events)

    third = spread(events[1], (1, 1, 1))
    project_with(0, first_bias, third[0])
    project_with(D // WIDE, None, third[1])
    project_with(2 * D // WIDE, value_bias, third[2])
    saves[1].start()
    first = head_masks()

    def attend(i):
        s, j = i // (HEADS // 2), i % (HEADS // 2)
        at = pl.ds(pl.multiple_of(s * SEQ, SEQ), SEQ)
        cut = lambda o: qkv[at, pl.ds(pl.multiple_of(o * D + j * LANES, LANES), LANES)]
        q, k, v = cut(0), cut(1), cut(2)
        q = q * jnp.asarray(HD ** (-0.5), low_type)
        zero = jnp.zeros_like(q)
        halves = []
        for mask in (first, ~first):
            probs = softmax_f32(dot_nt(jnp.where(mask, q, zero), k)).astype(low_type)
            halves.append(dot(probs, v))
        heads[at, pl.ds(pl.multiple_of(j * LANES, LANES), LANES)] = jnp.where(first, halves[0], halves[1]).astype(low_type)

    busy_loop(attention_pairs(rows), attend, events[2])
    saves[2].start()
    loads[1].wait()
    attn[...] = jnp.broadcast_to(bias(7), (rows, D))

    def project_out(j):
        attn[:, wide_at(j)] += dot(heads[...], block_of(w_o, 0, D // ROWS, 2 * j, 2))

    busy_loop(D // WIDE, project_out, events[3])
    saves[3].start()
    zero_sum = jnp.zeros((1, D), full_type)

    def norm_m(i, total):
        s = i // per
        value = attn[chunk_at(i), :]
        mid = x[chunk_at(i), :] + part(s, 2) * value
        middle[chunk_at(i), :] = mid
        hat, _ = norm_parts(mid)
        h2[chunk_at(i), :] = (hat * (1.0 + part(s, 4)) + part(s, 3)).astype(low_type)
        return total + rows_sum(value * value)

    attn_sum = lax.fori_loop(0, rows // CHUNK, norm_m, zero_sum)
    saves[4].start()
    saves[5].start()
    loads[2].wait()
    loads[3].wait()
    pre[0:1, :] = bias(8)
    mlp[...] = jnp.broadcast_to(bias(9), (rows, D))

    def feed(j):
        value = dot(h2[...], block_of(w_1, 0, D // ROWS, 2 * j, 2)) + pre[0:1, wide_at(j)]
        pre[:, wide_at(j)] = value
        act = gelu_parts(value)[0].astype(low_type)
        mlp[...] += dot(act, block_of(w_2, j * (WIDE // ROWS), WIDE // ROWS, 0, D // LANES))

    busy_loop(FF // WIDE, feed, events[4])
    saves[6].start()
    saves[7].start()

    def finish(i, carry):
        value = mlp[chunk_at(i), :]
        result = middle[chunk_at(i), :] + part(i // per, 5) * value
        out[chunk_at(i), :] = result
        return (carry[0] + rows_sum(result * result), carry[1] + rows_sum(value * value))

    out_sum, mlp_sum = lax.fori_loop(0, rows // CHUNK, finish, (zero_sum, zero_sum))
    sums[...] = jnp.zeros(sums.shape, full_type)
    sums[0:1, :] = out_sum
    sums[1:2, :] = attn_sum
    sums[2:3, :] = mlp_sum
    for copy in saves:
        copy.wait()


def forward_call(plans, raws, noisy, positions, basis, chosen):
    n = plans[0].devices
    zs = n // 8
    rows, few = noisy.shape[0], basis.shape[0]
    dma = pltpu.SemaphoreType.DMA
    np_, nb = len(plans), len(plans) + 1
    vm = pl.BlockSpec(memory_space=pltpu.VMEM)
    hbm = pl.BlockSpec(memory_space=pltpu.HBM)
    shape = jax.ShapeDtypeStruct
    saved_shapes = [shape((rows, width), kind) for _, width, kind in SAVED]
    out_shape = [shape((n * p.per, ROWS, LANES), low_type) for p in plans]
    out_shape += [shape((rows, D), full_type)] * (LAYERS + 1)
    out_shape += [shape((few, 6 * D), full_type)] * LAYERS + [shape((8, D), full_type)] * LAYERS
    out_shape += [shape((few, D), low_type), shape((few, D), full_type), shape((few, D), full_type)]
    out_shape += saved_shapes * LAYERS
    scratch = [pltpu.VMEM((p.before + 8, LANES), full_type) for p in plans]
    scratch += [pltpu.VMEM((p.after, LANES), full_type) for p in plans]
    scratch += [pltpu.VMEM((p.per, ROWS, LANES), low_type) for p in plans]
    scratch += [dma((np_,)), dma((2 * np_,)), dma((2 * np_,)), dma, dma((6,)), dma((len(SAVED),))]
    scratch += [dma((nb,)), dma((nb * (2 * (zs - 1) + 10 * zs),)), dma((nb, 2, zs)), dma((nb, zs)), dma((nb, zs, 2))]
    scratch += [dma((nb, zs)), dma((nb, zs, 2)), dma((nb, zs, 2, 2))]
    results = pl.pallas_call(
        functools.partial(forward_kernel, plans, zs, rows),
        out_shape=out_shape,
        in_specs=[hbm] * np_ + [vm] * 4,
        out_specs=[hbm] * np_ + [vm] * (LAYERS + 1 + 2 * LAYERS + 3) + [hbm] * (len(SAVED) * LAYERS),
        scratch_shapes=scratch,
        compiler_params=pltpu.CompilerParams(collective_id=0, has_side_effects=True, vmem_limit_bytes=62 * MB),
        name="gather_and_forward",
    )(*raws, noisy, positions, basis, chosen)
    feed = iter(results)
    take = lambda count: [next(feed) for _ in range(count)]
    units, stream, mods, sums = take(np_), take(LAYERS + 1), take(LAYERS), take(LAYERS)
    modulator, condition, time_pre = take(3)
    return units, stream, mods, sums, modulator, condition, time_pre, [take(len(SAVED)) for _ in range(LAYERS)]


class Reduce:
    def __init__(self, here, buckets, first, buffers, sems, frees):
        self.here = here
        self.buckets = buckets
        self.first = first
        self.kept, self.two, self.three, self.four, self.ring, self.other, self.own = buffers
        self.s1, self.r1, self.s2, self.r2, self.s3, self.r3, self.s4, self.r4, self.load_sem = sems
        self.free_two, self.free_three, self.free_four = frees
        self.planes = list(range(1, here.zs)) + [0]
        self.groups = [(b, k) for b in range(len(buckets)) for k in self.planes]
        self.order = ((1, 1), (1, 0), (0, 1), (0, 0))

    def limits(self, b):
        return self.buckets[b][2:4]

    def meets(self, b, k):
        lo, hi = self.limits(b)
        if lo == 0 and hi == self.here.zs:
            return None
        plane = lax.rem(self.here.z + self.here.zs - k, self.here.zs)
        return (plane >= lo) & (plane < hi)

    def guarded(self, b, k, run):
        test = self.meets(b, k)
        if test is None:
            run()
        else:
            pl.when(test)(run)

    def overlaps(self, b, other):
        return self.limits(b)[0] < self.limits(other)[1] and self.limits(other)[0] < self.limits(b)[1]

    def before(self, b, k, run):
        for other in range(b - 1, -1, -1):
            if self.overlaps(b, other):
                self.guarded(b, k, lambda: self.guarded(other, k, run))
                return

    def after(self, b, k, run):
        for other in range(b + 1, len(self.buckets)):
            if self.overlaps(b, other):
                self.guarded(b, k, lambda: self.guarded(other, k, run))
                self.after_rest(b, other, k, run)
                return

    def after_rest(self, b, done, k, run):
        for other in range(done + 1, len(self.buckets)):
            if self.overlaps(b, other) and not self.overlaps(done, other):
                self.guarded(b, k, lambda: self.guarded(other, k, run))

    def slot(self, b, k, dy, dx, dc):
        plan, grads = self.buckets[b][:2]
        return grads.at[pl.ds(self.here.slot(k, dy, dx, dc) * plan.per, plan.per)]

    def landed(self, b, k, dy, dx):
        return self.first[b].at[self.here.zero + k, self.here.zero + dy, self.here.zero + dx]

    def sibling(self, b, k, dy, dx):
        here = self.here
        return remote(
            self.slot(b, k, dy, dx, 1), self.landed(b, k, dy, dx), pick(self.s1, here, b, k, dy, dx), pick(self.r1, here, b, k, dy, dx), here.cpeer
        )

    def open(self, b):
        for k in self.planes:

            def run(k=k):
                for dy, dx in self.order:
                    self.sibling(b, k, dy, dx).start()

            self.guarded(b, k, run)

    def half(self, b):
        return self.buckets[b][0].half

    def buffer(self, ref, b, *spots):
        view = ref.at[tuple(self.here.zero + s for s in spots)]
        return view.at[pl.ds(0, self.half(b))]

    def place_of(self, g, i):
        return 6 if i == 3 else 3 * (g % 2) + i

    def loads(self, g, i):
        b, k = self.groups[g]
        dy, dx = self.order[i]
        per = self.buckets[b][0].per
        here = self.here
        at = self.place_of(g, i)
        one = pltpu.make_async_copy(self.slot(b, k, dy, dx, 0), pick(self.ring, here, at).at[pl.ds(0, per)], pick(self.load_sem, here, at, 0))
        two = pltpu.make_async_copy(self.landed(b, k, dy, dx), pick(self.other, here, i % 2).at[pl.ds(0, per)], pick(self.load_sem, here, at, 1))
        return one, two

    def prepare(self, g, i):
        b, k = self.groups[g]
        dy, dx = self.order[i]
        one, two = self.loads(g, i)
        one.start()
        arrived(self.landed(b, k, dy, dx), pick(self.r1, self.here, b, k, dy, dx))
        two.start()

    def second(self, g, h, i):
        b, k = self.groups[g]
        dy, dx = self.order[i]
        here, size = self.here, self.half(b)
        src = pick(self.ring, here, self.place_of(g, i)).at[pl.ds(h * size, size)]
        far = dx if h == 0 else dy
        return remote(src, self.buffer(self.two[h], b, k, far), pick(self.s2, here, h, k, far), pick(self.r2, here, h, k, far), here.ypeer if h == 0 else here.xpeer)

    def sends_of(self, g):
        return [(h, i) for i, (dy, dx) in enumerate(self.order) for h in range(2) if (dy, dx)[h]]

    def add(self, b, dst, at, one, one_at, two, two_at):
        step = self.half(b) // 2

        def body(i, carry):
            span = lambda ref, off: ref[pl.ds(off + i * step, step)].astype(full_type)
            dst[pl.ds(at + i * step, step)] = (span(one, one_at) + span(two, two_at)).astype(low_type)
            return carry

        lax.fori_loop(0, 2, body, 0)

    def phase_one(self, g, i):
        b, k = self.groups[g]
        here, size = self.here, self.half(b)
        if i == 0:
            for h in range(2):
                to_free = lambda h=h: pl.semaphore_wait(pick(self.free_two, here, h, k), 1)
                self.before(b, k, to_free)

        def run():
            dy, dx = self.order[i]
            if i == 0:
                self.prepare(g, 0)
            if i < 3:
                self.prepare(g, i + 1)
            for copy in self.loads(g, i):
                copy.wait()
            mine, theirs = pick(self.ring, here, self.place_of(g, i)), pick(self.other, here, i % 2)
            for h, moves in enumerate((dy, dx)):
                if moves:
                    self.add(b, mine, h * size, mine, h * size, theirs, h * size)
                    self.second(g, h, i).start()
                else:
                    self.add(b, self.buffer(self.kept[h], b, k, dx if h == 0 else dy), 0, mine, h * size, theirs, h * size)

        self.guarded(b, k, run)

    def third(self, g, h):
        b, k = self.groups[g]
        here = self.here
        return remote(
            self.buffer(self.two[h], b, k, 1), self.buffer(self.three[h], b, k), pick(self.s3, here, h, k), pick(self.r3, here, h, k), here.xpeer if h == 0 else here.ypeer
        )

    def phase_two(self, g, far):
        b, k = self.groups[g]
        here = self.here
        if far:
            for h in range(2):
                self.before(b, k, lambda h=h: pl.semaphore_wait(pick(self.free_three, here, h, k), 1))

        def run():
            for h in range(2):
                got, kept = self.buffer(self.two[h], b, k, far), self.buffer(self.kept[h], b, k, far)
                arrived(got, pick(self.r2, here, h, k, far))
                if far:
                    self.add(b, got, 0, got, 0, kept, 0)
                    self.third(g, h).start()
                else:
                    self.add(b, kept, 0, got, 0, kept, 0)

        self.guarded(b, k, run)

    def last(self, g, h):
        b, k = self.groups[g]
        here = self.here
        return remote(self.buffer(self.three[h], b, k), self.buffer(self.four, b, h, k - 1), pick(self.s4, here, h, k - 1), pick(self.r4, here, h, k - 1), here.below(k))

    def phase_three(self, g):
        b, k = self.groups[g]
        here, size = self.here, self.half(b)
        if k:
            self.before(b, k, lambda: pl.semaphore_wait(pick(self.free_four, here, k - 1), 1))

        def run():
            for h in range(2):
                got, kept = self.buffer(self.three[h], b, k), self.buffer(self.kept[h], b, k, 0)
                arrived(got, pick(self.r3, here, h, k))
                if k:
                    self.add(b, got, 0, got, 0, kept, 0)
                    self.last(g, h).start()
                else:
                    step = size // 2

                    def body(i, carry):
                        part = pl.ds(i * step, step)
                        self.own[pl.ds(h * size + i * step, step)] = got[part].astype(full_type) + kept[part].astype(full_type)
                        return carry

                    lax.fori_loop(0, 2, body, 0)

        self.guarded(b, k, run)

    def release_one(self, g):
        b, k = self.groups[g]

        def run():
            for h, i in self.sends_of(g):
                self.second(g, h, i).wait_send()

        self.guarded(b, k, run)

    def release_two(self, g):
        b, k = self.groups[g]
        here = self.here

        def run():
            for h in range(2):
                self.third(g, h).wait_send()
                if k:
                    self.last(g, h).wait_send()

        self.guarded(b, k, run)

        def free():
            for h in range(2):
                two_from, three_from = (here.ypeer, here.xpeer) if h == 0 else (here.xpeer, here.ypeer)
                pl.semaphore_signal(pick(self.free_two, here, h, k), inc=1, device_id=(two_from,), device_id_type=MESH)
                pl.semaphore_signal(pick(self.free_three, here, h, k), inc=1, device_id=(three_from,), device_id_type=MESH)

        self.after(b, k, free)

    def collect(self, b, out, sem):
        here, size = self.here, self.half(b)

        def run():
            for h in range(2):
                for k in range(1, here.zs):
                    arrived(self.buffer(self.four, b, h, k - 1), pick(self.r4, here, h, k - 1))
                step = size // 2

                def body(i, carry):
                    part = pl.ds(i * step, step)
                    where = pl.ds(h * size + i * step, step)
                    value = self.own[where]
                    for k in range(1, here.zs):
                        value = value + self.buffer(self.four, b, h, k - 1)[part].astype(full_type)
                    self.own[where] = value
                    return carry

                lax.fori_loop(0, 2, body, 0)
            copy = pltpu.make_async_copy(self.own.at[pl.ds(0, 2 * size)], out, sem)
            copy.start()
            copy.wait()

        self.guarded(b, 0, run)

        def free():
            for k in range(1, here.zs):
                pl.semaphore_signal(pick(self.free_four, here, k - 1), inc=1, device_id=(here.above(k),), device_id_type=MESH)

        self.after(b, 0, free)

    def steps(self, g, outs, sem):
        zs = self.here.zs
        total = len(self.groups)
        found = []
        if (g - 2) % zs == 0 and 0 < (g - 2) // zs <= len(self.buckets):
            b = (g - 2) // zs - 1
            found.append(functools.partial(self.collect, b, outs[b], sem))
        if g < total:
            if g >= 2:
                found.append(lambda: self.release_one(g - 2))
            found += [functools.partial(self.phase_one, g, i) for i in range(4)]
        if 0 <= g - 1 < total:
            found += [functools.partial(self.phase_two, g - 1, 1), functools.partial(self.phase_two, g - 1, 0)]
        if 0 <= g - 2 < total:
            found.append(functools.partial(self.phase_three, g - 2))
        if 0 <= g - 3 < total:
            found.append(lambda: self.release_two(g - 3))
        return found

    def close(self):
        total = len(self.groups)
        for g in (total - 2, total - 1):
            self.release_one(g)
        for b in range(len(self.buckets)):
            for k in self.planes:

                def run(b=b, k=k):
                    for dy, dx in self.order:
                        self.sibling(b, k, dy, dx).wait_send()

                self.guarded(b, k, run)


def unpack_rows(here, plan, units_f, rows_f, flat_f, held_before):
    top = here.me * plan.share // LANES - plan.margin
    for origin, chunks, count, first_unit, _, _ in plan.segments:
        lo = jnp.clip(plan.per * here.me - held_before - first_unit, 0, count)
        hi = jnp.clip(plan.per * here.me + plan.per + plan.units_after - first_unit, 0, count)

        def unit(u, carry):
            block = u // chunks
            row = origin + block * (ROWS * chunks) + (u - block * chunks) - top
            value = units_f[first_unit + u - plan.per * here.me + held_before]
            if chunks == 1:
                rows_f[pl.ds(row, ROWS), :] = value
            else:
                rows_f[pl.ds(row, ROWS, stride=chunks), :] = value
            return carry

        lax.fori_loop(lo, hi, unit, 0)
    shift = lax.rem(here.me * plan.share, LANES)
    turn = lax.rem(LANES - shift, LANES)
    lane = lax.broadcasted_iota(jnp.int32, (64, LANES), 1)
    spot = lax.broadcasted_iota(jnp.int32, (64, LANES), 0) * LANES + lane

    def unalign(i, squares):
        row = pl.multiple_of(i * 64, 64)
        level = pltpu.roll(rows_f[pl.ds(row + plan.margin, 64), :], turn, 1)
        below = pltpu.roll(rows_f[pl.ds(row + plan.margin + 1, 64), :], turn, 1)
        value = jnp.where(lane < LANES - shift, level, below)
        value = jnp.where(spot + row * LANES < plan.share, value, 0.0)
        flat_f[pl.ds(row, 64), :] = value
        return squares + jnp.sum((value * value).reshape(8, 8, LANES), axis=0)

    return lax.fori_loop(0, plan.raw // 64, unalign, jnp.zeros((8, LANES), full_type))


def put_row(stage, first, vector):
    for r in range(vector.shape[1] // LANES):
        stage[first + r : first + r + 1, :] = vector[:, r * LANES : (r + 1) * LANES]


B_Q, B_V, B_O, B_1, B_2 = 0, D, 2 * D, 3 * D, 3 * D + FF


def layer_backward_body(plan, rows, x_hbm, saved, units, grads, mod, grad, modulator_t, cond, held, sems, events):
    (qkv, heads, h_low, wide_f, tall_f, pre, w_1, w_2, w_qkv, w_o, d_qkv, g_low, slim, turned, dx, d_one, d_two, grad_mod, bias_out, bias_f, bias_low) = held
    load_sem, chunk_sem, out_sem = sems
    h1_h, qkv_h, heads_h, attn_h, middle_h, h2_h, pre_h, mlp_h = saved
    fetch = lambda i, src, dst: pltpu.make_async_copy(src, dst, load_sem.at[i])
    load_mlp, load_attn = fetch(0, mlp_h, wide_f), fetch(0, attn_h, wide_f)
    load_middle, load_x = fetch(1, middle_h, tall_f), fetch(1, x_hbm, tall_f)
    load_h2, load_h1 = fetch(2, h2_h, h_low), fetch(2, h1_h, h_low)
    load_heads, load_qkv = fetch(3, heads_h, heads), fetch(4, qkv_h, qkv)
    load_w_o, load_w_qkv = fetch(5, segment_ref(units, plan, 1), w_o), fetch(6, segment_ref(units, plan, 0), w_qkv)
    half = WIDE // ROWS
    wide_at = lambda j, base=0: pl.ds(pl.multiple_of(base + j * WIDE, LANES), WIDE)

    def chunk_loads(j):
        at = j % 2
        return (
            pltpu.make_async_copy(segment_ref(units, plan, 3).at[pl.ds(j * half, half)], w_2.at[at], chunk_sem.at[at, 0]),
            pltpu.make_async_copy(segment_ref(units, plan, 2).at[:, pl.ds(2 * j, 2)], w_1.at[at], chunk_sem.at[at, 1]),
            pltpu.make_async_copy(pre_h.at[:, wide_at(j)], pre.at[at], chunk_sem.at[at, 2]),
        )

    def mod_load(j):
        return pltpu.make_async_copy(segment_ref(units, plan, 4).at[:, pl.ds(2 * j, 2)], w_1.at[j % 2], chunk_sem.at[j % 2, 1])

    for copy in (load_mlp, load_h2) + chunk_loads(0) + (load_middle, load_w_o, load_heads, load_qkv, load_w_qkv):
        copy.start()
    part = lambda s, i: mod[pl.ds(s, 1), i * D : (i + 1) * D]
    per = SEQ // CHUNK
    grad_mod[...] = jnp.zeros(grad_mod.shape, full_type)
    bias_out[...] = jnp.zeros(bias_out.shape, full_type)

    def add_mod(s, i, value):
        grad_mod[pl.ds(s, 1), i * D : (i + 1) * D] += value

    def each_chunk(body):
        loop(rows // CHUNK, lambda i: body(pl.ds(pl.multiple_of(i * CHUNK, CHUNK), CHUNK), i // per))

    load_mlp.wait()

    def start_mlp(at, s):
        value = grad[at, :]
        low = (part(s, 5) * value).astype(low_type)
        g_low[at, :] = low
        bias_out[:, B_2 : B_2 + D] += rows_sum(low.astype(full_type))
        add_mod(s, 5, rows_sum(wide_f[at, :] * value))

    each_chunk(start_mlp)
    load_attn.start()
    load_h2.wait()
    turned[...] = h_low[...].astype(full_type).T.astype(low_type)
    load_h1.start()
    dx[...] = jnp.zeros(dx.shape, full_type)

    def outer(slot, segment, block, blocks, chunk, chunks, buffer):
        target = segment_ref(grads, plan, segment).at[pl.ds(block, blocks), pl.ds(chunk, chunks)]
        return pltpu.make_async_copy(buffer, target, out_sem.at[slot])

    def mlp_store(j, kind):
        at = j % 2
        if kind == 0:
            return outer(2 * at, 3, j * half, half, 0, D // LANES, d_one.at[at])
        return outer(2 * at + 1, 2, 0, D // ROWS, 2 * j, 2, d_two.at[at])

    steps = FF // WIDE

    def feed_back(j):
        at = j % 2

        @pl.when(j + 1 < steps)
        def _():
            for copy in chunk_loads(j + 1):
                copy.start()

        for copy in chunk_loads(j):
            copy.wait()

        @pl.when(j >= 2)
        def _():
            mlp_store(j - 2, 0).wait()
            mlp_store(j - 2, 1).wait()

        act, slope = gelu_parts(pre[at])
        grad_act = dot_nt(g_low[...], block_of(w_2.at[at], 0, half, 0, D // LANES))
        low = (grad_act * slope).astype(low_type)
        slim[...] = low
        bias_out[:, wide_at(j, B_1)] += rows_sum(low.astype(full_type))
        put_block(d_one.at[at], 0, 0, dot_tn(act.astype(low_type), g_low[...]))
        mlp_store(j, 0).start()
        put_block(d_two.at[at], 0, 0, dot(turned[...], slim[...]))
        mlp_store(j, 1).start()
        dx[...] += dot_nt(slim[...], block_of(w_1.at[at], 0, D // ROWS, 0, 2))

    busy_loop(steps, feed_back, events[0])
    load_middle.wait()
    load_attn.wait()

    def middle_back(at, s):
        value = dx[at, :]
        back, scaled = norm_back(tall_f[at, :], value, 1.0 + part(s, 4))
        add_mod(s, 3, rows_sum(value))
        add_mod(s, 4, rows_sum(scaled))
        total = grad[at, :] + back
        grad[at, :] = total
        low = (part(s, 2) * total).astype(low_type)
        g_low[at, :] = low
        bias_out[:, B_O : B_O + D] += rows_sum(low.astype(full_type))
        add_mod(s, 2, rows_sum(wide_f[at, :] * total))

    each_chunk(middle_back)
    load_x.start()
    load_w_o.wait()
    load_heads.wait()
    for j in (steps - 2, steps - 1):
        mlp_store(j, 0).wait()
        mlp_store(j, 1).wait()
    mod_load(0).start()
    turned[...] = heads[...].astype(full_type).T.astype(low_type)

    def wo_store(j):
        return outer(j % 2, 1, 0, D // ROWS, 2 * j, 2, d_two.at[j % 2])

    def out_back(j):
        @pl.when(j >= 2)
        def _():
            wo_store(j - 2).wait()

        put_block(d_two.at[j % 2], 0, 0, dot(turned[...], g_low[:, wide_at(j)]))
        wo_store(j).start()
        heads[:, wide_at(j)] = dot_nt(g_low[...], block_of(w_o, j * half, half, 0, D // LANES)).astype(low_type)

    busy_loop(D // WIDE, out_back, events[1])
    load_qkv.wait()
    first = head_masks()

    def attend_back(i):
        s, j = i // (HEADS // 2), i % (HEADS // 2)
        at = pl.ds(pl.multiple_of(s * SEQ, SEQ), SEQ)
        cut = lambda o: qkv[at, pl.ds(pl.multiple_of(o * D + j * LANES, LANES), LANES)]
        q, k, v = cut(0), cut(1), cut(2)
        go = heads[at, pl.ds(pl.multiple_of(j * LANES, LANES), LANES)]
        q = q * jnp.asarray(HD ** (-0.5), low_type)
        zero = jnp.zeros_like(q)
        dq, dk, dv = [], 0.0, 0.0
        for mask in (first, ~first):
            q_h, go_h = jnp.where(mask, q, zero), jnp.where(mask, go, zero)
            probs = softmax_f32(dot_nt(q_h, k))
            grad_probs = dot_nt(go_h, v)
            dv = dv + dot_tn(probs.astype(low_type), go_h)
            inner = jnp.sum(probs * grad_probs, axis=-1, keepdims=True)
            ds = (probs * (grad_probs - inner)).astype(low_type)
            dq.append(dot(ds, k) * HD ** (-0.5))
            dk = dk + dot_tn(ds, q_h)
        for o, value in enumerate((jnp.where(first, dq[0], dq[1]), dk, dv)):
            low = value.astype(low_type)
            d_qkv[at, pl.ds(pl.multiple_of(o * D + j * LANES, LANES), LANES)] = low
            if o != 1:
                start = (B_Q if o == 0 else B_V) + j * LANES
                bias_out[:, pl.ds(pl.multiple_of(start, LANES), LANES)] += rows_sum(low.astype(full_type))

    busy_loop(attention_pairs(rows), attend_back, events[2])
    load_h1.wait()
    load_w_qkv.wait()
    wo_store(1).wait()
    wo_store(2).wait()
    turned[...] = h_low[...].astype(full_type).T.astype(low_type)
    dx[...] = jnp.zeros(dx.shape, full_type)

    def qkv_store(j):
        return outer(j % 2, 0, 0, D // ROWS, 2 * j, 2, d_two.at[j % 2])

    def project_back(j):
        @pl.when(j >= 2)
        def _():
            qkv_store(j - 2).wait()

        put_block(d_two.at[j % 2], 0, 0, dot(turned[...], d_qkv[:, wide_at(j)]))
        qkv_store(j).start()
        dx[...] += dot_nt(d_qkv[:, wide_at(j)], block_of(w_qkv, 0, D // ROWS, 2 * j, 2))

    count = 3 * D // WIDE
    busy_loop(count, project_back, events[3])
    load_x.wait()

    def input_back(at, s):
        value = dx[at, :]
        back, scaled = norm_back(tall_f[at, :], value, 1.0 + part(s, 1))
        add_mod(s, 0, rows_sum(value))
        add_mod(s, 1, rows_sum(scaled))
        grad[at, :] += back

    each_chunk(input_back)
    for j in (count - 2, count - 1):
        qkv_store(j).wait()
    mod_steps = 6 * D // WIDE

    def mod_store(j):
        return outer(j % 2, 4, 0, D // ROWS, 2 * j, 2, d_two.at[j % 2])

    def mod_back(j):
        @pl.when(j + 1 < mod_steps)
        def _():
            mod_load(j + 1).start()

        mod_load(j).wait()

        @pl.when(j >= 2)
        def _():
            mod_store(j - 2).wait()

        low = grad_mod[:, wide_at(j)].astype(low_type)
        put_block(d_two.at[j % 2], 0, 0, dot(modulator_t[...], low))
        mod_store(j).start()
        cond[...] += dot_nt(low, block_of(w_1.at[j % 2], 0, D // ROWS, 0, 2))

    busy_loop(mod_steps, mod_back, events[4])
    bias_f[...] = jnp.zeros(bias_f.shape, full_type)
    bias_first = plan.segments[5][3]
    low_sum = rows_sum(grad_mod[...].astype(low_type).astype(full_type))
    for number, value in zip(range(5, 11), (bias_out[:, B_Q : B_Q + D], bias_out[:, B_V : B_V + D], bias_out[:, B_O : B_O + D], bias_out[:, B_1 : B_1 + FF], bias_out[:, B_2 : B_2 + D], low_sum)):
        put_row(bias_f, (plan.segments[number][3] - bias_first) * ROWS, value)
    bias_low[...] = bias_f[...].astype(low_type).reshape(bias_low.shape)
    store = pltpu.make_async_copy(bias_low, grads.at[pl.ds(bias_first, bias_low.shape[0])], out_sem.at[2])
    store.start()
    store.wait()
    for j in (mod_steps - 2, mod_steps - 1):
        mod_store(j).wait()


def backward_kernel(plans, zs, rows, *refs):
    np_ = len(plans)
    feed = iter(refs)
    take = lambda count: tuple(next(feed) for _ in range(count))
    one = lambda: next(feed)
    one()
    units = take(np_)
    stream = take(LAYERS)
    saved = [take(len(SAVED)) for _ in range(LAYERS)]
    grad_in, = take(1)
    mods = take(LAYERS)
    modulator, condition, time_pre, cond_in, noisy, basis, chosen, stats_in = take(8)
    root_grads = one()
    layer_grads = take(LAYERS)
    flats = take(np_)
    stats_out = one()
    first = take(np_ + 1)
    own_units = take(np_)
    halo_before, halo_after = take(np_), take(np_)
    buffers = ((one(), one()), (one(), one()), (one(), one()), one(), one(), one(), one())
    total, total_in = take(2)
    sems = take(9)
    frees = take(3)
    load_sem, chunk_sem, out_sem, own_sem, halo_s, halo_r, ss, sr = take(8)
    here = Place(zs)
    here.greet()
    root = plans[0]
    front_units = root.segments[FRONT][3]
    front_planes = min(zs, -(-front_units // (8 * root.per)))
    layers = list(reversed(range(LAYERS)))
    buckets = [(root, root_grads, front_planes, zs)]
    buckets += [(plans[1 + i], layer_grads[i], 0, zs) for i in layers]
    buckets += [(root, root_grads, 0, front_planes)]
    outs = [own_units[0]] + [own_units[1 + i] for i in layers] + [own_units[0]]
    work = Reduce(here, buckets, first, buffers, sems, frees)
    here.met()
    work.open(0)
    steps = [work.steps(g, outs, own_sem) for g in range(len(work.groups) + 4)]
    of_bucket = lambda b: [step for group in steps[b * zs : (b + 1) * zs] for step in group]

    def compute(grad, cond, modulator_t, *held):
        grad[...] = grad_in[...]
        cond[...] = cond_in[...]
        modulator_t[...] = modulator[...].astype(full_type).T.astype(low_type)
        for position, ordinal in enumerate(layers):
            layer_backward_body(
                plans[1 + ordinal], rows, stream[ordinal], saved[ordinal], units[1 + ordinal], layer_grads[ordinal],
                mods[ordinal], grad, modulator_t, cond, held, (load_sem, chunk_sem, out_sem), spread(of_bucket(position), (14, 3, 14, 8, 10)),
            )
            work.open(1 + position)
        embed_back(grad, cond)

    def embed_back(grad, cond):
        def run(front_w, front_f, front_low):
            load = pltpu.make_async_copy(units[0].at[pl.ds(root.segments[4][3], root.segments[4][2])], front_w, load_sem.at[0])
            load.start()
            events = spread(of_bucket(LAYERS), (1, 1, 1, 1))
            first_of = lambda number: root.segments[number][3]

            def put(number, value):
                chunks = value.shape[1] // LANES
                blocks = value.shape[0] // ROWS
                for b in range(blocks):
                    for c in range(chunks):
                        front_low[first_of(number) + b * chunks + c] = value[b * ROWS : (b + 1) * ROWS, c * LANES : (c + 1) * LANES].astype(low_type)

            def put_bias(number, value):
                front_f[...] = jnp.zeros(front_f.shape, full_type)
                put_row(front_f, 0, value)
                front_low[first_of(number)] = front_f[...].astype(low_type)

            for event in events[0]:
                event()
            low = grad[...].astype(low_type)
            put(0, dot_tn(noisy[...], low))
            put_bias(1, rows_sum(low.astype(full_type)))
            for event in events[1]:
                event()
            gate = silu_parts(condition[...])[1] * cond[...]
            g_low = gate.astype(low_type)
            pre = time_pre[...]
            act, slope = silu_parts(pre)
            put(4, dot_tn(act.astype(low_type), g_low))
            put_bias(5, rows_sum(g_low.astype(full_type)))
            few = g_low.shape[0]
            stacked = jnp.concatenate([gate[:, c * LANES : (c + 1) * LANES] for c in range(D // LANES)], axis=0)
            for event in events[2]:
                event()
            span = 16 * ROWS
            table_first, table_count = first_of(6), root.segments[6][2]
            for start in range(0, table_count * ROWS, span):
                size = min(span, table_count * ROWS - start)
                value = dot_tn(chosen[:, start : start + size], stacked.astype(low_type))
                front_low[table_first + start // ROWS : table_first + (start + size) // ROWS] = value.astype(low_type).reshape(size // ROWS, ROWS, LANES)
            load.wait()
            w_t2 = jnp.concatenate(
                [jnp.concatenate([front_w[b * (D // LANES) + c] for b in range(D // ROWS)], axis=0) for c in range(D // LANES)], axis=1
            )
            grad_pre = (dot_nt(g_low, w_t2) * slope).astype(low_type)
            put(2, dot_tn(basis[...], grad_pre))
            put_bias(3, rows_sum(grad_pre.astype(full_type)))
            store = pltpu.make_async_copy(front_low, root_grads.at[pl.ds(0, front_units)], load_sem.at[1])
            store.start()
            for event in events[3]:
                event()
            store.wait()

        pl.run_scoped(
            run,
            pltpu.VMEM((root.segments[4][2], ROWS, LANES), low_type),
            pltpu.VMEM((ROWS, LANES), full_type),
            pltpu.VMEM((front_units, ROWS, LANES), low_type),
        )

    plan = plans[1]
    bias_units = plan.units - plan.segments[5][3]
    f32 = lambda *dims: pltpu.VMEM(dims, full_type)
    bf16 = lambda *dims: pltpu.VMEM(dims, low_type)
    tile = (ROWS, LANES)
    few = modulator.shape[0]
    pl.run_scoped(
        compute,
        f32(rows, D), f32(few, D), bf16(D, few),
        bf16(rows, 3 * D), bf16(rows, D), bf16(rows, D), f32(rows, D), f32(rows, D), f32(2, rows, WIDE),
        bf16(2, D // ROWS, 2, *tile), bf16(2, WIDE // ROWS, D // LANES, *tile),
        segment_scratch(plan, 0), segment_scratch(plan, 1),
        bf16(rows, 3 * D), bf16(rows, D), bf16(rows, WIDE), bf16(D, rows), f32(rows, D),
        bf16(2, WIDE // ROWS, D // LANES, *tile), bf16(2, D // ROWS, 2, *tile),
        f32(few, 6 * D), f32(1, 4 * D + FF), f32(bias_units * ROWS, LANES), bf16(bias_units, *tile),
    )
    final = len(buckets) - 1
    work.open(final)

    def unpack(units_f, rows_f, flat_f):
        def halo(i):
            p = plans[i]
            forward = remote(own_units[i].at[pl.ds(p.per - p.units_before, p.units_before)], halo_before[i], halo_s.at[i, 0], halo_r.at[i, 0], here.following)
            backward = remote(own_units[i].at[pl.ds(0, p.units_after)], halo_after[i], halo_s.at[i, 1], halo_r.at[i, 1], here.prev)
            return forward, backward

        def finish(i):
            p = plans[i]
            base = p.units_before
            for copy in halo(i):
                copy.wait()
            parts = (
                pltpu.make_async_copy(halo_before[i], units_f.at[pl.ds(0, base)], load_sem.at[0]),
                pltpu.make_async_copy(own_units[i], units_f.at[pl.ds(base, p.per)], load_sem.at[1]),
                pltpu.make_async_copy(halo_after[i], units_f.at[pl.ds(base + p.per, p.units_after)], load_sem.at[2]),
            )
            for copy in parts:
                copy.start()
            for copy in parts:
                copy.wait()
            squares = unpack_rows(here, p, units_f, rows_f, flat_f, base)
            store = pltpu.make_async_copy(flat_f.at[pl.ds(0, p.raw)], flats[i], load_sem.at[3])
            store.start()
            store.wait()
            total[1] += squares

        total[0] = stats_in[...]
        total[1] = jnp.zeros((8, LANES), full_type)
        begun, done = {}, set()
        for g in range((LAYERS + 1) * zs, len(steps) + 1):
            for position, ordinal in enumerate(layers):
                i = 1 + ordinal
                if i not in begun and g > zs * (position + 2) + 2:
                    begun[i] = g
                    for copy in halo(i):
                        copy.start()
                elif i in begun and i not in done and g > begun[i]:
                    done.add(i)
                    finish(i)
            for step in steps[g] if g < len(steps) else ():
                step()
        for copy in halo(0):
            copy.start()
        finish(0)

    most = max(p.units_before + p.per + p.units_after for p in plans)
    pl.run_scoped(
        unpack,
        f32(most, *tile), f32(max(p.spread for p in plans), LANES), f32(max(p.raw for p in plans), LANES),
    )
    step = 0
    for to in ((here.cpeer,), (here.xpeer,), (here.ypeer,), tuple(here.above(k) for k in range(1, zs))):
        copies = []
        for peer in to:
            copies.append(remote(total, total_in.at[step], ss.at[step], sr.at[step], peer))
            copies[-1].start()
            step += 1
        for copy in copies:
            copy.wait()
        value = total[...]
        for i in range(len(to)):
            value = value + total_in[step - 1 - i]
        total[...] = value
    stats_out[...] = total[...]
    work.close()


def backward_call(plans, units, stream, saved, grad, mods, small, stats, root_grads):
    n = plans[0].devices
    zs = n // 8
    rows = grad.shape[0]
    np_, nb = len(plans), len(plans) + 1
    vm = pl.BlockSpec(memory_space=pltpu.VMEM)
    hbm = pl.BlockSpec(memory_space=pltpu.HBM)
    shape = jax.ShapeDtypeStruct
    dma, regular = pltpu.SemaphoreType.DMA, pltpu.SemaphoreType.REGULAR
    tile = (ROWS, LANES)
    layers = list(reversed(range(LAYERS)))
    order = [plans[0]] + [plans[1 + i] for i in layers] + [plans[0]]
    all_units = lambda p: shape((n * p.per,) + tile, low_type)
    out_shape = [all_units(p) for p in plans]
    out_shape += [shape((p.raw, LANES), full_type) for p in plans]
    out_shape += [shape((2, 8, LANES), full_type)]
    out_shape += [shape((zs, 2, 2, p.per) + tile, low_type) for p in order]
    out_shape += [shape((p.per,) + tile, full_type) for p in plans]
    out_shape += [shape((p.units_before,) + tile, full_type) for p in plans]
    out_shape += [shape((p.units_after,) + tile, full_type) for p in plans]
    most = max(p.per for p in plans)
    half = lambda *lead: pltpu.VMEM(lead + (most // 2,) + tile, low_type)
    hops = 2 + zs
    scratch = [half(zs, 2)] * 4 + [half(zs)] * 2 + [half(2, zs - 1)]
    scratch += [pltpu.VMEM((7, most) + tile, low_type), pltpu.VMEM((2, most) + tile, low_type)]
    scratch += [pltpu.VMEM((most,) + tile, full_type)]
    scratch += [pltpu.VMEM((2, 8, LANES), full_type), pltpu.VMEM((hops, 2, 8, LANES), full_type)]
    scratch += [dma((nb, zs, 2, 2))] * 2 + [dma((2, zs, 2))] * 2 + [dma((2, zs))] * 2 + [dma((2, zs - 1))] * 2 + [dma((7, 2))]
    scratch += [regular((2, zs)), regular((2, zs)), regular((zs - 1,))]
    scratch += [dma((7,)), dma((2, 3)), dma((4,)), dma, dma((np_, 2)), dma((np_, 2)), dma((hops,)), dma((hops,))]
    flat_saved = [array for group in saved for array in group]
    results = pl.pallas_call(
        functools.partial(backward_kernel, plans, zs, rows),
        out_shape=out_shape,
        in_specs=[hbm] * (1 + np_ + LAYERS + len(flat_saved)) + [vm] * (1 + LAYERS + len(small) + 1),
        out_specs=[hbm] * (2 * np_) + [vm] + [hbm] * (nb + 3 * np_),
        input_output_aliases={0: 0},
        scratch_shapes=scratch,
        compiler_params=pltpu.CompilerParams(collective_id=1, has_side_effects=True, vmem_limit_bytes=62 * MB),
        name="backward_and_reduce",
    )(root_grads, *units, *stream, *flat_saved, grad, *mods, *small, stats)
    return results[np_ : 2 * np_], results[2 * np_]


def model_step(layer_lists, pieces, latents, noise, times, labels, dropped, features, devices):
    sample_total = latents.shape[0] * devices
    residual, modulator, embed_saved = embed_forward(
        pieces, latents, noise, times, labels, dropped
    )
    loss_total = jnp.zeros((), full_type)
    inputs, kept, square_sums = [], [], []
    for ordinal in range(LAYERS):
        inputs.append(residual)
        residual, saved, sums = layer_forward(layer_lists[ordinal], residual, modulator)
        kept.append(saved)
        square_sums.append(sums)
        if ordinal + 1 == DEPTH_Z:
            part, proj_saved = projector_forward(pieces, residual, features)
            loss_total = loss_total + part
    target = noise - latents
    weight_t = 1.0 + 2.0 * times
    part, head_saved = head_forward(pieces, residual, modulator, target, weight_t)
    loss_total = loss_total + part
    grad_residual, grad_cond, head_grads = head_backward(
        pieces, head_saved, residual, modulator, weight_t, sample_total
    )
    layer_grads = [None] * LAYERS
    for ordinal in reversed(range(LAYERS)):
        if ordinal + 1 == DEPTH_Z:
            grad_proj, proj_grads = projector_backward(
                pieces, proj_saved, features, residual.shape[1], sample_total
            )
            grad_residual = grad_residual + grad_proj
        grad_residual, cond_part, layer_grads[ordinal] = layer_backward(
            layer_lists[ordinal], kept[ordinal], inputs[ordinal], modulator, grad_residual
        )
        grad_cond = grad_cond + cond_part
    embed_grads = embed_backward(pieces, embed_saved, grad_residual, grad_cond)
    return (loss_total, jnp.stack(square_sums), layer_grads, embed_grads + proj_grads + head_grads)


def adam_update(weight, grad, first, second, clip_factor):
    clipped = grad * clip_factor
    first_new = beta_one * first + (1.0 - beta_one) * clipped
    second_new = beta_two * second + (1.0 - beta_two) * clipped * clipped
    first_hat = first_new / (1.0 - beta_one**STEP)
    second_hat = second_new / (1.0 - beta_two**STEP)
    weight_new = weight - learn_rate * (
        first_hat / (jnp.sqrt(second_hat) + adam_eps) + decay_rate * weight
    )
    return (weight_new, first_new, second_new)


def vector_of(units, plan, number):
    _, _, count, first, shape, _ = plan.segments[number]
    flat = units[first : first + count].reshape(-1)[: math.prod(shape)]
    return flat.reshape(shape)


def matrix_of(units, plan, number):
    _, chunks, count, first, shape, _ = plan.segments[number]
    part = units[first : first + count].reshape(shape[0] // ROWS, chunks, ROWS, LANES)
    return part.transpose(0, 2, 1, 3).reshape(shape)


def units_of(grad, plan, number):
    _, chunks, count, _, shape, matrix = plan.segments[number]
    low = grad.astype(low_type)
    if matrix:
        low = low.reshape(shape[0] // ROWS, ROWS, chunks, LANES).transpose(0, 2, 1, 3)
        return low.reshape(count, ROWS, LANES)
    flat = jnp.pad(low.reshape(-1), ((0, count * UNIT - low.size),))
    return flat.reshape(count, ROWS, LANES)


def put_units(grads, plan, first_number, values):
    parts = [units_of(value, plan, first_number + i) for i, value in enumerate(values)]
    joined = jnp.concatenate(parts) if len(parts) > 1 else parts[0]
    return lax.dynamic_update_slice(grads, joined, (plan.segments[first_number][3], 0, 0))


def as_row(vector):
    return vector.astype(full_type).reshape(1, -1)


def by_kernels(plan, root_plan, layer_flat, root_flat, data, devices):
    latents, noise, times, labels, dropped, features = data
    samples = latents.shape[0]
    sample_total = samples * devices
    rows = samples * SEQ
    few = up(samples, ROWS)
    wide = D // LANES
    plans = (root_plan,) + (plan,) * LAYERS
    raws = [to_rows(root_flat, root_plan)]
    raws += [to_rows(layer_flat[ordinal], plan) for ordinal in range(LAYERS)]
    mixing = times[:, None, None]
    noisy_bf = ((1.0 - mixing) * latents + mixing * noise).astype(low_type)
    positions = jnp.tile(position_table(), (samples, 1))
    basis_bf = time_features(times).astype(low_type)
    classes = jnp.where(dropped == 1, CLS - 1, labels)
    extra = lambda value: jnp.pad(value, ((0, few - samples),) + ((0, 0),) * (value.ndim - 1))
    wanted = jnp.pad(classes, (0, few - samples), constant_values=-1)
    wanted = jnp.where(wanted < 0, -wide, wanted * wide)[None, :] + jnp.arange(wide)[:, None]
    wanted = jnp.where(wanted < 0, -1, wanted).reshape(-1, 1)
    table_rows = root_plan.segments[6][2] * ROWS
    chosen = (wanted == jnp.arange(table_rows, dtype=jnp.int32)[None, :]).astype(low_type)
    units, stream, mods, sums, modulator_rows, condition, time_pre, kept = forward_call(
        plans, raws, noisy_bf.reshape(rows, PD), positions, extra(basis_bf), chosen
    )
    root_units, *layer_units = units
    residual = stream[-1]
    target = jnp.pad((noise - latents).reshape(rows, PD), ((0, 0), (0, LANES - PD)))
    weight_t = jnp.broadcast_to(jnp.pad(1.0 + 2.0 * times, (0, 8 - samples))[:, None], (8, LANES))
    w_h = jnp.pad(vector_of(root_units, root_plan, 15), ((0, 0), (0, LANES - PD)))
    b_h = jnp.pad(as_row(vector_of(root_units, root_plan, 16)), ((0, 0), (0, LANES - PD)))
    biases = [as_row(vector_of(root_units, root_plan, i)) for i in (8, 10, 12, 14)]
    grad, losses, grad_cond, bias_grads, grad_w_h, root_grads = top_call(
        root_plan, sample_total, residual, features.reshape(rows, ZD), target, weight_t, modulator_rows, biases, w_h, b_h, root_units
    )
    loss_part = -proj_coeff / SEQ * losses[0, 0] + jnp.sum(losses[1]) / (SEQ * PD)
    cuts = jnp.split(bias_grads[0], (PH, 2 * PH, 2 * PH + ZD, 2 * PH + ZD + 2 * D))
    for number, value in zip((8, 10, 12), cuts):
        root_grads = put_units(root_grads, root_plan, number, [value])
    root_grads = put_units(root_grads, root_plan, 14, [cuts[3], grad_w_h[:, :PD], cuts[4][:PD]])
    square_sums = jnp.stack([jnp.sum(total[:3], axis=1) for total in sums])
    numbers = jnp.concatenate([loss_part[None], square_sums.reshape(-1)])
    stats = jnp.pad(numbers, (0, 8 * LANES - numbers.shape[0])).reshape(8, LANES)
    small = (modulator_rows, condition, time_pre, grad_cond, noisy_bf.reshape(rows, PD), extra(basis_bf), chosen)
    rows_out, stats = backward_call(
        plans, units, stream[:-1], kept, grad, mods, small, stats, root_grads
    )
    numbers = stats[0].reshape(-1)
    shard_root = rows_out[0].reshape(-1)[: root_plan.share]
    shard_layers = jnp.stack([r.reshape(-1)[: plan.share] for r in rows_out[1:]])
    stream_sums = numbers[1 : 1 + 3 * LAYERS].reshape(LAYERS, 3)
    return (shard_layers, shard_root, numbers[0], stream_sums, jnp.sum(stats[1]))


def by_collectives(layer_flat, root_flat, data, devices):
    whole = lambda part: lax.all_gather(part.astype(low_type), "fsdp", axis=0, tiled=True)
    layer_lists = [unflatten(whole(layer_flat[i]), layer_layout()) for i in range(LAYERS)]
    pieces = unflatten(whole(root_flat), root_layout())
    loss_part, square_sums, layer_grads, root_grads = model_step(
        layer_lists, pieces, *data, devices
    )

    def owned(grad_list, share):
        joined = jnp.concatenate([piece.reshape(-1) for piece in grad_list])
        joined = jnp.pad(joined, (0, share * devices - joined.shape[0]))
        return lax.psum_scatter(joined, "fsdp", scatter_dimension=0, tiled=True)

    shard_layers = jnp.stack([owned(grads, layer_flat.shape[1]) for grads in layer_grads])
    shard_root = owned(root_grads, root_flat.shape[0])
    local = jnp.sum(shard_layers * shard_layers) + jnp.sum(shard_root * shard_root)
    loss_sum, sums, square_total = lax.psum((loss_part, square_sums, local), "fsdp")
    return (shard_layers, shard_root, loss_sum, sums, square_total)


def shards(
    latents,
    noise,
    times,
    labels,
    dropped,
    features,
    layer_flat,
    layer_mean,
    layer_square,
    root_flat,
    root_mean,
    root_square,
):
    devices = lax.axis_size("fsdp")
    data = (latents, noise, times, labels, dropped, features)
    plan = Plan(layer_layout(), layer_flat.shape[1] * devices, devices)
    root_plan = Plan(root_layout(), root_flat.shape[0] * devices, devices)
    if devices % 8 == 0 and plan.fits and root_plan.fits:
        reduced = by_kernels(plan, root_plan, layer_flat, root_flat, data, devices)
    else:
        reduced = by_collectives(layer_flat, root_flat, data, devices)
    shard_layers, shard_root, loss_sum, stream_sums, square_total = reduced
    sample_total = latents.shape[0] * devices
    grad_norm = jnp.sqrt(square_total)
    clip_factor = clip_limit / jnp.maximum(grad_norm, clip_limit)
    activation_rms = jnp.sqrt(stream_sums / (sample_total * SEQ * D))
    new_layer, new_layer_mean, new_layer_square = adam_update(
        layer_flat, shard_layers, layer_mean, layer_square, clip_factor
    )
    new_root, new_root_mean, new_root_square = adam_update(
        root_flat, shard_root, root_mean, root_square, clip_factor
    )
    return (
        loss_sum,
        grad_norm,
        activation_rms,
        new_layer,
        new_layer_mean,
        new_layer_square,
        new_root,
        new_root_mean,
        new_root_square,
    )


def solution(mesh):
    in_specs = (
        P("fsdp", None, None),
        P("fsdp", None, None),
        P("fsdp"),
        P("fsdp"),
        P("fsdp"),
        P("fsdp", None, None),
        P(None, "fsdp"),
        P(None, "fsdp"),
        P(None, "fsdp"),
        P("fsdp"),
        P("fsdp"),
        P("fsdp"),
    )
    out_specs = (
        P(),
        P(),
        P(),
        P(None, "fsdp"),
        P(None, "fsdp"),
        P(None, "fsdp"),
        P("fsdp"),
        P("fsdp"),
        P("fsdp"),
    )
    return jax.shard_map(shards, mesh=mesh, in_specs=in_specs, out_specs=out_specs, check_vma=False)
```

```python
import functools
import math

import jax
import jax.numpy as jnp
from jax import lax
from jax.experimental import pallas as pl
from jax.experimental.pallas import tpu as pltpu
from jax.sharding import PartitionSpec as P

D = 768
HD = 64
FF = 3072
PD = 16
CLS = 1001
PH = 2048
ZD = 768
FREQ = 256
GRID = 16
LAYERS = 2
DEPTH_Z = 2
STEP = 10
SEQ = 256


norm_eps = 1e-06
clip_limit = 0.002
learn_rate = 0.08
beta_one = 0.5
beta_two = 0.5
adam_eps = 1e-08
decay_rate = 0.01
proj_coeff = 0.5
low_type = jnp.bfloat16
full_type = jnp.float32


LANES = 128
ROWS = 16
UNIT = LANES * ROWS
MESH = pl.DeviceIdType.MESH

def up(value, step):
    return -(-value // step) * step

class Plan:
    def __init__(self, layout, length, devices, reduced):
        self.length = length
        self.devices = devices
        self.share = length // devices
        self.segments = []
        offset = units = 0
        for shape in layout:
            amount = math.prod(shape)
            matrix = len(shape) == 2 and shape[0] % ROWS == 0 and shape[1] % LANES == 0
            chunks = shape[1] // LANES if matrix else 1
            count = up(amount, UNIT) // UNIT
            self.segments.append((offset // LANES, chunks, count, units, shape, matrix))
            offset += amount
            units += count
        self.units = units
        self.reduced = self.segments[reduced[0] : reduced[1]]
        self.moved = lambda u: self.reduced[0][3] <= u < self.reduced[-1][3] + self.reduced[-1][2]
        self.per = up(up(units, devices) // devices, 4)
        rows_of = []
        for base, chunks, count, _, _, _ in self.segments:
            for u in range(count):
                b, c = divmod(u, chunks)
                first = base + b * ROWS * chunks + c
                rows_of.append((first, first + (ROWS - 1) * chunks))
        before = after = 0
        for d in range(devices):
            start, stop = d * self.share // LANES, (d + 1) * self.share // LANES
            for lo, hi in rows_of[self.per * d : self.per * d + self.per]:
                before, after = max(before, start - lo), max(after, hi + 1 - stop)
        self.before, self.after = up(before, 8), up(after, 8)
        units_before = units_after = 0
        for u, (lo, hi) in enumerate(rows_of):
            if not self.moved(u):
                continue
            first = lo * LANES // self.share
            last = min(((hi + 1) * LANES - 1) // self.share, devices - 1)
            for d in range(first, last + 1):
                units_before = max(units_before, self.per * d - u)
                units_after = max(units_after, u + 1 - self.per * d - self.per)
        self.units_before, self.units_after = units_before, units_after
        self.half = self.per // 2
        self.raw = up(up(self.share, LANES) // LANES + 9, 64)
        self.ext = self.before + self.raw + self.after
        margin = tail = 0
        for d in range(devices):
            start = d * self.share // LANES
            lo = max(self.per * d - units_before, 0)
            for first, last in rows_of[lo : self.per * d + self.per + units_after]:
                margin, tail = max(margin, start - first), max(tail, last + 1 - start)
        self.margin = up(margin, 8)
        self.spread = up(max(tail, self.raw + 8), 8) + self.margin
        least = self.share // LANES
        self.fits = max(self.before, self.after) < least and max(units_before, units_after) < self.per

def place(index, zs):
    return index // 8, index // 4 % 2, index // 2 % 2, index % 2

def gather_kernel(plans, zs, *refs):
    nb = len(plans)
    raw_hbm = refs[:nb]
    outs = refs[nb : 2 * nb]
    raw, ext, tail, from_prev, from_next, slots = (refs[2 * nb + i * nb : 3 * nb + i * nb] for i in range(6))
    rest = refs[8 * nb :]
    load_sem, halo_send, halo_recv, own_sem, send_sem, zr, xa, xb, yb, ya, cr = rest
    n = zs * 8
    me = lax.axis_index("fsdp")
    z, y, x, c = place(me, zs)
    index = lambda zz, yy, xx, cc: ((zz * 2 + yy) * 2 + xx) * 2 + cc
    prev, following = lax.rem(me + n - 1, n), lax.rem(me + 1, n)
    xpeer, ypeer, cpeer = index(z, y, 1 - x, c), index(z, 1 - y, x, c), index(z, y, x, 1 - c)
    zpeer = [index(lax.rem(z + k, zs), y, x, c) for k in range(zs)]
    loads = []
    for b in range(nb):
        p = plans[b]
        loads.append(pltpu.make_async_copy(raw_hbm[b], raw[b].at[pl.ds(8, p.raw)], load_sem.at[b]))
        loads[b].start()
    barrier = pltpu.get_barrier_semaphore()
    peers = [prev, following, xpeer, ypeer, cpeer] + zpeer[1:]
    for peer in peers:
        pl.semaphore_signal(barrier, inc=1, device_id=(peer,), device_id_type=MESH)
    halos = []
    lane = lax.broadcasted_iota(jnp.int32, (64, LANES), 1)
    for b in range(nb):
        p = plans[b]
        shift = lax.rem(me * p.share, LANES)
        delta = (me + 1) * p.share // LANES - me * p.share // LANES
        raw[b][pl.ds(0, 8), :] = jnp.zeros((8, LANES), full_type)
        ext[b][pl.ds(0, p.before), :] = jnp.zeros((p.before, LANES), full_type)
        ext[b][pl.ds(p.before + p.raw, p.after), :] = jnp.zeros((p.after, LANES), full_type)
        loads[b].wait()

        def align(i, carry):
            row = pl.multiple_of(i * 64, 64)
            here = pltpu.roll(raw[b][pl.ds(row + 8, 64), :], shift, 1)
            above = pltpu.roll(raw[b][pl.ds(row + 7, 64), :], shift, 1)
            ext[b][pl.ds(row + p.before, 64), :] = jnp.where(lane >= shift, here, above)
            return carry

        lax.fori_loop(0, p.raw // 64, align, 0)
        tail[b][...] = ext[b][pl.ds(delta, p.before + 8), :]
        if b == 0:
            pl.semaphore_wait(barrier, len(peers))
        for s, (src, dst, to) in enumerate(((ext[b].at[pl.ds(p.before, p.after)], from_next[b], prev), (tail[b], from_prev[b], following))):
            copy = pltpu.make_async_remote_copy(src, dst, halo_send.at[2 * b + s], halo_recv.at[2 * b + s], device_id=(to,), device_id_type=MESH)
            copy.start()
            halos.append(copy)
    sends = []

    def send(src, dst, sem, to):
        copy = pltpu.make_async_remote_copy(src, dst, send_sem.at[len(sends)], sem, device_id=(to,), device_id_type=MESH)
        copy.start()
        sends.append(copy)

    def span(b, h):
        p = plans[b]
        return (0, p.half) if h == 0 else (p.half, p.per - p.half)

    def slot(k, dy, dx, dc):
        return index(lax.rem(z + zs - k, zs), 1 - y if dy else y, 1 - x if dx else x, 1 - c if dc else c)

    def part(b, h, k, dy, dx, dc=0):
        first, count = span(b, h)
        return outs[b].at[pl.ds(slot(k, dy, dx, dc) * plans[b].per + first, count)]

    def whole(b, k, dy, dx, dc=0):
        return outs[b].at[pl.ds(slot(k, dy, dx, dc) * plans[b].per, plans[b].per)]

    def arrived(ref, sem):
        pltpu.make_async_copy(ref, ref, sem).wait()

    owns = []
    for b in range(nb):
        p = plans[b]
        delta = (me + 1) * p.share // LANES - me * p.share // LANES
        for copy in halos[2 * b : 2 * b + 2]:
            copy.wait()
        ext[b][pl.ds(0, p.before + 8), :] += from_prev[b][...]
        ext[b][pl.ds(p.before + delta, p.after), :] += from_next[b][...]
        top = me * p.share // LANES - p.before
        for base, chunks, count, first_unit, _, _ in p.segments:
            lo = jnp.clip(p.per * me - first_unit, 0, count)
            hi = jnp.clip(p.per * me + p.per - first_unit, 0, count)

            def unit(u, carry):
                block = u // chunks
                row = base + block * (ROWS * chunks) + (u - block * chunks) - top
                if chunks == 1:
                    value = ext[b][pl.ds(row, ROWS), :]
                else:
                    value = ext[b][pl.ds(row, ROWS, stride=chunks), :]
                slots[b][first_unit + u - p.per * me] = value.astype(low_type)
                return carry

            lax.fori_loop(lo, hi, unit, 0)
        own = pltpu.make_async_copy(slots[b], whole(b, 0, 0, 0), own_sem.at[b])
        own.start()
        owns.append(own)
        mine = lambda h: slots[b].at[pl.ds(*span(b, h))]
        for k in range(1, zs):
            for h in range(2):
                send(mine(h), part(b, h, 0, 0, 0), zr.at[b, h, k], zpeer[k])
        send(mine(0), part(b, 0, 0, 0, 0), xa.at[b, 0], xpeer)
        send(mine(1), part(b, 1, 0, 0, 0), yb.at[b, 0], ypeer)
        send(mine(0), part(b, 0, 0, 0, 0), ya.at[b, 0, 0], ypeer)
        send(mine(1), part(b, 1, 0, 0, 0), xb.at[b, 0, 0], xpeer)
        send(slots[b], whole(b, 0, 0, 0), cr.at[b, 0, 0, 0], cpeer)
    for b in range(nb):
        for k in range(1, zs):
            arrived(part(b, 0, k, 0, 0), zr.at[b, 0, k])
            send(part(b, 0, k, 0, 0), part(b, 0, k, 0, 0), xa.at[b, k], xpeer)
            arrived(part(b, 1, k, 0, 0), zr.at[b, 1, k])
            send(part(b, 1, k, 0, 0), part(b, 1, k, 0, 0), yb.at[b, k], ypeer)
            send(part(b, 0, k, 0, 0), part(b, 0, k, 0, 0), ya.at[b, k, 0], ypeer)
            send(part(b, 1, k, 0, 0), part(b, 1, k, 0, 0), xb.at[b, k, 0], xpeer)
            send(whole(b, k, 0, 0), whole(b, k, 0, 0), cr.at[b, k, 0, 0], cpeer)
        for k in range(zs):
            arrived(part(b, 0, k, 0, 1), xa.at[b, k])
            send(part(b, 0, k, 0, 1), part(b, 0, k, 0, 1), ya.at[b, k, 1], ypeer)
            arrived(part(b, 1, k, 1, 0), yb.at[b, k])
            send(part(b, 1, k, 1, 0), part(b, 1, k, 1, 0), xb.at[b, k, 1], xpeer)
        for k in range(zs):
            arrived(part(b, 1, k, 0, 1), xb.at[b, k, 0])
            send(whole(b, k, 0, 1), whole(b, k, 0, 1), cr.at[b, k, 0, 1], cpeer)
            arrived(part(b, 0, k, 1, 0), ya.at[b, k, 0])
            send(whole(b, k, 1, 0), whole(b, k, 1, 0), cr.at[b, k, 1, 0], cpeer)
        for k in range(zs):
            arrived(part(b, 1, k, 1, 1), xb.at[b, k, 1])
            arrived(part(b, 0, k, 1, 1), ya.at[b, k, 1])
            send(whole(b, k, 1, 1), whole(b, k, 1, 1), cr.at[b, k, 1, 1], cpeer)
    for b in range(nb):
        owns[b].wait()
        for k in range(zs):
            for dy in range(2):
                for dx in range(2):
                    arrived(whole(b, k, dy, dx, 1), cr.at[b, k, dy, dx])
    for copy in sends:
        copy.wait_send()

def gather_units(plans, raws):
    n = plans[0].devices
    zs = n // 8
    nb = len(plans)
    per_bucket = 2 * (zs - 1) + 10 * zs
    dma = pltpu.SemaphoreType.DMA
    scratch = [pltpu.VMEM((p.raw + 8, LANES), full_type) for p in plans]
    scratch += [pltpu.VMEM((p.ext, LANES), full_type) for p in plans]
    scratch += [pltpu.VMEM((p.before + 8, LANES), full_type) for p in plans]
    scratch += [pltpu.VMEM((p.before + 8, LANES), full_type) for p in plans]
    scratch += [pltpu.VMEM((p.after, LANES), full_type) for p in plans]
    scratch += [pltpu.VMEM((p.per, ROWS, LANES), low_type) for p in plans]
    scratch += [dma((nb,)), dma((2 * nb,)), dma((2 * nb,)), dma((nb,)), dma((nb * per_bucket,))]
    scratch += [dma((nb, 2, zs)), dma((nb, zs)), dma((nb, zs, 2)), dma((nb, zs)), dma((nb, zs, 2)), dma((nb, zs, 2, 2))]
    return pl.pallas_call(
        functools.partial(gather_kernel, plans, zs),
        out_shape=[jax.ShapeDtypeStruct((n * p.per, ROWS, LANES), low_type) for p in plans],
        in_specs=[pl.BlockSpec(memory_space=pltpu.HBM)] * nb,
        out_specs=[pl.BlockSpec(memory_space=pltpu.HBM)] * nb,
        scratch_shapes=scratch,
        compiler_params=pltpu.CompilerParams(collective_id=0, has_side_effects=True, vmem_limit_bytes=48 * 1024 * 1024),
        name="gather_units",
    )(*raws)

AHEAD = 4


def reduce_kernel(plans, zs, *refs):
    nb = len(plans)
    take = lambda count: tuple(next(feed) for _ in range(count))
    feed = iter(refs)
    grads, (stats_in,) = take(nb), take(1)
    outs, (stats_out,), first = take(nb), take(1), take(nb)
    kept_a, kept_b, two_a, two_b, three_a, three_b, four = (take(nb) for _ in range(7))
    local, other = take(1)[0], take(1)[0]
    units_f, rows_f, flat_f = take(1)[0], take(1)[0], take(1)[0]
    from_prev, from_next = take(nb), take(nb)
    total, total_in = take(1)[0], take(1)[0]
    s1, r1, s2a, r2a, s2b, r2b, s3a, r3a, s3b, r3b, s4, r4, load_sem, halo_s, halo_r, out_sem, ss, sr = take(18)
    n = zs * 8
    me = lax.axis_index("fsdp")
    z, y, x, c = place(me, zs)
    index = lambda zz, yy, xx, cc: ((zz * 2 + yy) * 2 + xx) * 2 + cc
    prev, following = lax.rem(me + n - 1, n), lax.rem(me + 1, n)
    xpeer, ypeer, cpeer = index(z, y, 1 - x, c), index(z, 1 - y, x, c), index(z, y, x, 1 - c)
    below = lambda k: index(lax.rem(z + zs - k, zs), y, x, c)
    above = lambda k: index(lax.rem(z + k, zs), y, x, c)
    barrier = pltpu.get_barrier_semaphore()
    peers = [prev, following, xpeer, ypeer, cpeer] + [above(k) for k in range(1, zs)]
    for peer in peers:
        pl.semaphore_signal(barrier, inc=1, device_id=(peer,), device_id_type=MESH)
    pl.semaphore_wait(barrier, len(peers))

    def remote(src, dst, send_sem, recv_sem, to):
        return pltpu.make_async_remote_copy(src, dst, send_sem, recv_sem, device_id=(to,), device_id_type=MESH)

    def arrived(ref, sem):
        pltpu.make_async_copy(ref, ref, sem).wait()

    def slot(b, k, dy, dx, dc):
        where = index(lax.rem(z + zs - k, zs), 1 - y if dy else y, 1 - x if dx else x, 1 - c if dc else c)
        return grads[b].at[pl.ds(where * plans[b].per, plans[b].per)]

    order = ((1, 1), (1, 0), (0, 1), (0, 0))

    def sibling(b, k, dy, dx):
        return remote(slot(b, k, dy, dx, 1), first[b].at[k, dy, dx], s1.at[b, k, dy, dx], r1.at[b, k, dy, dx], cpeer)

    def add(p, dst, at, one, one_at, two, two_at):
        step = p.half // 2

        def body(i, carry):
            span = lambda ref, off: ref[pl.ds(off + i * step, step)].astype(full_type)
            dst[pl.ds(at + i * step, step)] = (span(one, one_at) + span(two, two_at)).astype(low_type)
            return carry

        lax.fori_loop(0, 2, body, 0)

    ring = local.shape[0]
    planes = list(range(1, zs)) + [0]
    used = []

    def send_of(b, h, k, dy, dx, src):
        if h == 0:
            return remote(src, two_a[b].at[k, dx], s2a.at[b, k, dx], r2a.at[b, k, dx], ypeer)
        return remote(src, two_b[b].at[k, dy], s2b.at[b, k, dy], r2b.at[b, k, dy], xpeer)

    steps = [(b, dy, dx, k) for b in range(nb) for k in planes for dy, dx in order]

    def loads(number):
        b, dy, dx, k = steps[number]
        at = number % ring
        p = plans[b]
        one = pltpu.make_async_copy(slot(b, k, dy, dx, 0), local.at[at, pl.ds(0, p.per)], load_sem.at[at, 0])
        two = pltpu.make_async_copy(first[b].at[k, dy, dx], other.at[number % 2, pl.ds(0, p.per)], load_sem.at[at, 1])
        return one, two

    pending = {}
    steps_args = lambda number: (steps[number][0], steps[number][3], steps[number][1], steps[number][2])

    def prepare(number):
        b, dy, dx, k = steps[number]
        for copy in pending.pop(number % ring, ()):
            copy.wait_send()
        one, two = loads(number)
        one.start()
        arrived(first[b].at[k, dy, dx], r1.at[b, k, dy, dx])
        two.start()

    def phase_one(number):
        b, dy, dx, k = steps[number]
        p = plans[b]
        at = number % ring
        if number == 0:
            for ahead in range(AHEAD):
                sibling(*steps_args(ahead)).start()
            prepare(0)
        if number + AHEAD < len(steps):
            sibling(*steps_args(number + AHEAD)).start()
        if number + 1 < len(steps):
            prepare(number + 1)
        for copy in loads(number):
            copy.wait()
        mine, theirs = local.at[at], other.at[number % 2]
        going = []
        if dy:
            add(p, mine, 0, mine, 0, theirs, 0)
            going.append(send_of(b, 0, k, dy, dx, local.at[at, pl.ds(0, p.half)]))
        else:
            add(p, kept_a[b].at[k, dx], 0, mine, 0, theirs, 0)
        if dx:
            add(p, mine, p.half, mine, p.half, theirs, p.half)
            going.append(send_of(b, 1, k, dy, dx, local.at[at, pl.ds(p.half, p.half)]))
        else:
            add(p, kept_b[b].at[k, dy], 0, mine, p.half, theirs, p.half)
        for copy in going:
            copy.start()
        pending[at] = going

    def three(b, h, k):
        if h == 0:
            return remote(two_a[b].at[k, 1], three_a[b].at[k], s3a.at[b, k], r3a.at[b, k], xpeer)
        return remote(two_b[b].at[k, 1], three_b[b].at[k], s3b.at[b, k], r3b.at[b, k], ypeer)

    def last(b, h, k):
        src = (three_a if h == 0 else three_b)[b].at[k]
        return remote(src, four[b].at[h, k - 1], s4.at[b, h, k - 1], r4.at[b, h, k - 1], below(k))

    def phase_two(b, k):
        p = plans[b]
        for far in (1, 0):
            for h, kept, two, sem in ((0, kept_a, two_a, r2a), (1, kept_b, two_b, r2b)):
                arrived(two[b].at[k, far], sem.at[b, k, far])
                if far:
                    add(p, two[b].at[k, 1], 0, two[b].at[k, 1], 0, kept[b].at[k, 1], 0)
                    three(b, h, k).start()
                else:
                    add(p, kept[b].at[k, 0], 0, two[b].at[k, 0], 0, kept[b].at[k, 0], 0)

    def phase_three(b, k):
        p = plans[b]
        for h, kept, got, sem in ((0, kept_a, three_a, r3a), (1, kept_b, three_b, r3b)):
            arrived(got[b].at[k], sem.at[b, k])
            if k:
                add(p, got[b].at[k], 0, got[b].at[k], 0, kept[b].at[k, 0], 0)
                last(b, h, k).start()

    def halo(b):
        p = plans[b]
        base = p.units_before
        held = units_f.at[b % 2]
        forward = remote(held.at[pl.ds(p.per, base)], from_prev[b], halo_s.at[b, 0], halo_r.at[b, 0], following)
        backward = remote(held.at[pl.ds(base, p.units_after)], from_next[b], halo_s.at[b, 1], halo_r.at[b, 1], prev)
        return forward, backward

    def collect(b):
        p = plans[b]
        base = p.units_before
        for h, kept, got in ((0, kept_a, three_a), (1, kept_b, three_b)):
            for k in range(1, zs):
                arrived(four[b].at[h, k - 1], r4.at[b, h, k - 1])
            step = p.half // 2

            def body(i, carry):
                part = pl.ds(i * step, step)
                value = kept[b][0, 0, part].astype(full_type) + got[b][0, part].astype(full_type)
                for k in range(1, zs):
                    value = value + four[b][h, k - 1, part].astype(full_type)
                units_f[b % 2, pl.ds(base + h * p.half + i * step, step)] = value
                return carry

            lax.fori_loop(0, 2, body, 0)
        for copy in halo(b):
            copy.start()

    def finish(b):
        p = plans[b]
        base = p.units_before
        for copy in halo(b):
            copy.wait()
        held = b % 2
        units_f[held, pl.ds(0, base)] = from_prev[b][...]
        units_f[held, pl.ds(base + p.per, p.units_after)] = from_next[b][...]
        top = me * p.share // LANES - p.margin
        for origin, chunks, count, first_unit, _, _ in p.segments:
            lo = jnp.clip(p.per * me - base - first_unit, 0, count)
            hi = jnp.clip(p.per * me + p.per + p.units_after - first_unit, 0, count)

            def unit(u, carry):
                block = u // chunks
                row = origin + block * (ROWS * chunks) + (u - block * chunks) - top
                value = units_f[held, first_unit + u - p.per * me + base]
                if chunks == 1:
                    rows_f[pl.ds(row, ROWS), :] = value
                else:
                    rows_f[pl.ds(row, ROWS, stride=chunks), :] = value
                return carry

            lax.fori_loop(lo, hi, unit, 0)
        shift = lax.rem(me * p.share, LANES)
        turn = lax.rem(LANES - shift, LANES)
        lane = lax.broadcasted_iota(jnp.int32, (64, LANES), 1)
        spot = lax.broadcasted_iota(jnp.int32, (64, LANES), 0) * LANES + lane
        if b:
            pltpu.make_async_copy(flat_f.at[pl.ds(0, plans[b - 1].raw)], outs[b - 1], out_sem.at[b - 1]).wait()

        def unalign(i, squares):
            row = pl.multiple_of(i * 64, 64)
            here = pltpu.roll(rows_f[pl.ds(row + p.margin, 64), :], turn, 1)
            below_row = pltpu.roll(rows_f[pl.ds(row + p.margin + 1, 64), :], turn, 1)
            value = jnp.where(lane < LANES - shift, here, below_row)
            value = jnp.where(spot + row * LANES < p.share, value, 0.0)
            flat_f[pl.ds(row, 64), :] = value
            return squares + jnp.sum((value * value).reshape(8, 8, LANES), axis=0)

        squares = lax.fori_loop(0, p.raw // 64, unalign, jnp.zeros((8, LANES), full_type))
        pltpu.make_async_copy(flat_f.at[pl.ds(0, p.raw)], outs[b], out_sem.at[b]).start()
        return squares

    squares = jnp.zeros((8, LANES), full_type)
    groups = [(b, k) for b in range(nb) for k in planes]
    for g in range(len(groups) + 2):
        if g < len(groups):
            for number in range(4 * g, 4 * g + 4):
                phase_one(number)
        if 0 <= g - 1 < len(groups):
            phase_two(*groups[g - 1])
        if 0 <= g - 2 < len(groups):
            phase_three(*groups[g - 2])
        b = (g - 3) // zs - 1
        if (g - 3) % zs == 0 and 0 <= b < nb - 1:
            collect(b)
        b = (g - 4) // zs - 1
        if (g - 4) % zs == 0 and 0 <= b < nb - 1:
            squares = squares + finish(b)
    collect(nb - 1)
    squares = squares + finish(nb - 1)
    pltpu.make_async_copy(flat_f.at[pl.ds(0, plans[nb - 1].raw)], outs[nb - 1], out_sem.at[nb - 1]).wait()
    total[0] = stats_in[...]
    total[1] = squares
    step = 0
    for to in ((cpeer,), (xpeer,), (ypeer,), tuple(above(k) for k in range(1, zs))):
        copies = []
        for peer in to:
            copies.append(remote(total, total_in.at[step], ss.at[step], sr.at[step], peer))
            copies[-1].start()
            step += 1
        for copy in copies:
            copy.wait()
        value = total[...]
        for i in range(len(to)):
            value = value + total_in[step - 1 - i]
        total[...] = value
    stats_out[...] = total[...]
    for group in pending.values():
        for copy in group:
            copy.wait_send()
    for b in range(nb):
        for dy, dx in order:
            for k in range(zs):
                sibling(b, k, dy, dx).wait_send()
        for h in range(2):
            for k in range(zs):
                three(b, h, k).wait_send()
                if k:
                    last(b, h, k).wait_send()

def reduce_units(plans, grads, stats):
    n = plans[0].devices
    zs = n // 8
    nb = len(plans)
    dma = pltpu.SemaphoreType.DMA
    most = max(p.per for p in plans)
    tile = (ROWS, LANES)
    half = lambda p, *lead: pltpu.VMEM(lead + (p.half,) + tile, low_type)
    scratch = [half(p, zs, 2) for p in plans] + [half(p, zs, 2) for p in plans]
    scratch += [half(p, zs, 2) for p in plans] + [half(p, zs, 2) for p in plans]
    scratch += [half(p, zs) for p in plans] + [half(p, zs) for p in plans]
    scratch += [half(p, 2, zs - 1) for p in plans]
    ring = 8
    scratch += [pltpu.VMEM((ring, most) + tile, low_type), pltpu.VMEM((2, most) + tile, low_type)]
    scratch += [pltpu.VMEM((2, max(p.units_before + p.per + p.units_after for p in plans)) + tile, full_type)]
    scratch += [pltpu.VMEM((max(p.spread for p in plans), LANES), full_type)]
    scratch += [pltpu.VMEM((max(p.raw for p in plans), LANES), full_type)]
    scratch += [pltpu.VMEM((p.units_before,) + tile, full_type) for p in plans]
    scratch += [pltpu.VMEM((p.units_after,) + tile, full_type) for p in plans]
    hops = 2 + zs
    scratch += [pltpu.VMEM((2, 8, LANES), full_type), pltpu.VMEM((hops, 2, 8, LANES), full_type)]
    scratch += [dma((nb, zs, 2, 2))] * 2 + [dma((nb, zs, 2))] * 4 + [dma((nb, zs))] * 4
    scratch += [dma((nb, 2, zs - 1))] * 2 + [dma((ring, 2)), dma((nb, 2)), dma((nb, 2)), dma((nb,)), dma((hops,)), dma((hops,))]
    anywhere = pl.BlockSpec(memory_space=pltpu.HBM)
    inside = pl.BlockSpec(memory_space=pltpu.VMEM)
    out_shape = [jax.ShapeDtypeStruct((p.raw, LANES), full_type) for p in plans]
    out_shape += [jax.ShapeDtypeStruct((2, 8, LANES), full_type)]
    out_shape += [jax.ShapeDtypeStruct((zs, 2, 2, p.per) + tile, low_type) for p in plans]
    results = pl.pallas_call(
        functools.partial(reduce_kernel, plans, zs),
        out_shape=out_shape,
        in_specs=[anywhere] * nb + [inside],
        out_specs=[anywhere] * nb + [inside] + [anywhere] * nb,
        scratch_shapes=scratch,
        compiler_params=pltpu.CompilerParams(collective_id=1, has_side_effects=True, vmem_limit_bytes=62 * 1024 * 1024),
        name="reduce_units",
    )(*grads, stats)
    return results[:nb], results[nb]

def to_rows(flat, plan):
    padded = jnp.pad(flat, ((0, plan.raw * LANES - flat.shape[0]),))
    return padded.reshape(plan.raw, LANES)


def layer_layout():
    return [
        (D, 3 * D),
        (D, D),
        (D, FF),
        (FF, D),
        (D, 6 * D),
        (D,),
        (D,),
        (D,),
        (FF,),
        (D,),
        (6 * D,),
    ]


def root_layout():
    return [
        (PD, D),
        (D,),
        (FREQ, D),
        (D,),
        (D, D),
        (D,),
        (CLS, D),
        (D, PH),
        (PH,),
        (PH, PH),
        (PH,),
        (PH, ZD),
        (ZD,),
        (D, 2 * D),
        (2 * D,),
        (D, PD),
        (PD,),
    ]


def unflatten(vector, layout):
    pieces = []
    offset = 0
    for dimensions in layout:
        amount = math.prod(dimensions)
        pieces.append(vector[offset : offset + amount].reshape(dimensions))
        offset += amount
    return pieces


def flatten_grads(grad_list, length):
    joined = jnp.concatenate([piece.reshape(-1) for piece in grad_list])
    return jnp.concatenate([joined, jnp.zeros((length - joined.shape[0],), full_type)])


def position_table():
    quarter = D // 4
    frequency = 1.0 / 10000.0 ** (jnp.arange(quarter, dtype=jnp.float32) / quarter)
    coords = jnp.arange(GRID, dtype=jnp.float32)
    angles = coords[:, None] * frequency[None, :]
    one_axis = jnp.concatenate([jnp.sin(angles), jnp.cos(angles)], axis=1)
    row_part = jnp.repeat(one_axis, GRID, axis=0)
    col_part = jnp.tile(one_axis, (GRID, 1))
    return jnp.concatenate([row_part, col_part], axis=1)


def time_features(times_in):
    half_freq = FREQ // 2
    frequency = jnp.exp(-math.log(10000.0) * jnp.arange(half_freq, dtype=jnp.float32) / half_freq)
    angles = times_in[:, None] * frequency[None, :]
    return jnp.concatenate([jnp.cos(angles), jnp.sin(angles)], axis=1)


def modulated_norm(values, offsets, scales):
    centred = values - jnp.mean(values, axis=-1, keepdims=True)
    spread = jnp.mean(centred * centred, axis=-1, keepdims=True)
    return centred * lax.rsqrt(spread + norm_eps) * (1.0 + scales) + offsets


def softmax_rows(scores):
    row_max = jnp.max(scores, axis=-1, keepdims=True)
    exponent = jnp.exp(scores - row_max)
    return exponent / jnp.sum(exponent, axis=-1, keepdims=True)


def gelu_tanh(values):
    return jax.nn.gelu(values, approximate=True)


def cosine_rows(predicted, target):
    target_full = target.astype(full_type)
    inner_sum = jnp.sum(predicted * target_full, axis=-1)
    return (
        inner_sum
        * lax.rsqrt(jnp.sum(predicted * predicted, axis=-1) + norm_eps)
        * lax.rsqrt(jnp.sum(target_full * target_full, axis=-1) + norm_eps)
    )


def silu_back(values, grad_in):
    _, pullback = jax.vjp(jax.nn.silu, values)
    return pullback(grad_in)[0]


def linear_fwd(inputs, weight):
    leading = inputs.shape[:-1]
    product = jnp.dot(
        inputs.reshape(-1, inputs.shape[-1]), weight, preferred_element_type=full_type
    )
    return product.reshape(leading + (weight.shape[1],))


def linear_back(inputs, weight, grad_out, with_input=True):
    rows_in = inputs.reshape(-1, inputs.shape[-1])
    rows_out = grad_out.reshape(-1, grad_out.shape[-1])
    grad_weight = lax.dot_general(
        rows_in, rows_out, (((0,), (0,)), ((), ())), preferred_element_type=full_type
    )
    grad_bias = jnp.sum(rows_out.astype(full_type), axis=0)
    grad_in = None
    if with_input:
        grad_in = lax.dot_general(
            rows_out, weight, (((1,), (1,)), ((), ())), preferred_element_type=full_type
        ).reshape(inputs.shape)
    return (grad_in, grad_weight, grad_bias)


def layer_forward(weights, residual, modulator):
    (
        w_attn_in,
        w_attn_out,
        w_mlp_in,
        w_mlp_out,
        w_modulate,
        b_query,
        b_value,
        b_attn_out,
        b_mlp_in,
        b_mlp_out,
        b_modulate,
    ) = weights
    samples_mb, seq_len = (residual.shape[0], residual.shape[1])
    head_count = D // HD
    modulation = jnp.split((linear_fwd(modulator, w_modulate) + b_modulate)[:, None, :], 6, axis=-1)
    normed_a = modulated_norm(residual, modulation[0], modulation[1]).astype(low_type)
    bias_qkv = jnp.concatenate([b_query, jnp.zeros_like(b_query), b_value])
    qkv_low = (linear_fwd(normed_a, w_attn_in) + bias_qkv).astype(low_type)
    qkv_low = qkv_low.reshape(samples_mb, seq_len, 3, head_count, HD)
    query_bf, key_bf, value_bf = (qkv_low[:, :, 0], qkv_low[:, :, 1], qkv_low[:, :, 2])
    scores = jnp.einsum(
        "bqhd,bkhd->bhqk", query_bf, key_bf, preferred_element_type=full_type
    ) * HD ** (-0.5)
    attn_probs = softmax_rows(scores)
    probs_bf = attn_probs.astype(low_type)
    heads_bf = jnp.einsum("bhqk,bkhd->bqhd", probs_bf, value_bf, preferred_element_type=full_type)
    heads_bf = heads_bf.astype(low_type).reshape(samples_mb, seq_len, D)
    attn_out = linear_fwd(heads_bf, w_attn_out) + b_attn_out
    middle = residual + modulation[2] * attn_out
    normed_m = modulated_norm(middle, modulation[3], modulation[4]).astype(low_type)
    mlp_pre = linear_fwd(normed_m, w_mlp_in) + b_mlp_in
    act_bf = gelu_tanh(mlp_pre).astype(low_type)
    mlp_out = linear_fwd(act_bf, w_mlp_out) + b_mlp_out
    residual_out = middle + modulation[5] * mlp_out
    square_sums = jnp.stack(
        [
            jnp.sum(residual_out * residual_out),
            jnp.sum(attn_out * attn_out),
            jnp.sum(mlp_out * mlp_out),
        ]
    )
    saved = (
        modulation,
        normed_a,
        query_bf,
        key_bf,
        value_bf,
        attn_probs,
        probs_bf,
        heads_bf,
        attn_out,
        middle,
        normed_m,
        mlp_pre,
        act_bf,
        mlp_out,
    )
    return (residual_out, saved, square_sums)


def layer_backward(weights, saved, residual, modulator, grad_out):
    w_attn_in, w_attn_out, w_mlp_in, w_mlp_out, w_modulate = weights[:5]
    (
        modulation,
        normed_a,
        query_bf,
        key_bf,
        value_bf,
        attn_probs,
        probs_bf,
        heads_bf,
        attn_out,
        middle,
        normed_m,
        mlp_pre,
        act_bf,
        mlp_out,
    ) = saved
    samples_mb, seq_len = (residual.shape[0], residual.shape[1])
    grad_mlp = (modulation[5] * grad_out).astype(low_type)
    grad_act, grad_w_mlp_out, grad_b_mlp_out = linear_back(act_bf, w_mlp_out, grad_mlp)
    _, gelu_pull = jax.vjp(gelu_tanh, mlp_pre)
    grad_pre = gelu_pull(grad_act)[0].astype(low_type)
    grad_normed_m, grad_w_mlp_in, grad_b_mlp_in = linear_back(normed_m, w_mlp_in, grad_pre)
    _, norm_pull_m = jax.vjp(modulated_norm, middle, modulation[3], modulation[4])
    grad_from_m, grad_shift_m, grad_scale_m = norm_pull_m(grad_normed_m)
    grad_middle = grad_out + grad_from_m
    grad_attn = (modulation[2] * grad_middle).astype(low_type)
    grad_heads, grad_w_attn_out, grad_b_attn_out = linear_back(heads_bf, w_attn_out, grad_attn)
    grad_heads_bf = grad_heads.astype(low_type).reshape(samples_mb, seq_len, D // HD, HD)
    grad_probs = jnp.einsum(
        "bqhd,bkhd->bhqk", grad_heads_bf, value_bf, preferred_element_type=full_type
    )
    grad_value = jnp.einsum(
        "bhqk,bqhd->bkhd", probs_bf, grad_heads_bf, preferred_element_type=full_type
    )
    grad_scores = attn_probs * (
        grad_probs - jnp.sum(attn_probs * grad_probs, axis=-1, keepdims=True)
    )
    grad_scores = grad_scores.astype(low_type)
    grad_query = jnp.einsum(
        "bhqk,bkhd->bqhd", grad_scores, key_bf, preferred_element_type=full_type
    ) * HD ** (-0.5)
    grad_key = jnp.einsum(
        "bhqk,bqhd->bkhd", grad_scores, query_bf, preferred_element_type=full_type
    ) * HD ** (-0.5)
    grad_qkv = jnp.stack([grad_query, grad_key, grad_value], axis=2).reshape(
        samples_mb, seq_len, 3 * D
    )
    grad_normed_a, grad_w_attn_in, grad_b_qkv = linear_back(
        normed_a, w_attn_in, grad_qkv.astype(low_type)
    )
    _, norm_pull_a = jax.vjp(modulated_norm, residual, modulation[0], modulation[1])
    grad_from_a, grad_shift_a, grad_scale_a = norm_pull_a(grad_normed_a)
    grad_gate_a = jnp.sum(attn_out * grad_middle, axis=1, keepdims=True)
    grad_gate_m = jnp.sum(mlp_out * grad_out, axis=1, keepdims=True)
    grad_mod = jnp.concatenate(
        [grad_shift_a, grad_scale_a, grad_gate_a, grad_shift_m, grad_scale_m, grad_gate_m], axis=-1
    )[:, 0, :].astype(low_type)
    grad_cond, grad_w_mod, grad_b_mod = linear_back(modulator, w_modulate, grad_mod)
    grad_list = [
        grad_w_attn_in,
        grad_w_attn_out,
        grad_w_mlp_in,
        grad_w_mlp_out,
        grad_w_mod,
        grad_b_qkv[:D],
        grad_b_qkv[2 * D :],
        grad_b_attn_out,
        grad_b_mlp_in,
        grad_b_mlp_out,
        grad_b_mod,
    ]
    return (grad_middle + grad_from_a, grad_cond, grad_list)


def embed_forward(pieces, latent_part, noise_part, times_part, labels_part, dropped_part):
    mixing = times_part[:, None, None]
    noisy_bf = ((1.0 - mixing) * latent_part + mixing * noise_part).astype(low_type)
    tokens = linear_fwd(noisy_bf, pieces[0]) + pieces[1] + position_table()
    basis_bf = time_features(times_part).astype(low_type)
    time_pre = linear_fwd(basis_bf, pieces[2]) + pieces[3]
    time_act = jax.nn.silu(time_pre).astype(low_type)
    time_emb = linear_fwd(time_act, pieces[4]) + pieces[5]
    classes = jnp.where(dropped_part == 1, CLS - 1, labels_part)
    onehot = (classes[:, None] == jnp.arange(CLS, dtype=jnp.int32)[None, :]).astype(low_type)
    condition = time_emb + jnp.dot(onehot, pieces[6], preferred_element_type=full_type)
    saved = (noisy_bf, basis_bf, time_pre, time_act, onehot, condition)
    return (tokens, jax.nn.silu(condition).astype(low_type), saved)


def embed_backward(pieces, saved, grad_tokens, grad_modulator):
    noisy_bf, basis_bf, time_pre, time_act, onehot, condition = saved
    grad_cond = silu_back(condition, grad_modulator)
    grad_table = lax.dot_general(
        onehot.astype(full_type),
        grad_cond,
        (((0,), (0,)), ((), ())),
        precision=lax.Precision.HIGHEST,
    )
    grad_time_act, grad_w_time_out, grad_b_time_out = linear_back(
        time_act, pieces[4], grad_cond.astype(low_type)
    )
    grad_time_pre = silu_back(time_pre, grad_time_act).astype(low_type)
    _, grad_w_time_in, grad_b_time_in = linear_back(basis_bf, pieces[2], grad_time_pre, False)
    _, grad_w_patch, grad_b_patch = linear_back(
        noisy_bf, pieces[0], grad_tokens.astype(low_type), False
    )
    return [
        grad_w_patch,
        grad_b_patch,
        grad_w_time_in,
        grad_b_time_in,
        grad_w_time_out,
        grad_b_time_out,
        grad_table,
    ]


def projector_forward(pieces, residual, features_part):
    residual_bf = residual.astype(low_type)
    pre_a = linear_fwd(residual_bf, pieces[7]) + pieces[8]
    act_a = jax.nn.silu(pre_a).astype(low_type)
    pre_b = linear_fwd(act_a, pieces[9]) + pieces[10]
    act_b = jax.nn.silu(pre_b).astype(low_type)
    predicted = linear_fwd(act_b, pieces[11]) + pieces[12]
    loss_part = -proj_coeff * jnp.sum(cosine_rows(predicted, features_part)) / residual.shape[1]
    return (loss_part, (residual_bf, pre_a, act_a, pre_b, act_b, predicted))


def projector_backward(pieces, saved, features_part, seq_len, sample_total):
    residual_bf, pre_a, act_a, pre_b, act_b, predicted = saved
    _, cosine_pull = jax.vjp(
        lambda predicted_in: cosine_rows(predicted_in, features_part), predicted
    )
    seed = jnp.full(predicted.shape[:2], -proj_coeff / (seq_len * sample_total), full_type)
    grad_pred = cosine_pull(seed)[0].astype(low_type)
    grad_act_b, grad_w_c, grad_b_c = linear_back(act_b, pieces[11], grad_pred)
    grad_pre_b = silu_back(pre_b, grad_act_b).astype(low_type)
    grad_act_a, grad_w_b, grad_b_b = linear_back(act_a, pieces[9], grad_pre_b)
    grad_pre_a = silu_back(pre_a, grad_act_a).astype(low_type)
    grad_residual, grad_w_a, grad_b_a = linear_back(residual_bf, pieces[7], grad_pre_a)
    return (grad_residual, [grad_w_a, grad_b_a, grad_w_b, grad_b_b, grad_w_c, grad_b_c])


def head_forward(pieces, residual, modulator, target, weight_t):
    modulation = (linear_fwd(modulator, pieces[13]) + pieces[14])[:, None, :]
    shift_f, scale_f = jnp.split(modulation, 2, axis=-1)
    normed = modulated_norm(residual, shift_f, scale_f).astype(low_type)
    deviation = linear_fwd(normed, pieces[15]) + pieces[16] - target
    loss_part = jnp.sum(weight_t * jnp.mean(deviation * deviation, axis=(1, 2)))
    return (loss_part, (shift_f, scale_f, normed, deviation))


def head_backward(pieces, saved, residual, modulator, weight_t, sample_total):
    shift_f, scale_f, normed, deviation = saved
    scaled = (
        2.0 * weight_t[:, None, None] / (deviation.shape[1] * deviation.shape[2] * sample_total)
    )
    grad_output = (scaled * deviation).astype(low_type)
    grad_normed, grad_w_head, grad_b_head = linear_back(normed, pieces[15], grad_output)
    _, pullback = jax.vjp(modulated_norm, residual, shift_f, scale_f)
    grad_residual, grad_shift, grad_scale = pullback(grad_normed)
    grad_mod = jnp.concatenate([grad_shift, grad_scale], axis=-1)[:, 0, :].astype(low_type)
    grad_cond, grad_w_mod, grad_b_mod = linear_back(modulator, pieces[13], grad_mod)
    return (grad_residual, grad_cond, [grad_w_mod, grad_b_mod, grad_w_head, grad_b_head])


WIDE = 2 * LANES
HEADS = D // HD
CHUNK = 64
MB = 1024 * 1024


def dot(one, two):
    return jnp.dot(one, two, preferred_element_type=full_type)


def dot_nt(one, two):
    return lax.dot_general(one, two, (((1,), (1,)), ((), ())), preferred_element_type=full_type)


def dot_tn(one, two):
    return lax.dot_general(one, two, (((0,), (0,)), ((), ())), preferred_element_type=full_type)


def block_of(w, block, blocks, chunk, chunks):
    pieces = [w[pl.ds(block, blocks), chunk + i].reshape(blocks * ROWS, LANES) for i in range(chunks)]
    return jnp.concatenate(pieces, axis=1) if chunks > 1 else pieces[0]


def put_block(out, block, chunk, value):
    blocks = value.shape[0] // ROWS
    for i in range(value.shape[1] // LANES):
        piece = value[:, i * LANES : (i + 1) * LANES].astype(low_type)
        out[pl.ds(block, blocks), chunk + i] = piece.reshape(blocks, ROWS, LANES)


def loop(count, body):
    lax.fori_loop(0, count, lambda i, carry: (body(i), carry)[1], 0)


def norm_parts(values):
    centred = values - jnp.mean(values, axis=-1, keepdims=True)
    spread = jnp.mean(centred * centred, axis=-1, keepdims=True)
    scale = lax.rsqrt(spread + norm_eps)
    return centred * scale, scale


def norm_back(values, grad, gain):
    hat, scale = norm_parts(values)
    inner = grad * gain
    mean_a = jnp.mean(inner, axis=-1, keepdims=True)
    mean_b = jnp.mean(inner * hat, axis=-1, keepdims=True)
    return scale * (inner - mean_a - hat * mean_b), grad * hat


def gelu_parts(values):
    root = math.sqrt(2.0 / math.pi)
    square = values * values
    bend = jnp.tanh(root * values * (1.0 + 0.044715 * square))
    half = 0.5 * (1.0 + bend)
    slope = half + 0.5 * values * (1.0 - bend * bend) * root * (1.0 + 3.0 * 0.044715 * square)
    return values * half, slope


def rows_sum(values):
    return jnp.sum(values, axis=0, keepdims=True)


def segment_ref(units, plan, number):
    _, chunks, count, first, shape, matrix = plan.segments[number]
    part = units.at[pl.ds(first, count)]
    if not matrix:
        return part
    return part.reshape(shape[0] // ROWS, chunks, ROWS, LANES)


def segment_scratch(plan, number):
    _, chunks, _, _, shape, _ = plan.segments[number]
    return pltpu.VMEM((shape[0] // ROWS, chunks, ROWS, LANES), low_type)


def attention_pairs(rows):
    return (rows // SEQ) * (HEADS // 2)


def head_masks():
    lane = lax.broadcasted_iota(jnp.int32, (SEQ, LANES), 1)
    return lane < HD


def softmax_f32(scores):
    exponent = jnp.exp(scores - jnp.max(scores, axis=-1, keepdims=True))
    return exponent * (1.0 / jnp.sum(exponent, axis=-1, keepdims=True))


def mods_kernel(plan, modulator, bias, units, out, w, sem):
    load = pltpu.make_async_copy(segment_ref(units, plan, 4), w, sem)
    load.start()
    load.wait()
    value = modulator[...]

    def body(j):
        cols = pl.ds(pl.multiple_of(j * WIDE, WIDE), WIDE)
        out[:, cols] = dot(value, block_of(w, 0, D // ROWS, 2 * j, 2)) + bias[:, cols]

    loop(6 * D // WIDE, body)


def mods_call(plan, modulator, bias, units):
    vm = pl.BlockSpec(memory_space=pltpu.VMEM)
    return pl.pallas_call(
        functools.partial(mods_kernel, plan),
        out_shape=jax.ShapeDtypeStruct((modulator.shape[0], 6 * D), full_type),
        in_specs=[vm, vm, pl.BlockSpec(memory_space=pltpu.HBM)],
        out_specs=vm,
        scratch_shapes=[segment_scratch(plan, 4), pltpu.SemaphoreType.DMA],
        compiler_params=pltpu.CompilerParams(vmem_limit_bytes=32 * MB),
        name="modulation",
    )(modulator, bias, units)


def mods_back_kernel(plan, modulator, grad, units, before, grads, cond, w, dw, sem):
    load = pltpu.make_async_copy(segment_ref(units, plan, 4), w, sem.at[0])
    load.start()
    turned = modulator[...].astype(full_type).T.astype(low_type)

    def weight(j):
        cols = pl.ds(pl.multiple_of(j * WIDE, WIDE), WIDE)
        put_block(dw, 0, 2 * j, dot(turned, grad[:, cols]))

    loop(6 * D // WIDE, weight)
    store = pltpu.make_async_copy(dw, segment_ref(grads, plan, 4), sem.at[1])
    store.start()
    load.wait()
    cond[...] = jnp.zeros(cond.shape, full_type)

    def back(j):
        cols = pl.ds(pl.multiple_of(j * WIDE, WIDE), WIDE)
        cond[...] += dot_nt(grad[:, cols], block_of(w, 0, D // ROWS, 2 * j, 2))

    loop(6 * D // WIDE, back)
    store.wait()


def mods_back_call(plan, modulator, grad, units, grads):
    vm = pl.BlockSpec(memory_space=pltpu.VMEM)
    anywhere = pl.BlockSpec(memory_space=pltpu.HBM)
    return pl.pallas_call(
        functools.partial(mods_back_kernel, plan),
        out_shape=[jax.ShapeDtypeStruct(grads.shape, low_type), jax.ShapeDtypeStruct((modulator.shape[0], D), full_type)],
        in_specs=[vm, vm, anywhere, anywhere],
        out_specs=[anywhere, vm],
        input_output_aliases={3: 0},
        scratch_shapes=[segment_scratch(plan, 4), segment_scratch(plan, 4), pltpu.SemaphoreType.DMA((2,))],
        compiler_params=pltpu.CompilerParams(vmem_limit_bytes=40 * MB),
        name="modulation_back",
    )(modulator, grad, units, grads)


SAVED = (("h1", D, low_type), ("qkv", 3 * D, low_type), ("heads", D, low_type), ("attn", D, full_type), ("middle", D, full_type), ("h2", D, low_type), ("pre", FF, full_type), ("mlp", D, full_type))


def layer_forward_kernel(plan, rows, x, mod, bias_qkv, bias_o, bias_1, bias_2, units, out, sums, *refs):
    ns = len(SAVED)
    saved_out = refs[:ns]
    h1, qkv, heads, attn, middle, h2, pre, mlp = refs[ns : 2 * ns]
    w_qkv, w_o, w_1, w_2, load_sem, save_sem = refs[2 * ns :]
    weights = (w_qkv, w_o, w_1, w_2)
    loads = [pltpu.make_async_copy(segment_ref(units, plan, i), weights[i], load_sem.at[i]) for i in range(4)]
    for copy in loads:
        copy.start()
    saves = [pltpu.make_async_copy(refs[ns + i], saved_out[i], save_sem.at[i]) for i in range(ns)]
    part = lambda s, i: mod[pl.ds(s, 1), i * D : (i + 1) * D]
    per = SEQ // CHUNK

    def norm_a(i):
        at = pl.ds(pl.multiple_of(i * CHUNK, CHUNK), CHUNK)
        s = i // per
        hat, _ = norm_parts(x[at, :])
        h1[at, :] = (hat * (1.0 + part(s, 1)) + part(s, 0)).astype(low_type)

    loop(rows // CHUNK, norm_a)
    saves[0].start()
    loads[0].wait()

    def project(j):
        cols = pl.ds(pl.multiple_of(j * WIDE, WIDE), WIDE)
        value = dot(h1[...], block_of(w_qkv, 0, D // ROWS, 2 * j, 2)) + bias_qkv[:, cols]
        qkv[:, cols] = value.astype(low_type)

    loop(3 * D // WIDE, project)
    saves[1].start()
    first = head_masks()

    def attend(i):
        s, j = i // (HEADS // 2), i % (HEADS // 2)
        at = pl.ds(pl.multiple_of(s * SEQ, SEQ), SEQ)
        cut = lambda o: qkv[at, pl.ds(pl.multiple_of(o * D + j * LANES, LANES), LANES)]
        q, k, v = cut(0), cut(1), cut(2)
        q = q * jnp.asarray(HD ** (-0.5), low_type)
        zero = jnp.zeros_like(q)
        halves = []
        for mask in (first, ~first):
            probs = softmax_f32(dot_nt(jnp.where(mask, q, zero), k)).astype(low_type)
            halves.append(dot(probs, v))
        heads[at, pl.ds(pl.multiple_of(j * LANES, LANES), LANES)] = jnp.where(first, halves[0], halves[1]).astype(low_type)

    loop(attention_pairs(rows), attend)
    saves[2].start()
    loads[1].wait()

    def project_out(j):
        cols = pl.ds(pl.multiple_of(j * WIDE, WIDE), WIDE)
        attn[:, cols] = dot(heads[...], block_of(w_o, 0, D // ROWS, 2 * j, 2)) + bias_o[:, cols]

    loop(D // WIDE, project_out)
    saves[3].start()
    zero_sum = jnp.zeros((1, D), full_type)

    def norm_m(i, total):
        at = pl.ds(pl.multiple_of(i * CHUNK, CHUNK), CHUNK)
        s = i // per
        value = attn[at, :]
        mid = x[at, :] + part(s, 2) * value
        middle[at, :] = mid
        hat, _ = norm_parts(mid)
        h2[at, :] = (hat * (1.0 + part(s, 4)) + part(s, 3)).astype(low_type)
        return total + rows_sum(value * value)

    attn_sum = lax.fori_loop(0, rows // CHUNK, norm_m, zero_sum)
    saves[4].start()
    saves[5].start()
    loads[2].wait()
    loads[3].wait()
    mlp[...] = jnp.broadcast_to(bias_2[...], (rows, D))

    def feed(j):
        cols = pl.ds(pl.multiple_of(j * WIDE, WIDE), WIDE)
        value = dot(h2[...], block_of(w_1, 0, D // ROWS, 2 * j, 2)) + bias_1[:, cols]
        pre[:, cols] = value
        act = gelu_parts(value)[0].astype(low_type)
        mlp[...] += dot(act, block_of(w_2, j * (WIDE // ROWS), WIDE // ROWS, 0, D // LANES))

    loop(FF // WIDE, feed)
    saves[6].start()
    saves[7].start()

    def finish(i, carry):
        at = pl.ds(pl.multiple_of(i * CHUNK, CHUNK), CHUNK)
        value = mlp[at, :]
        result = middle[at, :] + part(i // per, 5) * value
        out[at, :] = result
        return (carry[0] + rows_sum(result * result), carry[1] + rows_sum(value * value))

    out_sum, mlp_sum = lax.fori_loop(0, rows // CHUNK, finish, (zero_sum, zero_sum))
    sums[...] = jnp.zeros(sums.shape, full_type)
    sums[0:1, :] = out_sum
    sums[1:2, :] = attn_sum
    sums[2:3, :] = mlp_sum
    for copy in saves:
        copy.wait()


def layer_forward_call(plan, x, mod, biases, units):
    rows = x.shape[0]
    vm = pl.BlockSpec(memory_space=pltpu.VMEM)
    anywhere = pl.BlockSpec(memory_space=pltpu.HBM)
    dma = pltpu.SemaphoreType.DMA
    shapes = [((rows, width), kind) for _, width, kind in SAVED]
    results = pl.pallas_call(
        functools.partial(layer_forward_kernel, plan, rows),
        out_shape=[jax.ShapeDtypeStruct((rows, D), full_type), jax.ShapeDtypeStruct((8, D), full_type)]
        + [jax.ShapeDtypeStruct(*s) for s in shapes],
        in_specs=[vm] * 6 + [anywhere],
        out_specs=[vm, vm] + [anywhere] * len(SAVED),
        scratch_shapes=[pltpu.VMEM(*s) for s in shapes] + [segment_scratch(plan, i) for i in range(4)] + [dma((4,)), dma((len(SAVED),))],
        compiler_params=pltpu.CompilerParams(vmem_limit_bytes=56 * MB),
        name="layer_forward",
    )(x, mod, *biases, units)
    return results[0], results[1], results[2:]


def layer_backward_kernel(plan, rows, x, grad_in, mod, *refs):
    ns = len(SAVED)
    saved_hbm = refs[:ns]
    units, grad_out, grad_mod, bias_out, grads = refs[ns : ns + 5]
    h1, qkv, heads, attn, middle, h2, pre, mlp = refs[ns + 5 : 2 * ns + 5]
    w_qkv, w_o, w_1, w_2, d_qkv, g_low, wide, turned, dx, d_one, d_two, load_sem, save_sem, out_sem = refs[2 * ns + 5 :]
    weights = (w_qkv, w_o, w_1, w_2)
    inside = dict(zip(range(ns), refs[ns + 5 : 2 * ns + 5]))
    saves = [pltpu.make_async_copy(saved_hbm[i], inside[i], save_sem.at[i]) for i in range(ns)]
    loads = [pltpu.make_async_copy(segment_ref(units, plan, i), weights[i], load_sem.at[i]) for i in range(4)]
    for copy in (saves[7], saves[6], loads[3], saves[5], loads[2], saves[4], saves[3], loads[1], saves[2], saves[1], loads[0], saves[0]):
        copy.start()
    part = lambda s, i: mod[pl.ds(s, 1), i * D : (i + 1) * D]
    per = SEQ // CHUNK
    grad_mod[...] = jnp.zeros(grad_mod.shape, full_type)
    bias_out[...] = jnp.zeros(bias_out.shape, full_type)

    def add_mod(s, i, value):
        grad_mod[pl.ds(s, 1), i * D : (i + 1) * D] += value

    def each_chunk(body):
        loop(rows // CHUNK, lambda i: body(pl.ds(pl.multiple_of(i * CHUNK, CHUNK), CHUNK), i // per))

    B_Q, B_V, B_O, B_1, B_2 = 0, D, 2 * D, 3 * D, 3 * D + FF
    saves[7].wait()

    def start_mlp(at, s):
        grad = grad_in[at, :]
        low = (part(s, 5) * grad).astype(low_type)
        g_low[at, :] = low
        bias_out[:, B_2 : B_2 + D] += rows_sum(low.astype(full_type))
        add_mod(s, 5, rows_sum(mlp[at, :] * grad))

    each_chunk(start_mlp)
    saves[5].wait()
    turned[...] = h2[...].astype(full_type).T.astype(low_type)
    saves[6].wait()
    loads[3].wait()
    loads[2].wait()
    dx[...] = jnp.zeros(dx.shape, full_type)
    half = WIDE // ROWS

    def outer(slot, segment, block, blocks, chunk, chunks, buffer):
        target = segment_ref(grads, plan, segment).at[pl.ds(block, blocks), pl.ds(chunk, chunks)]
        return pltpu.make_async_copy(buffer, target, out_sem.at[slot])

    def mlp_store(j, kind):
        at = j % 2
        if kind == 0:
            return outer(2 * at, 3, j * half, half, 0, D // LANES, d_one.at[at])
        return outer(2 * at + 1, 2, 0, D // ROWS, 2 * j, 2, d_two.at[at])

    def feed_back(j):
        cols = pl.ds(pl.multiple_of(j * WIDE, WIDE), WIDE)
        at = j % 2

        @pl.when(j >= 2)
        def _():
            mlp_store(j - 2, 0).wait()
            mlp_store(j - 2, 1).wait()

        act, slope = gelu_parts(pre[:, cols])
        grad_act = dot_nt(g_low[...], block_of(w_2, j * half, half, 0, D // LANES))
        low = (grad_act * slope).astype(low_type)
        wide[...] = low
        bias_out[:, pl.ds(pl.multiple_of(B_1 + j * WIDE, WIDE), WIDE)] += rows_sum(low.astype(full_type))
        put_block(d_one.at[at], 0, 0, dot_tn(act.astype(low_type), g_low[...]))
        mlp_store(j, 0).start()
        put_block(d_two.at[at], 0, 0, dot(turned[...], wide[...]))
        mlp_store(j, 1).start()
        dx[...] += dot_nt(wide[...], block_of(w_1, 0, D // ROWS, 2 * j, 2))

    steps = FF // WIDE
    loop(steps, feed_back)
    saves[4].wait()
    saves[3].wait()

    def middle_back(at, s):
        grad = dx[at, :]
        back, scaled = norm_back(middle[at, :], grad, 1.0 + part(s, 4))
        add_mod(s, 3, rows_sum(grad))
        add_mod(s, 4, rows_sum(scaled))
        total = grad_in[at, :] + back
        grad_out[at, :] = total
        low = (part(s, 2) * total).astype(low_type)
        g_low[at, :] = low
        bias_out[:, B_O : B_O + D] += rows_sum(low.astype(full_type))
        add_mod(s, 2, rows_sum(attn[at, :] * total))

    each_chunk(middle_back)
    loads[1].wait()
    saves[2].wait()
    for j in (steps - 2, steps - 1):
        mlp_store(j, 0).wait()
        mlp_store(j, 1).wait()
    turned[...] = heads[...].astype(full_type).T.astype(low_type)

    def wo_store(j):
        return outer(j % 2, 1, 0, D // ROWS, 2 * j, 2, d_two.at[j % 2])

    def out_back(j):
        cols = pl.ds(pl.multiple_of(j * WIDE, WIDE), WIDE)

        @pl.when(j >= 2)
        def _():
            wo_store(j - 2).wait()

        put_block(d_two.at[j % 2], 0, 0, dot(turned[...], g_low[:, cols]))
        wo_store(j).start()
        heads[:, cols] = dot_nt(g_low[...], block_of(w_o, j * half, half, 0, D // LANES)).astype(low_type)

    loop(D // WIDE, out_back)
    saves[1].wait()
    first = head_masks()

    def attend_back(i):
        s, j = i // (HEADS // 2), i % (HEADS // 2)
        at = pl.ds(pl.multiple_of(s * SEQ, SEQ), SEQ)
        cut = lambda o: qkv[at, pl.ds(pl.multiple_of(o * D + j * LANES, LANES), LANES)]
        q, k, v = cut(0), cut(1), cut(2)
        go = heads[at, pl.ds(pl.multiple_of(j * LANES, LANES), LANES)]
        q = q * jnp.asarray(HD ** (-0.5), low_type)
        zero = jnp.zeros_like(q)
        dq, dk, dv = [], 0.0, 0.0
        for mask in (first, ~first):
            q_h, go_h = jnp.where(mask, q, zero), jnp.where(mask, go, zero)
            probs = softmax_f32(dot_nt(q_h, k))
            grad_probs = dot_nt(go_h, v)
            dv = dv + dot_tn(probs.astype(low_type), go_h)
            inner = jnp.sum(probs * grad_probs, axis=-1, keepdims=True)
            ds = (probs * (grad_probs - inner)).astype(low_type)
            dq.append(dot(ds, k) * HD ** (-0.5))
            dk = dk + dot_tn(ds, q_h)
        put = lambda o, value: d_qkv.at[at, pl.ds(pl.multiple_of(o * D + j * LANES, LANES), LANES)].set(value)
        for o, value in enumerate((jnp.where(first, dq[0], dq[1]), dk, dv)):
            low = value.astype(low_type)
            d_qkv[at, pl.ds(pl.multiple_of(o * D + j * LANES, LANES), LANES)] = low
            if o != 1:
                start = (B_Q if o == 0 else B_V) + j * LANES
                bias_out[:, pl.ds(pl.multiple_of(start, LANES), LANES)] += rows_sum(low.astype(full_type))

    loop(attention_pairs(rows), attend_back)
    saves[0].wait()
    loads[0].wait()
    wo_store(1).wait()
    wo_store(2).wait()
    turned[...] = h1[...].astype(full_type).T.astype(low_type)
    dx[...] = jnp.zeros(dx.shape, full_type)

    def qkv_store(j):
        return outer(j % 2, 0, 0, D // ROWS, 2 * j, 2, d_two.at[j % 2])

    def project_back(j):
        cols = pl.ds(pl.multiple_of(j * WIDE, WIDE), WIDE)

        @pl.when(j >= 2)
        def _():
            qkv_store(j - 2).wait()

        put_block(d_two.at[j % 2], 0, 0, dot(turned[...], d_qkv[:, cols]))
        qkv_store(j).start()
        dx[...] += dot_nt(d_qkv[:, cols], block_of(w_qkv, 0, D // ROWS, 2 * j, 2))

    count = 3 * D // WIDE
    loop(count, project_back)

    def input_back(at, s):
        grad = dx[at, :]
        back, scaled = norm_back(x[at, :], grad, 1.0 + part(s, 1))
        add_mod(s, 0, rows_sum(grad))
        add_mod(s, 1, rows_sum(scaled))
        grad_out[at, :] += back

    each_chunk(input_back)
    for j in (count - 2, count - 1):
        qkv_store(j).wait()


def layer_backward_call(plan, x, grad, mod, saved, units):
    rows = x.shape[0]
    vm = pl.BlockSpec(memory_space=pltpu.VMEM)
    anywhere = pl.BlockSpec(memory_space=pltpu.HBM)
    dma = pltpu.SemaphoreType.DMA
    shapes = [((rows, width), kind) for _, width, kind in SAVED]
    tile = (ROWS, LANES)
    return pl.pallas_call(
        functools.partial(layer_backward_kernel, plan, rows),
        out_shape=[
            jax.ShapeDtypeStruct((rows, D), full_type),
            jax.ShapeDtypeStruct((8, 6 * D), full_type),
            jax.ShapeDtypeStruct((1, 4 * D + FF), full_type),
            jax.ShapeDtypeStruct(units.shape, low_type),
        ],
        in_specs=[vm] * 3 + [anywhere] * (len(SAVED) + 1),
        out_specs=[vm, vm, vm, anywhere],
        scratch_shapes=[pltpu.VMEM(*s) for s in shapes]
        + [segment_scratch(plan, i) for i in range(4)]
        + [
            pltpu.VMEM((rows, 3 * D), low_type),
            pltpu.VMEM((rows, D), low_type),
            pltpu.VMEM((rows, WIDE), low_type),
            pltpu.VMEM((D, rows), low_type),
            pltpu.VMEM((rows, D), full_type),
            pltpu.VMEM((2, WIDE // ROWS, D // LANES) + tile, low_type),
            pltpu.VMEM((2, D // ROWS, 2) + tile, low_type),
            dma((4,)),
            dma((len(SAVED),)),
            dma((4,)),
        ],
        compiler_params=pltpu.CompilerParams(vmem_limit_bytes=60 * MB),
        name="layer_backward",
    )(x, grad, mod, *saved, units)


def sigmoid(values):
    return 1.0 / (1.0 + jnp.exp(-values))


def silu_parts(values):
    gate = sigmoid(values)
    return values * gate, gate * (1.0 + values * (1.0 - gate))


TOP = (7, 9, 11, 13)


def top_kernel(plan, rows, sample_total, x, features, target, weight_t, modulator, b_1, b_2, b_3, b_f, w_h, b_h, units, *refs):
    grad_x, stats, cond, bias_out, dw_h, grads = refs[:6]
    p_1, p_2, p_3, w_f, pre_a, act_a, pre_b, act_b, pred, low, g_b, g_a, hidden, modf, d_modf, stage, dw_f, load_sem, out_sem = refs[6:]
    weights = (p_1, p_2, p_3, w_f)
    loads = [pltpu.make_async_copy(segment_ref(units, plan, s), weights[i], load_sem.at[i]) for i, s in enumerate(TOP)]
    for copy in loads:
        copy.start()
    per = SEQ // CHUNK
    half = WIDE // ROWS
    stats[...] = jnp.zeros(stats.shape, full_type)
    bias_out[...] = jnp.zeros(bias_out.shape, full_type)
    d_modf[...] = jnp.zeros(d_modf.shape, full_type)
    A_1, A_2, A_3, A_F, A_H = 0, PH, 2 * PH, 2 * PH + ZD, 2 * PH + ZD + 2 * D
    wide_at = lambda j, base=0: pl.ds(pl.multiple_of(base + j * WIDE, LANES), WIDE)

    def each_chunk(body):
        loop(rows // CHUNK, lambda i: body(pl.ds(pl.multiple_of(i * CHUNK, CHUNK), CHUNK), i // per))

    def to_low(at, s):
        low[at, :] = x[at, :].astype(low_type)

    each_chunk(to_low)
    loads[0].wait()

    def first_layer(j):
        value = dot(low[...], block_of(p_1, 0, D // ROWS, 2 * j, 2)) + b_1[:, wide_at(j)]
        pre_a[:, wide_at(j)] = value
        act_a[:, wide_at(j)] = silu_parts(value)[0].astype(low_type)

    loop(PH // WIDE, first_layer)
    loads[1].wait()

    def second_layer(j):
        value = dot(act_a[...], block_of(p_2, 0, PH // ROWS, 2 * j, 2)) + b_2[:, wide_at(j)]
        pre_b[:, wide_at(j)] = value
        act_b[:, wide_at(j)] = silu_parts(value)[0].astype(low_type)

    loop(PH // WIDE, second_layer)
    loads[2].wait()

    def third_layer(j):
        pred[:, wide_at(j)] = dot(act_b[...], block_of(p_3, 0, PH // ROWS, 2 * j, 2)) + b_3[:, wide_at(j)]

    loop(ZD // WIDE, third_layer)
    seed = -proj_coeff / (SEQ * sample_total)

    def cosine(at, s):
        value = pred[at, :]
        want = features[at, :].astype(full_type)
        inner = jnp.sum(value * want, axis=-1, keepdims=True)
        scale_a = lax.rsqrt(jnp.sum(value * value, axis=-1, keepdims=True) + norm_eps)
        scale_b = lax.rsqrt(jnp.sum(want * want, axis=-1, keepdims=True) + norm_eps)
        both = scale_a * scale_b
        stats[0:1, 0:1] += jnp.sum(inner * both, axis=0, keepdims=True)
        grad = seed * (want * both - value * (inner * both * scale_a * scale_a))
        grad = grad.astype(low_type)
        hidden[at, :] = grad
        bias_out[:, A_3 : A_3 + ZD] += rows_sum(grad.astype(full_type))

    each_chunk(cosine)

    def store(segment, j, chunks):
        where = segment_ref(grads, plan, segment).at[pl.ds(j * half, half)]
        return pltpu.make_async_copy(stage.at[j % 2, :, pl.ds(0, chunks)], where, out_sem.at[j % 2])

    def stored(segment, j, chunks):
        @pl.when(j >= 2)
        def _():
            store(segment, j - 2, chunks).wait()

    def third_back(j):
        stored(11, j, ZD // LANES)
        put_block(stage.at[j % 2], 0, 0, dot_tn(act_b[:, wide_at(j)], hidden[...]))
        store(11, j, ZD // LANES).start()
        grad = dot_nt(hidden[...], block_of(p_3, j * half, half, 0, ZD // LANES))
        grad = (grad * silu_parts(pre_b[:, wide_at(j)])[1]).astype(low_type)
        g_b[:, wide_at(j)] = grad
        bias_out[:, wide_at(j, A_2)] += rows_sum(grad.astype(full_type))

    def drain(segment, count, chunks):
        for j in range(max(0, count - 2), count):
            store(segment, j, chunks).wait()

    loop(PH // WIDE, third_back)
    drain(11, PH // WIDE, ZD // LANES)
    span = 4 * LANES

    def second_back(j):
        stored(9, j, PH // LANES)
        for i in range(PH // span):
            put_block(stage.at[j % 2], 0, i * (span // LANES), dot_tn(act_a[:, wide_at(j)], g_b[:, i * span : (i + 1) * span]))
        store(9, j, PH // LANES).start()
        grad = dot_nt(g_b[...], block_of(p_2, j * half, half, 0, PH // LANES))
        grad = (grad * silu_parts(pre_a[:, wide_at(j)])[1]).astype(low_type)
        g_a[:, wide_at(j)] = grad
        bias_out[:, wide_at(j, A_1)] += rows_sum(grad.astype(full_type))

    loop(PH // WIDE, second_back)
    drain(9, PH // WIDE, PH // LANES)

    def first_back(j):
        stored(7, j, PH // LANES)
        for i in range(PH // span):
            put_block(stage.at[j % 2], 0, i * (span // LANES), dot_tn(low[:, wide_at(j)], g_a[:, i * span : (i + 1) * span]))
        store(7, j, PH // LANES).start()
        grad_x[:, wide_at(j)] = dot_nt(g_a[...], block_of(p_1, j * half, half, 0, PH // LANES))

    loop(D // WIDE, first_back)
    loads[3].wait()

    def final_mod(j):
        modf[:, wide_at(j)] = dot(modulator[...], block_of(w_f, 0, D // ROWS, 2 * j, 2)) + b_f[:, wide_at(j)]

    loop(2 * D // WIDE, final_mod)
    part = lambda s, i: modf[pl.ds(s, 1), i * D : (i + 1) * D]
    dw_h[...] = jnp.zeros(dw_h.shape, full_type)

    def head(at, s):
        hat, scale = norm_parts(x[at, :])
        gain = 1.0 + part(s, 1)
        normed = (hat * gain + part(s, 0)).astype(low_type)
        off = dot(normed, w_h[...]) + b_h[...] - target[at, :]
        weight = weight_t[pl.ds(s, 1), :]
        stats[1:2, :] += rows_sum(weight * off * off)
        grad = (2.0 * weight / (SEQ * PD * sample_total) * off).astype(low_type)
        bias_out[:, A_H : A_H + LANES] += rows_sum(grad.astype(full_type))
        dw_h[...] += dot_tn(normed, grad)
        back = dot_nt(grad, w_h[...])
        d_modf[pl.ds(s, 1), 0:D] += rows_sum(back)
        d_modf[pl.ds(s, 1), D : 2 * D] += rows_sum(back * hat)
        inner = back * gain
        mean_a = jnp.mean(inner, axis=-1, keepdims=True)
        mean_b = jnp.mean(inner * hat, axis=-1, keepdims=True)
        grad_x[at, :] += scale * (inner - mean_a - hat * mean_b)

    each_chunk(head)
    turned = modulator[...].astype(full_type).T.astype(low_type)
    cond[...] = jnp.zeros(cond.shape, full_type)

    def final_back(j):
        grad = d_modf[:, wide_at(j)].astype(low_type)
        bias_out[:, wide_at(j, A_F)] += rows_sum(grad.astype(full_type))
        put_block(dw_f, 0, 2 * j, dot(turned, grad))
        cond[...] += dot_nt(grad, block_of(w_f, 0, D // ROWS, 2 * j, 2))

    loop(2 * D // WIDE, final_back)
    last = pltpu.make_async_copy(dw_f, segment_ref(grads, plan, 13), out_sem.at[2])
    last.start()
    last.wait()
    drain(7, D // WIDE, PH // LANES)


def top_call(plan, sample_total, x, features, target, weight_t, modulator, biases, w_h, b_h, units):
    rows = x.shape[0]
    vm = pl.BlockSpec(memory_space=pltpu.VMEM)
    anywhere = pl.BlockSpec(memory_space=pltpu.HBM)
    dma = pltpu.SemaphoreType.DMA
    few = modulator.shape[0]
    f32 = lambda *shape: pltpu.VMEM(shape, full_type)
    bf16 = lambda *shape: pltpu.VMEM(shape, low_type)
    shape = lambda *dims: jax.ShapeDtypeStruct(dims, full_type)
    return pl.pallas_call(
        functools.partial(top_kernel, plan, rows, sample_total),
        out_shape=[
            shape(rows, D),
            shape(8, LANES),
            shape(few, D),
            shape(1, 2 * PH + ZD + 2 * D + LANES),
            shape(D, LANES),
            jax.ShapeDtypeStruct(units.shape, low_type),
        ],
        in_specs=[vm] * 11 + [anywhere],
        out_specs=[vm] * 5 + [anywhere],
        scratch_shapes=[segment_scratch(plan, s) for s in TOP]
        + [f32(rows, PH), bf16(rows, PH), f32(rows, PH), bf16(rows, PH), f32(rows, ZD), bf16(rows, D)]
        + [bf16(rows, PH), bf16(rows, PH), bf16(rows, ZD), f32(few, 2 * D), f32(few, 2 * D)]
        + [bf16(2, WIDE // ROWS, PH // LANES, ROWS, LANES), segment_scratch(plan, 13)]
        + [dma((4,)), dma((3,))],
        compiler_params=pltpu.CompilerParams(vmem_limit_bytes=60 * MB),
        name="projector_and_head",
    )(x, features, target, weight_t, modulator, *biases, w_h, b_h, units)


def busy_loop(count, body, events=()):
    size = max(1, -(-len(events) // count))

    def step(i):
        body(i)
        for first in range(0, len(events), size):

            @pl.when(i == first // size)
            def _():
                for event in events[first : first + size]:
                    event()

    loop(count, step)


def spread(events, weights):
    shares, done, total = [], 0, 0
    for weight in weights:
        total += weight
        upto = len(events) * total // sum(weights)
        shares.append(events[done:upto])
        done = upto
    return shares


def row_vector(units, rows):
    values = units.astype(full_type).reshape(-1, LANES)
    return jnp.concatenate([values[r : r + 1, :] for r in range(rows)], axis=1)


def pick(ref, here, *spots):
    return ref.at[tuple(here.zero + spot for spot in spots)]


class Place:
    def __init__(self, zs):
        self.zs = zs
        self.n = zs * 8
        self.me = lax.axis_index("fsdp")
        self.zero = self.me * 0
        self.z, self.y, self.x, self.c = place(self.me, zs)
        self.prev = lax.rem(self.me + self.n - 1, self.n)
        self.following = lax.rem(self.me + 1, self.n)
        self.xpeer = self.index(self.z, self.y, 1 - self.x, self.c)
        self.ypeer = self.index(self.z, 1 - self.y, self.x, self.c)
        self.cpeer = self.index(self.z, self.y, self.x, 1 - self.c)

    def index(self, z, y, x, c):
        return ((z * 2 + y) * 2 + x) * 2 + c

    def above(self, k):
        return self.index(lax.rem(self.z + k, self.zs), self.y, self.x, self.c)

    def below(self, k):
        return self.index(lax.rem(self.z + self.zs - k, self.zs), self.y, self.x, self.c)

    def slot(self, k, dy, dx, dc):
        z = lax.rem(self.z + self.zs - k, self.zs)
        flip = lambda value, change: 1 - value if change else value
        return self.index(z, flip(self.y, dy), flip(self.x, dx), flip(self.c, dc))

    def peers(self):
        return [self.prev, self.following, self.xpeer, self.ypeer, self.cpeer] + [self.above(k) for k in range(1, self.zs)]

    def greet(self):
        barrier = pltpu.get_barrier_semaphore()
        for peer in self.peers():
            pl.semaphore_signal(barrier, inc=1, device_id=(peer,), device_id_type=MESH)

    def met(self):
        pl.semaphore_wait(pltpu.get_barrier_semaphore(), len(self.peers()))


def remote(src, dst, send_sem, recv_sem, to):
    return pltpu.make_async_remote_copy(src, dst, send_sem, recv_sem, device_id=(to,), device_id_type=MESH)


def arrived(ref, sem):
    pltpu.make_async_copy(ref, ref, sem).wait()


class Gather:
    def __init__(self, here, buckets, sems):
        self.here = here
        self.buckets = buckets
        self.own_sem, self.send_sem, self.zr, self.xa, self.xb, self.yb, self.ya, self.cr = sems
        self.sent = []
        self.made = 0

    def guarded(self, b, k, run):
        plan, _, _, lo, hi = self.buckets[b]
        if lo == 0 and hi == self.here.zs:
            run()
            return
        source = lax.rem(self.here.z + self.here.zs - k, self.here.zs)
        pl.when((source >= lo) & (source < hi))(run)

    def sem(self, name, *spots):
        return lambda: pick(getattr(self, name), self.here, *spots)

    def send(self, b, k, src, dst, sem, to):
        number = self.made
        self.made += 1
        make = lambda: remote(src(), dst(), pick(self.send_sem, self.here, number), sem(), to())
        make().start()
        self.sent.append((b, k, make))

    def part(self, b, h, k, dy, dx, dc=0):
        plan, units = self.buckets[b][:2]
        return units.at[pl.ds(self.here.slot(k, dy, dx, dc) * plan.per + h * plan.half, plan.half)]

    def whole(self, b, k, dy, dx, dc=0):
        plan, units = self.buckets[b][:2]
        return units.at[pl.ds(self.here.slot(k, dy, dx, dc) * plan.per, plan.per)]

    def own_copy(self, b):
        return pltpu.make_async_copy(self.buckets[b][2], self.whole(b, 0, 0, 0), pick(self.own_sem, self.here, b))

    def start(self, b):
        here, slot = self.here, self.buckets[b][2]
        plan = self.buckets[b][0]

        def run():
            self.own_copy(b).start()
            mine = lambda h: lambda: slot.at[pl.ds(h * plan.half, plan.half)]
            to = lambda h: lambda: self.part(b, h, 0, 0, 0)
            for k in range(1, here.zs):
                for h in range(2):
                    self.send(b, 0, mine(h), to(h), self.sem("zr", b, h, k), lambda k=k: here.above(k))
            self.send(b, 0, mine(0), to(0), self.sem("xa", b, 0), lambda: here.xpeer)
            self.send(b, 0, mine(1), to(1), self.sem("yb", b, 0), lambda: here.ypeer)
            self.send(b, 0, mine(0), to(0), self.sem("ya", b, 0, 0), lambda: here.ypeer)
            self.send(b, 0, mine(1), to(1), self.sem("xb", b, 0, 0), lambda: here.xpeer)
            self.send(b, 0, lambda: slot, lambda: self.whole(b, 0, 0, 0), self.sem("cr", b, 0, 0, 0), lambda: here.cpeer)

        self.guarded(b, 0, run)

    def pass_on(self, b, k, h, dy, dx, sem, to):
        ref = lambda: self.part(b, h, k, dy, dx)
        self.send(b, k, ref, ref, sem, to)

    def share(self, b, k, dy, dx):
        ref = lambda: self.whole(b, k, dy, dx)
        self.send(b, k, ref, ref, self.sem("cr", b, k, dy, dx), lambda: self.here.cpeer)

    def events(self, b):
        here = self.here
        found = []

        def add(k, run):
            found.append(lambda: self.guarded(b, k, run))

        for k in range(1, here.zs):

            def from_z(k=k):
                arrived(self.part(b, 0, k, 0, 0), pick(self.zr, self.here, b, 0, k))
                self.pass_on(b, k, 0, 0, 0, self.sem("xa", b, k), lambda: here.xpeer)
                arrived(self.part(b, 1, k, 0, 0), pick(self.zr, self.here, b, 1, k))
                self.pass_on(b, k, 1, 0, 0, self.sem("yb", b, k), lambda: here.ypeer)
                self.pass_on(b, k, 0, 0, 0, self.sem("ya", b, k, 0), lambda: here.ypeer)
                self.pass_on(b, k, 1, 0, 0, self.sem("xb", b, k, 0), lambda: here.xpeer)
                self.share(b, k, 0, 0)

            add(k, from_z)
        for k in range(here.zs):

            def across(k=k):
                arrived(self.part(b, 0, k, 0, 1), pick(self.xa, self.here, b, k))
                self.pass_on(b, k, 0, 0, 1, self.sem("ya", b, k, 1), lambda: here.ypeer)
                arrived(self.part(b, 1, k, 1, 0), pick(self.yb, self.here, b, k))
                self.pass_on(b, k, 1, 1, 0, self.sem("xb", b, k, 1), lambda: here.xpeer)

            add(k, across)
        for k in range(here.zs):

            def beside(k=k):
                arrived(self.part(b, 1, k, 0, 1), pick(self.xb, self.here, b, k, 0))
                self.share(b, k, 0, 1)
                arrived(self.part(b, 0, k, 1, 0), pick(self.ya, self.here, b, k, 0))
                self.share(b, k, 1, 0)

            add(k, beside)
        for k in range(here.zs):

            def corner(k=k):
                arrived(self.part(b, 1, k, 1, 1), pick(self.xb, self.here, b, k, 1))
                arrived(self.part(b, 0, k, 1, 1), pick(self.ya, self.here, b, k, 1))
                self.share(b, k, 1, 1)

            add(k, corner)
        return found

    def complete(self, b):
        self.guarded(b, 0, lambda: self.own_copy(b).wait())
        for k in range(self.here.zs):

            def run(k=k):
                for dy in range(2):
                    for dx in range(2):
                        arrived(self.whole(b, k, dy, dx, 1), pick(self.cr, self.here, b, k, dy, dx))

            self.guarded(b, k, run)

    def drain(self):
        for b, k, make in self.sent:
            self.guarded(b, k, lambda: make().wait_send())


FRONT = 7


def cut_units(here, plan, ext, slot):
    top = here.me * plan.share // LANES - plan.before
    for base, chunks, count, first_unit, _, _ in plan.segments:
        lo = jnp.clip(plan.per * here.me - first_unit, 0, count)
        hi = jnp.clip(plan.per * here.me + plan.per - first_unit, 0, count)

        def unit(u, carry):
            block = u // chunks
            row = base + block * (ROWS * chunks) + (u - block * chunks) - top
            if chunks == 1:
                value = ext[pl.ds(row, ROWS), :]
            else:
                value = ext[pl.ds(row, ROWS, stride=chunks), :]
            slot[first_unit + u - plan.per * here.me] = value.astype(low_type)
            return carry

        lax.fori_loop(lo, hi, unit, 0)


def forward_kernel(plans, zs, rows, *refs):
    np_ = len(plans)
    feed = iter(refs)
    take = lambda count: tuple(next(feed) for _ in range(count))
    one = lambda: next(feed)
    raw_hbm = take(np_)
    noisy, positions, basis, chosen = take(4)
    units = take(np_)
    stream = take(LAYERS + 1)
    mods = take(LAYERS)
    sums = take(LAYERS)
    modulator, condition, time_pre = take(3)
    saved_out = [take(len(SAVED)) for _ in range(LAYERS)]
    from_prev, from_next, slots = take(np_), take(np_), take(np_)
    raw_sem, halo_send, halo_recv, front_sem, load_sem, save_sem = take(6)
    gather_sems = take(8)
    here = Place(zs)
    here.greet()
    root = plans[0]
    front_units = root.segments[FRONT][3]
    front_planes = min(zs, -(-front_units // (8 * root.per)))
    buckets = [(root, units[0], slots[0], 0, front_planes)]
    buckets += [(plans[1 + i], units[1 + i], slots[1 + i], 0, zs) for i in range(LAYERS)]
    buckets += [(root, units[0], slots[0], front_planes, zs)]
    gather = Gather(here, buckets, gather_sems)
    last = len(buckets) - 1
    starts = [[0]] + [[1 + i] for i in range(LAYERS)]
    starts[-1].append(last)

    def prepare(*scratch):
        raw, ext, tail = (scratch[i * np_ : (i + 1) * np_] for i in range(3))
        loads = [pltpu.make_async_copy(raw_hbm[i], raw[i].at[pl.ds(8, p.raw)], raw_sem.at[i]) for i, p in enumerate(plans)]
        for copy in loads:
            copy.start()
        lane = lax.broadcasted_iota(jnp.int32, (64, LANES), 1)
        halos = []
        for i, p in enumerate(plans):
            shift = lax.rem(here.me * p.share, LANES)
            delta = (here.me + 1) * p.share // LANES - here.me * p.share // LANES
            raw[i][pl.ds(0, 8), :] = jnp.zeros((8, LANES), full_type)
            ext[i][pl.ds(0, p.before), :] = jnp.zeros((p.before, LANES), full_type)
            ext[i][pl.ds(p.before + p.raw, p.after), :] = jnp.zeros((p.after, LANES), full_type)
            loads[i].wait()

            def align(j):
                row = pl.multiple_of(j * 64, 64)
                level = pltpu.roll(raw[i][pl.ds(row + 8, 64), :], shift, 1)
                above = pltpu.roll(raw[i][pl.ds(row + 7, 64), :], shift, 1)
                ext[i][pl.ds(row + p.before, 64), :] = jnp.where(lane >= shift, level, above)

            loop(p.raw // 64, align)
            tail[i][...] = ext[i][pl.ds(delta, p.before + 8), :]
            if i == 0:
                here.met()
            halos.append(remote(ext[i].at[pl.ds(p.before, p.after)], from_next[i], halo_send.at[2 * i], halo_recv.at[2 * i], here.prev))
            halos.append(remote(tail[i], from_prev[i], halo_send.at[2 * i + 1], halo_recv.at[2 * i + 1], here.following))
            halos[-2].start()
            halos[-1].start()
        for i, p in enumerate(plans):
            delta = (here.me + 1) * p.share // LANES - here.me * p.share // LANES
            halos[2 * i].wait()
            halos[2 * i + 1].wait()
            ext[i][pl.ds(0, p.before + 8), :] += from_prev[i][...]
            ext[i][pl.ds(p.before + delta, p.after), :] += from_next[i][...]
            cut_units(here, p, ext[i], slots[i])
            for b in starts[i]:
                gather.start(b)

    f32 = lambda *dims: pltpu.VMEM(dims, full_type)
    pl.run_scoped(
        prepare,
        *[f32(p.raw + 8, LANES) for p in plans],
        *[f32(p.ext, LANES) for p in plans],
        *[f32(p.before + 8, LANES) for p in plans],
    )
    for event in gather.events(0):
        event()
    gather.complete(0)

    def compute(front, w_qkv, w_o, w_1, w_2, w_mod, raw_bias, *held):
        copy = pltpu.make_async_copy(units[0].at[pl.ds(0, front_units)], front, front_sem)
        copy.start()
        copy.wait()
        matrix = lambda number, blocks: front_matrix(front, root, number, blocks)
        vector = lambda number: row_vector(front[pl.ds(root.segments[number][3], 1)], D // LANES)
        events = spread(gather.events(1), (1, 1, 1, 1))
        stream[0][...] = dot(noisy[...], matrix(0, 1)) + vector(1) + positions[...]
        for event in events[0]:
            event()
        pre = dot(basis[...], matrix(2, FREQ // ROWS)) + vector(3)
        time_pre[...] = pre
        act = silu_parts(pre)[0].astype(low_type)
        total = dot(act, matrix(4, D // ROWS)) + vector(5)
        few = basis.shape[0]
        first = root.segments[6][3]
        picked = dot(chosen[...], front[pl.ds(first, root.segments[6][2])].reshape(-1, LANES))
        total = total + jnp.concatenate([picked[i * few : (i + 1) * few, :] for i in range(D // LANES)], axis=1)
        condition[...] = total
        modulator[...] = silu_parts(total)[0].astype(low_type)
        for group in events[1:]:
            for event in group:
                event()
        for ordinal in range(LAYERS):
            gather.complete(1 + ordinal)
            queue = gather.events(2 + ordinal)
            layer_forward_body(
                plans[1 + ordinal], rows, stream[ordinal], modulator, mods[ordinal], units[1 + ordinal],
                stream[ordinal + 1], sums[ordinal], saved_out[ordinal], held, (w_qkv, w_o, w_1, w_2, w_mod), raw_bias,
                load_sem, save_sem, spread(queue, (18, 9, 12, 3, 12)),
            )
        gather.complete(last)

    plan = plans[1]
    bias_units = plan.units - plan.segments[5][3]
    pl.run_scoped(
        compute,
        pltpu.VMEM((front_units, ROWS, LANES), low_type),
        *[segment_scratch(plan, i) for i in range(5)],
        pltpu.VMEM((bias_units, ROWS, LANES), low_type),
        *[pltpu.VMEM((rows, width), kind) for _, width, kind in SAVED],
    )
    gather.drain()


def front_matrix(front, plan, number, blocks):
    _, chunks, _, first, _, _ = plan.segments[number]
    columns = [jnp.concatenate([front[first + b * chunks + c] for b in range(blocks)], axis=0) for c in range(chunks)]
    return jnp.concatenate(columns, axis=1)


def layer_forward_body(plan, rows, x, modulator, mod, units, out, sums, saved_out, held, weights, raw_bias, load_sem, save_sem, events):
    ns = len(SAVED)
    h1, qkv, heads, attn, middle, h2, pre, mlp = held
    w_qkv, w_o, w_1, w_2, w_mod = weights
    bias_first = plan.segments[5][3]
    loads = [pltpu.make_async_copy(segment_ref(units, plan, i), weights[i], load_sem.at[i]) for i in range(5)]
    bias_load = pltpu.make_async_copy(units.at[pl.ds(bias_first, raw_bias.shape[0])], raw_bias, load_sem.at[5])
    bias_load.start()
    for i in (4, 0, 1, 2, 3):
        loads[i].start()
    saves = [pltpu.make_async_copy(held[i], saved_out[i], save_sem.at[i]) for i in range(ns)]
    part = lambda s, i: mod[pl.ds(s, 1), i * D : (i + 1) * D]
    per = SEQ // CHUNK
    wide_at = lambda j: pl.ds(pl.multiple_of(j * WIDE, WIDE), WIDE)
    chunk_at = lambda i: pl.ds(pl.multiple_of(i * CHUNK, CHUNK), CHUNK)
    bias_load.wait()

    def bias(number):
        _, _, count, first, shape, _ = plan.segments[number]
        return row_vector(raw_bias[pl.ds(first - bias_first, count)], shape[0] // LANES)

    loads[4].wait()
    mod[...] = jnp.broadcast_to(bias(10), mod.shape)
    value_of = modulator[...]

    def modulate(j):
        mod[:, wide_at(j)] += dot(value_of, block_of(w_mod, 0, D // ROWS, 2 * j, 2))

    busy_loop(6 * D // WIDE, modulate, events[0])

    def norm_a(i):
        s = i // per
        hat, _ = norm_parts(x[chunk_at(i), :])
        h1[chunk_at(i), :] = (hat * (1.0 + part(s, 1)) + part(s, 0)).astype(low_type)

    loop(rows // CHUNK, norm_a)
    saves[0].start()
    loads[0].wait()
    first_bias, value_bias = bias(5), bias(6)

    def project_with(base, given, events):
        pieces = D // WIDE

        def project(j):
            value = dot(h1[...], block_of(w_qkv, 0, D // ROWS, 2 * (base + j), 2))
            cols = wide_at(base + j)
            if given is not None:
                value = value + mlp[0:1, wide_at(j)]
            qkv[:, cols] = value.astype(low_type)

        if given is not None:
            mlp[0:1, :] = given
        busy_loop(pieces, project, events)

    third = spread(events[1], (1, 1, 1))
    project_with(0, first_bias, third[0])
    project_with(D // WIDE, None, third[1])
    project_with(2 * D // WIDE, value_bias, third[2])
    saves[1].start()
    first = head_masks()

    def attend(i):
        s, j = i // (HEADS // 2), i % (HEADS // 2)
        at = pl.ds(pl.multiple_of(s * SEQ, SEQ), SEQ)
        cut = lambda o: qkv[at, pl.ds(pl.multiple_of(o * D + j * LANES, LANES), LANES)]
        q, k, v = cut(0), cut(1), cut(2)
        q = q * jnp.asarray(HD ** (-0.5), low_type)
        zero = jnp.zeros_like(q)
        halves = []
        for mask in (first, ~first):
            probs = softmax_f32(dot_nt(jnp.where(mask, q, zero), k)).astype(low_type)
            halves.append(dot(probs, v))
        heads[at, pl.ds(pl.multiple_of(j * LANES, LANES), LANES)] = jnp.where(first, halves[0], halves[1]).astype(low_type)

    busy_loop(attention_pairs(rows), attend, events[2])
    saves[2].start()
    loads[1].wait()
    attn[...] = jnp.broadcast_to(bias(7), (rows, D))

    def project_out(j):
        attn[:, wide_at(j)] += dot(heads[...], block_of(w_o, 0, D // ROWS, 2 * j, 2))

    busy_loop(D // WIDE, project_out, events[3])
    saves[3].start()
    zero_sum = jnp.zeros((1, D), full_type)

    def norm_m(i, total):
        s = i // per
        value = attn[chunk_at(i), :]
        mid = x[chunk_at(i), :] + part(s, 2) * value
        middle[chunk_at(i), :] = mid
        hat, _ = norm_parts(mid)
        h2[chunk_at(i), :] = (hat * (1.0 + part(s, 4)) + part(s, 3)).astype(low_type)
        return total + rows_sum(value * value)

    attn_sum = lax.fori_loop(0, rows // CHUNK, norm_m, zero_sum)
    saves[4].start()
    saves[5].start()
    loads[2].wait()
    loads[3].wait()
    pre[0:1, :] = bias(8)
    mlp[...] = jnp.broadcast_to(bias(9), (rows, D))

    def feed(j):
        value = dot(h2[...], block_of(w_1, 0, D // ROWS, 2 * j, 2)) + pre[0:1, wide_at(j)]
        pre[:, wide_at(j)] = value
        act = gelu_parts(value)[0].astype(low_type)
        mlp[...] += dot(act, block_of(w_2, j * (WIDE // ROWS), WIDE // ROWS, 0, D // LANES))

    busy_loop(FF // WIDE, feed, events[4])
    saves[6].start()
    saves[7].start()

    def finish(i, carry):
        value = mlp[chunk_at(i), :]
        result = middle[chunk_at(i), :] + part(i // per, 5) * value
        out[chunk_at(i), :] = result
        return (carry[0] + rows_sum(result * result), carry[1] + rows_sum(value * value))

    out_sum, mlp_sum = lax.fori_loop(0, rows // CHUNK, finish, (zero_sum, zero_sum))
    sums[...] = jnp.zeros(sums.shape, full_type)
    sums[0:1, :] = out_sum
    sums[1:2, :] = attn_sum
    sums[2:3, :] = mlp_sum
    for copy in saves:
        copy.wait()


def forward_call(plans, raws, noisy, positions, basis, chosen):
    n = plans[0].devices
    zs = n // 8
    rows, few = noisy.shape[0], basis.shape[0]
    dma = pltpu.SemaphoreType.DMA
    np_, nb = len(plans), len(plans) + 1
    vm = pl.BlockSpec(memory_space=pltpu.VMEM)
    hbm = pl.BlockSpec(memory_space=pltpu.HBM)
    shape = jax.ShapeDtypeStruct
    saved_shapes = [shape((rows, width), kind) for _, width, kind in SAVED]
    out_shape = [shape((n * p.per, ROWS, LANES), low_type) for p in plans]
    out_shape += [shape((rows, D), full_type)] * (LAYERS + 1)
    out_shape += [shape((few, 6 * D), full_type)] * LAYERS + [shape((8, D), full_type)] * LAYERS
    out_shape += [shape((few, D), low_type), shape((few, D), full_type), shape((few, D), full_type)]
    out_shape += saved_shapes * LAYERS
    scratch = [pltpu.VMEM((p.before + 8, LANES), full_type) for p in plans]
    scratch += [pltpu.VMEM((p.after, LANES), full_type) for p in plans]
    scratch += [pltpu.VMEM((p.per, ROWS, LANES), low_type) for p in plans]
    scratch += [dma((np_,)), dma((2 * np_,)), dma((2 * np_,)), dma, dma((6,)), dma((len(SAVED),))]
    scratch += [dma((nb,)), dma((nb * (2 * (zs - 1) + 10 * zs),)), dma((nb, 2, zs)), dma((nb, zs)), dma((nb, zs, 2))]
    scratch += [dma((nb, zs)), dma((nb, zs, 2)), dma((nb, zs, 2, 2))]
    results = pl.pallas_call(
        functools.partial(forward_kernel, plans, zs, rows),
        out_shape=out_shape,
        in_specs=[hbm] * np_ + [vm] * 4,
        out_specs=[hbm] * np_ + [vm] * (LAYERS + 1 + 2 * LAYERS + 3) + [hbm] * (len(SAVED) * LAYERS),
        scratch_shapes=scratch,
        compiler_params=pltpu.CompilerParams(collective_id=0, has_side_effects=True, vmem_limit_bytes=62 * MB),
        name="gather_and_forward",
    )(*raws, noisy, positions, basis, chosen)
    feed = iter(results)
    take = lambda count: [next(feed) for _ in range(count)]
    units, stream, mods, sums = take(np_), take(LAYERS + 1), take(LAYERS), take(LAYERS)
    modulator, condition, time_pre = take(3)
    return units, stream, mods, sums, modulator, condition, time_pre, [take(len(SAVED)) for _ in range(LAYERS)]


LOOK = 1


class Reduce:
    def __init__(self, here, buckets, first, buffers, sems, frees):
        self.here = here
        self.buckets = buckets
        self.first = first
        self.kept, self.two, self.three, self.four, self.ring, self.other, self.own = buffers
        self.s1, self.r1, self.s2, self.r2, self.s3, self.r3, self.s4, self.r4, self.load_sem = sems
        self.free_two, self.free_three, self.free_four = frees
        self.planes = list(range(1, here.zs)) + [0]
        self.groups = [(b, k) for b in range(len(buckets)) for k in self.planes]
        self.order = ((1, 1), (1, 0), (0, 1), (0, 0))

    def limits(self, b):
        return self.buckets[b][2:4]

    def meets(self, b, k):
        lo, hi = self.limits(b)
        if lo == 0 and hi == self.here.zs:
            return None
        plane = lax.rem(self.here.z + self.here.zs - k, self.here.zs)
        return (plane >= lo) & (plane < hi)

    def guarded(self, b, k, run):
        test = self.meets(b, k)
        if test is None:
            run()
        else:
            pl.when(test)(run)

    def overlaps(self, b, other):
        return self.limits(b)[0] < self.limits(other)[1] and self.limits(other)[0] < self.limits(b)[1]

    def before(self, b, k, run):
        for other in range(b - 1, -1, -1):
            if self.overlaps(b, other):
                self.guarded(b, k, lambda: self.guarded(other, k, run))
                return

    def after(self, b, k, run):
        for other in range(b + 1, len(self.buckets)):
            if self.overlaps(b, other):
                self.guarded(b, k, lambda: self.guarded(other, k, run))
                self.after_rest(b, other, k, run)
                return

    def after_rest(self, b, done, k, run):
        for other in range(done + 1, len(self.buckets)):
            if self.overlaps(b, other) and not self.overlaps(done, other):
                self.guarded(b, k, lambda: self.guarded(other, k, run))

    def slot(self, b, k, dy, dx, dc):
        plan, grads = self.buckets[b][:2]
        return grads.at[pl.ds(self.here.slot(k, dy, dx, dc) * plan.per, plan.per)]

    def landed(self, b, k, dy, dx):
        return self.first[b].at[self.here.zero + k, self.here.zero + dy, self.here.zero + dx]

    def sibling(self, b, k, dy, dx):
        here = self.here
        return remote(
            self.slot(b, k, dy, dx, 1), self.landed(b, k, dy, dx), pick(self.s1, here, b, k, dy, dx), pick(self.r1, here, b, k, dy, dx), here.cpeer
        )

    def open(self, b):
        for k in self.planes:

            def run(k=k):
                for dy, dx in self.order:
                    self.sibling(b, k, dy, dx).start()

            self.guarded(b, k, run)

    def half(self, b):
        return self.buckets[b][0].half

    def buffer(self, ref, b, *spots):
        view = ref.at[tuple(self.here.zero + s for s in spots)]
        return view.at[pl.ds(0, self.half(b))]

    def place_of(self, g, i):
        return 3 * (LOOK + 1) if i == 3 else 3 * (g % (LOOK + 1)) + i

    def loads(self, g, i):
        b, k = self.groups[g]
        dy, dx = self.order[i]
        per = self.buckets[b][0].per
        here = self.here
        at = self.place_of(g, i)
        one = pltpu.make_async_copy(self.slot(b, k, dy, dx, 0), pick(self.ring, here, at).at[pl.ds(0, per)], pick(self.load_sem, here, at, 0))
        two = pltpu.make_async_copy(self.landed(b, k, dy, dx), pick(self.other, here, i % 2).at[pl.ds(0, per)], pick(self.load_sem, here, at, 1))
        return one, two

    def prepare(self, g, i):
        b, k = self.groups[g]
        dy, dx = self.order[i]
        one, two = self.loads(g, i)
        one.start()
        arrived(self.landed(b, k, dy, dx), pick(self.r1, self.here, b, k, dy, dx))
        two.start()

    def second(self, g, h, i):
        b, k = self.groups[g]
        dy, dx = self.order[i]
        here, size = self.here, self.half(b)
        src = pick(self.ring, here, self.place_of(g, i)).at[pl.ds(h * size, size)]
        far = dx if h == 0 else dy
        return remote(src, self.buffer(self.two[h], b, k, far), pick(self.s2, here, h, k, far), pick(self.r2, here, h, k, far), here.ypeer if h == 0 else here.xpeer)

    def sends_of(self, g):
        return [(h, i) for i, (dy, dx) in enumerate(self.order) for h in range(2) if (dy, dx)[h]]

    def add(self, b, dst, at, one, one_at, two, two_at):
        step = self.half(b) // 2

        def body(i, carry):
            span = lambda ref, off: ref[pl.ds(off + i * step, step)].astype(full_type)
            dst[pl.ds(at + i * step, step)] = (span(one, one_at) + span(two, two_at)).astype(low_type)
            return carry

        lax.fori_loop(0, 2, body, 0)

    def phase_one(self, g, i):
        b, k = self.groups[g]
        here, size = self.here, self.half(b)
        if i == 0:
            for h in range(2):
                to_free = lambda h=h: pl.semaphore_wait(pick(self.free_two, here, h, k), 1)
                self.before(b, k, to_free)

        def run():
            dy, dx = self.order[i]
            if i == 0:
                self.prepare(g, 0)
            if i < 3:
                self.prepare(g, i + 1)
            for copy in self.loads(g, i):
                copy.wait()
            mine, theirs = pick(self.ring, here, self.place_of(g, i)), pick(self.other, here, i % 2)
            for h, moves in enumerate((dy, dx)):
                if moves:
                    self.add(b, mine, h * size, mine, h * size, theirs, h * size)
                    self.second(g, h, i).start()
                else:
                    self.add(b, self.buffer(self.kept[h], b, k, dx if h == 0 else dy), 0, mine, h * size, theirs, h * size)

        self.guarded(b, k, run)

    def third(self, g, h):
        b, k = self.groups[g]
        here = self.here
        return remote(
            self.buffer(self.two[h], b, k, 1), self.buffer(self.three[h], b, k), pick(self.s3, here, h, k), pick(self.r3, here, h, k), here.xpeer if h == 0 else here.ypeer
        )

    def phase_two(self, g, far):
        b, k = self.groups[g]
        here = self.here
        if far:
            for h in range(2):
                self.before(b, k, lambda h=h: pl.semaphore_wait(pick(self.free_three, here, h, k), 1))

        def run():
            for h in range(2):
                got, kept = self.buffer(self.two[h], b, k, far), self.buffer(self.kept[h], b, k, far)
                arrived(got, pick(self.r2, here, h, k, far))
                if far:
                    self.add(b, got, 0, got, 0, kept, 0)
                    self.third(g, h).start()
                else:
                    self.add(b, kept, 0, got, 0, kept, 0)

        self.guarded(b, k, run)

    def last(self, g, h):
        b, k = self.groups[g]
        here = self.here
        return remote(self.buffer(self.three[h], b, k), self.buffer(self.four, b, b % 2, h, k - 1), pick(self.s4, here, b % 2, h, k - 1), pick(self.r4, here, b % 2, h, k - 1), here.below(k))

    def phase_three(self, g):
        b, k = self.groups[g]
        here, size = self.here, self.half(b)
        if k:
            if b >= 2:
                to_free = lambda: pl.semaphore_wait(pick(self.free_four, here, k - 1), 1)
                self.guarded(b, k, lambda: self.guarded(b - 2, k, to_free))

        def run():
            for h in range(2):
                got, kept = self.buffer(self.three[h], b, k), self.buffer(self.kept[h], b, k, 0)
                arrived(got, pick(self.r3, here, h, k))
                if k:
                    self.add(b, got, 0, got, 0, kept, 0)
                    self.last(g, h).start()
                else:
                    step = size // 2

                    def body(i, carry):
                        part = pl.ds(i * step, step)
                        self.own[pl.ds(h * size + i * step, step)] = got[part].astype(full_type) + kept[part].astype(full_type)
                        return carry

                    lax.fori_loop(0, 2, body, 0)

        self.guarded(b, k, run)

    def release_one(self, g):
        b, k = self.groups[g]

        def run():
            for h, i in self.sends_of(g):
                self.second(g, h, i).wait_send()

        self.guarded(b, k, run)

    def release_two(self, g):
        b, k = self.groups[g]
        here = self.here

        def run():
            for h in range(2):
                self.third(g, h).wait_send()

        self.guarded(b, k, run)

        def free():
            for h in range(2):
                to = here.ypeer if h == 0 else here.xpeer
                pl.semaphore_signal(pick(self.free_two, here, h, k), inc=1, device_id=(to,), device_id_type=MESH)

        self.after(b, k, free)

    def release_three(self, g):
        b, k = self.groups[g]
        here = self.here

        def run():
            for h in range(2):
                self.last(g, h).wait_send()

        if k:
            self.guarded(b, k, run)

        def free():
            for h in range(2):
                to = here.xpeer if h == 0 else here.ypeer
                pl.semaphore_signal(pick(self.free_three, here, h, k), inc=1, device_id=(to,), device_id_type=MESH)

        self.after(b, k, free)

    def collect(self, b, out, sem):
        here, size = self.here, self.half(b)

        def run():
            for h in range(2):
                for k in range(1, here.zs):
                    arrived(self.buffer(self.four, b, b % 2, h, k - 1), pick(self.r4, here, b % 2, h, k - 1))
                step = size // 2

                def body(i, carry):
                    part = pl.ds(i * step, step)
                    where = pl.ds(h * size + i * step, step)
                    value = self.own[where]
                    for k in range(1, here.zs):
                        value = value + self.buffer(self.four, b, b % 2, h, k - 1)[part].astype(full_type)
                    self.own[where] = value
                    return carry

                lax.fori_loop(0, 2, body, 0)
            copy = pltpu.make_async_copy(self.own.at[pl.ds(0, 2 * size)], out, sem)
            copy.start()
            copy.wait()

        self.guarded(b, 0, run)

        def free():
            for k in range(1, here.zs):
                pl.semaphore_signal(pick(self.free_four, here, k - 1), inc=1, device_id=(here.above(k),), device_id_type=MESH)

        if b + 2 < len(self.buckets):
            self.guarded(b, 0, lambda: self.guarded(b + 2, 0, free))

    def steps(self, g, outs, sem):
        zs = self.here.zs
        total = len(self.groups)
        found = []
        done = g - LOOK - 1
        if done % zs == 0 and 0 < done // zs <= len(self.buckets):
            b = done // zs - 1
            found.append(functools.partial(self.collect, b, outs[b], sem))
        if g < total:
            if g >= LOOK + 1:
                found.append(functools.partial(self.release_one, g - LOOK - 1))
            found += [functools.partial(self.phase_one, g, i) for i in range(4)]
        if 0 <= g - LOOK - zs < total - zs:
            found.append(functools.partial(self.release_three, g - LOOK - zs))
        if 0 <= g - LOOK < total:
            found += [functools.partial(self.phase_two, g - LOOK, 1), functools.partial(self.phase_two, g - LOOK, 0)]
        if 0 <= g - LOOK - 1 < total:
            found.append(functools.partial(self.phase_three, g - LOOK - 1))
        if 0 <= g - LOOK - 2 < total:
            found.append(functools.partial(self.release_two, g - LOOK - 2))
        return found

    def close(self):
        total = len(self.groups)
        for g in range(total - LOOK - 1, total):
            self.release_one(g)
        for g in range(total - self.here.zs, total):
            self.release_three(g)
        for b in range(len(self.buckets)):
            for k in self.planes:

                def run(b=b, k=k):
                    for dy, dx in self.order:
                        self.sibling(b, k, dy, dx).wait_send()

                self.guarded(b, k, run)


def unpack_rows(here, plan, segments, units_f, rows_f, flat_f, held_before):
    top = here.me * plan.share // LANES - plan.margin
    for origin, chunks, count, first_unit, _, _ in segments:
        lo = jnp.clip(plan.per * here.me - held_before - first_unit, 0, count)
        hi = jnp.clip(plan.per * here.me + plan.per + plan.units_after - first_unit, 0, count)

        def unit(u, carry):
            block = u // chunks
            row = origin + block * (ROWS * chunks) + (u - block * chunks) - top
            value = units_f[first_unit + u - plan.per * here.me + held_before]
            if chunks == 1:
                rows_f[pl.ds(row, ROWS), :] = value
            else:
                rows_f[pl.ds(row, ROWS, stride=chunks), :] = value
            return carry

        lax.fori_loop(lo, hi, unit, 0)
    shift = lax.rem(here.me * plan.share, LANES)
    turn = lax.rem(LANES - shift, LANES)
    lane = lax.broadcasted_iota(jnp.int32, (64, LANES), 1)
    spot = lax.broadcasted_iota(jnp.int32, (64, LANES), 0) * LANES + lane

    def unalign(i, squares):
        row = pl.multiple_of(i * 64, 64)
        level = pltpu.roll(rows_f[pl.ds(row + plan.margin, 64), :], turn, 1)
        below = pltpu.roll(rows_f[pl.ds(row + plan.margin + 1, 64), :], turn, 1)
        value = jnp.where(lane < LANES - shift, level, below)
        value = jnp.where(spot + row * LANES < plan.share, value, 0.0)
        flat_f[pl.ds(row, 64), :] = value
        return squares + jnp.sum((value * value).reshape(8, 8, LANES), axis=0)

    return lax.fori_loop(0, plan.raw // 64, unalign, jnp.zeros((8, LANES), full_type))


def put_row(stage, first, vector):
    for r in range(vector.shape[1] // LANES):
        stage[first + r : first + r + 1, :] = vector[:, r * LANES : (r + 1) * LANES]


B_Q, B_V, B_O, B_1, B_2 = 0, D, 2 * D, 3 * D, 3 * D + FF


def layer_backward_body(plan, rows, x_hbm, saved, units, grads, mod, grad, modulator, cond, note, samples, held, sems, events):
    (qkv, heads, h_low, wide_f, tall_f, pre, w_1, w_2, w_qkv, w_o, d_qkv, g_low, slim, turned, dx, d_one, d_two, grad_mod, bias_out) = held
    load_sem, chunk_sem, out_sem = sems
    h1_h, qkv_h, heads_h, attn_h, middle_h, h2_h, pre_h, mlp_h = saved
    fetch = lambda i, src, dst: pltpu.make_async_copy(src, dst, load_sem.at[i])
    load_mlp, load_attn = fetch(0, mlp_h, wide_f), fetch(0, attn_h, wide_f)
    load_middle, load_x = fetch(1, middle_h, tall_f), fetch(1, x_hbm, tall_f)
    load_h2, load_h1 = fetch(2, h2_h, h_low), fetch(2, h1_h, h_low)
    load_heads, load_qkv = fetch(3, heads_h, heads), fetch(4, qkv_h, qkv)
    load_w_o, load_w_qkv = fetch(5, segment_ref(units, plan, 1), w_o), fetch(6, segment_ref(units, plan, 0), w_qkv)
    half = WIDE // ROWS
    wide_at = lambda j, base=0: pl.ds(pl.multiple_of(base + j * WIDE, LANES), WIDE)

    def chunk_loads(j):
        at = j % 2
        return (
            pltpu.make_async_copy(segment_ref(units, plan, 3).at[pl.ds(j * half, half)], w_2.at[at], chunk_sem.at[at, 0]),
            pltpu.make_async_copy(segment_ref(units, plan, 2).at[:, pl.ds(2 * j, 2)], w_1.at[at], chunk_sem.at[at, 1]),
            pltpu.make_async_copy(pre_h.at[:, wide_at(j)], pre.at[at], chunk_sem.at[at, 2]),
        )

    def mod_load(j):
        return pltpu.make_async_copy(segment_ref(units, plan, 4).at[:, pl.ds(2 * j, 2)], w_1.at[j % 2], chunk_sem.at[j % 2, 1])

    for copy in (load_mlp, load_h2) + chunk_loads(0) + (load_middle, load_w_o, load_heads, load_qkv, load_w_qkv):
        copy.start()
    part = lambda s, i: mod[pl.ds(s, 1), i * D : (i + 1) * D]
    per = SEQ // CHUNK
    grad_mod[...] = jnp.zeros(grad_mod.shape, full_type)
    bias_out[...] = jnp.zeros(bias_out.shape, full_type)

    def add_mod(s, i, value):
        grad_mod[pl.ds(s, 1), i * D : (i + 1) * D] += value

    def each_chunk(body):
        loop(rows // CHUNK, lambda i: body(pl.ds(pl.multiple_of(i * CHUNK, CHUNK), CHUNK), i // per))

    load_mlp.wait()

    def start_mlp(at, s):
        value = grad[at, :]
        low = (part(s, 5) * value).astype(low_type)
        g_low[at, :] = low
        bias_out[:, B_2 : B_2 + D] += rows_sum(low.astype(full_type))
        add_mod(s, 5, rows_sum(wide_f[at, :] * value))

    each_chunk(start_mlp)
    load_attn.start()
    load_h2.wait()
    turned[...] = h_low[...].astype(full_type).T.astype(low_type)
    load_h1.start()
    dx[...] = jnp.zeros(dx.shape, full_type)

    def outer(slot, segment, block, blocks, chunk, chunks, buffer):
        target = segment_ref(grads, plan, segment).at[pl.ds(block, blocks), pl.ds(chunk, chunks)]
        return pltpu.make_async_copy(buffer, target, out_sem.at[slot])

    def mlp_store(j, kind):
        at = j % 2
        if kind == 0:
            return outer(2 * at, 3, j * half, half, 0, D // LANES, d_one.at[at])
        return outer(2 * at + 1, 2, 0, D // ROWS, 2 * j, 2, d_two.at[at])

    steps = FF // WIDE

    def feed_back(j):
        at = j % 2

        @pl.when(j + 1 < steps)
        def _():
            for copy in chunk_loads(j + 1):
                copy.start()

        for copy in chunk_loads(j):
            copy.wait()

        @pl.when(j >= 2)
        def _():
            mlp_store(j - 2, 0).wait()
            mlp_store(j - 2, 1).wait()

        act, slope = gelu_parts(pre[at])
        grad_act = dot_nt(g_low[...], block_of(w_2.at[at], 0, half, 0, D // LANES))
        low = (grad_act * slope).astype(low_type)
        slim[...] = low
        bias_out[:, wide_at(j, B_1)] += rows_sum(low.astype(full_type))
        put_block(d_one.at[at], 0, 0, dot_tn(act.astype(low_type), g_low[...]))
        mlp_store(j, 0).start()
        put_block(d_two.at[at], 0, 0, dot(turned[...], slim[...]))
        mlp_store(j, 1).start()
        dx[...] += dot_nt(slim[...], block_of(w_1.at[at], 0, D // ROWS, 0, 2))

    busy_loop(steps, feed_back, events[0])
    load_middle.wait()
    load_attn.wait()

    def middle_back(at, s):
        value = dx[at, :]
        back, scaled = norm_back(tall_f[at, :], value, 1.0 + part(s, 4))
        add_mod(s, 3, rows_sum(value))
        add_mod(s, 4, rows_sum(scaled))
        total = grad[at, :] + back
        grad[at, :] = total
        low = (part(s, 2) * total).astype(low_type)
        g_low[at, :] = low
        bias_out[:, B_O : B_O + D] += rows_sum(low.astype(full_type))
        add_mod(s, 2, rows_sum(wide_f[at, :] * total))

    each_chunk(middle_back)
    load_x.start()
    load_w_o.wait()
    load_heads.wait()
    for j in (steps - 2, steps - 1):
        mlp_store(j, 0).wait()
        mlp_store(j, 1).wait()
    mod_load(0).start()
    turned[...] = heads[...].astype(full_type).T.astype(low_type)

    def wo_store(j):
        return outer(j % 2, 1, 0, D // ROWS, 2 * j, 2, d_two.at[j % 2])

    def out_back(j):
        @pl.when(j >= 2)
        def _():
            wo_store(j - 2).wait()

        put_block(d_two.at[j % 2], 0, 0, dot(turned[...], g_low[:, wide_at(j)]))
        wo_store(j).start()
        heads[:, wide_at(j)] = dot_nt(g_low[...], block_of(w_o, j * half, half, 0, D // LANES)).astype(low_type)

    busy_loop(D // WIDE, out_back, events[1])
    load_qkv.wait()
    first = head_masks()

    def attend_back(i):
        s, j = i // (HEADS // 2), i % (HEADS // 2)
        at = pl.ds(pl.multiple_of(s * SEQ, SEQ), SEQ)
        cut = lambda o: qkv[at, pl.ds(pl.multiple_of(o * D + j * LANES, LANES), LANES)]
        q, k, v = cut(0), cut(1), cut(2)
        go = heads[at, pl.ds(pl.multiple_of(j * LANES, LANES), LANES)]
        q = q * jnp.asarray(HD ** (-0.5), low_type)
        zero = jnp.zeros_like(q)
        dq, dk, dv = [], 0.0, 0.0
        for mask in (first, ~first):
            q_h, go_h = jnp.where(mask, q, zero), jnp.where(mask, go, zero)
            probs = softmax_f32(dot_nt(q_h, k))
            grad_probs = dot_nt(go_h, v)
            dv = dv + dot_tn(probs.astype(low_type), go_h)
            inner = jnp.sum(probs * grad_probs, axis=-1, keepdims=True)
            ds = (probs * (grad_probs - inner)).astype(low_type)
            dq.append(dot(ds, k) * HD ** (-0.5))
            dk = dk + dot_tn(ds, q_h)
        for o, value in enumerate((jnp.where(first, dq[0], dq[1]), dk, dv)):
            low = value.astype(low_type)
            d_qkv[at, pl.ds(pl.multiple_of(o * D + j * LANES, LANES), LANES)] = low
            if o != 1:
                start = (B_Q if o == 0 else B_V) + j * LANES
                bias_out[:, pl.ds(pl.multiple_of(start, LANES), LANES)] += rows_sum(low.astype(full_type))

    busy_loop(attention_pairs(rows), attend_back, events[2])
    load_h1.wait()
    load_w_qkv.wait()
    wo_store(1).wait()
    wo_store(2).wait()
    turned[...] = h_low[...].astype(full_type).T.astype(low_type)
    dx[...] = jnp.zeros(dx.shape, full_type)

    def qkv_store(j):
        return outer(j % 2, 0, 0, D // ROWS, 2 * j, 2, d_two.at[j % 2])

    def project_back(j):
        @pl.when(j >= 2)
        def _():
            qkv_store(j - 2).wait()

        put_block(d_two.at[j % 2], 0, 0, dot(turned[...], d_qkv[:, wide_at(j)]))
        qkv_store(j).start()
        dx[...] += dot_nt(d_qkv[:, wide_at(j)], block_of(w_qkv, 0, D // ROWS, 2 * j, 2))

    count = 3 * D // WIDE
    busy_loop(count, project_back, events[3])
    load_x.wait()

    def input_back(at, s):
        value = dx[at, :]
        back, scaled = norm_back(tall_f[at, :], value, 1.0 + part(s, 1))
        add_mod(s, 0, rows_sum(value))
        add_mod(s, 1, rows_sum(scaled))
        grad[at, :] += back

    each_chunk(input_back)
    for j in (count - 2, count - 1):
        qkv_store(j).wait()
    mod_steps = 6 * D // WIDE

    def mod_back(j):
        @pl.when(j + 1 < mod_steps)
        def _():
            mod_load(j + 1).start()

        mod_load(j).wait()
        low = grad_mod[:, wide_at(j)].astype(low_type)
        cond[...] += dot_nt(low, block_of(w_1.at[j % 2], 0, D // ROWS, 0, 2))

    busy_loop(mod_steps, mod_back, events[4])
    put_samples(note, 0, grad_mod[...], samples)
    put_row(note, samples * MOD_CHUNKS, bias_out[...])
    put_samples(note, samples * MOD_CHUNKS + BIAS_ROWS, modulator[...].astype(full_type), samples)


MOD_CHUNKS = 6 * D // LANES
BIAS_ROWS = (4 * D + FF) // LANES
WIDTH = D // LANES
FREQ_CHUNKS = FREQ // LANES


def note_rows(samples):
    layer = samples * (MOD_CHUNKS + WIDTH) + BIAS_ROWS
    front = samples * (3 * WIDTH + FREQ_CHUNKS + 1) + WIDTH + ROWS * WIDTH
    return up(max(layer, front), ROWS)


def put_samples(stage, first, values, samples):
    for j in range(values.shape[1] // LANES):
        stage[first + j * samples : first + (j + 1) * samples, :] = values[0:samples, j * LANES : (j + 1) * LANES]


class Notes:
    def __init__(self, here, count, samples, owners, boxes, low, send_sem, recv_sem, own_sem):
        self.here, self.count, self.samples = here, count, samples
        self.owners, self.boxes, self.low = owners, boxes, low
        self.send_sem, self.recv_sem, self.own_sem = send_sem, recv_sem, own_sem

    def owned(self, i):
        first, last = self.owners[i]
        return (self.here.me >= first) & (self.here.me <= last)

    def copies(self, i):
        here = self.here
        first, last = self.owners[i]
        box = self.boxes[i].at[here.me]
        for to in range(first, last + 1):
            make = lambda to=to: remote(self.low.at[here.zero + i], box, pick(self.send_sem, here, i, to - first), pick(self.recv_sem, here, i), to)
            yield to, make

    def own(self, i):
        return pltpu.make_async_copy(self.low.at[self.here.zero + i], self.boxes[i].at[self.here.me], pick(self.own_sem, self.here, i))

    def send(self, i, stage):
        self.low[i] = stage[...].astype(low_type)
        for to, make in self.copies(i):
            pl.when(self.here.me != to)(lambda: make().start())
        pl.when(self.owned(i))(lambda: self.own(i).start())

    def receive(self, i):
        n = self.here.n
        arrived(self.boxes[i].at[pl.ds(0, n - 1)], pick(self.recv_sem, self.here, i))
        self.own(i).wait()

    def drain(self, count):
        for i in range(count):
            for to, make in self.copies(i):
                pl.when(self.here.me != to)(lambda: make().wait_send())


def all_samples(notes_f, count, n, samples, first, chunk):
    row = first + chunk * samples
    return jnp.concatenate([notes_f[pl.ds(row + s, n, stride=count), :] for s in range(samples)], axis=0)


def all_summed(notes_f, count, n, first, rows):
    def body(d, value):
        return value + notes_f[pl.ds(d * count + first, rows), :]

    return lax.fori_loop(0, n, body, jnp.zeros((rows, LANES), full_type))


def window(plan, chunks):
    return up(-(-plan.raw // chunks) + 1, 8)


def first_of_window(here, plan, base, chunks, depth):
    start = here.me * plan.share // LANES
    far = plan.length // LANES + 1
    first = (start - base + far * chunks) // chunks - far
    first = jnp.clip(first, -window(plan, chunks), depth)
    return first, first * chunks + base - (start - plan.margin)


def add_outer(here, plan, base, chunks, depth, rows_f, left_of, right_of):
    size = window(plan, chunks)
    first, row = first_of_window(here, plan, base, chunks, depth)
    left = left_of(first, size)
    near = (row >= 0) & (row + size * chunks <= rows_f.shape[0])

    @pl.when(near)
    def _():
        for c in range(chunks):
            rows_f[pl.ds(row + c, size, stride=chunks), :] += dot(left, right_of(c))


def add_rows(here, plan, base, rows_f, value):
    start = here.me * plan.share // LANES
    stop = (here.me + 1) * plan.share // LANES

    @pl.when((base >= start) & (base < stop))
    def _():
        rows_f[pl.ds(base - start + plan.margin, value.shape[0]), :] += value


def turned_left(turned, size, depth, chunk_of):
    turned[...] = jnp.zeros(turned.shape, full_type)
    for j in range(depth // LANES):
        turned[size + j * LANES : size + (j + 1) * LANES, :] = chunk_of(j).T
    return lambda first, count: turned[pl.ds(first + size, count), :].astype(low_type)


def layer_extra(here, plan, notes_f, count, n, samples, turned, rows_f):
    base = plan.segments[4][0]
    read = lambda first, chunk: all_samples(notes_f, count, n, samples, first, chunk)
    modulator_first = samples * MOD_CHUNKS + BIAS_ROWS
    left_of = turned_left(turned, window(plan, MOD_CHUNKS), D, lambda j: read(modulator_first, j))
    add_outer(here, plan, base, MOD_CHUNKS, D, rows_f, left_of, lambda c: read(0, c).astype(low_type))
    add_rows(here, plan, plan.segments[5][0], rows_f, all_summed(notes_f, count, n, samples * MOD_CHUNKS, BIAS_ROWS))
    mod_bias = jnp.concatenate([rows_sum(read(0, c)) for c in range(MOD_CHUNKS)], axis=0)
    add_rows(here, plan, plan.segments[10][0], rows_f, mod_bias)


def front_extra(here, plan, notes_f, count, n, samples, turned, rows_f):
    read = lambda first, chunk: all_samples(notes_f, count, n, samples, first, chunk)
    base = lambda number: plan.segments[number][0]
    g_cond, g_time = 0, samples * WIDTH
    act, basis, classes = 2 * samples * WIDTH, 3 * samples * WIDTH, samples * (3 * WIDTH + FREQ_CHUNKS)
    patch_bias = classes + samples
    add_rows(here, plan, base(0), rows_f, all_summed(notes_f, count, n, patch_bias + WIDTH, ROWS * WIDTH))
    add_rows(here, plan, base(1), rows_f, all_summed(notes_f, count, n, patch_bias, WIDTH))
    size = window(plan, WIDTH)
    low = lambda first: lambda c: read(first, c).astype(low_type)
    add_outer(here, plan, base(2), WIDTH, FREQ, rows_f, turned_left(turned, size, FREQ, lambda j: read(basis, j)), low(g_time))
    add_outer(here, plan, base(4), WIDTH, D, rows_f, turned_left(turned, size, D, lambda j: read(act, j)), low(g_cond))
    kind = read(classes, 0).T
    kind = kind[0:1, :] * CLASS_SPLIT + kind[HD : HD + 1, :]

    def picked(first, rows):
        line = lax.broadcasted_iota(jnp.int32, (rows, n * samples), 0) + first
        return (line.astype(full_type) == kind).astype(low_type)

    add_outer(here, plan, base(6), WIDTH, CLS, rows_f, picked, low(g_cond))
    for number, first in ((3, g_time), (5, g_cond)):
        value = jnp.concatenate([rows_sum(read(first, c)) for c in range(WIDTH)], axis=0)
        add_rows(here, plan, base(number), rows_f, value)


CLASS_SPLIT = 32


def owner_range(plan, numbers):
    first = plan.segments[numbers[0]][0] * LANES // plan.share
    stop = plan.segments[numbers[-1]]
    end = stop[0] * LANES + math.prod(stop[4])
    return first, min((end - 1) // plan.share, plan.devices - 1)


def held_whole(plan, numbers):
    for number in numbers:
        base, _, _, _, shape, _ = plan.segments[number]
        start, stop = base * LANES // plan.share, (base * LANES + math.prod(shape) - 1) // plan.share
        if start != stop or base < start * plan.share // LANES or base >= (start + 1) * plan.share // LANES:
            return False
    return True


SHARES = (1.0, 1.0, 0.2)
LAST_PHASE = LAYERS
WEIGHTS = (14, 3, 14, 8, 10)


def backward_kernel(plans, zs, rows, *refs):
    np_ = len(plans)
    feed = iter(refs)
    take = lambda count: tuple(next(feed) for _ in range(count))
    one = lambda: next(feed)
    root_grads = one()
    units = take(np_)
    stream = take(LAYERS)
    saved = [take(len(SAVED)) for _ in range(LAYERS)]
    grad_in, = take(1)
    mods = take(LAYERS)
    modulator, condition, time_pre, cond_in, noisy, basis, classes, stats_in = take(8)
    layer_grads = take(LAYERS)
    flats = take(np_)
    stats_out = one()
    first = take(np_)
    own_units = take(np_)
    halo_before, halo_after, boxes = take(np_), take(np_), take(np_)
    buffers = ((one(), one()), (one(), one()), (one(), one()), one(), one(), one(), one())
    total, total_in = take(2)
    sems = take(9)
    frees = take(3)
    load_sem, chunk_sem, out_sem, own_sem, halo_s, halo_r, ss, sr, note_s, note_r, note_own = take(11)
    note, note_low = take(2)
    here = Place(zs)
    here.greet()
    root = plans[0]
    samples = rows // SEQ
    layers = list(reversed(range(LAYERS)))
    planes = lambda p: min(zs, -(-p.segments[4][3] // (8 * p.per)))
    buckets = [(root, root_grads, 0, zs)]
    buckets += [(plans[1 + i], layer_grads[i], 0, planes(plans[1 + i])) for i in layers]
    outs = [own_units[0]] + [own_units[1 + i] for i in layers]
    owners = [owner_range(root, range(FRONT))] + [owner_range(p, range(4, 11)) for p in plans[1:]]
    notes = Notes(here, note.shape[0], samples, owners, boxes, note_low, note_s, note_r, note_own)
    hosts = sorted({d for lo, hi in owners for d in range(lo, hi + 1)})
    hosting = functools.reduce(lambda a, b: a | b, [notes.owned(i) for i in range(np_)])

    @pl.when(hosting)
    def _():
        for to in range(here.n):

            @pl.when(here.me != to)
            def _():
                pl.semaphore_signal(pltpu.get_barrier_semaphore(), inc=1, device_id=(to,), device_id_type=MESH)

    pl.semaphore_wait(pltpu.get_barrier_semaphore(), len(here.peers()) + len(hosts) - hosting.astype(jnp.int32))
    work = Reduce(here, buckets, first, buffers, sems, frees)
    work.open(0)
    steps = [work.steps(g, outs, own_sem) for g in range(len(work.groups) + LOOK + 2)]
    flat = [(g, step) for g, group in enumerate(steps) for step in group]
    upto = lambda b: sum(len(group) for group in steps[: b * zs])
    cuts = [0]
    for position, share in enumerate(SHARES):
        cuts.append(max(cuts[-1], upto(position) + int(share * (upto(position + 1) - upto(position)))))
    of_phase = lambda p: [step for _, step in flat[cuts[p] : cuts[p + 1]]]

    def compute(grad, cond, *held):
        grad[...] = grad_in[...]
        cond[...] = cond_in[...]
        for position, ordinal in enumerate(layers):
            layer_backward_body(
                plans[1 + ordinal], rows, stream[ordinal], saved[ordinal], units[1 + ordinal], layer_grads[ordinal],
                mods[ordinal], grad, modulator, cond, note, samples, held, (load_sem, chunk_sem, out_sem), spread(of_phase(position), WEIGHTS),
            )
            work.open(1 + position)
            notes.send(1 + ordinal, note)
        embed_back(grad, cond)

    def embed_back(grad, cond):
        def run(front_w):
            load = pltpu.make_async_copy(units[0].at[pl.ds(root.segments[4][3], root.segments[4][2])], front_w, load_sem.at[0])
            load.start()
            events = spread(of_phase(LAYERS), (1, 1))
            low = grad[...].astype(low_type)
            patch = dot_tn(noisy[...], low)
            at = samples * (3 * WIDTH + FREQ_CHUNKS)
            note[at : at + samples, :] = classes[0:samples, :]
            put_row(note, at + samples, rows_sum(low.astype(full_type)))
            for c in range(WIDTH):
                note[pl.ds(at + samples + WIDTH + c, ROWS, stride=WIDTH), :] = patch[:, c * LANES : (c + 1) * LANES]
            for event in events[0]:
                event()
            g_low = (silu_parts(condition[...])[1] * cond[...]).astype(low_type)
            act, slope = silu_parts(time_pre[...])
            load.wait()
            w_t2 = jnp.concatenate(
                [jnp.concatenate([front_w[b * WIDTH + c] for b in range(D // ROWS)], axis=0) for c in range(WIDTH)], axis=1
            )
            grad_pre = dot_nt(g_low, w_t2) * slope
            put_samples(note, 0, g_low.astype(full_type), samples)
            put_samples(note, samples * WIDTH, grad_pre, samples)
            put_samples(note, 2 * samples * WIDTH, act, samples)
            put_samples(note, 3 * samples * WIDTH, basis[...].astype(full_type), samples)
            notes.send(0, note)
            for event in events[1]:
                event()

        pl.run_scoped(run, pltpu.VMEM((root.segments[4][2], ROWS, LANES), low_type))

    plan = plans[1]
    f32 = lambda *dims: pltpu.VMEM(dims, full_type)
    bf16 = lambda *dims: pltpu.VMEM(dims, low_type)
    tile = (ROWS, LANES)
    few = modulator.shape[0]
    pl.run_scoped(
        compute,
        f32(rows, D), f32(few, D),
        bf16(rows, 3 * D), bf16(rows, D), bf16(rows, D), f32(rows, D), f32(rows, D), f32(2, rows, WIDE),
        bf16(2, D // ROWS, 2, *tile), bf16(2, WIDE // ROWS, D // LANES, *tile),
        segment_scratch(plan, 0), segment_scratch(plan, 1),
        bf16(rows, 3 * D), bf16(rows, D), bf16(rows, WIDE), bf16(D, rows), f32(rows, D),
        bf16(2, WIDE // ROWS, D // LANES, *tile), bf16(2, D // ROWS, 2, *tile),
        f32(few, 6 * D), f32(1, 4 * D + FF),
    )

    def unpack(units_f, rows_f, flat_f, box, notes_f, *turned):
        def halo(i):
            p = plans[i]
            forward = remote(own_units[i].at[pl.ds(p.per - p.units_before, p.units_before)], halo_before[i], halo_s.at[i, 0], halo_r.at[i, 0], here.following)
            backward = remote(own_units[i].at[pl.ds(0, p.units_after)], halo_after[i], halo_s.at[i, 1], halo_r.at[i, 1], here.prev)
            return forward, backward

        def finish(i):
            p = plans[i]
            base = p.units_before
            for copy in halo(i):
                copy.wait()
            parts = (
                pltpu.make_async_copy(halo_before[i], units_f.at[pl.ds(0, base)], load_sem.at[0]),
                pltpu.make_async_copy(own_units[i], units_f.at[pl.ds(base, p.per)], load_sem.at[1]),
                pltpu.make_async_copy(halo_after[i], units_f.at[pl.ds(base + p.per, p.units_after)], load_sem.at[2]),
            )
            for copy in parts:
                copy.start()
            for copy in parts:
                copy.wait()
            rows_f[...] = jnp.zeros(rows_f.shape, full_type)

            @pl.when(notes.owned(i))
            def _():
                notes.receive(i)
                copy = pltpu.make_async_copy(boxes[i], box, load_sem.at[4])
                copy.start()
                copy.wait()
                count = box.shape[1]

                def widen(d):
                    notes_f[pl.ds(pl.multiple_of(d * count, ROWS), count), :] = box[d].astype(full_type)

                loop(here.n, widen)
                extra = layer_extra if i else front_extra
                extra(here, p, notes_f, count, here.n, samples, turned[1 if i else 0], rows_f)

            squares = unpack_rows(here, p, p.reduced, units_f, rows_f, flat_f, base)
            store = pltpu.make_async_copy(flat_f.at[pl.ds(0, p.raw)], flats[i], load_sem.at[3])
            store.start()
            store.wait()
            total[1] += squares

        total[0] = stats_in[...]
        total[1] = jnp.zeros((8, LANES), full_type)
        ready = [0] + [1 + ordinal for ordinal in layers]
        begun, done = {}, set()

        def between(g):
            for b, i in enumerate(ready):
                if i not in begun and g > zs * (b + 1) + LOOK + 1:
                    begun[i] = g
                    for copy in halo(i):
                        copy.start()
                elif i in begun and i not in done and g > begun[i]:
                    done.add(i)
                    finish(i)
                    return

        seen = -1
        for g, step in flat[cuts[-1] :]:
            if g != seen and g > LAST_PHASE * zs:
                between(g)
            seen = g
            step()
        for extra in range(2 * len(ready)):
            between(len(steps) + extra)

    most = max(p.units_before + p.per + p.units_after for p in plans)
    pl.run_scoped(
        unpack,
        f32(most, *tile), f32(max(max(p.spread, p.margin + c * window(p, c)) for p in plans for c in (WIDTH, MOD_CHUNKS)), LANES),
        f32(max(p.raw for p in plans), LANES),
        pltpu.VMEM(boxes[0].shape, low_type), f32(boxes[0].shape[0] * boxes[0].shape[1], LANES),
        f32(D + 2 * window(root, WIDTH), samples * here.n), f32(D + 2 * window(plan, MOD_CHUNKS), samples * here.n),
    )
    step = 0
    for to in ((here.cpeer,), (here.xpeer,), (here.ypeer,), tuple(here.above(k) for k in range(1, zs))):
        copies = []
        for peer in to:
            copies.append(remote(total, total_in.at[step], ss.at[step], sr.at[step], peer))
            copies[-1].start()
            step += 1
        for copy in copies:
            copy.wait()
        value = total[...]
        for i in range(len(to)):
            value = value + total_in[step - 1 - i]
        total[...] = value
    stats_out[...] = total[...]
    notes.drain(np_)
    work.close()


def backward_call(plans, units, stream, saved, grad, mods, small, stats, root_grads):
    n = plans[0].devices
    zs = n // 8
    rows = grad.shape[0]
    np_ = nb = len(plans)
    count = note_rows(rows // SEQ)
    vm = pl.BlockSpec(memory_space=pltpu.VMEM)
    hbm = pl.BlockSpec(memory_space=pltpu.HBM)
    shape = jax.ShapeDtypeStruct
    dma, regular = pltpu.SemaphoreType.DMA, pltpu.SemaphoreType.REGULAR
    tile = (ROWS, LANES)
    layers = list(reversed(range(LAYERS)))
    order = [plans[0]] + [plans[1 + i] for i in layers]
    all_units = lambda p: shape((n * p.per,) + tile, low_type)
    out_shape = [all_units(p) for p in plans[1:]]
    out_shape += [shape((p.raw, LANES), full_type) for p in plans]
    out_shape += [shape((2, 8, LANES), full_type)]
    out_shape += [shape((zs, 2, 2, p.per) + tile, low_type) for p in order]
    out_shape += [shape((p.per,) + tile, full_type) for p in plans]
    out_shape += [shape((p.units_before,) + tile, full_type) for p in plans]
    out_shape += [shape((p.units_after,) + tile, full_type) for p in plans]
    out_shape += [shape((n, count, LANES), low_type) for p in plans]
    most = max(p.per for p in plans)
    half = lambda *lead: pltpu.VMEM(lead + (most // 2,) + tile, low_type)
    hops = 2 + zs
    scratch = [half(zs, 2)] * 4 + [half(zs)] * 2 + [half(2, 2, zs - 1)]
    scratch += [pltpu.VMEM((3 * LOOK + 4, most) + tile, low_type), pltpu.VMEM((2, most) + tile, low_type)]
    scratch += [pltpu.VMEM((most,) + tile, full_type)]
    scratch += [pltpu.VMEM((2, 8, LANES), full_type), pltpu.VMEM((hops, 2, 8, LANES), full_type)]
    scratch += [dma((nb, zs, 2, 2))] * 2 + [dma((2, zs, 2))] * 2 + [dma((2, zs))] * 2 + [dma((2, 2, zs - 1))] * 2 + [dma((3 * LOOK + 4, 2))]
    scratch += [regular((2, zs)), regular((2, zs)), regular((zs - 1,))]
    scratch += [dma((7,)), dma((2, 3)), dma((4,)), dma, dma((np_, 2)), dma((np_, 2)), dma((hops,)), dma((hops,))]
    scratch += [dma((np_, n)), dma((np_,)), dma((np_,))]
    scratch += [pltpu.VMEM((count, LANES), full_type), pltpu.VMEM((np_, count, LANES), low_type)]
    flat_saved = [array for group in saved for array in group]
    results = pl.pallas_call(
        functools.partial(backward_kernel, plans, zs, rows),
        out_shape=out_shape,
        in_specs=[hbm] * (1 + np_ + LAYERS + len(flat_saved)) + [vm] * (1 + LAYERS + len(small) + 1),
        out_specs=[hbm] * (2 * np_ - 1) + [vm] + [hbm] * (nb + 4 * np_),
        scratch_shapes=scratch,
        compiler_params=pltpu.CompilerParams(collective_id=1, has_side_effects=True, vmem_limit_bytes=62 * MB),
        name="backward_and_reduce",
    )(root_grads, *units, *stream, *flat_saved, grad, *mods, *small, stats)
    return results[np_ - 1 : 2 * np_ - 1], results[2 * np_ - 1]


def model_step(layer_lists, pieces, latents, noise, times, labels, dropped, features, devices):
    sample_total = latents.shape[0] * devices
    residual, modulator, embed_saved = embed_forward(
        pieces, latents, noise, times, labels, dropped
    )
    loss_total = jnp.zeros((), full_type)
    inputs, kept, square_sums = [], [], []
    for ordinal in range(LAYERS):
        inputs.append(residual)
        residual, saved, sums = layer_forward(layer_lists[ordinal], residual, modulator)
        kept.append(saved)
        square_sums.append(sums)
        if ordinal + 1 == DEPTH_Z:
            part, proj_saved = projector_forward(pieces, residual, features)
            loss_total = loss_total + part
    target = noise - latents
    weight_t = 1.0 + 2.0 * times
    part, head_saved = head_forward(pieces, residual, modulator, target, weight_t)
    loss_total = loss_total + part
    grad_residual, grad_cond, head_grads = head_backward(
        pieces, head_saved, residual, modulator, weight_t, sample_total
    )
    layer_grads = [None] * LAYERS
    for ordinal in reversed(range(LAYERS)):
        if ordinal + 1 == DEPTH_Z:
            grad_proj, proj_grads = projector_backward(
                pieces, proj_saved, features, residual.shape[1], sample_total
            )
            grad_residual = grad_residual + grad_proj
        grad_residual, cond_part, layer_grads[ordinal] = layer_backward(
            layer_lists[ordinal], kept[ordinal], inputs[ordinal], modulator, grad_residual
        )
        grad_cond = grad_cond + cond_part
    embed_grads = embed_backward(pieces, embed_saved, grad_residual, grad_cond)
    return (loss_total, jnp.stack(square_sums), layer_grads, embed_grads + proj_grads + head_grads)


def adam_update(weight, grad, first, second, clip_factor):
    clipped = grad * clip_factor
    first_new = beta_one * first + (1.0 - beta_one) * clipped
    second_new = beta_two * second + (1.0 - beta_two) * clipped * clipped
    first_hat = first_new / (1.0 - beta_one**STEP)
    second_hat = second_new / (1.0 - beta_two**STEP)
    weight_new = weight - learn_rate * (
        first_hat / (jnp.sqrt(second_hat) + adam_eps) + decay_rate * weight
    )
    return (weight_new, first_new, second_new)


def vector_of(units, plan, number):
    _, _, count, first, shape, _ = plan.segments[number]
    flat = units[first : first + count].reshape(-1)[: math.prod(shape)]
    return flat.reshape(shape)


def matrix_of(units, plan, number):
    _, chunks, count, first, shape, _ = plan.segments[number]
    part = units[first : first + count].reshape(shape[0] // ROWS, chunks, ROWS, LANES)
    return part.transpose(0, 2, 1, 3).reshape(shape)


def units_of(grad, plan, number):
    _, chunks, count, _, shape, matrix = plan.segments[number]
    low = grad.astype(low_type)
    if matrix:
        low = low.reshape(shape[0] // ROWS, ROWS, chunks, LANES).transpose(0, 2, 1, 3)
        return low.reshape(count, ROWS, LANES)
    flat = jnp.pad(low.reshape(-1), ((0, count * UNIT - low.size),))
    return flat.reshape(count, ROWS, LANES)


def put_units(grads, plan, first_number, values):
    parts = [units_of(value, plan, first_number + i) for i, value in enumerate(values)]
    joined = jnp.concatenate(parts) if len(parts) > 1 else parts[0]
    return lax.dynamic_update_slice(grads, joined, (plan.segments[first_number][3], 0, 0))


def as_row(vector):
    return vector.astype(full_type).reshape(1, -1)


def by_kernels(plan, root_plan, layer_flat, root_flat, data, devices):
    latents, noise, times, labels, dropped, features = data
    samples = latents.shape[0]
    sample_total = samples * devices
    rows = samples * SEQ
    few = up(samples, ROWS)
    wide = D // LANES
    plans = (root_plan,) + (plan,) * LAYERS
    raws = [to_rows(root_flat, root_plan)]
    raws += [to_rows(layer_flat[ordinal], plan) for ordinal in range(LAYERS)]
    mixing = times[:, None, None]
    noisy_bf = ((1.0 - mixing) * latents + mixing * noise).astype(low_type)
    positions = jnp.tile(position_table(), (samples, 1))
    basis_bf = time_features(times).astype(low_type)
    classes = jnp.where(dropped == 1, CLS - 1, labels)
    extra = lambda value: jnp.pad(value, ((0, few - samples),) + ((0, 0),) * (value.ndim - 1))
    wanted = jnp.pad(classes, (0, few - samples), constant_values=-1)
    wanted = jnp.where(wanted < 0, -wide, wanted * wide)[None, :] + jnp.arange(wide)[:, None]
    wanted = jnp.where(wanted < 0, -1, wanted).reshape(-1, 1)
    table_rows = root_plan.segments[6][2] * ROWS
    chosen = (wanted == jnp.arange(table_rows, dtype=jnp.int32)[None, :]).astype(low_type)
    units, stream, mods, sums, modulator_rows, condition, time_pre, kept = forward_call(
        plans, raws, noisy_bf.reshape(rows, PD), positions, extra(basis_bf), chosen
    )
    root_units, *layer_units = units
    residual = stream[-1]
    target = jnp.pad((noise - latents).reshape(rows, PD), ((0, 0), (0, LANES - PD)))
    weight_t = jnp.broadcast_to(jnp.pad(1.0 + 2.0 * times, (0, 8 - samples))[:, None], (8, LANES))
    w_h = jnp.pad(vector_of(root_units, root_plan, 15), ((0, 0), (0, LANES - PD)))
    b_h = jnp.pad(as_row(vector_of(root_units, root_plan, 16)), ((0, 0), (0, LANES - PD)))
    biases = [as_row(vector_of(root_units, root_plan, i)) for i in (8, 10, 12, 14)]
    grad, losses, grad_cond, bias_grads, grad_w_h, root_grads = top_call(
        root_plan, sample_total, residual, features.reshape(rows, ZD), target, weight_t, modulator_rows, biases, w_h, b_h, root_units
    )
    loss_part = -proj_coeff / SEQ * losses[0, 0] + jnp.sum(losses[1]) / (SEQ * PD)
    cuts = jnp.split(bias_grads[0], (PH, 2 * PH, 2 * PH + ZD, 2 * PH + ZD + 2 * D))
    for number, value in zip((8, 10, 12), cuts):
        root_grads = put_units(root_grads, root_plan, number, [value])
    root_grads = put_units(root_grads, root_plan, 14, [cuts[3], grad_w_h[:, :PD], cuts[4][:PD]])
    square_sums = jnp.stack([jnp.sum(total[:3], axis=1) for total in sums])
    numbers = jnp.concatenate([loss_part[None], square_sums.reshape(-1)])
    stats = jnp.pad(numbers, (0, 8 * LANES - numbers.shape[0])).reshape(8, LANES)
    class_parts = jnp.stack([classes // CLASS_SPLIT, classes % CLASS_SPLIT], axis=1)
    class_rows = extra(jnp.repeat(class_parts.astype(full_type), LANES // 2, axis=1))
    small = (modulator_rows, condition, time_pre, grad_cond, noisy_bf.reshape(rows, PD), extra(basis_bf), class_rows)
    rows_out, stats = backward_call(
        plans, units, stream[:-1], kept, grad, mods, small, stats, root_grads
    )
    numbers = stats[0].reshape(-1)
    shard_root = rows_out[0].reshape(-1)[: root_plan.share]
    shard_layers = jnp.stack([r.reshape(-1)[: plan.share] for r in rows_out[1:]])
    stream_sums = numbers[1 : 1 + 3 * LAYERS].reshape(LAYERS, 3)
    return (shard_layers, shard_root, numbers[0], stream_sums, jnp.sum(stats[1]))


def by_collectives(layer_flat, root_flat, data, devices):
    whole = lambda part: lax.all_gather(part.astype(low_type), "fsdp", axis=0, tiled=True)
    layer_lists = [unflatten(whole(layer_flat[i]), layer_layout()) for i in range(LAYERS)]
    pieces = unflatten(whole(root_flat), root_layout())
    loss_part, square_sums, layer_grads, root_grads = model_step(
        layer_lists, pieces, *data, devices
    )

    def owned(grad_list, share):
        joined = jnp.concatenate([piece.reshape(-1) for piece in grad_list])
        joined = jnp.pad(joined, (0, share * devices - joined.shape[0]))
        return lax.psum_scatter(joined, "fsdp", scatter_dimension=0, tiled=True)

    shard_layers = jnp.stack([owned(grads, layer_flat.shape[1]) for grads in layer_grads])
    shard_root = owned(root_grads, root_flat.shape[0])
    local = jnp.sum(shard_layers * shard_layers) + jnp.sum(shard_root * shard_root)
    loss_sum, sums, square_total = lax.psum((loss_part, square_sums, local), "fsdp")
    return (shard_layers, shard_root, loss_sum, sums, square_total)


def shards(
    latents,
    noise,
    times,
    labels,
    dropped,
    features,
    layer_flat,
    layer_mean,
    layer_square,
    root_flat,
    root_mean,
    root_square,
):
    devices = lax.axis_size("fsdp")
    data = (latents, noise, times, labels, dropped, features)
    plan = Plan(layer_layout(), layer_flat.shape[1] * devices, devices, (0, 4))
    root_plan = Plan(root_layout(), root_flat.shape[0] * devices, devices, (FRONT, None))
    alone = held_whole(plan, range(5, 11)) and held_whole(root_plan, (0, 1, 3, 5))
    if devices % 8 == 0 and plan.fits and root_plan.fits and alone:
        reduced = by_kernels(plan, root_plan, layer_flat, root_flat, data, devices)
    else:
        reduced = by_collectives(layer_flat, root_flat, data, devices)
    shard_layers, shard_root, loss_sum, stream_sums, square_total = reduced
    sample_total = latents.shape[0] * devices
    grad_norm = jnp.sqrt(square_total)
    clip_factor = clip_limit / jnp.maximum(grad_norm, clip_limit)
    activation_rms = jnp.sqrt(stream_sums / (sample_total * SEQ * D))
    new_layer, new_layer_mean, new_layer_square = adam_update(
        layer_flat, shard_layers, layer_mean, layer_square, clip_factor
    )
    new_root, new_root_mean, new_root_square = adam_update(
        root_flat, shard_root, root_mean, root_square, clip_factor
    )
    return (
        loss_sum,
        grad_norm,
        activation_rms,
        new_layer,
        new_layer_mean,
        new_layer_square,
        new_root,
        new_root_mean,
        new_root_square,
    )


def solution(mesh):
    in_specs = (
        P("fsdp", None, None),
        P("fsdp", None, None),
        P("fsdp"),
        P("fsdp"),
        P("fsdp"),
        P("fsdp", None, None),
        P(None, "fsdp"),
        P(None, "fsdp"),
        P(None, "fsdp"),
        P("fsdp"),
        P("fsdp"),
        P("fsdp"),
    )
    out_specs = (
        P(),
        P(),
        P(),
        P(None, "fsdp"),
        P(None, "fsdp"),
        P(None, "fsdp"),
        P("fsdp"),
        P("fsdp"),
        P("fsdp"),
    )
    return jax.shard_map(shards, mesh=mesh, in_specs=in_specs, out_specs=out_specs, check_vma=False)
```

```python
import functools
import math

import jax
import jax.numpy as jnp
from jax import lax
from jax.experimental import pallas as pl
from jax.experimental.pallas import tpu as pltpu
from jax.sharding import PartitionSpec as P

D = 768
HD = 64
FF = 3072
PD = 16
CLS = 1001
PH = 2048
ZD = 768
FREQ = 256
GRID = 16
LAYERS = 2
DEPTH_Z = 2
STEP = 10
SEQ = 256


norm_eps = 1e-06
clip_limit = 0.002
learn_rate = 0.08
beta_one = 0.5
beta_two = 0.5
adam_eps = 1e-08
decay_rate = 0.01
proj_coeff = 0.5
low_type = jnp.bfloat16
full_type = jnp.float32


LANES = 128
ROWS = 16
UNIT = LANES * ROWS
MESH = pl.DeviceIdType.MESH

def up(value, step):
    return -(-value // step) * step

class Plan:
    def __init__(self, layout, length, devices, reduced):
        self.length = length
        self.devices = devices
        self.share = length // devices
        self.segments = []
        offset = units = 0
        for shape in layout:
            amount = math.prod(shape)
            matrix = len(shape) == 2 and shape[0] % ROWS == 0 and shape[1] % LANES == 0
            chunks = shape[1] // LANES if matrix else 1
            count = up(amount, UNIT) // UNIT
            self.segments.append((offset // LANES, chunks, count, units, shape, matrix))
            offset += amount
            units += count
        self.units = units
        self.reduced = self.segments[reduced[0] : reduced[1]]
        self.moved = lambda u: self.reduced[0][3] <= u < self.reduced[-1][3] + self.reduced[-1][2]
        self.per = up(up(units, devices) // devices, 4)
        rows_of = []
        for base, chunks, count, _, _, _ in self.segments:
            for u in range(count):
                b, c = divmod(u, chunks)
                first = base + b * ROWS * chunks + c
                rows_of.append((first, first + (ROWS - 1) * chunks))
        before = after = 0
        for d in range(devices):
            start, stop = d * self.share // LANES, (d + 1) * self.share // LANES
            for lo, hi in rows_of[self.per * d : self.per * d + self.per]:
                before, after = max(before, start - lo), max(after, hi + 1 - stop)
        self.before, self.after = up(before, 8), up(after, 8)
        units_before = units_after = 0
        for u, (lo, hi) in enumerate(rows_of):
            if not self.moved(u):
                continue
            first = lo * LANES // self.share
            last = min(((hi + 1) * LANES - 1) // self.share, devices - 1)
            for d in range(first, last + 1):
                units_before = max(units_before, self.per * d - u)
                units_after = max(units_after, u + 1 - self.per * d - self.per)
        self.units_before, self.units_after = units_before, units_after
        self.half = self.per // 2
        self.raw = up(up(self.share, LANES) // LANES + 9, 64)
        self.ext = self.before + self.raw + self.after
        margin = tail = 0
        for d in range(devices):
            start = d * self.share // LANES
            lo = max(self.per * d - units_before, 0)
            for first, last in rows_of[lo : self.per * d + self.per + units_after]:
                margin, tail = max(margin, start - first), max(tail, last + 1 - start)
        self.margin = up(margin, 8)
        self.spread = up(max(tail, self.raw + 8), 8) + self.margin
        least = self.share // LANES
        self.fits = max(self.before, self.after) < least and max(units_before, units_after) < self.per

def place(index, zs):
    return index // 8, index // 4 % 2, index // 2 % 2, index % 2

def gather_kernel(plans, zs, *refs):
    nb = len(plans)
    raw_hbm = refs[:nb]
    outs = refs[nb : 2 * nb]
    raw, ext, tail, from_prev, from_next, slots = (refs[2 * nb + i * nb : 3 * nb + i * nb] for i in range(6))
    rest = refs[8 * nb :]
    load_sem, halo_send, halo_recv, own_sem, send_sem, zr, xa, xb, yb, ya, cr = rest
    n = zs * 8
    me = lax.axis_index("fsdp")
    z, y, x, c = place(me, zs)
    index = lambda zz, yy, xx, cc: ((zz * 2 + yy) * 2 + xx) * 2 + cc
    prev, following = lax.rem(me + n - 1, n), lax.rem(me + 1, n)
    xpeer, ypeer, cpeer = index(z, y, 1 - x, c), index(z, 1 - y, x, c), index(z, y, x, 1 - c)
    zpeer = [index(lax.rem(z + k, zs), y, x, c) for k in range(zs)]
    loads = []
    for b in range(nb):
        p = plans[b]
        loads.append(pltpu.make_async_copy(raw_hbm[b], raw[b].at[pl.ds(8, p.raw)], load_sem.at[b]))
        loads[b].start()
    barrier = pltpu.get_barrier_semaphore()
    peers = [prev, following, xpeer, ypeer, cpeer] + zpeer[1:]
    for peer in peers:
        pl.semaphore_signal(barrier, inc=1, device_id=(peer,), device_id_type=MESH)
    halos = []
    lane = lax.broadcasted_iota(jnp.int32, (64, LANES), 1)
    for b in range(nb):
        p = plans[b]
        shift = lax.rem(me * p.share, LANES)
        delta = (me + 1) * p.share // LANES - me * p.share // LANES
        raw[b][pl.ds(0, 8), :] = jnp.zeros((8, LANES), full_type)
        ext[b][pl.ds(0, p.before), :] = jnp.zeros((p.before, LANES), full_type)
        ext[b][pl.ds(p.before + p.raw, p.after), :] = jnp.zeros((p.after, LANES), full_type)
        loads[b].wait()

        def align(i, carry):
            row = pl.multiple_of(i * 64, 64)
            here = pltpu.roll(raw[b][pl.ds(row + 8, 64), :], shift, 1)
            above = pltpu.roll(raw[b][pl.ds(row + 7, 64), :], shift, 1)
            ext[b][pl.ds(row + p.before, 64), :] = jnp.where(lane >= shift, here, above)
            return carry

        lax.fori_loop(0, p.raw // 64, align, 0)
        tail[b][...] = ext[b][pl.ds(delta, p.before + 8), :]
        if b == 0:
            pl.semaphore_wait(barrier, len(peers))
        for s, (src, dst, to) in enumerate(((ext[b].at[pl.ds(p.before, p.after)], from_next[b], prev), (tail[b], from_prev[b], following))):
            copy = pltpu.make_async_remote_copy(src, dst, halo_send.at[2 * b + s], halo_recv.at[2 * b + s], device_id=(to,), device_id_type=MESH)
            copy.start()
            halos.append(copy)
    sends = []

    def send(src, dst, sem, to):
        copy = pltpu.make_async_remote_copy(src, dst, send_sem.at[len(sends)], sem, device_id=(to,), device_id_type=MESH)
        copy.start()
        sends.append(copy)

    def span(b, h):
        p = plans[b]
        return (0, p.half) if h == 0 else (p.half, p.per - p.half)

    def slot(k, dy, dx, dc):
        return index(lax.rem(z + zs - k, zs), 1 - y if dy else y, 1 - x if dx else x, 1 - c if dc else c)

    def part(b, h, k, dy, dx, dc=0):
        first, count = span(b, h)
        return outs[b].at[pl.ds(slot(k, dy, dx, dc) * plans[b].per + first, count)]

    def whole(b, k, dy, dx, dc=0):
        return outs[b].at[pl.ds(slot(k, dy, dx, dc) * plans[b].per, plans[b].per)]

    def arrived(ref, sem):
        pltpu.make_async_copy(ref, ref, sem).wait()

    owns = []
    for b in range(nb):
        p = plans[b]
        delta = (me + 1) * p.share // LANES - me * p.share // LANES
        for copy in halos[2 * b : 2 * b + 2]:
            copy.wait()
        ext[b][pl.ds(0, p.before + 8), :] += from_prev[b][...]
        ext[b][pl.ds(p.before + delta, p.after), :] += from_next[b][...]
        top = me * p.share // LANES - p.before
        for base, chunks, count, first_unit, _, _ in p.segments:
            lo = jnp.clip(p.per * me - first_unit, 0, count)
            hi = jnp.clip(p.per * me + p.per - first_unit, 0, count)

            def unit(u, carry):
                block = u // chunks
                row = base + block * (ROWS * chunks) + (u - block * chunks) - top
                if chunks == 1:
                    value = ext[b][pl.ds(row, ROWS), :]
                else:
                    value = ext[b][pl.ds(row, ROWS, stride=chunks), :]
                slots[b][first_unit + u - p.per * me] = value.astype(low_type)
                return carry

            lax.fori_loop(lo, hi, unit, 0)
        own = pltpu.make_async_copy(slots[b], whole(b, 0, 0, 0), own_sem.at[b])
        own.start()
        owns.append(own)
        mine = lambda h: slots[b].at[pl.ds(*span(b, h))]
        for k in range(1, zs):
            for h in range(2):
                send(mine(h), part(b, h, 0, 0, 0), zr.at[b, h, k], zpeer[k])
        send(mine(0), part(b, 0, 0, 0, 0), xa.at[b, 0], xpeer)
        send(mine(1), part(b, 1, 0, 0, 0), yb.at[b, 0], ypeer)
        send(mine(0), part(b, 0, 0, 0, 0), ya.at[b, 0, 0], ypeer)
        send(mine(1), part(b, 1, 0, 0, 0), xb.at[b, 0, 0], xpeer)
        send(slots[b], whole(b, 0, 0, 0), cr.at[b, 0, 0, 0], cpeer)
    for b in range(nb):
        for k in range(1, zs):
            arrived(part(b, 0, k, 0, 0), zr.at[b, 0, k])
            send(part(b, 0, k, 0, 0), part(b, 0, k, 0, 0), xa.at[b, k], xpeer)
            arrived(part(b, 1, k, 0, 0), zr.at[b, 1, k])
            send(part(b, 1, k, 0, 0), part(b, 1, k, 0, 0), yb.at[b, k], ypeer)
            send(part(b, 0, k, 0, 0), part(b, 0, k, 0, 0), ya.at[b, k, 0], ypeer)
            send(part(b, 1, k, 0, 0), part(b, 1, k, 0, 0), xb.at[b, k, 0], xpeer)
            send(whole(b, k, 0, 0), whole(b, k, 0, 0), cr.at[b, k, 0, 0], cpeer)
        for k in range(zs):
            arrived(part(b, 0, k, 0, 1), xa.at[b, k])
            send(part(b, 0, k, 0, 1), part(b, 0, k, 0, 1), ya.at[b, k, 1], ypeer)
            arrived(part(b, 1, k, 1, 0), yb.at[b, k])
            send(part(b, 1, k, 1, 0), part(b, 1, k, 1, 0), xb.at[b, k, 1], xpeer)
        for k in range(zs):
            arrived(part(b, 1, k, 0, 1), xb.at[b, k, 0])
            send(whole(b, k, 0, 1), whole(b, k, 0, 1), cr.at[b, k, 0, 1], cpeer)
            arrived(part(b, 0, k, 1, 0), ya.at[b, k, 0])
            send(whole(b, k, 1, 0), whole(b, k, 1, 0), cr.at[b, k, 1, 0], cpeer)
        for k in range(zs):
            arrived(part(b, 1, k, 1, 1), xb.at[b, k, 1])
            arrived(part(b, 0, k, 1, 1), ya.at[b, k, 1])
            send(whole(b, k, 1, 1), whole(b, k, 1, 1), cr.at[b, k, 1, 1], cpeer)
    for b in range(nb):
        owns[b].wait()
        for k in range(zs):
            for dy in range(2):
                for dx in range(2):
                    arrived(whole(b, k, dy, dx, 1), cr.at[b, k, dy, dx])
    for copy in sends:
        copy.wait_send()

def gather_units(plans, raws):
    n = plans[0].devices
    zs = n // 8
    nb = len(plans)
    per_bucket = 2 * (zs - 1) + 10 * zs
    dma = pltpu.SemaphoreType.DMA
    scratch = [pltpu.VMEM((p.raw + 8, LANES), full_type) for p in plans]
    scratch += [pltpu.VMEM((p.ext, LANES), full_type) for p in plans]
    scratch += [pltpu.VMEM((p.before + 8, LANES), full_type) for p in plans]
    scratch += [pltpu.VMEM((p.before + 8, LANES), full_type) for p in plans]
    scratch += [pltpu.VMEM((p.after, LANES), full_type) for p in plans]
    scratch += [pltpu.VMEM((p.per, ROWS, LANES), low_type) for p in plans]
    scratch += [dma((nb,)), dma((2 * nb,)), dma((2 * nb,)), dma((nb,)), dma((nb * per_bucket,))]
    scratch += [dma((nb, 2, zs)), dma((nb, zs)), dma((nb, zs, 2)), dma((nb, zs)), dma((nb, zs, 2)), dma((nb, zs, 2, 2))]
    return pl.pallas_call(
        functools.partial(gather_kernel, plans, zs),
        out_shape=[jax.ShapeDtypeStruct((n * p.per, ROWS, LANES), low_type) for p in plans],
        in_specs=[pl.BlockSpec(memory_space=pltpu.HBM)] * nb,
        out_specs=[pl.BlockSpec(memory_space=pltpu.HBM)] * nb,
        scratch_shapes=scratch,
        compiler_params=pltpu.CompilerParams(collective_id=0, has_side_effects=True, vmem_limit_bytes=48 * 1024 * 1024),
        name="gather_units",
    )(*raws)

AHEAD = 4


def reduce_kernel(plans, zs, *refs):
    nb = len(plans)
    take = lambda count: tuple(next(feed) for _ in range(count))
    feed = iter(refs)
    grads, (stats_in,) = take(nb), take(1)
    outs, (stats_out,), first = take(nb), take(1), take(nb)
    kept_a, kept_b, two_a, two_b, three_a, three_b, four = (take(nb) for _ in range(7))
    local, other = take(1)[0], take(1)[0]
    units_f, rows_f, flat_f = take(1)[0], take(1)[0], take(1)[0]
    from_prev, from_next = take(nb), take(nb)
    total, total_in = take(1)[0], take(1)[0]
    s1, r1, s2a, r2a, s2b, r2b, s3a, r3a, s3b, r3b, s4, r4, load_sem, halo_s, halo_r, out_sem, ss, sr = take(18)
    n = zs * 8
    me = lax.axis_index("fsdp")
    z, y, x, c = place(me, zs)
    index = lambda zz, yy, xx, cc: ((zz * 2 + yy) * 2 + xx) * 2 + cc
    prev, following = lax.rem(me + n - 1, n), lax.rem(me + 1, n)
    xpeer, ypeer, cpeer = index(z, y, 1 - x, c), index(z, 1 - y, x, c), index(z, y, x, 1 - c)
    below = lambda k: index(lax.rem(z + zs - k, zs), y, x, c)
    above = lambda k: index(lax.rem(z + k, zs), y, x, c)
    barrier = pltpu.get_barrier_semaphore()
    peers = [prev, following, xpeer, ypeer, cpeer] + [above(k) for k in range(1, zs)]
    for peer in peers:
        pl.semaphore_signal(barrier, inc=1, device_id=(peer,), device_id_type=MESH)
    pl.semaphore_wait(barrier, len(peers))

    def remote(src, dst, send_sem, recv_sem, to):
        return pltpu.make_async_remote_copy(src, dst, send_sem, recv_sem, device_id=(to,), device_id_type=MESH)

    def arrived(ref, sem):
        pltpu.make_async_copy(ref, ref, sem).wait()

    def slot(b, k, dy, dx, dc):
        where = index(lax.rem(z + zs - k, zs), 1 - y if dy else y, 1 - x if dx else x, 1 - c if dc else c)
        return grads[b].at[pl.ds(where * plans[b].per, plans[b].per)]

    order = ((1, 1), (1, 0), (0, 1), (0, 0))

    def sibling(b, k, dy, dx):
        return remote(slot(b, k, dy, dx, 1), first[b].at[k, dy, dx], s1.at[b, k, dy, dx], r1.at[b, k, dy, dx], cpeer)

    def add(p, dst, at, one, one_at, two, two_at):
        step = p.half // 2

        def body(i, carry):
            span = lambda ref, off: ref[pl.ds(off + i * step, step)].astype(full_type)
            dst[pl.ds(at + i * step, step)] = (span(one, one_at) + span(two, two_at)).astype(low_type)
            return carry

        lax.fori_loop(0, 2, body, 0)

    ring = local.shape[0]
    planes = list(range(1, zs)) + [0]
    used = []

    def send_of(b, h, k, dy, dx, src):
        if h == 0:
            return remote(src, two_a[b].at[k, dx], s2a.at[b, k, dx], r2a.at[b, k, dx], ypeer)
        return remote(src, two_b[b].at[k, dy], s2b.at[b, k, dy], r2b.at[b, k, dy], xpeer)

    steps = [(b, dy, dx, k) for b in range(nb) for k in planes for dy, dx in order]

    def loads(number):
        b, dy, dx, k = steps[number]
        at = number % ring
        p = plans[b]
        one = pltpu.make_async_copy(slot(b, k, dy, dx, 0), local.at[at, pl.ds(0, p.per)], load_sem.at[at, 0])
        two = pltpu.make_async_copy(first[b].at[k, dy, dx], other.at[number % 2, pl.ds(0, p.per)], load_sem.at[at, 1])
        return one, two

    pending = {}
    steps_args = lambda number: (steps[number][0], steps[number][3], steps[number][1], steps[number][2])

    def prepare(number):
        b, dy, dx, k = steps[number]
        for copy in pending.pop(number % ring, ()):
            copy.wait_send()
        one, two = loads(number)
        one.start()
        arrived(first[b].at[k, dy, dx], r1.at[b, k, dy, dx])
        two.start()

    def phase_one(number):
        b, dy, dx, k = steps[number]
        p = plans[b]
        at = number % ring
        if number == 0:
            for ahead in range(AHEAD):
                sibling(*steps_args(ahead)).start()
            prepare(0)
        if number + AHEAD < len(steps):
            sibling(*steps_args(number + AHEAD)).start()
        if number + 1 < len(steps):
            prepare(number + 1)
        for copy in loads(number):
            copy.wait()
        mine, theirs = local.at[at], other.at[number % 2]
        going = []
        if dy:
            add(p, mine, 0, mine, 0, theirs, 0)
            going.append(send_of(b, 0, k, dy, dx, local.at[at, pl.ds(0, p.half)]))
        else:
            add(p, kept_a[b].at[k, dx], 0, mine, 0, theirs, 0)
        if dx:
            add(p, mine, p.half, mine, p.half, theirs, p.half)
            going.append(send_of(b, 1, k, dy, dx, local.at[at, pl.ds(p.half, p.half)]))
        else:
            add(p, kept_b[b].at[k, dy], 0, mine, p.half, theirs, p.half)
        for copy in going:
            copy.start()
        pending[at] = going

    def three(b, h, k):
        if h == 0:
            return remote(two_a[b].at[k, 1], three_a[b].at[k], s3a.at[b, k], r3a.at[b, k], xpeer)
        return remote(two_b[b].at[k, 1], three_b[b].at[k], s3b.at[b, k], r3b.at[b, k], ypeer)

    def last(b, h, k):
        src = (three_a if h == 0 else three_b)[b].at[k]
        return remote(src, four[b].at[h, k - 1], s4.at[b, h, k - 1], r4.at[b, h, k - 1], below(k))

    def phase_two(b, k):
        p = plans[b]
        for far in (1, 0):
            for h, kept, two, sem in ((0, kept_a, two_a, r2a), (1, kept_b, two_b, r2b)):
                arrived(two[b].at[k, far], sem.at[b, k, far])
                if far:
                    add(p, two[b].at[k, 1], 0, two[b].at[k, 1], 0, kept[b].at[k, 1], 0)
                    three(b, h, k).start()
                else:
                    add(p, kept[b].at[k, 0], 0, two[b].at[k, 0], 0, kept[b].at[k, 0], 0)

    def phase_three(b, k):
        p = plans[b]
        for h, kept, got, sem in ((0, kept_a, three_a, r3a), (1, kept_b, three_b, r3b)):
            arrived(got[b].at[k], sem.at[b, k])
            if k:
                add(p, got[b].at[k], 0, got[b].at[k], 0, kept[b].at[k, 0], 0)
                last(b, h, k).start()

    def halo(b):
        p = plans[b]
        base = p.units_before
        held = units_f.at[b % 2]
        forward = remote(held.at[pl.ds(p.per, base)], from_prev[b], halo_s.at[b, 0], halo_r.at[b, 0], following)
        backward = remote(held.at[pl.ds(base, p.units_after)], from_next[b], halo_s.at[b, 1], halo_r.at[b, 1], prev)
        return forward, backward

    def collect(b):
        p = plans[b]
        base = p.units_before
        for h, kept, got in ((0, kept_a, three_a), (1, kept_b, three_b)):
            for k in range(1, zs):
                arrived(four[b].at[h, k - 1], r4.at[b, h, k - 1])
            step = p.half // 2

            def body(i, carry):
                part = pl.ds(i * step, step)
                value = kept[b][0, 0, part].astype(full_type) + got[b][0, part].astype(full_type)
                for k in range(1, zs):
                    value = value + four[b][h, k - 1, part].astype(full_type)
                units_f[b % 2, pl.ds(base + h * p.half + i * step, step)] = value
                return carry

            lax.fori_loop(0, 2, body, 0)
        for copy in halo(b):
            copy.start()

    def finish(b):
        p = plans[b]
        base = p.units_before
        for copy in halo(b):
            copy.wait()
        held = b % 2
        units_f[held, pl.ds(0, base)] = from_prev[b][...]
        units_f[held, pl.ds(base + p.per, p.units_after)] = from_next[b][...]
        top = me * p.share // LANES - p.margin
        for origin, chunks, count, first_unit, _, _ in p.segments:
            lo = jnp.clip(p.per * me - base - first_unit, 0, count)
            hi = jnp.clip(p.per * me + p.per + p.units_after - first_unit, 0, count)

            def unit(u, carry):
                block = u // chunks
                row = origin + block * (ROWS * chunks) + (u - block * chunks) - top
                value = units_f[held, first_unit + u - p.per * me + base]
                if chunks == 1:
                    rows_f[pl.ds(row, ROWS), :] = value
                else:
                    rows_f[pl.ds(row, ROWS, stride=chunks), :] = value
                return carry

            lax.fori_loop(lo, hi, unit, 0)
        shift = lax.rem(me * p.share, LANES)
        turn = lax.rem(LANES - shift, LANES)
        lane = lax.broadcasted_iota(jnp.int32, (64, LANES), 1)
        spot = lax.broadcasted_iota(jnp.int32, (64, LANES), 0) * LANES + lane
        if b:
            pltpu.make_async_copy(flat_f.at[pl.ds(0, plans[b - 1].raw)], outs[b - 1], out_sem.at[b - 1]).wait()

        def unalign(i, squares):
            row = pl.multiple_of(i * 64, 64)
            here = pltpu.roll(rows_f[pl.ds(row + p.margin, 64), :], turn, 1)
            below_row = pltpu.roll(rows_f[pl.ds(row + p.margin + 1, 64), :], turn, 1)
            value = jnp.where(lane < LANES - shift, here, below_row)
            value = jnp.where(spot + row * LANES < p.share, value, 0.0)
            flat_f[pl.ds(row, 64), :] = value
            return squares + jnp.sum((value * value).reshape(8, 8, LANES), axis=0)

        squares = lax.fori_loop(0, p.raw // 64, unalign, jnp.zeros((8, LANES), full_type))
        pltpu.make_async_copy(flat_f.at[pl.ds(0, p.raw)], outs[b], out_sem.at[b]).start()
        return squares

    squares = jnp.zeros((8, LANES), full_type)
    groups = [(b, k) for b in range(nb) for k in planes]
    for g in range(len(groups) + 2):
        if g < len(groups):
            for number in range(4 * g, 4 * g + 4):
                phase_one(number)
        if 0 <= g - 1 < len(groups):
            phase_two(*groups[g - 1])
        if 0 <= g - 2 < len(groups):
            phase_three(*groups[g - 2])
        b = (g - 3) // zs - 1
        if (g - 3) % zs == 0 and 0 <= b < nb - 1:
            collect(b)
        b = (g - 4) // zs - 1
        if (g - 4) % zs == 0 and 0 <= b < nb - 1:
            squares = squares + finish(b)
    collect(nb - 1)
    squares = squares + finish(nb - 1)
    pltpu.make_async_copy(flat_f.at[pl.ds(0, plans[nb - 1].raw)], outs[nb - 1], out_sem.at[nb - 1]).wait()
    total[0] = stats_in[...]
    total[1] = squares
    step = 0
    for to in ((cpeer,), (xpeer,), (ypeer,), tuple(above(k) for k in range(1, zs))):
        copies = []
        for peer in to:
            copies.append(remote(total, total_in.at[step], ss.at[step], sr.at[step], peer))
            copies[-1].start()
            step += 1
        for copy in copies:
            copy.wait()
        value = total[...]
        for i in range(len(to)):
            value = value + total_in[step - 1 - i]
        total[...] = value
    stats_out[...] = total[...]
    for group in pending.values():
        for copy in group:
            copy.wait_send()
    for b in range(nb):
        for dy, dx in order:
            for k in range(zs):
                sibling(b, k, dy, dx).wait_send()
        for h in range(2):
            for k in range(zs):
                three(b, h, k).wait_send()
                if k:
                    last(b, h, k).wait_send()

def reduce_units(plans, grads, stats):
    n = plans[0].devices
    zs = n // 8
    nb = len(plans)
    dma = pltpu.SemaphoreType.DMA
    most = max(p.per for p in plans)
    tile = (ROWS, LANES)
    half = lambda p, *lead: pltpu.VMEM(lead + (p.half,) + tile, low_type)
    scratch = [half(p, zs, 2) for p in plans] + [half(p, zs, 2) for p in plans]
    scratch += [half(p, zs, 2) for p in plans] + [half(p, zs, 2) for p in plans]
    scratch += [half(p, zs) for p in plans] + [half(p, zs) for p in plans]
    scratch += [half(p, 2, zs - 1) for p in plans]
    ring = 8
    scratch += [pltpu.VMEM((ring, most) + tile, low_type), pltpu.VMEM((2, most) + tile, low_type)]
    scratch += [pltpu.VMEM((2, max(p.units_before + p.per + p.units_after for p in plans)) + tile, full_type)]
    scratch += [pltpu.VMEM((max(p.spread for p in plans), LANES), full_type)]
    scratch += [pltpu.VMEM((max(p.raw for p in plans), LANES), full_type)]
    scratch += [pltpu.VMEM((p.units_before,) + tile, full_type) for p in plans]
    scratch += [pltpu.VMEM((p.units_after,) + tile, full_type) for p in plans]
    hops = 2 + zs
    scratch += [pltpu.VMEM((2, 8, LANES), full_type), pltpu.VMEM((hops, 2, 8, LANES), full_type)]
    scratch += [dma((nb, zs, 2, 2))] * 2 + [dma((nb, zs, 2))] * 4 + [dma((nb, zs))] * 4
    scratch += [dma((nb, 2, zs - 1))] * 2 + [dma((ring, 2)), dma((nb, 2)), dma((nb, 2)), dma((nb,)), dma((hops,)), dma((hops,))]
    anywhere = pl.BlockSpec(memory_space=pltpu.HBM)
    inside = pl.BlockSpec(memory_space=pltpu.VMEM)
    out_shape = [jax.ShapeDtypeStruct((p.raw, LANES), full_type) for p in plans]
    out_shape += [jax.ShapeDtypeStruct((2, 8, LANES), full_type)]
    out_shape += [jax.ShapeDtypeStruct((zs, 2, 2, p.per) + tile, low_type) for p in plans]
    results = pl.pallas_call(
        functools.partial(reduce_kernel, plans, zs),
        out_shape=out_shape,
        in_specs=[anywhere] * nb + [inside],
        out_specs=[anywhere] * nb + [inside] + [anywhere] * nb,
        scratch_shapes=scratch,
        compiler_params=pltpu.CompilerParams(collective_id=1, has_side_effects=True, vmem_limit_bytes=62 * 1024 * 1024),
        name="reduce_units",
    )(*grads, stats)
    return results[:nb], results[nb]

def to_rows(flat, plan):
    padded = jnp.pad(flat, ((0, plan.raw * LANES - flat.shape[0]),))
    return padded.reshape(plan.raw, LANES)


def layer_layout():
    return [
        (D, 3 * D),
        (D, D),
        (D, FF),
        (FF, D),
        (D, 6 * D),
        (D,),
        (D,),
        (D,),
        (FF,),
        (D,),
        (6 * D,),
    ]


def root_layout():
    return [
        (PD, D),
        (D,),
        (FREQ, D),
        (D,),
        (D, D),
        (D,),
        (CLS, D),
        (D, PH),
        (PH,),
        (PH, PH),
        (PH,),
        (PH, ZD),
        (ZD,),
        (D, 2 * D),
        (2 * D,),
        (D, PD),
        (PD,),
    ]


def unflatten(vector, layout):
    pieces = []
    offset = 0
    for dimensions in layout:
        amount = math.prod(dimensions)
        pieces.append(vector[offset : offset + amount].reshape(dimensions))
        offset += amount
    return pieces


def flatten_grads(grad_list, length):
    joined = jnp.concatenate([piece.reshape(-1) for piece in grad_list])
    return jnp.concatenate([joined, jnp.zeros((length - joined.shape[0],), full_type)])


def position_table():
    quarter = D // 4
    frequency = 1.0 / 10000.0 ** (jnp.arange(quarter, dtype=jnp.float32) / quarter)
    coords = jnp.arange(GRID, dtype=jnp.float32)
    angles = coords[:, None] * frequency[None, :]
    one_axis = jnp.concatenate([jnp.sin(angles), jnp.cos(angles)], axis=1)
    row_part = jnp.repeat(one_axis, GRID, axis=0)
    col_part = jnp.tile(one_axis, (GRID, 1))
    return jnp.concatenate([row_part, col_part], axis=1)


def time_features(times_in):
    half_freq = FREQ // 2
    frequency = jnp.exp(-math.log(10000.0) * jnp.arange(half_freq, dtype=jnp.float32) / half_freq)
    angles = times_in[:, None] * frequency[None, :]
    return jnp.concatenate([jnp.cos(angles), jnp.sin(angles)], axis=1)


def modulated_norm(values, offsets, scales):
    centred = values - jnp.mean(values, axis=-1, keepdims=True)
    spread = jnp.mean(centred * centred, axis=-1, keepdims=True)
    return centred * lax.rsqrt(spread + norm_eps) * (1.0 + scales) + offsets


def softmax_rows(scores):
    row_max = jnp.max(scores, axis=-1, keepdims=True)
    exponent = jnp.exp(scores - row_max)
    return exponent / jnp.sum(exponent, axis=-1, keepdims=True)


def gelu_tanh(values):
    return jax.nn.gelu(values, approximate=True)


def cosine_rows(predicted, target):
    target_full = target.astype(full_type)
    inner_sum = jnp.sum(predicted * target_full, axis=-1)
    return (
        inner_sum
        * lax.rsqrt(jnp.sum(predicted * predicted, axis=-1) + norm_eps)
        * lax.rsqrt(jnp.sum(target_full * target_full, axis=-1) + norm_eps)
    )


def silu_back(values, grad_in):
    _, pullback = jax.vjp(jax.nn.silu, values)
    return pullback(grad_in)[0]


def linear_fwd(inputs, weight):
    leading = inputs.shape[:-1]
    product = jnp.dot(
        inputs.reshape(-1, inputs.shape[-1]), weight, preferred_element_type=full_type
    )
    return product.reshape(leading + (weight.shape[1],))


def linear_back(inputs, weight, grad_out, with_input=True):
    rows_in = inputs.reshape(-1, inputs.shape[-1])
    rows_out = grad_out.reshape(-1, grad_out.shape[-1])
    grad_weight = lax.dot_general(
        rows_in, rows_out, (((0,), (0,)), ((), ())), preferred_element_type=full_type
    )
    grad_bias = jnp.sum(rows_out.astype(full_type), axis=0)
    grad_in = None
    if with_input:
        grad_in = lax.dot_general(
            rows_out, weight, (((1,), (1,)), ((), ())), preferred_element_type=full_type
        ).reshape(inputs.shape)
    return (grad_in, grad_weight, grad_bias)


def layer_forward(weights, residual, modulator):
    (
        w_attn_in,
        w_attn_out,
        w_mlp_in,
        w_mlp_out,
        w_modulate,
        b_query,
        b_value,
        b_attn_out,
        b_mlp_in,
        b_mlp_out,
        b_modulate,
    ) = weights
    samples_mb, seq_len = (residual.shape[0], residual.shape[1])
    head_count = D // HD
    modulation = jnp.split((linear_fwd(modulator, w_modulate) + b_modulate)[:, None, :], 6, axis=-1)
    normed_a = modulated_norm(residual, modulation[0], modulation[1]).astype(low_type)
    bias_qkv = jnp.concatenate([b_query, jnp.zeros_like(b_query), b_value])
    qkv_low = (linear_fwd(normed_a, w_attn_in) + bias_qkv).astype(low_type)
    qkv_low = qkv_low.reshape(samples_mb, seq_len, 3, head_count, HD)
    query_bf, key_bf, value_bf = (qkv_low[:, :, 0], qkv_low[:, :, 1], qkv_low[:, :, 2])
    scores = jnp.einsum(
        "bqhd,bkhd->bhqk", query_bf, key_bf, preferred_element_type=full_type
    ) * HD ** (-0.5)
    attn_probs = softmax_rows(scores)
    probs_bf = attn_probs.astype(low_type)
    heads_bf = jnp.einsum("bhqk,bkhd->bqhd", probs_bf, value_bf, preferred_element_type=full_type)
    heads_bf = heads_bf.astype(low_type).reshape(samples_mb, seq_len, D)
    attn_out = linear_fwd(heads_bf, w_attn_out) + b_attn_out
    middle = residual + modulation[2] * attn_out
    normed_m = modulated_norm(middle, modulation[3], modulation[4]).astype(low_type)
    mlp_pre = linear_fwd(normed_m, w_mlp_in) + b_mlp_in
    act_bf = gelu_tanh(mlp_pre).astype(low_type)
    mlp_out = linear_fwd(act_bf, w_mlp_out) + b_mlp_out
    residual_out = middle + modulation[5] * mlp_out
    square_sums = jnp.stack(
        [
            jnp.sum(residual_out * residual_out),
            jnp.sum(attn_out * attn_out),
            jnp.sum(mlp_out * mlp_out),
        ]
    )
    saved = (
        modulation,
        normed_a,
        query_bf,
        key_bf,
        value_bf,
        attn_probs,
        probs_bf,
        heads_bf,
        attn_out,
        middle,
        normed_m,
        mlp_pre,
        act_bf,
        mlp_out,
    )
    return (residual_out, saved, square_sums)


def layer_backward(weights, saved, residual, modulator, grad_out):
    w_attn_in, w_attn_out, w_mlp_in, w_mlp_out, w_modulate = weights[:5]
    (
        modulation,
        normed_a,
        query_bf,
        key_bf,
        value_bf,
        attn_probs,
        probs_bf,
        heads_bf,
        attn_out,
        middle,
        normed_m,
        mlp_pre,
        act_bf,
        mlp_out,
    ) = saved
    samples_mb, seq_len = (residual.shape[0], residual.shape[1])
    grad_mlp = (modulation[5] * grad_out).astype(low_type)
    grad_act, grad_w_mlp_out, grad_b_mlp_out = linear_back(act_bf, w_mlp_out, grad_mlp)
    _, gelu_pull = jax.vjp(gelu_tanh, mlp_pre)
    grad_pre = gelu_pull(grad_act)[0].astype(low_type)
    grad_normed_m, grad_w_mlp_in, grad_b_mlp_in = linear_back(normed_m, w_mlp_in, grad_pre)
    _, norm_pull_m = jax.vjp(modulated_norm, middle, modulation[3], modulation[4])
    grad_from_m, grad_shift_m, grad_scale_m = norm_pull_m(grad_normed_m)
    grad_middle = grad_out + grad_from_m
    grad_attn = (modulation[2] * grad_middle).astype(low_type)
    grad_heads, grad_w_attn_out, grad_b_attn_out = linear_back(heads_bf, w_attn_out, grad_attn)
    grad_heads_bf = grad_heads.astype(low_type).reshape(samples_mb, seq_len, D // HD, HD)
    grad_probs = jnp.einsum(
        "bqhd,bkhd->bhqk", grad_heads_bf, value_bf, preferred_element_type=full_type
    )
    grad_value = jnp.einsum(
        "bhqk,bqhd->bkhd", probs_bf, grad_heads_bf, preferred_element_type=full_type
    )
    grad_scores = attn_probs * (
        grad_probs - jnp.sum(attn_probs * grad_probs, axis=-1, keepdims=True)
    )
    grad_scores = grad_scores.astype(low_type)
    grad_query = jnp.einsum(
        "bhqk,bkhd->bqhd", grad_scores, key_bf, preferred_element_type=full_type
    ) * HD ** (-0.5)
    grad_key = jnp.einsum(
        "bhqk,bqhd->bkhd", grad_scores, query_bf, preferred_element_type=full_type
    ) * HD ** (-0.5)
    grad_qkv = jnp.stack([grad_query, grad_key, grad_value], axis=2).reshape(
        samples_mb, seq_len, 3 * D
    )
    grad_normed_a, grad_w_attn_in, grad_b_qkv = linear_back(
        normed_a, w_attn_in, grad_qkv.astype(low_type)
    )
    _, norm_pull_a = jax.vjp(modulated_norm, residual, modulation[0], modulation[1])
    grad_from_a, grad_shift_a, grad_scale_a = norm_pull_a(grad_normed_a)
    grad_gate_a = jnp.sum(attn_out * grad_middle, axis=1, keepdims=True)
    grad_gate_m = jnp.sum(mlp_out * grad_out, axis=1, keepdims=True)
    grad_mod = jnp.concatenate(
        [grad_shift_a, grad_scale_a, grad_gate_a, grad_shift_m, grad_scale_m, grad_gate_m], axis=-1
    )[:, 0, :].astype(low_type)
    grad_cond, grad_w_mod, grad_b_mod = linear_back(modulator, w_modulate, grad_mod)
    grad_list = [
        grad_w_attn_in,
        grad_w_attn_out,
        grad_w_mlp_in,
        grad_w_mlp_out,
        grad_w_mod,
        grad_b_qkv[:D],
        grad_b_qkv[2 * D :],
        grad_b_attn_out,
        grad_b_mlp_in,
        grad_b_mlp_out,
        grad_b_mod,
    ]
    return (grad_middle + grad_from_a, grad_cond, grad_list)


def embed_forward(pieces, latent_part, noise_part, times_part, labels_part, dropped_part):
    mixing = times_part[:, None, None]
    noisy_bf = ((1.0 - mixing) * latent_part + mixing * noise_part).astype(low_type)
    tokens = linear_fwd(noisy_bf, pieces[0]) + pieces[1] + position_table()
    basis_bf = time_features(times_part).astype(low_type)
    time_pre = linear_fwd(basis_bf, pieces[2]) + pieces[3]
    time_act = jax.nn.silu(time_pre).astype(low_type)
    time_emb = linear_fwd(time_act, pieces[4]) + pieces[5]
    classes = jnp.where(dropped_part == 1, CLS - 1, labels_part)
    onehot = (classes[:, None] == jnp.arange(CLS, dtype=jnp.int32)[None, :]).astype(low_type)
    condition = time_emb + jnp.dot(onehot, pieces[6], preferred_element_type=full_type)
    saved = (noisy_bf, basis_bf, time_pre, time_act, onehot, condition)
    return (tokens, jax.nn.silu(condition).astype(low_type), saved)


def embed_backward(pieces, saved, grad_tokens, grad_modulator):
    noisy_bf, basis_bf, time_pre, time_act, onehot, condition = saved
    grad_cond = silu_back(condition, grad_modulator)
    grad_table = lax.dot_general(
        onehot.astype(full_type),
        grad_cond,
        (((0,), (0,)), ((), ())),
        precision=lax.Precision.HIGHEST,
    )
    grad_time_act, grad_w_time_out, grad_b_time_out = linear_back(
        time_act, pieces[4], grad_cond.astype(low_type)
    )
    grad_time_pre = silu_back(time_pre, grad_time_act).astype(low_type)
    _, grad_w_time_in, grad_b_time_in = linear_back(basis_bf, pieces[2], grad_time_pre, False)
    _, grad_w_patch, grad_b_patch = linear_back(
        noisy_bf, pieces[0], grad_tokens.astype(low_type), False
    )
    return [
        grad_w_patch,
        grad_b_patch,
        grad_w_time_in,
        grad_b_time_in,
        grad_w_time_out,
        grad_b_time_out,
        grad_table,
    ]


def projector_forward(pieces, residual, features_part):
    residual_bf = residual.astype(low_type)
    pre_a = linear_fwd(residual_bf, pieces[7]) + pieces[8]
    act_a = jax.nn.silu(pre_a).astype(low_type)
    pre_b = linear_fwd(act_a, pieces[9]) + pieces[10]
    act_b = jax.nn.silu(pre_b).astype(low_type)
    predicted = linear_fwd(act_b, pieces[11]) + pieces[12]
    loss_part = -proj_coeff * jnp.sum(cosine_rows(predicted, features_part)) / residual.shape[1]
    return (loss_part, (residual_bf, pre_a, act_a, pre_b, act_b, predicted))


def projector_backward(pieces, saved, features_part, seq_len, sample_total):
    residual_bf, pre_a, act_a, pre_b, act_b, predicted = saved
    _, cosine_pull = jax.vjp(
        lambda predicted_in: cosine_rows(predicted_in, features_part), predicted
    )
    seed = jnp.full(predicted.shape[:2], -proj_coeff / (seq_len * sample_total), full_type)
    grad_pred = cosine_pull(seed)[0].astype(low_type)
    grad_act_b, grad_w_c, grad_b_c = linear_back(act_b, pieces[11], grad_pred)
    grad_pre_b = silu_back(pre_b, grad_act_b).astype(low_type)
    grad_act_a, grad_w_b, grad_b_b = linear_back(act_a, pieces[9], grad_pre_b)
    grad_pre_a = silu_back(pre_a, grad_act_a).astype(low_type)
    grad_residual, grad_w_a, grad_b_a = linear_back(residual_bf, pieces[7], grad_pre_a)
    return (grad_residual, [grad_w_a, grad_b_a, grad_w_b, grad_b_b, grad_w_c, grad_b_c])


def head_forward(pieces, residual, modulator, target, weight_t):
    modulation = (linear_fwd(modulator, pieces[13]) + pieces[14])[:, None, :]
    shift_f, scale_f = jnp.split(modulation, 2, axis=-1)
    normed = modulated_norm(residual, shift_f, scale_f).astype(low_type)
    deviation = linear_fwd(normed, pieces[15]) + pieces[16] - target
    loss_part = jnp.sum(weight_t * jnp.mean(deviation * deviation, axis=(1, 2)))
    return (loss_part, (shift_f, scale_f, normed, deviation))


def head_backward(pieces, saved, residual, modulator, weight_t, sample_total):
    shift_f, scale_f, normed, deviation = saved
    scaled = (
        2.0 * weight_t[:, None, None] / (deviation.shape[1] * deviation.shape[2] * sample_total)
    )
    grad_output = (scaled * deviation).astype(low_type)
    grad_normed, grad_w_head, grad_b_head = linear_back(normed, pieces[15], grad_output)
    _, pullback = jax.vjp(modulated_norm, residual, shift_f, scale_f)
    grad_residual, grad_shift, grad_scale = pullback(grad_normed)
    grad_mod = jnp.concatenate([grad_shift, grad_scale], axis=-1)[:, 0, :].astype(low_type)
    grad_cond, grad_w_mod, grad_b_mod = linear_back(modulator, pieces[13], grad_mod)
    return (grad_residual, grad_cond, [grad_w_mod, grad_b_mod, grad_w_head, grad_b_head])


WIDE = 2 * LANES
HEADS = D // HD
CHUNK = 64
MB = 1024 * 1024


def dot(one, two):
    return jnp.dot(one, two, preferred_element_type=full_type)


def dot_nt(one, two):
    return lax.dot_general(one, two, (((1,), (1,)), ((), ())), preferred_element_type=full_type)


def dot_tn(one, two):
    return lax.dot_general(one, two, (((0,), (0,)), ((), ())), preferred_element_type=full_type)


def block_of(w, block, blocks, chunk, chunks):
    pieces = [w[pl.ds(block, blocks), chunk + i].reshape(blocks * ROWS, LANES) for i in range(chunks)]
    return jnp.concatenate(pieces, axis=1) if chunks > 1 else pieces[0]


def put_block(out, block, chunk, value):
    blocks = value.shape[0] // ROWS
    for i in range(value.shape[1] // LANES):
        piece = value[:, i * LANES : (i + 1) * LANES].astype(low_type)
        out[pl.ds(block, blocks), chunk + i] = piece.reshape(blocks, ROWS, LANES)


def loop(count, body):
    lax.fori_loop(0, count, lambda i, carry: (body(i), carry)[1], 0)


def norm_parts(values):
    centred = values - jnp.mean(values, axis=-1, keepdims=True)
    spread = jnp.mean(centred * centred, axis=-1, keepdims=True)
    scale = lax.rsqrt(spread + norm_eps)
    return centred * scale, scale


def norm_back(values, grad, gain):
    hat, scale = norm_parts(values)
    inner = grad * gain
    mean_a = jnp.mean(inner, axis=-1, keepdims=True)
    mean_b = jnp.mean(inner * hat, axis=-1, keepdims=True)
    return scale * (inner - mean_a - hat * mean_b), grad * hat


def gelu_parts(values):
    root = math.sqrt(2.0 / math.pi)
    square = values * values
    bend = jnp.tanh(root * values * (1.0 + 0.044715 * square))
    half = 0.5 * (1.0 + bend)
    slope = half + 0.5 * values * (1.0 - bend * bend) * root * (1.0 + 3.0 * 0.044715 * square)
    return values * half, slope


def rows_sum(values):
    return jnp.sum(values, axis=0, keepdims=True)


def segment_ref(units, plan, number):
    _, chunks, count, first, shape, matrix = plan.segments[number]
    part = units.at[pl.ds(first, count)]
    if not matrix:
        return part
    return part.reshape(shape[0] // ROWS, chunks, ROWS, LANES)


def segment_scratch(plan, number):
    _, chunks, _, _, shape, _ = plan.segments[number]
    return pltpu.VMEM((shape[0] // ROWS, chunks, ROWS, LANES), low_type)


def attention_pairs(rows):
    return (rows // SEQ) * (HEADS // 2)


def head_masks():
    lane = lax.broadcasted_iota(jnp.int32, (SEQ, LANES), 1)
    return lane < HD


def softmax_f32(scores):
    exponent = jnp.exp(scores - jnp.max(scores, axis=-1, keepdims=True))
    return exponent * (1.0 / jnp.sum(exponent, axis=-1, keepdims=True))


def mods_kernel(plan, modulator, bias, units, out, w, sem):
    load = pltpu.make_async_copy(segment_ref(units, plan, 4), w, sem)
    load.start()
    load.wait()
    value = modulator[...]

    def body(j):
        cols = pl.ds(pl.multiple_of(j * WIDE, WIDE), WIDE)
        out[:, cols] = dot(value, block_of(w, 0, D // ROWS, 2 * j, 2)) + bias[:, cols]

    loop(6 * D // WIDE, body)


def mods_call(plan, modulator, bias, units):
    vm = pl.BlockSpec(memory_space=pltpu.VMEM)
    return pl.pallas_call(
        functools.partial(mods_kernel, plan),
        out_shape=jax.ShapeDtypeStruct((modulator.shape[0], 6 * D), full_type),
        in_specs=[vm, vm, pl.BlockSpec(memory_space=pltpu.HBM)],
        out_specs=vm,
        scratch_shapes=[segment_scratch(plan, 4), pltpu.SemaphoreType.DMA],
        compiler_params=pltpu.CompilerParams(vmem_limit_bytes=32 * MB),
        name="modulation",
    )(modulator, bias, units)


def mods_back_kernel(plan, modulator, grad, units, before, grads, cond, w, dw, sem):
    load = pltpu.make_async_copy(segment_ref(units, plan, 4), w, sem.at[0])
    load.start()
    turned = modulator[...].astype(full_type).T.astype(low_type)

    def weight(j):
        cols = pl.ds(pl.multiple_of(j * WIDE, WIDE), WIDE)
        put_block(dw, 0, 2 * j, dot(turned, grad[:, cols]))

    loop(6 * D // WIDE, weight)
    store = pltpu.make_async_copy(dw, segment_ref(grads, plan, 4), sem.at[1])
    store.start()
    load.wait()
    cond[...] = jnp.zeros(cond.shape, full_type)

    def back(j):
        cols = pl.ds(pl.multiple_of(j * WIDE, WIDE), WIDE)
        cond[...] += dot_nt(grad[:, cols], block_of(w, 0, D // ROWS, 2 * j, 2))

    loop(6 * D // WIDE, back)
    store.wait()


def mods_back_call(plan, modulator, grad, units, grads):
    vm = pl.BlockSpec(memory_space=pltpu.VMEM)
    anywhere = pl.BlockSpec(memory_space=pltpu.HBM)
    return pl.pallas_call(
        functools.partial(mods_back_kernel, plan),
        out_shape=[jax.ShapeDtypeStruct(grads.shape, low_type), jax.ShapeDtypeStruct((modulator.shape[0], D), full_type)],
        in_specs=[vm, vm, anywhere, anywhere],
        out_specs=[anywhere, vm],
        input_output_aliases={3: 0},
        scratch_shapes=[segment_scratch(plan, 4), segment_scratch(plan, 4), pltpu.SemaphoreType.DMA((2,))],
        compiler_params=pltpu.CompilerParams(vmem_limit_bytes=40 * MB),
        name="modulation_back",
    )(modulator, grad, units, grads)


SAVED = (("h1", D, low_type), ("qkv", 3 * D, low_type), ("heads", D, low_type), ("attn", D, full_type), ("middle", D, full_type), ("h2", D, low_type), ("pre", FF, full_type), ("mlp", D, full_type))


def layer_forward_kernel(plan, rows, x, mod, bias_qkv, bias_o, bias_1, bias_2, units, out, sums, *refs):
    ns = len(SAVED)
    saved_out = refs[:ns]
    h1, qkv, heads, attn, middle, h2, pre, mlp = refs[ns : 2 * ns]
    w_qkv, w_o, w_1, w_2, load_sem, save_sem = refs[2 * ns :]
    weights = (w_qkv, w_o, w_1, w_2)
    loads = [pltpu.make_async_copy(segment_ref(units, plan, i), weights[i], load_sem.at[i]) for i in range(4)]
    for copy in loads:
        copy.start()
    saves = [pltpu.make_async_copy(refs[ns + i], saved_out[i], save_sem.at[i]) for i in range(ns)]
    part = lambda s, i: mod[pl.ds(s, 1), i * D : (i + 1) * D]
    per = SEQ // CHUNK

    def norm_a(i):
        at = pl.ds(pl.multiple_of(i * CHUNK, CHUNK), CHUNK)
        s = i // per
        hat, _ = norm_parts(x[at, :])
        h1[at, :] = (hat * (1.0 + part(s, 1)) + part(s, 0)).astype(low_type)

    loop(rows // CHUNK, norm_a)
    saves[0].start()
    loads[0].wait()

    def project(j):
        cols = pl.ds(pl.multiple_of(j * WIDE, WIDE), WIDE)
        value = dot(h1[...], block_of(w_qkv, 0, D // ROWS, 2 * j, 2)) + bias_qkv[:, cols]
        qkv[:, cols] = value.astype(low_type)

    loop(3 * D // WIDE, project)
    saves[1].start()
    first = head_masks()

    def attend(i):
        s, j = i // (HEADS // 2), i % (HEADS // 2)
        at = pl.ds(pl.multiple_of(s * SEQ, SEQ), SEQ)
        cut = lambda o: qkv[at, pl.ds(pl.multiple_of(o * D + j * LANES, LANES), LANES)]
        q, k, v = cut(0), cut(1), cut(2)
        q = q * jnp.asarray(HD ** (-0.5), low_type)
        zero = jnp.zeros_like(q)
        halves = []
        for mask in (first, ~first):
            probs = softmax_f32(dot_nt(jnp.where(mask, q, zero), k)).astype(low_type)
            halves.append(dot(probs, v))
        heads[at, pl.ds(pl.multiple_of(j * LANES, LANES), LANES)] = jnp.where(first, halves[0], halves[1]).astype(low_type)

    loop(attention_pairs(rows), attend)
    saves[2].start()
    loads[1].wait()

    def project_out(j):
        cols = pl.ds(pl.multiple_of(j * WIDE, WIDE), WIDE)
        attn[:, cols] = dot(heads[...], block_of(w_o, 0, D // ROWS, 2 * j, 2)) + bias_o[:, cols]

    loop(D // WIDE, project_out)
    saves[3].start()
    zero_sum = jnp.zeros((1, D), full_type)

    def norm_m(i, total):
        at = pl.ds(pl.multiple_of(i * CHUNK, CHUNK), CHUNK)
        s = i // per
        value = attn[at, :]
        mid = x[at, :] + part(s, 2) * value
        middle[at, :] = mid
        hat, _ = norm_parts(mid)
        h2[at, :] = (hat * (1.0 + part(s, 4)) + part(s, 3)).astype(low_type)
        return total + rows_sum(value * value)

    attn_sum = lax.fori_loop(0, rows // CHUNK, norm_m, zero_sum)
    saves[4].start()
    saves[5].start()
    loads[2].wait()
    loads[3].wait()
    mlp[...] = jnp.broadcast_to(bias_2[...], (rows, D))

    def feed(j):
        cols = pl.ds(pl.multiple_of(j * WIDE, WIDE), WIDE)
        value = dot(h2[...], block_of(w_1, 0, D // ROWS, 2 * j, 2)) + bias_1[:, cols]
        pre[:, cols] = value
        act = gelu_parts(value)[0].astype(low_type)
        mlp[...] += dot(act, block_of(w_2, j * (WIDE // ROWS), WIDE // ROWS, 0, D // LANES))

    loop(FF // WIDE, feed)
    saves[6].start()
    saves[7].start()

    def finish(i, carry):
        at = pl.ds(pl.multiple_of(i * CHUNK, CHUNK), CHUNK)
        value = mlp[at, :]
        result = middle[at, :] + part(i // per, 5) * value
        out[at, :] = result
        return (carry[0] + rows_sum(result * result), carry[1] + rows_sum(value * value))

    out_sum, mlp_sum = lax.fori_loop(0, rows // CHUNK, finish, (zero_sum, zero_sum))
    sums[...] = jnp.zeros(sums.shape, full_type)
    sums[0:1, :] = out_sum
    sums[1:2, :] = attn_sum
    sums[2:3, :] = mlp_sum
    for copy in saves:
        copy.wait()


def layer_forward_call(plan, x, mod, biases, units):
    rows = x.shape[0]
    vm = pl.BlockSpec(memory_space=pltpu.VMEM)
    anywhere = pl.BlockSpec(memory_space=pltpu.HBM)
    dma = pltpu.SemaphoreType.DMA
    shapes = [((rows, width), kind) for _, width, kind in SAVED]
    results = pl.pallas_call(
        functools.partial(layer_forward_kernel, plan, rows),
        out_shape=[jax.ShapeDtypeStruct((rows, D), full_type), jax.ShapeDtypeStruct((8, D), full_type)]
        + [jax.ShapeDtypeStruct(*s) for s in shapes],
        in_specs=[vm] * 6 + [anywhere],
        out_specs=[vm, vm] + [anywhere] * len(SAVED),
        scratch_shapes=[pltpu.VMEM(*s) for s in shapes] + [segment_scratch(plan, i) for i in range(4)] + [dma((4,)), dma((len(SAVED),))],
        compiler_params=pltpu.CompilerParams(vmem_limit_bytes=56 * MB),
        name="layer_forward",
    )(x, mod, *biases, units)
    return results[0], results[1], results[2:]


def layer_backward_kernel(plan, rows, x, grad_in, mod, *refs):
    ns = len(SAVED)
    saved_hbm = refs[:ns]
    units, grad_out, grad_mod, bias_out, grads = refs[ns : ns + 5]
    h1, qkv, heads, attn, middle, h2, pre, mlp = refs[ns + 5 : 2 * ns + 5]
    w_qkv, w_o, w_1, w_2, d_qkv, g_low, wide, turned, dx, d_one, d_two, load_sem, save_sem, out_sem = refs[2 * ns + 5 :]
    weights = (w_qkv, w_o, w_1, w_2)
    inside = dict(zip(range(ns), refs[ns + 5 : 2 * ns + 5]))
    saves = [pltpu.make_async_copy(saved_hbm[i], inside[i], save_sem.at[i]) for i in range(ns)]
    loads = [pltpu.make_async_copy(segment_ref(units, plan, i), weights[i], load_sem.at[i]) for i in range(4)]
    for copy in (saves[7], saves[6], loads[3], saves[5], loads[2], saves[4], saves[3], loads[1], saves[2], saves[1], loads[0], saves[0]):
        copy.start()
    part = lambda s, i: mod[pl.ds(s, 1), i * D : (i + 1) * D]
    per = SEQ // CHUNK
    grad_mod[...] = jnp.zeros(grad_mod.shape, full_type)
    bias_out[...] = jnp.zeros(bias_out.shape, full_type)

    def add_mod(s, i, value):
        grad_mod[pl.ds(s, 1), i * D : (i + 1) * D] += value

    def each_chunk(body):
        loop(rows // CHUNK, lambda i: body(pl.ds(pl.multiple_of(i * CHUNK, CHUNK), CHUNK), i // per))

    B_Q, B_V, B_O, B_1, B_2 = 0, D, 2 * D, 3 * D, 3 * D + FF
    saves[7].wait()

    def start_mlp(at, s):
        grad = grad_in[at, :]
        low = (part(s, 5) * grad).astype(low_type)
        g_low[at, :] = low
        bias_out[:, B_2 : B_2 + D] += rows_sum(low.astype(full_type))
        add_mod(s, 5, rows_sum(mlp[at, :] * grad))

    each_chunk(start_mlp)
    saves[5].wait()
    turned[...] = h2[...].astype(full_type).T.astype(low_type)
    saves[6].wait()
    loads[3].wait()
    loads[2].wait()
    dx[...] = jnp.zeros(dx.shape, full_type)
    half = WIDE // ROWS

    def outer(slot, segment, block, blocks, chunk, chunks, buffer):
        target = segment_ref(grads, plan, segment).at[pl.ds(block, blocks), pl.ds(chunk, chunks)]
        return pltpu.make_async_copy(buffer, target, out_sem.at[slot])

    def mlp_store(j, kind):
        at = j % 2
        if kind == 0:
            return outer(2 * at, 3, j * half, half, 0, D // LANES, d_one.at[at])
        return outer(2 * at + 1, 2, 0, D // ROWS, 2 * j, 2, d_two.at[at])

    def feed_back(j):
        cols = pl.ds(pl.multiple_of(j * WIDE, WIDE), WIDE)
        at = j % 2

        @pl.when(j >= 2)
        def _():
            mlp_store(j - 2, 0).wait()
            mlp_store(j - 2, 1).wait()

        act, slope = gelu_parts(pre[:, cols])
        grad_act = dot_nt(g_low[...], block_of(w_2, j * half, half, 0, D // LANES))
        low = (grad_act * slope).astype(low_type)
        wide[...] = low
        bias_out[:, pl.ds(pl.multiple_of(B_1 + j * WIDE, WIDE), WIDE)] += rows_sum(low.astype(full_type))
        put_block(d_one.at[at], 0, 0, dot_tn(act.astype(low_type), g_low[...]))
        mlp_store(j, 0).start()
        put_block(d_two.at[at], 0, 0, dot(turned[...], wide[...]))
        mlp_store(j, 1).start()
        dx[...] += dot_nt(wide[...], block_of(w_1, 0, D // ROWS, 2 * j, 2))

    steps = FF // WIDE
    loop(steps, feed_back)
    saves[4].wait()
    saves[3].wait()

    def middle_back(at, s):
        grad = dx[at, :]
        back, scaled = norm_back(middle[at, :], grad, 1.0 + part(s, 4))
        add_mod(s, 3, rows_sum(grad))
        add_mod(s, 4, rows_sum(scaled))
        total = grad_in[at, :] + back
        grad_out[at, :] = total
        low = (part(s, 2) * total).astype(low_type)
        g_low[at, :] = low
        bias_out[:, B_O : B_O + D] += rows_sum(low.astype(full_type))
        add_mod(s, 2, rows_sum(attn[at, :] * total))

    each_chunk(middle_back)
    loads[1].wait()
    saves[2].wait()
    for j in (steps - 2, steps - 1):
        mlp_store(j, 0).wait()
        mlp_store(j, 1).wait()
    turned[...] = heads[...].astype(full_type).T.astype(low_type)

    def wo_store(j):
        return outer(j % 2, 1, 0, D // ROWS, 2 * j, 2, d_two.at[j % 2])

    def out_back(j):
        cols = pl.ds(pl.multiple_of(j * WIDE, WIDE), WIDE)

        @pl.when(j >= 2)
        def _():
            wo_store(j - 2).wait()

        put_block(d_two.at[j % 2], 0, 0, dot(turned[...], g_low[:, cols]))
        wo_store(j).start()
        heads[:, cols] = dot_nt(g_low[...], block_of(w_o, j * half, half, 0, D // LANES)).astype(low_type)

    loop(D // WIDE, out_back)
    saves[1].wait()
    first = head_masks()

    def attend_back(i):
        s, j = i // (HEADS // 2), i % (HEADS // 2)
        at = pl.ds(pl.multiple_of(s * SEQ, SEQ), SEQ)
        cut = lambda o: qkv[at, pl.ds(pl.multiple_of(o * D + j * LANES, LANES), LANES)]
        q, k, v = cut(0), cut(1), cut(2)
        go = heads[at, pl.ds(pl.multiple_of(j * LANES, LANES), LANES)]
        q = q * jnp.asarray(HD ** (-0.5), low_type)
        zero = jnp.zeros_like(q)
        dq, dk, dv = [], 0.0, 0.0
        for mask in (first, ~first):
            q_h, go_h = jnp.where(mask, q, zero), jnp.where(mask, go, zero)
            probs = softmax_f32(dot_nt(q_h, k))
            grad_probs = dot_nt(go_h, v)
            dv = dv + dot_tn(probs.astype(low_type), go_h)
            inner = jnp.sum(probs * grad_probs, axis=-1, keepdims=True)
            ds = (probs * (grad_probs - inner)).astype(low_type)
            dq.append(dot(ds, k) * HD ** (-0.5))
            dk = dk + dot_tn(ds, q_h)
        put = lambda o, value: d_qkv.at[at, pl.ds(pl.multiple_of(o * D + j * LANES, LANES), LANES)].set(value)
        for o, value in enumerate((jnp.where(first, dq[0], dq[1]), dk, dv)):
            low = value.astype(low_type)
            d_qkv[at, pl.ds(pl.multiple_of(o * D + j * LANES, LANES), LANES)] = low
            if o != 1:
                start = (B_Q if o == 0 else B_V) + j * LANES
                bias_out[:, pl.ds(pl.multiple_of(start, LANES), LANES)] += rows_sum(low.astype(full_type))

    loop(attention_pairs(rows), attend_back)
    saves[0].wait()
    loads[0].wait()
    wo_store(1).wait()
    wo_store(2).wait()
    turned[...] = h1[...].astype(full_type).T.astype(low_type)
    dx[...] = jnp.zeros(dx.shape, full_type)

    def qkv_store(j):
        return outer(j % 2, 0, 0, D // ROWS, 2 * j, 2, d_two.at[j % 2])

    def project_back(j):
        cols = pl.ds(pl.multiple_of(j * WIDE, WIDE), WIDE)

        @pl.when(j >= 2)
        def _():
            qkv_store(j - 2).wait()

        put_block(d_two.at[j % 2], 0, 0, dot(turned[...], d_qkv[:, cols]))
        qkv_store(j).start()
        dx[...] += dot_nt(d_qkv[:, cols], block_of(w_qkv, 0, D // ROWS, 2 * j, 2))

    count = 3 * D // WIDE
    loop(count, project_back)

    def input_back(at, s):
        grad = dx[at, :]
        back, scaled = norm_back(x[at, :], grad, 1.0 + part(s, 1))
        add_mod(s, 0, rows_sum(grad))
        add_mod(s, 1, rows_sum(scaled))
        grad_out[at, :] += back

    each_chunk(input_back)
    for j in (count - 2, count - 1):
        qkv_store(j).wait()


def layer_backward_call(plan, x, grad, mod, saved, units):
    rows = x.shape[0]
    vm = pl.BlockSpec(memory_space=pltpu.VMEM)
    anywhere = pl.BlockSpec(memory_space=pltpu.HBM)
    dma = pltpu.SemaphoreType.DMA
    shapes = [((rows, width), kind) for _, width, kind in SAVED]
    tile = (ROWS, LANES)
    return pl.pallas_call(
        functools.partial(layer_backward_kernel, plan, rows),
        out_shape=[
            jax.ShapeDtypeStruct((rows, D), full_type),
            jax.ShapeDtypeStruct((8, 6 * D), full_type),
            jax.ShapeDtypeStruct((1, 4 * D + FF), full_type),
            jax.ShapeDtypeStruct(units.shape, low_type),
        ],
        in_specs=[vm] * 3 + [anywhere] * (len(SAVED) + 1),
        out_specs=[vm, vm, vm, anywhere],
        scratch_shapes=[pltpu.VMEM(*s) for s in shapes]
        + [segment_scratch(plan, i) for i in range(4)]
        + [
            pltpu.VMEM((rows, 3 * D), low_type),
            pltpu.VMEM((rows, D), low_type),
            pltpu.VMEM((rows, WIDE), low_type),
            pltpu.VMEM((D, rows), low_type),
            pltpu.VMEM((rows, D), full_type),
            pltpu.VMEM((2, WIDE // ROWS, D // LANES) + tile, low_type),
            pltpu.VMEM((2, D // ROWS, 2) + tile, low_type),
            dma((4,)),
            dma((len(SAVED),)),
            dma((4,)),
        ],
        compiler_params=pltpu.CompilerParams(vmem_limit_bytes=60 * MB),
        name="layer_backward",
    )(x, grad, mod, *saved, units)


def sigmoid(values):
    return 1.0 / (1.0 + jnp.exp(-values))


def silu_parts(values):
    gate = sigmoid(values)
    return values * gate, gate * (1.0 + values * (1.0 - gate))


TOP = (7, 9, 11, 13)


def top_kernel(plan, rows, sample_total, x, features, target, weight_t, modulator, b_1, b_2, b_3, b_f, w_h, b_h, units, *refs):
    grad_x, stats, cond, bias_out, dw_h, grads = refs[:6]
    p_1, p_2, p_3, w_f, pre_a, act_a, pre_b, act_b, pred, low, g_b, g_a, hidden, modf, d_modf, stage, dw_f, load_sem, out_sem = refs[6:]
    weights = (p_1, p_2, p_3, w_f)
    loads = [pltpu.make_async_copy(segment_ref(units, plan, s), weights[i], load_sem.at[i]) for i, s in enumerate(TOP)]
    for copy in loads:
        copy.start()
    per = SEQ // CHUNK
    half = WIDE // ROWS
    stats[...] = jnp.zeros(stats.shape, full_type)
    bias_out[...] = jnp.zeros(bias_out.shape, full_type)
    d_modf[...] = jnp.zeros(d_modf.shape, full_type)
    A_1, A_2, A_3, A_F, A_H = 0, PH, 2 * PH, 2 * PH + ZD, 2 * PH + ZD + 2 * D
    wide_at = lambda j, base=0: pl.ds(pl.multiple_of(base + j * WIDE, LANES), WIDE)

    def each_chunk(body):
        loop(rows // CHUNK, lambda i: body(pl.ds(pl.multiple_of(i * CHUNK, CHUNK), CHUNK), i // per))

    def to_low(at, s):
        low[at, :] = x[at, :].astype(low_type)

    each_chunk(to_low)
    loads[0].wait()

    def first_layer(j):
        value = dot(low[...], block_of(p_1, 0, D // ROWS, 2 * j, 2)) + b_1[:, wide_at(j)]
        pre_a[:, wide_at(j)] = value
        act_a[:, wide_at(j)] = silu_parts(value)[0].astype(low_type)

    loop(PH // WIDE, first_layer)
    loads[1].wait()

    def second_layer(j):
        value = dot(act_a[...], block_of(p_2, 0, PH // ROWS, 2 * j, 2)) + b_2[:, wide_at(j)]
        pre_b[:, wide_at(j)] = value
        act_b[:, wide_at(j)] = silu_parts(value)[0].astype(low_type)

    loop(PH // WIDE, second_layer)
    loads[2].wait()

    def third_layer(j):
        pred[:, wide_at(j)] = dot(act_b[...], block_of(p_3, 0, PH // ROWS, 2 * j, 2)) + b_3[:, wide_at(j)]

    loop(ZD // WIDE, third_layer)
    seed = -proj_coeff / (SEQ * sample_total)

    def cosine(at, s):
        value = pred[at, :]
        want = features[at, :].astype(full_type)
        inner = jnp.sum(value * want, axis=-1, keepdims=True)
        scale_a = lax.rsqrt(jnp.sum(value * value, axis=-1, keepdims=True) + norm_eps)
        scale_b = lax.rsqrt(jnp.sum(want * want, axis=-1, keepdims=True) + norm_eps)
        both = scale_a * scale_b
        stats[0:1, 0:1] += jnp.sum(inner * both, axis=0, keepdims=True)
        grad = seed * (want * both - value * (inner * both * scale_a * scale_a))
        grad = grad.astype(low_type)
        hidden[at, :] = grad
        bias_out[:, A_3 : A_3 + ZD] += rows_sum(grad.astype(full_type))

    each_chunk(cosine)

    def store(segment, j, chunks):
        where = segment_ref(grads, plan, segment).at[pl.ds(j * half, half)]
        return pltpu.make_async_copy(stage.at[j % 2, :, pl.ds(0, chunks)], where, out_sem.at[j % 2])

    def stored(segment, j, chunks):
        @pl.when(j >= 2)
        def _():
            store(segment, j - 2, chunks).wait()

    def third_back(j):
        stored(11, j, ZD // LANES)
        put_block(stage.at[j % 2], 0, 0, dot_tn(act_b[:, wide_at(j)], hidden[...]))
        store(11, j, ZD // LANES).start()
        grad = dot_nt(hidden[...], block_of(p_3, j * half, half, 0, ZD // LANES))
        grad = (grad * silu_parts(pre_b[:, wide_at(j)])[1]).astype(low_type)
        g_b[:, wide_at(j)] = grad
        bias_out[:, wide_at(j, A_2)] += rows_sum(grad.astype(full_type))

    def drain(segment, count, chunks):
        for j in range(max(0, count - 2), count):
            store(segment, j, chunks).wait()

    loop(PH // WIDE, third_back)
    drain(11, PH // WIDE, ZD // LANES)
    span = 4 * LANES

    def second_back(j):
        stored(9, j, PH // LANES)
        for i in range(PH // span):
            put_block(stage.at[j % 2], 0, i * (span // LANES), dot_tn(act_a[:, wide_at(j)], g_b[:, i * span : (i + 1) * span]))
        store(9, j, PH // LANES).start()
        grad = dot_nt(g_b[...], block_of(p_2, j * half, half, 0, PH // LANES))
        grad = (grad * silu_parts(pre_a[:, wide_at(j)])[1]).astype(low_type)
        g_a[:, wide_at(j)] = grad
        bias_out[:, wide_at(j, A_1)] += rows_sum(grad.astype(full_type))

    loop(PH // WIDE, second_back)
    drain(9, PH // WIDE, PH // LANES)

    def first_back(j):
        stored(7, j, PH // LANES)
        for i in range(PH // span):
            put_block(stage.at[j % 2], 0, i * (span // LANES), dot_tn(low[:, wide_at(j)], g_a[:, i * span : (i + 1) * span]))
        store(7, j, PH // LANES).start()
        grad_x[:, wide_at(j)] = dot_nt(g_a[...], block_of(p_1, j * half, half, 0, PH // LANES))

    loop(D // WIDE, first_back)
    loads[3].wait()

    def final_mod(j):
        modf[:, wide_at(j)] = dot(modulator[...], block_of(w_f, 0, D // ROWS, 2 * j, 2)) + b_f[:, wide_at(j)]

    loop(2 * D // WIDE, final_mod)
    part = lambda s, i: modf[pl.ds(s, 1), i * D : (i + 1) * D]
    dw_h[...] = jnp.zeros(dw_h.shape, full_type)

    def head(at, s):
        hat, scale = norm_parts(x[at, :])
        gain = 1.0 + part(s, 1)
        normed = (hat * gain + part(s, 0)).astype(low_type)
        off = dot(normed, w_h[...]) + b_h[...] - target[at, :]
        weight = weight_t[pl.ds(s, 1), :]
        stats[1:2, :] += rows_sum(weight * off * off)
        grad = (2.0 * weight / (SEQ * PD * sample_total) * off).astype(low_type)
        bias_out[:, A_H : A_H + LANES] += rows_sum(grad.astype(full_type))
        dw_h[...] += dot_tn(normed, grad)
        back = dot_nt(grad, w_h[...])
        d_modf[pl.ds(s, 1), 0:D] += rows_sum(back)
        d_modf[pl.ds(s, 1), D : 2 * D] += rows_sum(back * hat)
        inner = back * gain
        mean_a = jnp.mean(inner, axis=-1, keepdims=True)
        mean_b = jnp.mean(inner * hat, axis=-1, keepdims=True)
        grad_x[at, :] += scale * (inner - mean_a - hat * mean_b)

    each_chunk(head)
    turned = modulator[...].astype(full_type).T.astype(low_type)
    cond[...] = jnp.zeros(cond.shape, full_type)

    def final_back(j):
        grad = d_modf[:, wide_at(j)].astype(low_type)
        bias_out[:, wide_at(j, A_F)] += rows_sum(grad.astype(full_type))
        put_block(dw_f, 0, 2 * j, dot(turned, grad))
        cond[...] += dot_nt(grad, block_of(w_f, 0, D // ROWS, 2 * j, 2))

    loop(2 * D // WIDE, final_back)
    last = pltpu.make_async_copy(dw_f, segment_ref(grads, plan, 13), out_sem.at[2])
    last.start()
    last.wait()
    drain(7, D // WIDE, PH // LANES)


def top_call(plan, sample_total, x, features, target, weight_t, modulator, biases, w_h, b_h, units):
    rows = x.shape[0]
    vm = pl.BlockSpec(memory_space=pltpu.VMEM)
    anywhere = pl.BlockSpec(memory_space=pltpu.HBM)
    dma = pltpu.SemaphoreType.DMA
    few = modulator.shape[0]
    f32 = lambda *shape: pltpu.VMEM(shape, full_type)
    bf16 = lambda *shape: pltpu.VMEM(shape, low_type)
    shape = lambda *dims: jax.ShapeDtypeStruct(dims, full_type)
    return pl.pallas_call(
        functools.partial(top_kernel, plan, rows, sample_total),
        out_shape=[
            shape(rows, D),
            shape(8, LANES),
            shape(few, D),
            shape(1, 2 * PH + ZD + 2 * D + LANES),
            shape(D, LANES),
            jax.ShapeDtypeStruct(units.shape, low_type),
        ],
        in_specs=[vm] * 11 + [anywhere],
        out_specs=[vm] * 5 + [anywhere],
        scratch_shapes=[segment_scratch(plan, s) for s in TOP]
        + [f32(rows, PH), bf16(rows, PH), f32(rows, PH), bf16(rows, PH), f32(rows, ZD), bf16(rows, D)]
        + [bf16(rows, PH), bf16(rows, PH), bf16(rows, ZD), f32(few, 2 * D), f32(few, 2 * D)]
        + [bf16(2, WIDE // ROWS, PH // LANES, ROWS, LANES), segment_scratch(plan, 13)]
        + [dma((4,)), dma((3,))],
        compiler_params=pltpu.CompilerParams(vmem_limit_bytes=60 * MB),
        name="projector_and_head",
    )(x, features, target, weight_t, modulator, *biases, w_h, b_h, units)


def busy_loop(count, body, events=()):
    size = max(1, -(-len(events) // count))

    def step(i):
        body(i)
        for first in range(0, len(events), size):

            @pl.when(i == first // size)
            def _():
                for event in events[first : first + size]:
                    event()

    loop(count, step)


def spread(events, weights):
    shares, done, total = [], 0, 0
    for weight in weights:
        total += weight
        upto = len(events) * total // sum(weights)
        shares.append(events[done:upto])
        done = upto
    return shares


def row_vector(units, rows):
    values = units.astype(full_type).reshape(-1, LANES)
    return jnp.concatenate([values[r : r + 1, :] for r in range(rows)], axis=1)


def pick(ref, here, *spots):
    return ref.at[tuple(here.zero + spot for spot in spots)]


class Place:
    def __init__(self, zs):
        self.zs = zs
        self.n = zs * 8
        self.me = lax.axis_index("fsdp")
        self.zero = self.me * 0
        self.z, self.y, self.x, self.c = place(self.me, zs)
        self.prev = lax.rem(self.me + self.n - 1, self.n)
        self.following = lax.rem(self.me + 1, self.n)
        self.xpeer = self.index(self.z, self.y, 1 - self.x, self.c)
        self.ypeer = self.index(self.z, 1 - self.y, self.x, self.c)
        self.cpeer = self.index(self.z, self.y, self.x, 1 - self.c)

    def index(self, z, y, x, c):
        return ((z * 2 + y) * 2 + x) * 2 + c

    def above(self, k):
        return self.index(lax.rem(self.z + k, self.zs), self.y, self.x, self.c)

    def below(self, k):
        return self.index(lax.rem(self.z + self.zs - k, self.zs), self.y, self.x, self.c)

    def slot(self, k, dy, dx, dc):
        z = lax.rem(self.z + self.zs - k, self.zs)
        flip = lambda value, change: 1 - value if change else value
        return self.index(z, flip(self.y, dy), flip(self.x, dx), flip(self.c, dc))

    def peers(self):
        return [self.prev, self.following, self.xpeer, self.ypeer, self.cpeer] + [self.above(k) for k in range(1, self.zs)]

    def greet(self):
        barrier = pltpu.get_barrier_semaphore()
        for peer in self.peers():
            pl.semaphore_signal(barrier, inc=1, device_id=(peer,), device_id_type=MESH)

    def met(self):
        pl.semaphore_wait(pltpu.get_barrier_semaphore(), len(self.peers()))


def remote(src, dst, send_sem, recv_sem, to):
    return pltpu.make_async_remote_copy(src, dst, send_sem, recv_sem, device_id=(to,), device_id_type=MESH)


def arrived(ref, sem):
    pltpu.make_async_copy(ref, ref, sem).wait()


class Gather:
    def __init__(self, here, buckets, sems):
        self.here = here
        self.buckets = buckets
        self.own_sem, self.send_sem, self.zr, self.xa, self.xb, self.yb, self.ya, self.cr = sems
        self.sent = []
        self.made = 0

    def guarded(self, b, k, run):
        plan, _, _, lo, hi = self.buckets[b]
        if lo == 0 and hi == self.here.zs:
            run()
            return
        source = lax.rem(self.here.z + self.here.zs - k, self.here.zs)
        pl.when((source >= lo) & (source < hi))(run)

    def sem(self, name, *spots):
        return lambda: pick(getattr(self, name), self.here, *spots)

    def send(self, b, k, src, dst, sem, to):
        number = self.made
        self.made += 1
        make = lambda: remote(src(), dst(), pick(self.send_sem, self.here, number), sem(), to())
        make().start()
        self.sent.append((b, k, make))

    def part(self, b, h, k, dy, dx, dc=0):
        plan, units = self.buckets[b][:2]
        return units.at[pl.ds(self.here.slot(k, dy, dx, dc) * plan.per + h * plan.half, plan.half)]

    def whole(self, b, k, dy, dx, dc=0):
        plan, units = self.buckets[b][:2]
        return units.at[pl.ds(self.here.slot(k, dy, dx, dc) * plan.per, plan.per)]

    def own_copy(self, b):
        return pltpu.make_async_copy(self.buckets[b][2], self.whole(b, 0, 0, 0), pick(self.own_sem, self.here, b))

    def start(self, b):
        here, slot = self.here, self.buckets[b][2]
        plan = self.buckets[b][0]

        def run():
            self.own_copy(b).start()
            mine = lambda h: lambda: slot.at[pl.ds(h * plan.half, plan.half)]
            to = lambda h: lambda: self.part(b, h, 0, 0, 0)
            for k in range(1, here.zs):
                for h in range(2):
                    self.send(b, 0, mine(h), to(h), self.sem("zr", b, h, k), lambda k=k: here.above(k))
            self.send(b, 0, mine(0), to(0), self.sem("xa", b, 0), lambda: here.xpeer)
            self.send(b, 0, mine(1), to(1), self.sem("yb", b, 0), lambda: here.ypeer)
            self.send(b, 0, mine(0), to(0), self.sem("ya", b, 0, 0), lambda: here.ypeer)
            self.send(b, 0, mine(1), to(1), self.sem("xb", b, 0, 0), lambda: here.xpeer)
            self.send(b, 0, lambda: slot, lambda: self.whole(b, 0, 0, 0), self.sem("cr", b, 0, 0, 0), lambda: here.cpeer)

        self.guarded(b, 0, run)

    def pass_on(self, b, k, h, dy, dx, sem, to):
        ref = lambda: self.part(b, h, k, dy, dx)
        self.send(b, k, ref, ref, sem, to)

    def share(self, b, k, dy, dx):
        ref = lambda: self.whole(b, k, dy, dx)
        self.send(b, k, ref, ref, self.sem("cr", b, k, dy, dx), lambda: self.here.cpeer)

    def events(self, b):
        here = self.here
        found = []

        def add(k, run):
            found.append(lambda: self.guarded(b, k, run))

        for k in range(1, here.zs):

            def from_z(k=k):
                arrived(self.part(b, 0, k, 0, 0), pick(self.zr, self.here, b, 0, k))
                self.pass_on(b, k, 0, 0, 0, self.sem("xa", b, k), lambda: here.xpeer)
                arrived(self.part(b, 1, k, 0, 0), pick(self.zr, self.here, b, 1, k))
                self.pass_on(b, k, 1, 0, 0, self.sem("yb", b, k), lambda: here.ypeer)
                self.pass_on(b, k, 0, 0, 0, self.sem("ya", b, k, 0), lambda: here.ypeer)
                self.pass_on(b, k, 1, 0, 0, self.sem("xb", b, k, 0), lambda: here.xpeer)
                self.share(b, k, 0, 0)

            add(k, from_z)
        for k in range(here.zs):

            def across(k=k):
                arrived(self.part(b, 0, k, 0, 1), pick(self.xa, self.here, b, k))
                self.pass_on(b, k, 0, 0, 1, self.sem("ya", b, k, 1), lambda: here.ypeer)
                arrived(self.part(b, 1, k, 1, 0), pick(self.yb, self.here, b, k))
                self.pass_on(b, k, 1, 1, 0, self.sem("xb", b, k, 1), lambda: here.xpeer)

            add(k, across)
        for k in range(here.zs):

            def beside(k=k):
                arrived(self.part(b, 1, k, 0, 1), pick(self.xb, self.here, b, k, 0))
                self.share(b, k, 0, 1)
                arrived(self.part(b, 0, k, 1, 0), pick(self.ya, self.here, b, k, 0))
                self.share(b, k, 1, 0)

            add(k, beside)
        for k in range(here.zs):

            def corner(k=k):
                arrived(self.part(b, 1, k, 1, 1), pick(self.xb, self.here, b, k, 1))
                arrived(self.part(b, 0, k, 1, 1), pick(self.ya, self.here, b, k, 1))
                self.share(b, k, 1, 1)

            add(k, corner)
        return found

    def complete(self, b):
        self.guarded(b, 0, lambda: self.own_copy(b).wait())
        for k in range(self.here.zs):

            def run(k=k):
                for dy in range(2):
                    for dx in range(2):
                        arrived(self.whole(b, k, dy, dx, 1), pick(self.cr, self.here, b, k, dy, dx))

            self.guarded(b, k, run)

    def drain(self):
        for b, k, make in self.sent:
            self.guarded(b, k, lambda: make().wait_send())


FRONT = 7


def cut_units(here, plan, ext, slot):
    top = here.me * plan.share // LANES - plan.before
    for base, chunks, count, first_unit, _, _ in plan.segments:
        lo = jnp.clip(plan.per * here.me - first_unit, 0, count)
        hi = jnp.clip(plan.per * here.me + plan.per - first_unit, 0, count)

        def unit(u, carry):
            block = u // chunks
            row = base + block * (ROWS * chunks) + (u - block * chunks) - top
            if chunks == 1:
                value = ext[pl.ds(row, ROWS), :]
            else:
                value = ext[pl.ds(row, ROWS, stride=chunks), :]
            slot[first_unit + u - plan.per * here.me] = value.astype(low_type)
            return carry

        lax.fori_loop(lo, hi, unit, 0)


def forward_kernel(plans, zs, rows, *refs):
    np_ = len(plans)
    feed = iter(refs)
    take = lambda count: tuple(next(feed) for _ in range(count))
    one = lambda: next(feed)
    raw_hbm = take(2)
    noisy, positions, basis, chosen = take(4)
    units = take(np_)
    stream = take(LAYERS + 1)
    mods = take(LAYERS)
    sums = take(LAYERS)
    modulator, condition, time_pre = take(3)
    saved_out = [take(len(SAVED)) for _ in range(LAYERS)]
    from_prev, from_next, slots = take(np_), take(np_), take(np_)
    raw_sem, halo_send, halo_recv, front_sem, load_sem, save_sem = take(6)
    gather_sems = take(8)
    here = Place(zs)
    here.greet()
    root = plans[0]
    front_units = root.segments[FRONT][3]
    front_planes = min(zs, -(-front_units // (8 * root.per)))
    buckets = [(root, units[0], slots[0], 0, front_planes)]
    buckets += [(plans[1 + i], units[1 + i], slots[1 + i], 0, zs) for i in range(LAYERS)]
    buckets += [(root, units[0], slots[0], front_planes, zs)]
    gather = Gather(here, buckets, gather_sems)
    last = len(buckets) - 1
    starts = [[0]] + [[1 + i] for i in range(LAYERS)]
    starts[-1].append(last)

    def prepare(*scratch):
        raw, ext, tail = scratch[:2], scratch[2 : 2 + np_], scratch[2 + np_ :]
        counts = (1,) + (LAYERS,) * LAYERS
        pad = 8 * LAYERS
        loads = [pltpu.make_async_copy(raw_hbm[i], raw[i].at[pl.ds(pad, raw_hbm[i].shape[0])], raw_sem.at[i]) for i in range(2)]
        for i in range(2):
            loads[i].start()
            raw[i][pl.ds(0, pad), :] = jnp.zeros((pad, LANES), full_type)
        lane = lax.broadcasted_iota(jnp.int32, (64, LANES), 1)
        halos = []
        for i, p in enumerate(plans):
            shift = lax.rem(here.me * p.share, LANES)
            delta = (here.me + 1) * p.share // LANES - here.me * p.share // LANES
            ext[i][pl.ds(0, p.before), :] = jnp.zeros((p.before, LANES), full_type)
            ext[i][pl.ds(p.before + p.raw, p.after), :] = jnp.zeros((p.after, LANES), full_type)
            if i < 2:
                loads[i].wait()
            every = counts[i]

            def rows_from(start):
                source = raw[min(i, 1)]
                first = pad + every * start + max(i - 1, 0)
                if every == 1:
                    return source[pl.ds(first, 64), :]
                return source[pl.ds(first, 64, stride=every), :]

            def align(j):
                row = pl.multiple_of(j * 64, 64)
                level = pltpu.roll(rows_from(row), shift, 1)
                above = pltpu.roll(rows_from(row - 1), shift, 1)
                ext[i][pl.ds(row + p.before, 64), :] = jnp.where(lane >= shift, level, above)

            loop(p.raw // 64, align)
            tail[i][...] = ext[i][pl.ds(delta, p.before + 8), :]
            if i == 0:
                here.met()
            halos.append(remote(ext[i].at[pl.ds(p.before, p.after)], from_next[i], halo_send.at[2 * i], halo_recv.at[2 * i], here.prev))
            halos.append(remote(tail[i], from_prev[i], halo_send.at[2 * i + 1], halo_recv.at[2 * i + 1], here.following))
            halos[-2].start()
            halos[-1].start()
        for i, p in enumerate(plans):
            delta = (here.me + 1) * p.share // LANES - here.me * p.share // LANES
            halos[2 * i].wait()
            halos[2 * i + 1].wait()
            ext[i][pl.ds(0, p.before + 8), :] += from_prev[i][...]
            ext[i][pl.ds(p.before + delta, p.after), :] += from_next[i][...]
            cut_units(here, p, ext[i], slots[i])
            for b in starts[i]:
                gather.start(b)

    f32 = lambda *dims: pltpu.VMEM(dims, full_type)
    pl.run_scoped(
        prepare,
        f32(plans[0].raw + 8 * LAYERS, LANES), f32(LAYERS * (plans[1].raw + 8), LANES),
        *[f32(p.ext, LANES) for p in plans],
        *[f32(p.before + 8, LANES) for p in plans],
    )
    for event in gather.events(0):
        event()
    gather.complete(0)

    def compute(front, w_qkv, w_o, w_1, w_2, w_mod, raw_bias, *held):
        copy = pltpu.make_async_copy(units[0].at[pl.ds(0, front_units)], front, front_sem)
        copy.start()
        copy.wait()
        matrix = lambda number, blocks: front_matrix(front, root, number, blocks)
        vector = lambda number: row_vector(front[pl.ds(root.segments[number][3], 1)], D // LANES)
        events = spread(gather.events(1), (1, 1, 1, 1))
        stream[0][...] = dot(noisy[...], matrix(0, 1)) + vector(1) + positions[...]
        for event in events[0]:
            event()
        pre = dot(basis[...], matrix(2, FREQ // ROWS)) + vector(3)
        time_pre[...] = pre
        act = silu_parts(pre)[0].astype(low_type)
        total = dot(act, matrix(4, D // ROWS)) + vector(5)
        few = basis.shape[0]
        first = root.segments[6][3]
        picked = dot(chosen[...], front[pl.ds(first, root.segments[6][2])].reshape(-1, LANES))
        total = total + jnp.concatenate([picked[i * few : (i + 1) * few, :] for i in range(D // LANES)], axis=1)
        condition[...] = total
        modulator[...] = silu_parts(total)[0].astype(low_type)
        for group in events[1:]:
            for event in group:
                event()
        for ordinal in range(LAYERS):
            gather.complete(1 + ordinal)
            queue = gather.events(2 + ordinal)
            layer_forward_body(
                plans[1 + ordinal], rows, stream[ordinal], modulator, mods[ordinal], units[1 + ordinal],
                stream[ordinal + 1], sums[ordinal], saved_out[ordinal], held, (w_qkv, w_o, w_1, w_2, w_mod), raw_bias,
                load_sem, save_sem, spread(queue, (18, 9, 12, 3, 12)),
            )
        gather.complete(last)

    plan = plans[1]
    bias_units = plan.units - plan.segments[5][3]
    pl.run_scoped(
        compute,
        pltpu.VMEM((front_units, ROWS, LANES), low_type),
        *[segment_scratch(plan, i) for i in range(5)],
        pltpu.VMEM((bias_units, ROWS, LANES), low_type),
        *[pltpu.VMEM((rows, width), kind) for _, width, kind in SAVED],
    )
    gather.drain()


def front_matrix(front, plan, number, blocks):
    _, chunks, _, first, _, _ = plan.segments[number]
    columns = [jnp.concatenate([front[first + b * chunks + c] for b in range(blocks)], axis=0) for c in range(chunks)]
    return jnp.concatenate(columns, axis=1)


def layer_forward_body(plan, rows, x, modulator, mod, units, out, sums, saved_out, held, weights, raw_bias, load_sem, save_sem, events):
    ns = len(SAVED)
    h1, qkv, heads, attn, middle, h2, pre, mlp = held
    w_qkv, w_o, w_1, w_2, w_mod = weights
    bias_first = plan.segments[5][3]
    loads = [pltpu.make_async_copy(segment_ref(units, plan, i), weights[i], load_sem.at[i]) for i in range(5)]
    bias_load = pltpu.make_async_copy(units.at[pl.ds(bias_first, raw_bias.shape[0])], raw_bias, load_sem.at[5])
    bias_load.start()
    for i in (4, 0, 1, 2, 3):
        loads[i].start()
    saves = [pltpu.make_async_copy(held[i], saved_out[i], save_sem.at[i]) for i in range(ns)]
    part = lambda s, i: mod[pl.ds(s, 1), i * D : (i + 1) * D]
    per = SEQ // CHUNK
    wide_at = lambda j: pl.ds(pl.multiple_of(j * WIDE, WIDE), WIDE)
    chunk_at = lambda i: pl.ds(pl.multiple_of(i * CHUNK, CHUNK), CHUNK)
    bias_load.wait()

    def bias(number):
        _, _, count, first, shape, _ = plan.segments[number]
        return row_vector(raw_bias[pl.ds(first - bias_first, count)], shape[0] // LANES)

    loads[4].wait()
    mod[...] = jnp.broadcast_to(bias(10), mod.shape)
    value_of = modulator[...]

    def modulate(j):
        mod[:, wide_at(j)] += dot(value_of, block_of(w_mod, 0, D // ROWS, 2 * j, 2))

    busy_loop(6 * D // WIDE, modulate, events[0])

    def norm_a(i):
        s = i // per
        hat, _ = norm_parts(x[chunk_at(i), :])
        h1[chunk_at(i), :] = (hat * (1.0 + part(s, 1)) + part(s, 0)).astype(low_type)

    loop(rows // CHUNK, norm_a)
    saves[0].start()
    loads[0].wait()
    first_bias, value_bias = bias(5), bias(6)

    def project_with(base, given, events):
        pieces = D // WIDE

        def project(j):
            value = dot(h1[...], block_of(w_qkv, 0, D // ROWS, 2 * (base + j), 2))
            cols = wide_at(base + j)
            if given is not None:
                value = value + mlp[0:1, wide_at(j)]
            qkv[:, cols] = value.astype(low_type)

        if given is not None:
            mlp[0:1, :] = given
        busy_loop(pieces, project, events)

    third = spread(events[1], (1, 1, 1))
    project_with(0, first_bias, third[0])
    project_with(D // WIDE, None, third[1])
    project_with(2 * D // WIDE, value_bias, third[2])
    saves[1].start()
    first = head_masks()

    def attend(i):
        s, j = i // (HEADS // 2), i % (HEADS // 2)
        at = pl.ds(pl.multiple_of(s * SEQ, SEQ), SEQ)
        cut = lambda o: qkv[at, pl.ds(pl.multiple_of(o * D + j * LANES, LANES), LANES)]
        q, k, v = cut(0), cut(1), cut(2)
        q = q * jnp.asarray(HD ** (-0.5), low_type)
        zero = jnp.zeros_like(q)
        halves = []
        for mask in (first, ~first):
            probs = softmax_f32(dot_nt(jnp.where(mask, q, zero), k)).astype(low_type)
            halves.append(dot(probs, v))
        heads[at, pl.ds(pl.multiple_of(j * LANES, LANES), LANES)] = jnp.where(first, halves[0], halves[1]).astype(low_type)

    busy_loop(attention_pairs(rows), attend, events[2])
    saves[2].start()
    loads[1].wait()
    attn[...] = jnp.broadcast_to(bias(7), (rows, D))

    def project_out(j):
        attn[:, wide_at(j)] += dot(heads[...], block_of(w_o, 0, D // ROWS, 2 * j, 2))

    busy_loop(D // WIDE, project_out, events[3])
    saves[3].start()
    zero_sum = jnp.zeros((1, D), full_type)

    def norm_m(i, total):
        s = i // per
        value = attn[chunk_at(i), :]
        mid = x[chunk_at(i), :] + part(s, 2) * value
        middle[chunk_at(i), :] = mid
        hat, _ = norm_parts(mid)
        h2[chunk_at(i), :] = (hat * (1.0 + part(s, 4)) + part(s, 3)).astype(low_type)
        return total + rows_sum(value * value)

    attn_sum = lax.fori_loop(0, rows // CHUNK, norm_m, zero_sum)
    saves[4].start()
    saves[5].start()
    loads[2].wait()
    loads[3].wait()
    pre[0:1, :] = bias(8)
    mlp[...] = jnp.broadcast_to(bias(9), (rows, D))

    def feed(j):
        value = dot(h2[...], block_of(w_1, 0, D // ROWS, 2 * j, 2)) + pre[0:1, wide_at(j)]
        pre[:, wide_at(j)] = value
        act = gelu_parts(value)[0].astype(low_type)
        mlp[...] += dot(act, block_of(w_2, j * (WIDE // ROWS), WIDE // ROWS, 0, D // LANES))

    busy_loop(FF // WIDE, feed, events[4])
    saves[6].start()
    saves[7].start()

    def finish(i, carry):
        value = mlp[chunk_at(i), :]
        result = middle[chunk_at(i), :] + part(i // per, 5) * value
        out[chunk_at(i), :] = result
        return (carry[0] + rows_sum(result * result), carry[1] + rows_sum(value * value))

    out_sum, mlp_sum = lax.fori_loop(0, rows // CHUNK, finish, (zero_sum, zero_sum))
    sums[...] = jnp.zeros(sums.shape, full_type)
    sums[0:1, :] = out_sum
    sums[1:2, :] = attn_sum
    sums[2:3, :] = mlp_sum
    for copy in saves:
        copy.wait()


def forward_call(plans, raws, noisy, positions, basis, chosen):
    n = plans[0].devices
    zs = n // 8
    rows, few = noisy.shape[0], basis.shape[0]
    dma = pltpu.SemaphoreType.DMA
    np_, nb = len(plans), len(plans) + 1
    vm = pl.BlockSpec(memory_space=pltpu.VMEM)
    hbm = pl.BlockSpec(memory_space=pltpu.HBM)
    shape = jax.ShapeDtypeStruct
    saved_shapes = [shape((rows, width), kind) for _, width, kind in SAVED]
    out_shape = [shape((n * p.per, ROWS, LANES), low_type) for p in plans]
    out_shape += [shape((rows, D), full_type)] * (LAYERS + 1)
    out_shape += [shape((few, 6 * D), full_type)] * LAYERS + [shape((8, D), full_type)] * LAYERS
    out_shape += [shape((few, D), low_type), shape((few, D), full_type), shape((few, D), full_type)]
    out_shape += saved_shapes * LAYERS
    scratch = [pltpu.VMEM((p.before + 8, LANES), full_type) for p in plans]
    scratch += [pltpu.VMEM((p.after, LANES), full_type) for p in plans]
    scratch += [pltpu.VMEM((p.per, ROWS, LANES), low_type) for p in plans]
    scratch += [dma((np_,)), dma((2 * np_,)), dma((2 * np_,)), dma, dma((6,)), dma((len(SAVED),))]
    scratch += [dma((nb,)), dma((nb * (2 * (zs - 1) + 10 * zs),)), dma((nb, 2, zs)), dma((nb, zs)), dma((nb, zs, 2))]
    scratch += [dma((nb, zs)), dma((nb, zs, 2)), dma((nb, zs, 2, 2))]
    results = pl.pallas_call(
        functools.partial(forward_kernel, plans, zs, rows),
        out_shape=out_shape,
        in_specs=[hbm] * 2 + [vm] * 4,
        out_specs=[hbm] * np_ + [vm] * (LAYERS + 1 + 2 * LAYERS + 3) + [hbm] * (len(SAVED) * LAYERS),
        scratch_shapes=scratch,
        compiler_params=pltpu.CompilerParams(collective_id=0, has_side_effects=True, vmem_limit_bytes=62 * MB),
        name="gather_and_forward",
    )(*raws, noisy, positions, basis, chosen)
    feed = iter(results)
    take = lambda count: [next(feed) for _ in range(count)]
    units, stream, mods, sums = take(np_), take(LAYERS + 1), take(LAYERS), take(LAYERS)
    modulator, condition, time_pre = take(3)
    return units, stream, mods, sums, modulator, condition, time_pre, [take(len(SAVED)) for _ in range(LAYERS)]


LOOK = 1


class Reduce:
    def __init__(self, here, buckets, first, buffers, sems, frees):
        self.here = here
        self.buckets = buckets
        self.first = first
        self.kept, self.two, self.three, self.four, self.ring, self.other, self.own = buffers
        self.s1, self.r1, self.s2, self.r2, self.s3, self.r3, self.s4, self.r4, self.load_sem = sems
        self.free_two, self.free_three, self.free_four = frees
        self.planes = list(range(1, here.zs)) + [0]
        self.groups = [(b, k) for b in range(len(buckets)) for k in self.planes]
        self.order = ((1, 1), (1, 0), (0, 1), (0, 0))

    def limits(self, b):
        return self.buckets[b][2:4]

    def meets(self, b, k):
        lo, hi = self.limits(b)
        if lo == 0 and hi == self.here.zs:
            return None
        plane = lax.rem(self.here.z + self.here.zs - k, self.here.zs)
        return (plane >= lo) & (plane < hi)

    def guarded(self, b, k, run):
        test = self.meets(b, k)
        if test is None:
            run()
        else:
            pl.when(test)(run)

    def overlaps(self, b, other):
        return self.limits(b)[0] < self.limits(other)[1] and self.limits(other)[0] < self.limits(b)[1]

    def before(self, b, k, run):
        for other in range(b - 1, -1, -1):
            if self.overlaps(b, other):
                self.guarded(b, k, lambda: self.guarded(other, k, run))
                return

    def after(self, b, k, run):
        for other in range(b + 1, len(self.buckets)):
            if self.overlaps(b, other):
                self.guarded(b, k, lambda: self.guarded(other, k, run))
                self.after_rest(b, other, k, run)
                return

    def after_rest(self, b, done, k, run):
        for other in range(done + 1, len(self.buckets)):
            if self.overlaps(b, other) and not self.overlaps(done, other):
                self.guarded(b, k, lambda: self.guarded(other, k, run))

    def slot(self, b, k, dy, dx, dc):
        plan, grads = self.buckets[b][:2]
        return grads.at[pl.ds(self.here.slot(k, dy, dx, dc) * plan.per, plan.per)]

    def landed(self, b, k, dy, dx):
        return self.first[b].at[self.here.zero + k, self.here.zero + dy, self.here.zero + dx]

    def sibling(self, b, k, dy, dx):
        here = self.here
        return remote(
            self.slot(b, k, dy, dx, 1), self.landed(b, k, dy, dx), pick(self.s1, here, b, k, dy, dx), pick(self.r1, here, b, k, dy, dx), here.cpeer
        )

    def open(self, b):
        for k in self.planes:

            def run(k=k):
                for dy, dx in self.order:
                    self.sibling(b, k, dy, dx).start()

            self.guarded(b, k, run)

    def half(self, b):
        return self.buckets[b][0].half

    def buffer(self, ref, b, *spots):
        view = ref.at[tuple(self.here.zero + s for s in spots)]
        return view.at[pl.ds(0, self.half(b))]

    def place_of(self, g, i):
        return 3 * (LOOK + 1) if i == 3 else 3 * (g % (LOOK + 1)) + i

    def loads(self, g, i):
        b, k = self.groups[g]
        dy, dx = self.order[i]
        per = self.buckets[b][0].per
        here = self.here
        at = self.place_of(g, i)
        one = pltpu.make_async_copy(self.slot(b, k, dy, dx, 0), pick(self.ring, here, at).at[pl.ds(0, per)], pick(self.load_sem, here, at, 0))
        two = pltpu.make_async_copy(self.landed(b, k, dy, dx), pick(self.other, here, i % 2).at[pl.ds(0, per)], pick(self.load_sem, here, at, 1))
        return one, two

    def prepare(self, g, i):
        b, k = self.groups[g]
        dy, dx = self.order[i]
        one, two = self.loads(g, i)
        one.start()
        arrived(self.landed(b, k, dy, dx), pick(self.r1, self.here, b, k, dy, dx))
        two.start()

    def second(self, g, h, i):
        b, k = self.groups[g]
        dy, dx = self.order[i]
        here, size = self.here, self.half(b)
        src = pick(self.ring, here, self.place_of(g, i)).at[pl.ds(h * size, size)]
        far = dx if h == 0 else dy
        return remote(src, self.buffer(self.two[h], b, k, far), pick(self.s2, here, h, k, far), pick(self.r2, here, h, k, far), here.ypeer if h == 0 else here.xpeer)

    def sends_of(self, g):
        return [(h, i) for i, (dy, dx) in enumerate(self.order) for h in range(2) if (dy, dx)[h]]

    def add(self, b, dst, at, one, one_at, two, two_at):
        step = self.half(b) // 2

        def body(i, carry):
            span = lambda ref, off: ref[pl.ds(off + i * step, step)].astype(full_type)
            dst[pl.ds(at + i * step, step)] = (span(one, one_at) + span(two, two_at)).astype(low_type)
            return carry

        lax.fori_loop(0, 2, body, 0)

    def phase_one(self, g, i):
        b, k = self.groups[g]
        here, size = self.here, self.half(b)
        if i == 0:
            for h in range(2):
                to_free = lambda h=h: pl.semaphore_wait(pick(self.free_two, here, h, k), 1)
                self.before(b, k, to_free)

        def run():
            dy, dx = self.order[i]
            if i == 0:
                self.prepare(g, 0)
            if i < 3:
                self.prepare(g, i + 1)
            for copy in self.loads(g, i):
                copy.wait()
            mine, theirs = pick(self.ring, here, self.place_of(g, i)), pick(self.other, here, i % 2)
            for h, moves in enumerate((dy, dx)):
                if moves:
                    self.add(b, mine, h * size, mine, h * size, theirs, h * size)
                    self.second(g, h, i).start()
                else:
                    self.add(b, self.buffer(self.kept[h], b, k, dx if h == 0 else dy), 0, mine, h * size, theirs, h * size)

        self.guarded(b, k, run)

    def third(self, g, h):
        b, k = self.groups[g]
        here = self.here
        return remote(
            self.buffer(self.two[h], b, k, 1), self.buffer(self.three[h], b, k), pick(self.s3, here, h, k), pick(self.r3, here, h, k), here.xpeer if h == 0 else here.ypeer
        )

    def phase_two(self, g, far):
        b, k = self.groups[g]
        here = self.here
        if far:
            for h in range(2):
                self.before(b, k, lambda h=h: pl.semaphore_wait(pick(self.free_three, here, h, k), 1))

        def run():
            for h in range(2):
                got, kept = self.buffer(self.two[h], b, k, far), self.buffer(self.kept[h], b, k, far)
                arrived(got, pick(self.r2, here, h, k, far))
                if far:
                    self.add(b, got, 0, got, 0, kept, 0)
                    self.third(g, h).start()
                else:
                    self.add(b, kept, 0, got, 0, kept, 0)

        self.guarded(b, k, run)

    def last(self, g, h):
        b, k = self.groups[g]
        here = self.here
        return remote(self.buffer(self.three[h], b, k), self.buffer(self.four, b, b % 2, h, k - 1), pick(self.s4, here, b % 2, h, k - 1), pick(self.r4, here, b % 2, h, k - 1), here.below(k))

    def phase_three(self, g):
        b, k = self.groups[g]
        here, size = self.here, self.half(b)
        if k:
            if b >= 2:
                to_free = lambda: pl.semaphore_wait(pick(self.free_four, here, k - 1), 1)
                self.guarded(b, k, lambda: self.guarded(b - 2, k, to_free))

        def run():
            for h in range(2):
                got, kept = self.buffer(self.three[h], b, k), self.buffer(self.kept[h], b, k, 0)
                arrived(got, pick(self.r3, here, h, k))
                if k:
                    self.add(b, got, 0, got, 0, kept, 0)
                    self.last(g, h).start()
                else:
                    step = size // 2

                    def body(i, carry):
                        part = pl.ds(i * step, step)
                        self.own[pl.ds(h * size + i * step, step)] = got[part].astype(full_type) + kept[part].astype(full_type)
                        return carry

                    lax.fori_loop(0, 2, body, 0)

        self.guarded(b, k, run)

    def release_one(self, g):
        b, k = self.groups[g]

        def run():
            for h, i in self.sends_of(g):
                self.second(g, h, i).wait_send()

        self.guarded(b, k, run)

    def release_two(self, g):
        b, k = self.groups[g]
        here = self.here

        def run():
            for h in range(2):
                self.third(g, h).wait_send()

        self.guarded(b, k, run)

        def free():
            for h in range(2):
                to = here.ypeer if h == 0 else here.xpeer
                pl.semaphore_signal(pick(self.free_two, here, h, k), inc=1, device_id=(to,), device_id_type=MESH)

        self.after(b, k, free)

    def release_three(self, g):
        b, k = self.groups[g]
        here = self.here

        def run():
            for h in range(2):
                self.last(g, h).wait_send()

        if k:
            self.guarded(b, k, run)

        def free():
            for h in range(2):
                to = here.xpeer if h == 0 else here.ypeer
                pl.semaphore_signal(pick(self.free_three, here, h, k), inc=1, device_id=(to,), device_id_type=MESH)

        self.after(b, k, free)

    def collect(self, b, out, sem):
        here, size = self.here, self.half(b)

        def run():
            for h in range(2):
                for k in range(1, here.zs):
                    arrived(self.buffer(self.four, b, b % 2, h, k - 1), pick(self.r4, here, b % 2, h, k - 1))
                step = size // 2

                def body(i, carry):
                    part = pl.ds(i * step, step)
                    where = pl.ds(h * size + i * step, step)
                    value = self.own[where]
                    for k in range(1, here.zs):
                        value = value + self.buffer(self.four, b, b % 2, h, k - 1)[part].astype(full_type)
                    self.own[where] = value
                    return carry

                lax.fori_loop(0, 2, body, 0)
            copy = pltpu.make_async_copy(self.own.at[pl.ds(0, 2 * size)], out, sem)
            copy.start()
            copy.wait()

        self.guarded(b, 0, run)

        def free():
            for k in range(1, here.zs):
                pl.semaphore_signal(pick(self.free_four, here, k - 1), inc=1, device_id=(here.above(k),), device_id_type=MESH)

        if b + 2 < len(self.buckets):
            self.guarded(b, 0, lambda: self.guarded(b + 2, 0, free))

    def steps(self, g, outs, sem):
        zs = self.here.zs
        total = len(self.groups)
        found = []
        done = g - LOOK - 1
        if done % zs == 0 and 0 < done // zs <= len(self.buckets):
            b = done // zs - 1
            found.append(functools.partial(self.collect, b, outs[b], sem))
        if g < total:
            if g >= LOOK + 1:
                found.append(functools.partial(self.release_one, g - LOOK - 1))
            found += [functools.partial(self.phase_one, g, i) for i in range(4)]
        if 0 <= g - LOOK - zs < total - zs:
            found.append(functools.partial(self.release_three, g - LOOK - zs))
        if 0 <= g - LOOK < total:
            found += [functools.partial(self.phase_two, g - LOOK, 1), functools.partial(self.phase_two, g - LOOK, 0)]
        if 0 <= g - LOOK - 1 < total:
            found.append(functools.partial(self.phase_three, g - LOOK - 1))
        if 0 <= g - LOOK - 2 < total:
            found.append(functools.partial(self.release_two, g - LOOK - 2))
        return found

    def close(self):
        total = len(self.groups)
        for g in range(total - LOOK - 1, total):
            self.release_one(g)
        for g in range(total - self.here.zs, total):
            self.release_three(g)
        for b in range(len(self.buckets)):
            for k in self.planes:

                def run(b=b, k=k):
                    for dy, dx in self.order:
                        self.sibling(b, k, dy, dx).wait_send()

                self.guarded(b, k, run)


def unpack_rows(here, plan, segments, units_f, rows_f, flat_f, held_before):
    top = here.me * plan.share // LANES - plan.margin
    for origin, chunks, count, first_unit, _, _ in segments:
        lo = jnp.clip(plan.per * here.me - held_before - first_unit, 0, count)
        hi = jnp.clip(plan.per * here.me + plan.per + plan.units_after - first_unit, 0, count)

        def unit(u, carry):
            block = u // chunks
            row = origin + block * (ROWS * chunks) + (u - block * chunks) - top
            value = units_f[first_unit + u - plan.per * here.me + held_before]
            if chunks == 1:
                rows_f[pl.ds(row, ROWS), :] = value
            else:
                rows_f[pl.ds(row, ROWS, stride=chunks), :] = value
            return carry

        lax.fori_loop(lo, hi, unit, 0)
    shift = lax.rem(here.me * plan.share, LANES)
    turn = lax.rem(LANES - shift, LANES)
    lane = lax.broadcasted_iota(jnp.int32, (64, LANES), 1)
    spot = lax.broadcasted_iota(jnp.int32, (64, LANES), 0) * LANES + lane

    def unalign(i, squares):
        row = pl.multiple_of(i * 64, 64)
        level = pltpu.roll(rows_f[pl.ds(row + plan.margin, 64), :], turn, 1)
        below = pltpu.roll(rows_f[pl.ds(row + plan.margin + 1, 64), :], turn, 1)
        value = jnp.where(lane < LANES - shift, level, below)
        value = jnp.where(spot + row * LANES < plan.share, value, 0.0)
        flat_f[pl.ds(row, 64), :] = value
        return squares + jnp.sum((value * value).reshape(8, 8, LANES), axis=0)

    return lax.fori_loop(0, plan.raw // 64, unalign, jnp.zeros((8, LANES), full_type))


def put_row(stage, first, vector):
    for r in range(vector.shape[1] // LANES):
        stage[first + r : first + r + 1, :] = vector[:, r * LANES : (r + 1) * LANES]


B_Q, B_V, B_O, B_1, B_2 = 0, D, 2 * D, 3 * D, 3 * D + FF


def layer_backward_body(plan, rows, x_hbm, saved, units, grads, mod, grad, modulator, cond, note, samples, held, sems, events):
    (qkv, heads, h_low, wide_f, tall_f, pre, w_1, w_2, w_qkv, w_o, d_qkv, g_low, slim, turned, dx, d_one, d_two, grad_mod, bias_out) = held
    load_sem, chunk_sem, out_sem = sems
    h1_h, qkv_h, heads_h, attn_h, middle_h, h2_h, pre_h, mlp_h = saved
    fetch = lambda i, src, dst: pltpu.make_async_copy(src, dst, load_sem.at[i])
    load_mlp, load_attn = fetch(0, mlp_h, wide_f), fetch(0, attn_h, wide_f)
    load_middle, load_x = fetch(1, middle_h, tall_f), fetch(1, x_hbm, tall_f)
    load_h2, load_h1 = fetch(2, h2_h, h_low), fetch(2, h1_h, h_low)
    load_heads, load_qkv = fetch(3, heads_h, heads), fetch(4, qkv_h, qkv)
    load_w_o, load_w_qkv = fetch(5, segment_ref(units, plan, 1), w_o), fetch(6, segment_ref(units, plan, 0), w_qkv)
    half = WIDE // ROWS
    wide_at = lambda j, base=0: pl.ds(pl.multiple_of(base + j * WIDE, LANES), WIDE)

    def chunk_loads(j):
        at = j % 2
        return (
            pltpu.make_async_copy(segment_ref(units, plan, 3).at[pl.ds(j * half, half)], w_2.at[at], chunk_sem.at[at, 0]),
            pltpu.make_async_copy(segment_ref(units, plan, 2).at[:, pl.ds(2 * j, 2)], w_1.at[at], chunk_sem.at[at, 1]),
            pltpu.make_async_copy(pre_h.at[:, wide_at(j)], pre.at[at], chunk_sem.at[at, 2]),
        )

    def mod_load(j):
        return pltpu.make_async_copy(segment_ref(units, plan, 4).at[:, pl.ds(2 * j, 2)], w_1.at[j % 2], chunk_sem.at[j % 2, 1])

    for copy in (load_mlp, load_h2) + chunk_loads(0) + (load_middle, load_w_o, load_heads, load_qkv, load_w_qkv):
        copy.start()
    part = lambda s, i: mod[pl.ds(s, 1), i * D : (i + 1) * D]
    per = SEQ // CHUNK
    grad_mod[...] = jnp.zeros(grad_mod.shape, full_type)
    bias_out[...] = jnp.zeros(bias_out.shape, full_type)

    def add_mod(s, i, value):
        grad_mod[pl.ds(s, 1), i * D : (i + 1) * D] += value

    def each_chunk(body):
        loop(rows // CHUNK, lambda i: body(pl.ds(pl.multiple_of(i * CHUNK, CHUNK), CHUNK), i // per))

    load_mlp.wait()

    def start_mlp(at, s):
        value = grad[at, :]
        low = (part(s, 5) * value).astype(low_type)
        g_low[at, :] = low
        bias_out[:, B_2 : B_2 + D] += rows_sum(low.astype(full_type))
        add_mod(s, 5, rows_sum(wide_f[at, :] * value))

    each_chunk(start_mlp)
    load_attn.start()
    load_h2.wait()
    turned[...] = h_low[...].astype(full_type).T.astype(low_type)
    load_h1.start()
    dx[...] = jnp.zeros(dx.shape, full_type)

    def outer(slot, segment, block, blocks, chunk, chunks, buffer):
        target = segment_ref(grads, plan, segment).at[pl.ds(block, blocks), pl.ds(chunk, chunks)]
        return pltpu.make_async_copy(buffer, target, out_sem.at[slot])

    def mlp_store(j, kind):
        at = j % 2
        if kind == 0:
            return outer(2 * at, 3, j * half, half, 0, D // LANES, d_one.at[at])
        return outer(2 * at + 1, 2, 0, D // ROWS, 2 * j, 2, d_two.at[at])

    steps = FF // WIDE

    def feed_back(j):
        at = j % 2

        @pl.when(j + 1 < steps)
        def _():
            for copy in chunk_loads(j + 1):
                copy.start()

        for copy in chunk_loads(j):
            copy.wait()

        @pl.when(j >= 2)
        def _():
            mlp_store(j - 2, 0).wait()
            mlp_store(j - 2, 1).wait()

        act, slope = gelu_parts(pre[at])
        grad_act = dot_nt(g_low[...], block_of(w_2.at[at], 0, half, 0, D // LANES))
        low = (grad_act * slope).astype(low_type)
        slim[...] = low
        bias_out[:, wide_at(j, B_1)] += rows_sum(low.astype(full_type))
        put_block(d_one.at[at], 0, 0, dot_tn(act.astype(low_type), g_low[...]))
        mlp_store(j, 0).start()
        put_block(d_two.at[at], 0, 0, dot(turned[...], slim[...]))
        mlp_store(j, 1).start()
        dx[...] += dot_nt(slim[...], block_of(w_1.at[at], 0, D // ROWS, 0, 2))

    busy_loop(steps, feed_back, events[0])
    load_middle.wait()
    load_attn.wait()

    def middle_back(at, s):
        value = dx[at, :]
        back, scaled = norm_back(tall_f[at, :], value, 1.0 + part(s, 4))
        add_mod(s, 3, rows_sum(value))
        add_mod(s, 4, rows_sum(scaled))
        total = grad[at, :] + back
        grad[at, :] = total
        low = (part(s, 2) * total).astype(low_type)
        g_low[at, :] = low
        bias_out[:, B_O : B_O + D] += rows_sum(low.astype(full_type))
        add_mod(s, 2, rows_sum(wide_f[at, :] * total))

    each_chunk(middle_back)
    load_x.start()
    load_w_o.wait()
    load_heads.wait()
    for j in (steps - 2, steps - 1):
        mlp_store(j, 0).wait()
        mlp_store(j, 1).wait()
    mod_load(0).start()
    turned[...] = heads[...].astype(full_type).T.astype(low_type)

    def wo_store(j):
        return outer(j % 2, 1, 0, D // ROWS, 2 * j, 2, d_two.at[j % 2])

    def out_back(j):
        @pl.when(j >= 2)
        def _():
            wo_store(j - 2).wait()

        put_block(d_two.at[j % 2], 0, 0, dot(turned[...], g_low[:, wide_at(j)]))
        wo_store(j).start()
        heads[:, wide_at(j)] = dot_nt(g_low[...], block_of(w_o, j * half, half, 0, D // LANES)).astype(low_type)

    busy_loop(D // WIDE, out_back, events[1])
    load_qkv.wait()
    first = head_masks()

    def attend_back(i):
        s, j = i // (HEADS // 2), i % (HEADS // 2)
        at = pl.ds(pl.multiple_of(s * SEQ, SEQ), SEQ)
        cut = lambda o: qkv[at, pl.ds(pl.multiple_of(o * D + j * LANES, LANES), LANES)]
        q, k, v = cut(0), cut(1), cut(2)
        go = heads[at, pl.ds(pl.multiple_of(j * LANES, LANES), LANES)]
        q = q * jnp.asarray(HD ** (-0.5), low_type)
        zero = jnp.zeros_like(q)
        dq, dk, dv = [], 0.0, 0.0
        for mask in (first, ~first):
            q_h, go_h = jnp.where(mask, q, zero), jnp.where(mask, go, zero)
            probs = softmax_f32(dot_nt(q_h, k))
            grad_probs = dot_nt(go_h, v)
            dv = dv + dot_tn(probs.astype(low_type), go_h)
            inner = jnp.sum(probs * grad_probs, axis=-1, keepdims=True)
            ds = (probs * (grad_probs - inner)).astype(low_type)
            dq.append(dot(ds, k) * HD ** (-0.5))
            dk = dk + dot_tn(ds, q_h)
        for o, value in enumerate((jnp.where(first, dq[0], dq[1]), dk, dv)):
            low = value.astype(low_type)
            d_qkv[at, pl.ds(pl.multiple_of(o * D + j * LANES, LANES), LANES)] = low
            if o != 1:
                start = (B_Q if o == 0 else B_V) + j * LANES
                bias_out[:, pl.ds(pl.multiple_of(start, LANES), LANES)] += rows_sum(low.astype(full_type))

    busy_loop(attention_pairs(rows), attend_back, events[2])
    load_h1.wait()
    load_w_qkv.wait()
    wo_store(1).wait()
    wo_store(2).wait()
    turned[...] = h_low[...].astype(full_type).T.astype(low_type)
    dx[...] = jnp.zeros(dx.shape, full_type)

    def qkv_store(j):
        return outer(j % 2, 0, 0, D // ROWS, 2 * j, 2, d_two.at[j % 2])

    def project_back(j):
        @pl.when(j >= 2)
        def _():
            qkv_store(j - 2).wait()

        put_block(d_two.at[j % 2], 0, 0, dot(turned[...], d_qkv[:, wide_at(j)]))
        qkv_store(j).start()
        dx[...] += dot_nt(d_qkv[:, wide_at(j)], block_of(w_qkv, 0, D // ROWS, 2 * j, 2))

    count = 3 * D // WIDE
    busy_loop(count, project_back, events[3])
    load_x.wait()

    def input_back(at, s):
        value = dx[at, :]
        back, scaled = norm_back(tall_f[at, :], value, 1.0 + part(s, 1))
        add_mod(s, 0, rows_sum(value))
        add_mod(s, 1, rows_sum(scaled))
        grad[at, :] += back

    each_chunk(input_back)
    for j in (count - 2, count - 1):
        qkv_store(j).wait()
    mod_steps = 6 * D // WIDE

    def mod_back(j):
        @pl.when(j + 1 < mod_steps)
        def _():
            mod_load(j + 1).start()

        mod_load(j).wait()
        low = grad_mod[:, wide_at(j)].astype(low_type)
        cond[...] += dot_nt(low, block_of(w_1.at[j % 2], 0, D // ROWS, 0, 2))

    busy_loop(mod_steps, mod_back, events[4])
    put_samples(note, 0, grad_mod[...], samples)
    put_row(note, samples * MOD_CHUNKS, bias_out[...])
    put_samples(note, samples * MOD_CHUNKS + BIAS_ROWS, modulator[...].astype(full_type), samples)


MOD_CHUNKS = 6 * D // LANES
BIAS_ROWS = (4 * D + FF) // LANES
WIDTH = D // LANES
FREQ_CHUNKS = FREQ // LANES


def note_rows(samples):
    layer = samples * (MOD_CHUNKS + WIDTH) + BIAS_ROWS
    front = samples * (3 * WIDTH + FREQ_CHUNKS + 1) + WIDTH + ROWS * WIDTH
    return up(max(layer, front), ROWS)


def put_samples(stage, first, values, samples):
    for j in range(values.shape[1] // LANES):
        stage[first + j * samples : first + (j + 1) * samples, :] = values[0:samples, j * LANES : (j + 1) * LANES]


class Notes:
    def __init__(self, here, count, samples, owners, boxes, low, send_sem, recv_sem, own_sem):
        self.here, self.count, self.samples = here, count, samples
        self.owners, self.boxes, self.low = owners, boxes, low
        self.send_sem, self.recv_sem, self.own_sem = send_sem, recv_sem, own_sem

    def owned(self, i):
        first, last = self.owners[i]
        return (self.here.me >= first) & (self.here.me <= last)

    def copies(self, i):
        here = self.here
        first, last = self.owners[i]
        box = self.boxes[i].at[here.me]
        for to in range(first, last + 1):
            make = lambda to=to: remote(self.low.at[here.zero + i], box, pick(self.send_sem, here, i, to - first), pick(self.recv_sem, here, i), to)
            yield to, make

    def own(self, i):
        return pltpu.make_async_copy(self.low.at[self.here.zero + i], self.boxes[i].at[self.here.me], pick(self.own_sem, self.here, i))

    def send(self, i, stage):
        self.low[i] = stage[...].astype(low_type)
        for to, make in self.copies(i):
            pl.when(self.here.me != to)(lambda: make().start())
        pl.when(self.owned(i))(lambda: self.own(i).start())

    def receive(self, i):
        n = self.here.n
        arrived(self.boxes[i].at[pl.ds(0, n - 1)], pick(self.recv_sem, self.here, i))
        self.own(i).wait()

    def drain(self, count):
        for i in range(count):
            for to, make in self.copies(i):
                pl.when(self.here.me != to)(lambda: make().wait_send())


def all_samples(notes_f, count, n, samples, first, chunk):
    row = first + chunk * samples
    return jnp.concatenate([notes_f[pl.ds(row + s, n, stride=count), :] for s in range(samples)], axis=0)


def all_summed(notes_f, count, n, first, rows):
    def body(d, value):
        return value + notes_f[pl.ds(d * count + first, rows), :]

    return lax.fori_loop(0, n, body, jnp.zeros((rows, LANES), full_type))


def window(plan, chunks):
    return up(-(-plan.raw // chunks) + 1, 8)


def first_of_window(here, plan, base, chunks, depth):
    start = here.me * plan.share // LANES
    far = plan.length // LANES + 1
    first = (start - base + far * chunks) // chunks - far
    first = jnp.clip(first, -window(plan, chunks), depth)
    return first, first * chunks + base - (start - plan.margin)


def add_outer(here, plan, base, chunks, depth, rows_f, left_of, right_of):
    size = window(plan, chunks)
    first, row = first_of_window(here, plan, base, chunks, depth)
    left = left_of(first, size)
    near = (row >= 0) & (row + size * chunks <= rows_f.shape[0])

    @pl.when(near)
    def _():
        for c in range(chunks):
            rows_f[pl.ds(row + c, size, stride=chunks), :] += dot(left, right_of(c))


def add_rows(here, plan, base, rows_f, value):
    start = here.me * plan.share // LANES
    stop = (here.me + 1) * plan.share // LANES

    @pl.when((base >= start) & (base < stop))
    def _():
        rows_f[pl.ds(base - start + plan.margin, value.shape[0]), :] += value


def turned_left(turned, size, depth, chunk_of):
    turned[...] = jnp.zeros(turned.shape, full_type)
    for j in range(depth // LANES):
        turned[size + j * LANES : size + (j + 1) * LANES, :] = chunk_of(j).T
    return lambda first, count: turned[pl.ds(first + size, count), :].astype(low_type)


def layer_extra(here, plan, notes_f, count, n, samples, turned, rows_f):
    base = plan.segments[4][0]
    read = lambda first, chunk: all_samples(notes_f, count, n, samples, first, chunk)
    modulator_first = samples * MOD_CHUNKS + BIAS_ROWS
    left_of = turned_left(turned, window(plan, MOD_CHUNKS), D, lambda j: read(modulator_first, j))
    add_outer(here, plan, base, MOD_CHUNKS, D, rows_f, left_of, lambda c: read(0, c).astype(low_type))
    add_rows(here, plan, plan.segments[5][0], rows_f, all_summed(notes_f, count, n, samples * MOD_CHUNKS, BIAS_ROWS))
    mod_bias = jnp.concatenate([rows_sum(read(0, c)) for c in range(MOD_CHUNKS)], axis=0)
    add_rows(here, plan, plan.segments[10][0], rows_f, mod_bias)


def front_extra(here, plan, notes_f, count, n, samples, turned, rows_f):
    read = lambda first, chunk: all_samples(notes_f, count, n, samples, first, chunk)
    base = lambda number: plan.segments[number][0]
    g_cond, g_time = 0, samples * WIDTH
    act, basis, classes = 2 * samples * WIDTH, 3 * samples * WIDTH, samples * (3 * WIDTH + FREQ_CHUNKS)
    patch_bias = classes + samples
    add_rows(here, plan, base(0), rows_f, all_summed(notes_f, count, n, patch_bias + WIDTH, ROWS * WIDTH))
    add_rows(here, plan, base(1), rows_f, all_summed(notes_f, count, n, patch_bias, WIDTH))
    size = window(plan, WIDTH)
    low = lambda first: lambda c: read(first, c).astype(low_type)
    add_outer(here, plan, base(2), WIDTH, FREQ, rows_f, turned_left(turned, size, FREQ, lambda j: read(basis, j)), low(g_time))
    add_outer(here, plan, base(4), WIDTH, D, rows_f, turned_left(turned, size, D, lambda j: read(act, j)), low(g_cond))
    kind = read(classes, 0).T
    kind = kind[0:1, :] * CLASS_SPLIT + kind[HD : HD + 1, :]

    def picked(first, rows):
        line = lax.broadcasted_iota(jnp.int32, (rows, n * samples), 0) + first
        return (line.astype(full_type) == kind).astype(low_type)

    add_outer(here, plan, base(6), WIDTH, CLS, rows_f, picked, low(g_cond))
    for number, first in ((3, g_time), (5, g_cond)):
        value = jnp.concatenate([rows_sum(read(first, c)) for c in range(WIDTH)], axis=0)
        add_rows(here, plan, base(number), rows_f, value)


CLASS_SPLIT = 32


def owner_range(plan, numbers):
    first = plan.segments[numbers[0]][0] * LANES // plan.share
    stop = plan.segments[numbers[-1]]
    end = stop[0] * LANES + math.prod(stop[4])
    return first, min((end - 1) // plan.share, plan.devices - 1)


def held_whole(plan, numbers):
    for number in numbers:
        base, _, _, _, shape, _ = plan.segments[number]
        start, stop = base * LANES // plan.share, (base * LANES + math.prod(shape) - 1) // plan.share
        if start != stop or base < start * plan.share // LANES or base >= (start + 1) * plan.share // LANES:
            return False
    return True


SHARES = (1.0, 1.0, 0.2)
LAST_PHASE = LAYERS
WEIGHTS = (14, 3, 14, 8, 10)


def backward_kernel(plans, zs, rows, *refs):
    np_ = len(plans)
    feed = iter(refs)
    take = lambda count: tuple(next(feed) for _ in range(count))
    one = lambda: next(feed)
    root_grads = one()
    units = take(np_)
    stream = take(LAYERS)
    saved = [take(len(SAVED)) for _ in range(LAYERS)]
    grad_in, = take(1)
    mods = take(LAYERS)
    modulator, condition, time_pre, cond_in, noisy, basis, classes, stats_in = take(8)
    layer_grads = take(LAYERS)
    flats = take(np_)
    stats_out = one()
    first = take(np_)
    own_units = take(np_)
    halo_before, halo_after, boxes = take(np_), take(np_), take(np_)
    buffers = ((one(), one()), (one(), one()), (one(), one()), one(), one(), one(), one())
    total, total_in = take(2)
    sems = take(9)
    frees = take(3)
    load_sem, chunk_sem, out_sem, own_sem, halo_s, halo_r, ss, sr, note_s, note_r, note_own = take(11)
    note, note_low = take(2)
    here = Place(zs)
    here.greet()
    root = plans[0]
    samples = rows // SEQ
    layers = list(reversed(range(LAYERS)))
    planes = lambda p: min(zs, -(-p.segments[4][3] // (8 * p.per)))
    buckets = [(root, root_grads, 0, zs)]
    buckets += [(plans[1 + i], layer_grads[i], 0, planes(plans[1 + i])) for i in layers]
    outs = [own_units[0]] + [own_units[1 + i] for i in layers]
    owners = [owner_range(root, range(FRONT))] + [owner_range(p, range(4, 11)) for p in plans[1:]]
    notes = Notes(here, note.shape[0], samples, owners, boxes, note_low, note_s, note_r, note_own)
    hosts = sorted({d for lo, hi in owners for d in range(lo, hi + 1)})
    hosting = functools.reduce(lambda a, b: a | b, [notes.owned(i) for i in range(np_)])

    @pl.when(hosting)
    def _():
        for to in range(here.n):

            @pl.when(here.me != to)
            def _():
                pl.semaphore_signal(pltpu.get_barrier_semaphore(), inc=1, device_id=(to,), device_id_type=MESH)

    pl.semaphore_wait(pltpu.get_barrier_semaphore(), len(here.peers()) + len(hosts) - hosting.astype(jnp.int32))
    work = Reduce(here, buckets, first, buffers, sems, frees)
    work.open(0)
    steps = [work.steps(g, outs, own_sem) for g in range(len(work.groups) + LOOK + 2)]
    flat = [(g, step) for g, group in enumerate(steps) for step in group]
    upto = lambda b: sum(len(group) for group in steps[: b * zs])
    cuts = [0]
    for position, share in enumerate(SHARES):
        cuts.append(max(cuts[-1], upto(position) + int(share * (upto(position + 1) - upto(position)))))
    of_phase = lambda p: [step for _, step in flat[cuts[p] : cuts[p + 1]]]

    def compute(grad, cond, *held):
        grad[...] = grad_in[...]
        cond[...] = cond_in[...]
        for position, ordinal in enumerate(layers):
            layer_backward_body(
                plans[1 + ordinal], rows, stream[ordinal], saved[ordinal], units[1 + ordinal], layer_grads[ordinal],
                mods[ordinal], grad, modulator, cond, note, samples, held, (load_sem, chunk_sem, out_sem), spread(of_phase(position), WEIGHTS),
            )
            work.open(1 + position)
            notes.send(1 + ordinal, note)
        embed_back(grad, cond)

    def embed_back(grad, cond):
        def run(front_w):
            load = pltpu.make_async_copy(units[0].at[pl.ds(root.segments[4][3], root.segments[4][2])], front_w, load_sem.at[0])
            load.start()
            events = spread(of_phase(LAYERS), (1, 1))
            low = grad[...].astype(low_type)
            patch = dot_tn(noisy[...], low)
            at = samples * (3 * WIDTH + FREQ_CHUNKS)
            note[at : at + samples, :] = classes[0:samples, :]
            put_row(note, at + samples, rows_sum(low.astype(full_type)))
            for c in range(WIDTH):
                note[pl.ds(at + samples + WIDTH + c, ROWS, stride=WIDTH), :] = patch[:, c * LANES : (c + 1) * LANES]
            for event in events[0]:
                event()
            g_low = (silu_parts(condition[...])[1] * cond[...]).astype(low_type)
            act, slope = silu_parts(time_pre[...])
            load.wait()
            w_t2 = jnp.concatenate(
                [jnp.concatenate([front_w[b * WIDTH + c] for b in range(D // ROWS)], axis=0) for c in range(WIDTH)], axis=1
            )
            grad_pre = dot_nt(g_low, w_t2) * slope
            put_samples(note, 0, g_low.astype(full_type), samples)
            put_samples(note, samples * WIDTH, grad_pre, samples)
            put_samples(note, 2 * samples * WIDTH, act, samples)
            put_samples(note, 3 * samples * WIDTH, basis[...].astype(full_type), samples)
            notes.send(0, note)
            for event in events[1]:
                event()

        pl.run_scoped(run, pltpu.VMEM((root.segments[4][2], ROWS, LANES), low_type))

    plan = plans[1]
    f32 = lambda *dims: pltpu.VMEM(dims, full_type)
    bf16 = lambda *dims: pltpu.VMEM(dims, low_type)
    tile = (ROWS, LANES)
    few = modulator.shape[0]
    pl.run_scoped(
        compute,
        f32(rows, D), f32(few, D),
        bf16(rows, 3 * D), bf16(rows, D), bf16(rows, D), f32(rows, D), f32(rows, D), f32(2, rows, WIDE),
        bf16(2, D // ROWS, 2, *tile), bf16(2, WIDE // ROWS, D // LANES, *tile),
        segment_scratch(plan, 0), segment_scratch(plan, 1),
        bf16(rows, 3 * D), bf16(rows, D), bf16(rows, WIDE), bf16(D, rows), f32(rows, D),
        bf16(2, WIDE // ROWS, D // LANES, *tile), bf16(2, D // ROWS, 2, *tile),
        f32(few, 6 * D), f32(1, 4 * D + FF),
    )

    def unpack(units_f, rows_f, flat_f, box, notes_f, *turned):
        def halo(i):
            p = plans[i]
            forward = remote(own_units[i].at[pl.ds(p.per - p.units_before, p.units_before)], halo_before[i], halo_s.at[i, 0], halo_r.at[i, 0], here.following)
            backward = remote(own_units[i].at[pl.ds(0, p.units_after)], halo_after[i], halo_s.at[i, 1], halo_r.at[i, 1], here.prev)
            return forward, backward

        def finish(i):
            p = plans[i]
            base = p.units_before
            for copy in halo(i):
                copy.wait()
            parts = (
                pltpu.make_async_copy(halo_before[i], units_f.at[pl.ds(0, base)], load_sem.at[0]),
                pltpu.make_async_copy(own_units[i], units_f.at[pl.ds(base, p.per)], load_sem.at[1]),
                pltpu.make_async_copy(halo_after[i], units_f.at[pl.ds(base + p.per, p.units_after)], load_sem.at[2]),
            )
            for copy in parts:
                copy.start()
            for copy in parts:
                copy.wait()
            rows_f[...] = jnp.zeros(rows_f.shape, full_type)

            @pl.when(notes.owned(i))
            def _():
                notes.receive(i)
                copy = pltpu.make_async_copy(boxes[i], box, load_sem.at[4])
                copy.start()
                copy.wait()
                count = box.shape[1]

                def widen(d):
                    notes_f[pl.ds(pl.multiple_of(d * count, ROWS), count), :] = box[d].astype(full_type)

                loop(here.n, widen)
                extra = layer_extra if i else front_extra
                extra(here, p, notes_f, count, here.n, samples, turned[1 if i else 0], rows_f)

            squares = unpack_rows(here, p, p.reduced, units_f, rows_f, flat_f, base)
            store = pltpu.make_async_copy(flat_f.at[pl.ds(0, p.raw)], flats[i], load_sem.at[3])
            store.start()
            store.wait()
            total[1] += squares

        total[0] = stats_in[...]
        total[1] = jnp.zeros((8, LANES), full_type)
        ready = [0] + [1 + ordinal for ordinal in layers]
        begun, done = {}, set()

        def between(g):
            for b, i in enumerate(ready):
                if i not in begun and g > zs * (b + 1) + LOOK + 1:
                    begun[i] = g
                    for copy in halo(i):
                        copy.start()
                elif i in begun and i not in done and g > begun[i]:
                    done.add(i)
                    finish(i)
                    return

        seen = -1
        for g, step in flat[cuts[-1] :]:
            if g != seen and g > LAST_PHASE * zs:
                between(g)
            seen = g
            step()
        for extra in range(2 * len(ready)):
            between(len(steps) + extra)

    most = max(p.units_before + p.per + p.units_after for p in plans)
    pl.run_scoped(
        unpack,
        f32(most, *tile), f32(max(max(p.spread, p.margin + c * window(p, c)) for p in plans for c in (WIDTH, MOD_CHUNKS)), LANES),
        f32(max(p.raw for p in plans), LANES),
        pltpu.VMEM(boxes[0].shape, low_type), f32(boxes[0].shape[0] * boxes[0].shape[1], LANES),
        f32(D + 2 * window(root, WIDTH), samples * here.n), f32(D + 2 * window(plan, MOD_CHUNKS), samples * here.n),
    )
    step = 0
    for to in ((here.cpeer,), (here.xpeer,), (here.ypeer,), tuple(here.above(k) for k in range(1, zs))):
        copies = []
        for peer in to:
            copies.append(remote(total, total_in.at[step], ss.at[step], sr.at[step], peer))
            copies[-1].start()
            step += 1
        for copy in copies:
            copy.wait()
        value = total[...]
        for i in range(len(to)):
            value = value + total_in[step - 1 - i]
        total[...] = value
    stats_out[...] = total[...]
    notes.drain(np_)
    work.close()


def backward_call(plans, units, stream, saved, grad, mods, small, stats, root_grads):
    n = plans[0].devices
    zs = n // 8
    rows = grad.shape[0]
    np_ = nb = len(plans)
    count = note_rows(rows // SEQ)
    vm = pl.BlockSpec(memory_space=pltpu.VMEM)
    hbm = pl.BlockSpec(memory_space=pltpu.HBM)
    shape = jax.ShapeDtypeStruct
    dma, regular = pltpu.SemaphoreType.DMA, pltpu.SemaphoreType.REGULAR
    tile = (ROWS, LANES)
    layers = list(reversed(range(LAYERS)))
    order = [plans[0]] + [plans[1 + i] for i in layers]
    all_units = lambda p: shape((n * p.per,) + tile, low_type)
    out_shape = [all_units(p) for p in plans[1:]]
    out_shape += [shape((p.raw, LANES), full_type) for p in plans]
    out_shape += [shape((2, 8, LANES), full_type)]
    out_shape += [shape((zs, 2, 2, p.per) + tile, low_type) for p in order]
    out_shape += [shape((p.per,) + tile, full_type) for p in plans]
    out_shape += [shape((p.units_before,) + tile, full_type) for p in plans]
    out_shape += [shape((p.units_after,) + tile, full_type) for p in plans]
    out_shape += [shape((n, count, LANES), low_type) for p in plans]
    most = max(p.per for p in plans)
    half = lambda *lead: pltpu.VMEM(lead + (most // 2,) + tile, low_type)
    hops = 2 + zs
    scratch = [half(zs, 2)] * 4 + [half(zs)] * 2 + [half(2, 2, zs - 1)]
    scratch += [pltpu.VMEM((3 * LOOK + 4, most) + tile, low_type), pltpu.VMEM((2, most) + tile, low_type)]
    scratch += [pltpu.VMEM((most,) + tile, full_type)]
    scratch += [pltpu.VMEM((2, 8, LANES), full_type), pltpu.VMEM((hops, 2, 8, LANES), full_type)]
    scratch += [dma((nb, zs, 2, 2))] * 2 + [dma((2, zs, 2))] * 2 + [dma((2, zs))] * 2 + [dma((2, 2, zs - 1))] * 2 + [dma((3 * LOOK + 4, 2))]
    scratch += [regular((2, zs)), regular((2, zs)), regular((zs - 1,))]
    scratch += [dma((7,)), dma((2, 3)), dma((4,)), dma, dma((np_, 2)), dma((np_, 2)), dma((hops,)), dma((hops,))]
    scratch += [dma((np_, n)), dma((np_,)), dma((np_,))]
    scratch += [pltpu.VMEM((count, LANES), full_type), pltpu.VMEM((np_, count, LANES), low_type)]
    flat_saved = [array for group in saved for array in group]
    results = pl.pallas_call(
        functools.partial(backward_kernel, plans, zs, rows),
        out_shape=out_shape,
        in_specs=[hbm] * (1 + np_ + LAYERS + len(flat_saved)) + [vm] * (1 + LAYERS + len(small) + 1),
        out_specs=[hbm] * (2 * np_ - 1) + [vm] + [hbm] * (nb + 4 * np_),
        scratch_shapes=scratch,
        compiler_params=pltpu.CompilerParams(collective_id=1, has_side_effects=True, vmem_limit_bytes=62 * MB),
        name="backward_and_reduce",
    )(root_grads, *units, *stream, *flat_saved, grad, *mods, *small, stats)
    return results[np_ - 1 : 2 * np_ - 1], results[2 * np_ - 1]


def model_step(layer_lists, pieces, latents, noise, times, labels, dropped, features, devices):
    sample_total = latents.shape[0] * devices
    residual, modulator, embed_saved = embed_forward(
        pieces, latents, noise, times, labels, dropped
    )
    loss_total = jnp.zeros((), full_type)
    inputs, kept, square_sums = [], [], []
    for ordinal in range(LAYERS):
        inputs.append(residual)
        residual, saved, sums = layer_forward(layer_lists[ordinal], residual, modulator)
        kept.append(saved)
        square_sums.append(sums)
        if ordinal + 1 == DEPTH_Z:
            part, proj_saved = projector_forward(pieces, residual, features)
            loss_total = loss_total + part
    target = noise - latents
    weight_t = 1.0 + 2.0 * times
    part, head_saved = head_forward(pieces, residual, modulator, target, weight_t)
    loss_total = loss_total + part
    grad_residual, grad_cond, head_grads = head_backward(
        pieces, head_saved, residual, modulator, weight_t, sample_total
    )
    layer_grads = [None] * LAYERS
    for ordinal in reversed(range(LAYERS)):
        if ordinal + 1 == DEPTH_Z:
            grad_proj, proj_grads = projector_backward(
                pieces, proj_saved, features, residual.shape[1], sample_total
            )
            grad_residual = grad_residual + grad_proj
        grad_residual, cond_part, layer_grads[ordinal] = layer_backward(
            layer_lists[ordinal], kept[ordinal], inputs[ordinal], modulator, grad_residual
        )
        grad_cond = grad_cond + cond_part
    embed_grads = embed_backward(pieces, embed_saved, grad_residual, grad_cond)
    return (loss_total, jnp.stack(square_sums), layer_grads, embed_grads + proj_grads + head_grads)


def adam_update(weight, grad, first, second, clip_factor):
    clipped = grad * clip_factor
    first_new = beta_one * first + (1.0 - beta_one) * clipped
    second_new = beta_two * second + (1.0 - beta_two) * clipped * clipped
    first_hat = first_new / (1.0 - beta_one**STEP)
    second_hat = second_new / (1.0 - beta_two**STEP)
    weight_new = weight - learn_rate * (
        first_hat / (jnp.sqrt(second_hat) + adam_eps) + decay_rate * weight
    )
    return (weight_new, first_new, second_new)


def vector_of(units, plan, number):
    _, _, count, first, shape, _ = plan.segments[number]
    flat = units[first : first + count].reshape(-1)[: math.prod(shape)]
    return flat.reshape(shape)


def matrix_of(units, plan, number):
    _, chunks, count, first, shape, _ = plan.segments[number]
    part = units[first : first + count].reshape(shape[0] // ROWS, chunks, ROWS, LANES)
    return part.transpose(0, 2, 1, 3).reshape(shape)


def units_of(grad, plan, number):
    _, chunks, count, _, shape, matrix = plan.segments[number]
    low = grad.astype(low_type)
    if matrix:
        low = low.reshape(shape[0] // ROWS, ROWS, chunks, LANES).transpose(0, 2, 1, 3)
        return low.reshape(count, ROWS, LANES)
    flat = jnp.pad(low.reshape(-1), ((0, count * UNIT - low.size),))
    return flat.reshape(count, ROWS, LANES)


def put_units(grads, plan, first_number, values):
    parts = [units_of(value, plan, first_number + i) for i, value in enumerate(values)]
    joined = jnp.concatenate(parts) if len(parts) > 1 else parts[0]
    return lax.dynamic_update_slice(grads, joined, (plan.segments[first_number][3], 0, 0))


def as_row(vector):
    return vector.astype(full_type).reshape(1, -1)


def by_kernels(plan, root_plan, layer_flat, root_flat, data, devices):
    latents, noise, times, labels, dropped, features = data
    samples = latents.shape[0]
    sample_total = samples * devices
    rows = samples * SEQ
    few = up(samples, ROWS)
    wide = D // LANES
    plans = (root_plan,) + (plan,) * LAYERS
    padded = jnp.pad(layer_flat, ((0, 0), (0, plan.raw * LANES - plan.share)))
    turns = padded.reshape(LAYERS, plan.raw, LANES).transpose(1, 0, 2).reshape(LAYERS * plan.raw, LANES)
    raws = [to_rows(root_flat, root_plan), turns]
    mixing = times[:, None, None]
    noisy_bf = ((1.0 - mixing) * latents + mixing * noise).astype(low_type)
    positions = jnp.tile(position_table(), (samples, 1))
    basis_bf = time_features(times).astype(low_type)
    classes = jnp.where(dropped == 1, CLS - 1, labels)
    extra = lambda value: jnp.pad(value, ((0, few - samples),) + ((0, 0),) * (value.ndim - 1))
    wanted = jnp.pad(classes, (0, few - samples), constant_values=-1)
    wanted = jnp.where(wanted < 0, -wide, wanted * wide)[None, :] + jnp.arange(wide)[:, None]
    wanted = jnp.where(wanted < 0, -1, wanted).reshape(-1, 1)
    table_rows = root_plan.segments[6][2] * ROWS
    chosen = (wanted == jnp.arange(table_rows, dtype=jnp.int32)[None, :]).astype(low_type)
    units, stream, mods, sums, modulator_rows, condition, time_pre, kept = forward_call(
        plans, raws, noisy_bf.reshape(rows, PD), positions, extra(basis_bf), chosen
    )
    root_units, *layer_units = units
    residual = stream[-1]
    target = jnp.pad((noise - latents).reshape(rows, PD), ((0, 0), (0, LANES - PD)))
    weight_t = jnp.broadcast_to(jnp.pad(1.0 + 2.0 * times, (0, 8 - samples))[:, None], (8, LANES))
    w_h = jnp.pad(vector_of(root_units, root_plan, 15), ((0, 0), (0, LANES - PD)))
    b_h = jnp.pad(as_row(vector_of(root_units, root_plan, 16)), ((0, 0), (0, LANES - PD)))
    biases = [as_row(vector_of(root_units, root_plan, i)) for i in (8, 10, 12, 14)]
    grad, losses, grad_cond, bias_grads, grad_w_h, root_grads = top_call(
        root_plan, sample_total, residual, features.reshape(rows, ZD), target, weight_t, modulator_rows, biases, w_h, b_h, root_units
    )
    loss_part = -proj_coeff / SEQ * losses[0, 0] + jnp.sum(losses[1]) / (SEQ * PD)
    cuts = jnp.split(bias_grads[0], (PH, 2 * PH, 2 * PH + ZD, 2 * PH + ZD + 2 * D))
    for number, value in zip((8, 10, 12), cuts):
        root_grads = put_units(root_grads, root_plan, number, [value])
    root_grads = put_units(root_grads, root_plan, 14, [cuts[3], grad_w_h[:, :PD], cuts[4][:PD]])
    square_sums = jnp.stack([jnp.sum(total[:3], axis=1) for total in sums])
    numbers = jnp.concatenate([loss_part[None], square_sums.reshape(-1)])
    stats = jnp.pad(numbers, (0, 8 * LANES - numbers.shape[0])).reshape(8, LANES)
    class_parts = jnp.stack([classes // CLASS_SPLIT, classes % CLASS_SPLIT], axis=1)
    class_rows = extra(jnp.repeat(class_parts.astype(full_type), LANES // 2, axis=1))
    small = (modulator_rows, condition, time_pre, grad_cond, noisy_bf.reshape(rows, PD), extra(basis_bf), class_rows)
    rows_out, stats = backward_call(
        plans, units, stream[:-1], kept, grad, mods, small, stats, root_grads
    )
    numbers = stats[0].reshape(-1)
    shard_root = rows_out[0].reshape(-1)[: root_plan.share]
    shard_layers = jnp.stack([r.reshape(-1)[: plan.share] for r in rows_out[1:]])
    stream_sums = numbers[1 : 1 + 3 * LAYERS].reshape(LAYERS, 3)
    return (shard_layers, shard_root, numbers[0], stream_sums, jnp.sum(stats[1]))


def by_collectives(layer_flat, root_flat, data, devices):
    whole = lambda part: lax.all_gather(part.astype(low_type), "fsdp", axis=0, tiled=True)
    layer_lists = [unflatten(whole(layer_flat[i]), layer_layout()) for i in range(LAYERS)]
    pieces = unflatten(whole(root_flat), root_layout())
    loss_part, square_sums, layer_grads, root_grads = model_step(
        layer_lists, pieces, *data, devices
    )

    def owned(grad_list, share):
        joined = jnp.concatenate([piece.reshape(-1) for piece in grad_list])
        joined = jnp.pad(joined, (0, share * devices - joined.shape[0]))
        return lax.psum_scatter(joined, "fsdp", scatter_dimension=0, tiled=True)

    shard_layers = jnp.stack([owned(grads, layer_flat.shape[1]) for grads in layer_grads])
    shard_root = owned(root_grads, root_flat.shape[0])
    local = jnp.sum(shard_layers * shard_layers) + jnp.sum(shard_root * shard_root)
    loss_sum, sums, square_total = lax.psum((loss_part, square_sums, local), "fsdp")
    return (shard_layers, shard_root, loss_sum, sums, square_total)


def shards(
    latents,
    noise,
    times,
    labels,
    dropped,
    features,
    layer_flat,
    layer_mean,
    layer_square,
    root_flat,
    root_mean,
    root_square,
):
    devices = lax.axis_size("fsdp")
    data = (latents, noise, times, labels, dropped, features)
    plan = Plan(layer_layout(), layer_flat.shape[1] * devices, devices, (0, 4))
    root_plan = Plan(root_layout(), root_flat.shape[0] * devices, devices, (FRONT, None))
    alone = held_whole(plan, range(5, 11)) and held_whole(root_plan, (0, 1, 3, 5))
    if devices % 8 == 0 and plan.fits and root_plan.fits and alone:
        reduced = by_kernels(plan, root_plan, layer_flat, root_flat, data, devices)
    else:
        reduced = by_collectives(layer_flat, root_flat, data, devices)
    shard_layers, shard_root, loss_sum, stream_sums, square_total = reduced
    sample_total = latents.shape[0] * devices
    grad_norm = jnp.sqrt(square_total)
    clip_factor = clip_limit / jnp.maximum(grad_norm, clip_limit)
    activation_rms = jnp.sqrt(stream_sums / (sample_total * SEQ * D))
    new_layer, new_layer_mean, new_layer_square = adam_update(
        layer_flat, shard_layers, layer_mean, layer_square, clip_factor
    )
    new_root, new_root_mean, new_root_square = adam_update(
        root_flat, shard_root, root_mean, root_square, clip_factor
    )
    return (
        loss_sum,
        grad_norm,
        activation_rms,
        new_layer,
        new_layer_mean,
        new_layer_square,
        new_root,
        new_root_mean,
        new_root_square,
    )


def solution(mesh):
    in_specs = (
        P("fsdp", None, None),
        P("fsdp", None, None),
        P("fsdp"),
        P("fsdp"),
        P("fsdp"),
        P("fsdp", None, None),
        P(None, "fsdp"),
        P(None, "fsdp"),
        P(None, "fsdp"),
        P("fsdp"),
        P("fsdp"),
        P("fsdp"),
    )
    out_specs = (
        P(),
        P(),
        P(),
        P(None, "fsdp"),
        P(None, "fsdp"),
        P(None, "fsdp"),
        P("fsdp"),
        P("fsdp"),
        P("fsdp"),
    )
    return jax.shard_map(shards, mesh=mesh, in_specs=in_specs, out_specs=out_specs, check_vma=False)
```
